32 devices in a mesh: rows: 8 (over z, x), lon: 4 (over y, core).
Axes of the slice: x: 2, y: 2, z: 4, core: 2. Of those that a mesh axis runs over, the one named last changes fastest.
Arguments:
- tokens: bfloat16 [96, 180, 768], P('rows', 'lon'), may hold values from -6 to 6
- row_map: int32 [96], replicated, may hold values from -1 to 89, as said below
- cotangent: bfloat16 [96, 180, 768], P('rows', 'lon'), may hold values from -6 to 6
- norm_gain: float32 [768], replicated, may hold values from 0.1 to 1.9
- norm_shift: float32 [768], replicated, may hold values from -3 to 3
- mix_in: bfloat16 [2, 8, 96, 96], replicated, may hold values from -0.4375 to 0.4375
- mix_in_bias: float32 [2, 8, 96], replicated, may hold values from -3 to 3
- mix_out: bfloat16 [2, 8, 96, 96], replicated, may hold values from -1 to 1
- mix_out_bias: float32 [2, 8, 96], replicated, may hold values from -0.12 to 0.12
- post_gain: float32 [768], replicated, may hold values from 0.1 to 1.9
- post_shift: float32 [768], replicated, may hold values from -3 to 3
- fc_in: bfloat16 [768, 3072], replicated, may hold values from -0.21875 to 0.21875
- fc_in_bias: float32 [3072], replicated, may hold values from -3 to 3
- fc_out: bfloat16 [3072, 768], replicated, may hold values from -0.109375 to 0.109375
- fc_out_bias: float32 [768], replicated, may hold values from -3 to 3
Outputs:
- block_output: bfloat16 [96, 180, 768], P('rows', 'lon')
- tokens_grad: float32 [96, 180, 768], P('rows', 'lon')
- norm_gain_grad: float32 [768], replicated
- norm_shift_grad: float32 [768], replicated
- mix_in_grad: float32 [2, 8, 96, 96], replicated
- mix_in_bias_grad: float32 [2, 8, 96], replicated
- mix_out_grad: float32 [2, 8, 96, 96], replicated
- mix_out_bias_grad: float32 [2, 8, 96], replicated
- post_gain_grad: float32 [768], replicated
- post_shift_grad: float32 [768], replicated
- fc_in_grad: float32 [768, 3072], P(None, ('rows', 'lon'))
- fc_in_bias_grad: float32 [3072], P(('rows', 'lon'))
- fc_out_grad: float32 [3072, 768], P(('rows', 'lon'))
- fc_out_bias_grad: float32 [768], replicated
The draws below stay inside these ranges and needn't reach their ends.
Inputs may be any that keep to these rules, and one draw needn't show every extreme that they name: `row_map`: every field-row number below 90 stands in exactly one slot; all other slots hold -1. Field-row q is latitude q mod 90 of field q // 90.
All inputs are finite; a program needn't handle non-finite values.
Results may differ from the reference program's by a relative error of at most 0.015.
The reference program's roundings to bfloat16 on the way count: a program that leaves them out, or rounds other values in their place, can miss the bound.
Values may be sent and summed in bfloat16 or wider, within the bound.
A program may use at most 192 MiB of HBM per device.

```python
import math
import jax
import jax.numpy as jnp
from jax import lax

C = 768
NBLK = 8
BS = 96
FF = 3072
H = 90
W = 180
SLOTS = 96
IMG = 1
KX = 91


def draw_row_map(key, part):
    key = jax.random.fold_in(key, 11)
    ordering = jax.random.permutation(key, SLOTS)
    return jnp.where(ordering < IMG * H, ordering, -1).astype(jnp.int32)


def draw_mix_out(key, part):
    key = jax.random.fold_in(key, 23)
    column_key = jax.random.fold_in(key, 1)
    entry_key = jax.random.fold_in(key, 2)
    column_log = jax.random.uniform(column_key, (1, NBLK, 1, BS), jnp.float32, math.log(0.01), 0.0)
    column_scale = jnp.exp(column_log)
    base = jnp.clip(jax.random.normal(entry_key, (2, NBLK, BS, BS), jnp.float32), -3.5, 3.5)
    scaled = base * column_scale * (1.0 / math.sqrt(2.0 * BS))
    return scaled.astype(jnp.bfloat16)


def shard_levels(rng, shape, split, low, high):
    factor_of = 1.0
    for dim, blocks in split:
        steps = jax.random.uniform(jax.random.fold_in(jax.random.fold_in(rng, 6), dim), (blocks,), jnp.float32, low / len(split), high / len(split))
        factor_of = factor_of * jnp.repeat(jnp.exp(steps), shape[dim] // blocks).reshape((-1,) + (1,) * (len(shape) - 1 - dim))
    return factor_of


def normal_values(rng, extent, scale, limit, cuts=(), kind=jnp.bfloat16):
    factor_of = shard_levels(rng, extent, cuts, -0.22, 0.18) if cuts else 1.0
    array = jax.random.normal(rng, extent, jnp.float32) * scale * factor_of
    return jnp.minimum(jnp.maximum(array, -limit), limit).astype(kind)


def setup_inputs(seed: int = 0) -> dict:
    streams_of = jax.random.split(jax.random.key(seed), 16)
    return {
        "tokens": normal_values(streams_of[0], (SLOTS, W, C), 1.0, 6.0, ((0, 8), (1, 4))),
        "row_map": draw_row_map(jax.random.fold_in(streams_of[15], 71), 0),
        "cotangent": normal_values(streams_of[2], (SLOTS, W, C), 1.0, 6.0, ((0, 8), (1, 4))),
        "norm_gain": jnp.clip(1.0 + 0.18 * jax.random.normal(streams_of[3], (C,), jnp.float32), 0.1, 1.9),
        "norm_shift": normal_values(streams_of[4], (C,), 0.5, 3.0, (), jnp.float32),
        "mix_in": normal_values(streams_of[5], (2, NBLK, BS, BS), (2 * BS) ** -0.5, 0.4375),
        "mix_in_bias": normal_values(streams_of[6], (2, NBLK, BS), 0.5, 3.0, (), jnp.float32),
        "mix_out": draw_mix_out(jax.random.fold_in(streams_of[15], 71), 0),
        "mix_out_bias": normal_values(streams_of[8], (2, NBLK, BS), 0.02, 0.12, (), jnp.float32),
        "post_gain": jnp.clip(1.0 + 0.18 * jax.random.normal(streams_of[9], (C,), jnp.float32), 0.1, 1.9),
        "post_shift": normal_values(streams_of[10], (C,), 0.5, 3.0, (), jnp.float32),
        "fc_in": normal_values(streams_of[11], (C, FF), C ** -0.5, 0.21875),
        "fc_in_bias": normal_values(streams_of[12], (FF,), 0.5, 3.0, (), jnp.float32),
        "fc_out": normal_values(streams_of[13], (FF, C), FF ** -0.5, 0.109375),
        "fc_out_bias": normal_values(streams_of[14], (C,), 0.5, 3.0, (), jnp.float32),
    }


@jax.custom_vjp
def low(v):
    return lax.optimization_barrier(v.astype(jnp.bfloat16)).astype(jnp.float32)

@jax.custom_vjp
def low_back(v):
    return v

def low_keep(v):
    return (low(v), None)

def low_pass(kept, grad):
    return (grad,)

def back_keep(v):
    return (v, None)

def back_low(kept, grad):
    return (low(grad),)
low.defvjp(low_keep, low_pass)
low_back.defvjp(back_keep, back_low)
norm_eps = 1e-06
shrink_level = 0.01
highest = lax.Precision.HIGHEST

def layer_norm(values, gain_row, shift_row):
    center = values - lax.optimization_barrier(jnp.mean(values, axis=-1, keepdims=True))
    spread = lax.rsqrt(lax.optimization_barrier(jnp.mean(center * center, axis=-1, keepdims=True)) + norm_eps)
    return center * spread * gain_row + shift_row

def smooth_gate(values):
    return jax.nn.gelu(values, approximate=False)

def soft_shrink(values):
    return values - shrink_level * values * lax.rsqrt(values * values + shrink_level * shrink_level)

def make_tables():
    lon_index = jnp.arange(W, dtype=jnp.int32)
    wave_index = jnp.arange(KX, dtype=jnp.int32)
    angle = (lon_index[:, None] * wave_index[None, :] % W).astype(jnp.float32) * (2.0 * math.pi / W)
    scale = 1.0 / math.sqrt(W)
    lon_cos = (jnp.cos(angle) * scale).astype(jnp.bfloat16).astype(jnp.float32)
    lon_sin = (-jnp.sin(angle) * scale).astype(jnp.bfloat16).astype(jnp.float32)
    factor = jnp.where((wave_index == 0) | (wave_index == W // 2), 1.0, 2.0).astype(jnp.float32)
    inv_cos = factor[:, None] * lon_cos.T
    inv_sin = factor[:, None] * lon_sin.T
    lat_index = jnp.arange(H, dtype=jnp.int32)
    lat_angle = (lat_index[:, None] * lat_index[None, :] % H).astype(jnp.float32) * (2.0 * math.pi / H)
    lat_scale = 1.0 / math.sqrt(H)
    lat_cos = (jnp.cos(lat_angle) * lat_scale).astype(jnp.bfloat16).astype(jnp.float32)
    lat_sin = (jnp.sin(lat_angle) * lat_scale).astype(jnp.bfloat16).astype(jnp.float32)
    return (lon_cos, lon_sin, inv_cos, inv_sin, lat_cos, lat_sin)

def complex_mix(real_part, imag_part, weight, bias):
    leading = real_part.shape[:-1]
    real_blocks = real_part.reshape(leading + (NBLK, BS))
    imag_blocks = imag_part.reshape(leading + (NBLK, BS))

    def block_product(values, matrix):
        return jnp.einsum('...bk,bkj->...bj', values, matrix, precision=highest).reshape(real_part.shape)
    real_out = block_product(real_blocks, weight[0]) - block_product(imag_blocks, weight[1]) + bias[0].reshape(C)
    imag_out = block_product(imag_blocks, weight[0]) + block_product(real_blocks, weight[1]) + bias[1].reshape(C)
    return (real_out, imag_out)

def one_image(params, tables, image):
    norm_gain, norm_shift, mix_in, mix_in_bias, mix_out, mix_out_bias, post_gain, post_shift, fc_in, fc_in_bias, fc_out, fc_out_bias = params
    lon_cos, lon_sin, inv_cos, inv_sin, lat_cos, lat_sin = tables
    normed = layer_norm(image, norm_gain, norm_shift)
    normed_low = low(normed)
    lon_real = low(low_back(jnp.einsum('lwc,wk->lkc', normed_low, lon_cos, precision=highest)))
    lon_imag = low(low_back(jnp.einsum('lwc,wk->lkc', normed_low, lon_sin, precision=highest)))
    lat_real = low(low_back(jnp.einsum('yl,lkc->ykc', lat_cos, lon_real, precision=highest) + jnp.einsum('yl,lkc->ykc', lat_sin, lon_imag, precision=highest)))
    lat_imag = low(low_back(jnp.einsum('yl,lkc->ykc', lat_cos, lon_imag, precision=highest) - jnp.einsum('yl,lkc->ykc', lat_sin, lon_real, precision=highest)))
    inner_real, inner_imag = complex_mix(lat_real, lat_imag, mix_in, mix_in_bias)
    gated_real = low(smooth_gate(low_back(inner_real)))
    gated_imag = low(smooth_gate(low_back(inner_imag)))
    outer_real, outer_imag = complex_mix(gated_real, gated_imag, mix_out, mix_out_bias)
    shrunk_real = low(low_back(soft_shrink(low_back(outer_real))))
    shrunk_imag = low(low_back(soft_shrink(low_back(outer_imag))))
    back_real = low(low_back(jnp.einsum('yl,ykc->lkc', lat_cos, shrunk_real, precision=highest) - jnp.einsum('yl,ykc->lkc', lat_sin, shrunk_imag, precision=highest)))
    back_imag = low(low_back(jnp.einsum('yl,ykc->lkc', lat_cos, shrunk_imag, precision=highest) + jnp.einsum('yl,ykc->lkc', lat_sin, shrunk_real, precision=highest)))
    filtered = low_back(jnp.einsum('lkc,kw->lwc', back_real, inv_cos, precision=highest) + jnp.einsum('lkc,kw->lwc', back_imag, inv_sin, precision=highest))
    residual = filtered + normed + image
    post_normed = low(layer_norm(residual, post_gain, post_shift)).reshape(-1, C)
    hidden = low(smooth_gate(low_back(jnp.dot(post_normed, fc_in, precision=highest) + fc_in_bias)))
    return residual + (jnp.dot(hidden, fc_out, precision=highest) + fc_out_bias).reshape(residual.shape)

def reference(tokens, row_map, cotangent, norm_gain, norm_shift, mix_in, mix_in_bias, mix_out, mix_out_bias, post_gain, post_shift, fc_in, fc_in_bias, fc_out, fc_out_bias):
    field_rows = IMG * H
    slot_live = row_map >= 0
    target = jnp.where(slot_live, row_map, field_rows).astype(jnp.int32)
    slot_of_row = jnp.zeros((field_rows,), jnp.int32).at[target].set(jnp.arange(SLOTS, dtype=jnp.int32), mode='drop')
    row_index = jnp.where(slot_live, row_map, 0).astype(jnp.int32)
    grid = tokens.astype(jnp.float32)[slot_of_row].reshape(IMG, H, W, C)
    cot_grid = cotangent.astype(jnp.float32)[slot_of_row].reshape(IMG, H, W, C)
    params = (norm_gain.astype(jnp.float32), norm_shift.astype(jnp.float32), mix_in.astype(jnp.float32), mix_in_bias.astype(jnp.float32), mix_out.astype(jnp.float32), mix_out_bias.astype(jnp.float32), post_gain.astype(jnp.float32), post_shift.astype(jnp.float32), fc_in.astype(jnp.float32), fc_in_bias.astype(jnp.float32), fc_out.astype(jnp.float32), fc_out_bias.astype(jnp.float32))
    tables = make_tables()

    def forward(weights, fields):

        def per_image(image):
            return one_image(weights, tables, image)
        return lax.map(jax.checkpoint(per_image), fields)
    outputs, pullback = jax.vjp(forward, params, grid)
    param_grads, grid_grad = pullback(cot_grid)
    mask = slot_live.astype(jnp.float32)[:, None, None]
    block_output = (outputs.reshape(field_rows, W, C)[row_index] * mask).astype(jnp.bfloat16)
    tokens_grad = grid_grad.reshape(field_rows, W, C)[row_index] * mask
    return (block_output, tokens_grad, param_grads[0], param_grads[1], param_grads[2], param_grads[3], param_grads[4], param_grads[5], param_grads[6], param_grads[7], param_grads[8], param_grads[9], param_grads[10], param_grads[11])
```

```python
import functools
import math

import jax
import jax.numpy as jnp
import ml_dtypes
import numpy as np
from jax import lax
from jax.experimental import pallas as pl
from jax.experimental.pallas import tpu as pltpu
from jax.sharding import PartitionSpec as P

H = 90
W = 180
KX = 91
HALVES = 2
HIDDEN_BLOCK = 256
VMEM_BYTES = 58 * 1024 * 1024

norm_eps = 1e-06
shrink_level = 0.01
half_root = 0.7071067811865476
normal_peak = 0.3989422804014327
MESH = pl.DeviceIdType.MESH
f32 = jnp.float32
bf16 = jnp.bfloat16


def round_up(value, step):
    return -(-value // step) * step


class Sizes:
    def __init__(self, rows_count, lon_count, slots, channels):
        self.rows = rows_count
        self.lon = lon_count
        self.devices = rows_count * lon_count
        self.images = slots * 15 // (16 * H)
        self.per_image = self.devices // self.images
        self.groups = self.per_image // HALVES
        self.waves = -(-KX // self.groups)
        self.slots_here = slots // self.devices
        self.lons_here = W // lon_count
        self.lons_pad = round_up(self.lons_here, 16)
        self.tokens = lon_count * self.slots_here * self.lons_pad
        self.piece = round_up(self.slots_here * 2 * self.waves, 8)
        self.spectrum = self.groups * self.piece
        self.band = self.per_image * self.piece
        self.modes = round_up(H * self.waves, 16)
        self.virtual_slots = self.per_image * self.slots_here
        self.channels = channels
        self.half = channels // HALVES


def lon_tables(size):
    wave = np.arange(size.groups * size.waves)
    lon_index = np.arange(W)
    product = (lon_index[:, None] * wave[None, :]) % W
    angle = product.astype(np.float32) * np.float32(2.0 * math.pi / W)
    scale = np.float32(1.0 / math.sqrt(W))
    cosine = (np.cos(angle) * scale).astype(ml_dtypes.bfloat16).astype(np.float32)
    sine = (-np.sin(angle) * scale).astype(ml_dtypes.bfloat16).astype(np.float32)
    live = (wave < KX).astype(np.float32)
    factor = np.where((wave == 0) | (wave == W // 2), 1.0, 2.0).astype(np.float32)
    both = np.stack([cosine, sine]) * live
    result = []
    for weight in (np.ones_like(factor), factor):
        table = np.zeros(
            (
                size.groups,
                size.piece,
                size.lon,
                size.slots_here,
                size.lons_pad,
            ),
            np.float32,
        )
        values = (both * weight).reshape(2, size.lon, size.lons_here, size.groups, size.waves)
        values = np.transpose(values, (3, 0, 4, 1, 2)).reshape(
            size.groups, 2 * size.waves, size.lon, size.lons_here
        )
        for slot in range(size.slots_here):
            start = slot * 2 * size.waves
            table[:, start : start + 2 * size.waves, :, slot, : size.lons_here] = values
        flat = table.reshape(size.spectrum, size.tokens).astype(ml_dtypes.bfloat16)
        result.append(flat)
        result.append(np.ascontiguousarray(flat.T))
    return result


def lat_parts(size):
    lat_index = np.arange(H)
    angle = ((lat_index[:, None] * lat_index[None, :]) % H).astype(np.float32) * np.float32(
        2.0 * math.pi / H
    )
    scale = np.float32(1.0 / math.sqrt(H))
    cosine = np.zeros((96, 96), np.float32)
    sine = np.zeros((96, 96), np.float32)
    cosine[:H, :H] = np.cos(angle) * scale
    sine[:H, :H] = np.sin(angle) * scale
    spread_rows = np.zeros((2, size.modes, 2, 96), np.float32)
    row_wave = np.full((2, size.modes), -1, np.int32)
    for part in range(2):
        for lat in range(H):
            for wave in range(size.waves):
                spread_rows[part, lat * size.waves + wave, part, lat] = 1.0
                row_wave[part, lat * size.waves + wave] = wave
    spread_cols = np.zeros((2, 128, size.per_image, size.piece), np.float32)
    col_wave = np.full((size.per_image, size.piece), -2, np.int32)
    for device in range(size.per_image):
        for slot in range(size.slots_here):
            for part in range(2):
                for wave in range(size.waves):
                    place = (slot * 2 + part) * size.waves + wave
                    spread_cols[part, device * size.slots_here + slot, device, place] = 1.0
                    col_wave[device, place] = wave
    low = ml_dtypes.bfloat16
    return (
        cosine.astype(low),
        sine.astype(low),
        spread_rows.reshape(2 * size.modes, 192).astype(low),
        spread_cols.reshape(256, size.band).astype(low),
        row_wave.reshape(-1),
        col_wave.reshape(-1),
    )


def smooth_gate(values):
    return 0.5 * values * (1.0 + lax.erf(values * half_root))


def gate_both(values):
    half_phi = 0.5 * (1.0 + lax.erf(values * half_root))
    density = values * normal_peak * jnp.exp(-0.5 * values * values)
    return values * half_phi, half_phi + density


def gate_slope(values):
    return gate_both(values)[1]


def soft_shrink(values):
    return values - shrink_level * values * lax.rsqrt(values * values + shrink_level * shrink_level)


def shrink_slope(values):
    inverse = lax.rsqrt(values * values + shrink_level * shrink_level)
    return 1.0 - shrink_level * shrink_level * shrink_level * inverse * inverse * inverse


def norm_parts(values):
    center = values - jnp.mean(values, axis=-1, keepdims=True)
    spread = lax.rsqrt(jnp.mean(center * center, axis=-1, keepdims=True) + norm_eps)
    return center * spread, spread


def norm_back(scaled, unit, spread):
    return spread * (
        scaled
        - jnp.mean(scaled, axis=-1, keepdims=True)
        - unit * jnp.mean(scaled * unit, axis=-1, keepdims=True)
    )


def mm(left, right):
    return jnp.dot(left, right, preferred_element_type=f32)


def mm_t(left, right):
    return lax.dot_general(left, right, (((1,), (1,)), ((), ())), preferred_element_type=f32)


def t_mm(left, right):
    return lax.dot_general(left, right, (((0,), (0,)), ((), ())), preferred_element_type=f32)


def whole(count):
    return [pl.BlockSpec(memory_space=pltpu.VMEM)] * count


def call_local(kernel, name, outs, scratch=()):
    def run(*operands):
        return pl.pallas_call(
            kernel,
            out_shape=outs,
            in_specs=whole(len(operands)),
            out_specs=jax.tree.map(lambda _: pl.BlockSpec(memory_space=pltpu.VMEM), outs),
            scratch_shapes=list(scratch),
            compiler_params=pltpu.CompilerParams(vmem_limit_bytes=VMEM_BYTES),
            name=name,
        )(*operands)

    return run


def struct(shape, dtype):
    return jax.ShapeDtypeStruct(shape, dtype)


def tables_kernel(rows_ref, cos_ref, sin_ref, er_ref, ec_ref, rw_ref, cw_ref, rwt_ref, cwt_ref, lat_ref, lat_t_ref):
    lat_of = lax.broadcasted_iota(jnp.int32, (96, 128), 0)
    hot = (lat_of == rows_ref[...]).astype(f32).astype(bf16)
    cosine = mm(cos_ref[...], hot)
    sine = mm(sin_ref[...], hot)
    top = jnp.concatenate([cosine, sine], axis=1)
    bottom = jnp.concatenate([-sine, cosine], axis=1)
    base = jnp.concatenate([top, bottom], axis=0).astype(bf16)
    columns = mm(base, ec_ref[...]).astype(bf16)
    table = mm(er_ref[...], columns)
    lat_ref[...] = jnp.where(rw_ref[...] == cw_ref[...], table, 0.0).astype(bf16)
    table_t = lax.dot_general(columns, er_ref[...], (((0,), (1,)), ((), ())), preferred_element_type=f32)
    lat_t_ref[...] = jnp.where(cwt_ref[...] == rwt_ref[...], table_t, 0.0).astype(bf16)


def make_lat_tables(size, slot_lat):
    cosine, sine, spread_rows, spread_cols, row_wave, col_wave = lat_parts(size)
    rows = jnp.full((1, 128), -1, jnp.int32).at[0, : size.virtual_slots].set(slot_lat)
    return call_local(
        tables_kernel,
        "lat_tables",
        (
            struct((2 * size.modes, size.band), bf16),
            struct((size.band, 2 * size.modes), bf16),
        ),
    )(
        rows,
        jnp.asarray(cosine),
        jnp.asarray(sine),
        jnp.asarray(spread_rows),
        jnp.asarray(spread_cols),
        jnp.asarray(row_wave[:, None]),
        jnp.asarray(col_wave[None, :]),
        jnp.asarray(row_wave[None, :]),
        jnp.asarray(col_wave[:, None]),
    )


def pad_plane(size, plane):
    extra = size.lons_pad - size.lons_here
    return jnp.concatenate([plane, jnp.zeros((extra, plane.shape[1]), plane.dtype)], axis=0)


def planes(size):
    for source in range(size.lon):
        for slot in range(size.slots_here):
            yield source, slot, (source * size.slots_here + slot) * size.lons_pad


def write_pieces(size, values, out_ref):
    for half in range(HALVES):
        for group in range(size.groups):
            out_ref[half * size.groups + group] = values[
                group * size.piece : (group + 1) * size.piece,
                half * size.half : (half + 1) * size.half,
            ].astype(bf16)


def read_pieces(ref, first, count):
    return jnp.concatenate([ref[first + i].astype(f32) for i in range(count)], axis=0).astype(bf16)


def read_spectrum(size, ref):
    return jnp.concatenate(
        [read_pieces(ref, half * size.groups, size.groups) for half in range(HALVES)], axis=1
    )


def first_kernel(size, x_ref, vectors_ref, table_ref, send_ref, low_ref):
    gain, shift = vectors_ref[0:1, :], vectors_ref[1:2, :]
    for source, slot, start in planes(size):
        x = pad_plane(size, x_ref[source, slot].astype(f32))
        unit, _ = norm_parts(x)
        low_ref[start : start + size.lons_pad, :] = (unit * gain + shift).astype(bf16)
    write_pieces(size, mm(table_ref[...], low_ref[...]), send_ref)


def mix_kernel(size, recv_ref, lat_ref, lat_t_ref, w1_ref, b1_ref, w2_ref, b2_ref, send_ref, band_ref, inner_ref, gated_ref, outer_ref):
    spectrum = read_pieces(recv_ref, 0, size.per_image)
    modes = mm(lat_ref[...], spectrum)
    band = jnp.concatenate([modes[: size.modes], modes[size.modes :]], axis=1).astype(bf16)
    band_ref[...] = band
    inner = mm(band, w1_ref[...]) + b1_ref[...]
    inner_ref[...] = inner
    gated = smooth_gate(inner).astype(bf16)
    gated_ref[...] = gated
    outer = mm(gated, w2_ref[...]) + b2_ref[...]
    outer_ref[...] = outer
    shrunk = soft_shrink(outer)
    stacked = jnp.concatenate([shrunk[:, : size.half], shrunk[:, size.half :]], axis=0).astype(bf16)
    back = mm(lat_t_ref[...], stacked)
    for source in range(size.per_image):
        send_ref[source] = back[source * size.piece : (source + 1) * size.piece].astype(bf16)


def write_blocks(total, half, first, out_ref):
    block_size = out_ref.shape[1]
    blocks = half // block_size
    for block in range(blocks):
        near = slice(block * block_size, (block + 1) * block_size)
        far = slice(half + block * block_size, half + (block + 1) * block_size)
        out_ref[first + block] = total[near, near] + total[far, far]
        out_ref[first + blocks + block] = total[near, far] - total[far, near]


def mix_back_kernel(size, recv_ref, lat_ref, lat_t_ref, w1_ref, w2_ref, band_ref, inner_ref, gated_ref, outer_ref, send_ref, grad_ref, bias_ref):
    half = size.half
    spectrum = read_pieces(recv_ref, 0, size.per_image)
    modes = mm(lat_ref[...], spectrum)
    upstream = jnp.concatenate([modes[: size.modes], modes[size.modes :]], axis=1).astype(bf16)
    outer_grad = (upstream.astype(f32) * shrink_slope(outer_ref[...])).astype(bf16)
    write_blocks(t_mm(gated_ref[...], outer_grad), half, grad_ref.shape[0] // 2, grad_ref)
    inner_grad = (mm_t(outer_grad, w2_ref[...]) * gate_slope(inner_ref[...])).astype(bf16)
    write_blocks(t_mm(band_ref[...], inner_grad), half, 0, grad_ref)
    bias_ref[0:1, :] = jnp.sum(inner_grad.astype(f32), axis=0, keepdims=True)
    bias_ref[1:2, :] = jnp.sum(outer_grad.astype(f32), axis=0, keepdims=True)
    band_grad = mm_t(inner_grad, w1_ref[...])
    stacked = jnp.concatenate([band_grad[:, :half], band_grad[:, half:]], axis=0).astype(bf16)
    back = mm(lat_t_ref[...], stacked)
    for source in range(size.per_image):
        send_ref[source] = back[source * size.piece : (source + 1) * size.piece].astype(bf16)


def mlp_kernel(
    size,
    live_ref,
    recv_ref,
    x_ref,
    dy_ref,
    inv_t_ref,
    inv_ref,
    vectors_ref,
    fc_in_ref,
    fc_in_bias_ref,
    fc_out_ref,
    block_ref,
    dh_ref,
    send_ref,
    wide_ref,
    hidden_bias_ref,
    small_ref,
    res_ref,
    low_ref,
    up_ref,
    acc_ref,
    back_ref,
):
    step = pl.program_id(0)
    gain1, shift1, gain2, shift2, out_bias = [vectors_ref[i : i + 1, :] for i in range(5)]

    @pl.when(step == 0)
    def _():
        res_ref[...] = mm(inv_t_ref[...], read_spectrum(size, recv_ref))
        up_sum = jnp.zeros((1, size.channels), f32)
        for source, slot, start in planes(size):
            part = slice(start, start + size.lons_pad)
            x = pad_plane(size, x_ref[source, slot].astype(f32))
            unit, _ = norm_parts(x)
            residual = res_ref[part, :] + (unit * gain1 + shift1) + x
            res_ref[part, :] = residual
            unit, _ = norm_parts(residual)
            low_ref[part, :] = (unit * gain2 + shift2).astype(bf16)
            up = pad_plane(size, dy_ref[source, slot].astype(f32) * live_ref[0, slot])
            up_ref[part, :] = up.astype(bf16)
            up_sum = up_sum + jnp.sum(up, axis=0, keepdims=True)
        small_ref[0:1, :] = up_sum
        acc_ref[...] = jnp.zeros_like(acc_ref)
        back_ref[...] = jnp.zeros_like(back_ref)

    low = low_ref[...]
    up = up_ref[...]
    gate, slope = gate_both(mm(low, fc_in_ref[...]) + fc_in_bias_ref[...])
    hidden = gate.astype(bf16)
    acc_ref[...] += mm(hidden, fc_out_ref[...])
    hidden_grad = (mm_t(up, fc_out_ref[...]) * slope).astype(bf16)
    hidden_bias_ref[...] = jnp.sum(hidden_grad.astype(f32), axis=0, keepdims=True)
    back_ref[...] += mm_t(hidden_grad, fc_in_ref[...])
    wide_ref[:, : size.channels] = t_mm(hidden_grad, low).astype(bf16)
    wide_ref[:, size.channels :] = t_mm(hidden, up).astype(bf16)

    @pl.when(step == pl.num_programs(0) - 1)
    def _():
        gain_sum = jnp.zeros((1, size.channels), f32)
        shift_sum = jnp.zeros((1, size.channels), f32)
        for source, slot, start in planes(size):
            part = slice(start, start + size.lons_pad)
            residual = res_ref[part, :]
            block = (residual + (acc_ref[part, :] + out_bias)) * live_ref[0, slot]
            block_ref[source, slot] = block[: size.lons_here].astype(bf16)
            unit, spread = norm_parts(residual)
            grad = back_ref[part, :]
            gain_sum = gain_sum + jnp.sum(grad * unit, axis=0, keepdims=True)
            shift_sum = shift_sum + jnp.sum(grad, axis=0, keepdims=True)
            grad = up_ref[part, :].astype(f32) + norm_back(grad * gain2, unit, spread)
            dh_ref[part, :] = grad
            low_ref[part, :] = grad.astype(bf16)
        small_ref[1:2, :] = gain_sum
        small_ref[2:3, :] = shift_sum
        write_pieces(size, mm(inv_ref[...], low_ref[...]), send_ref)


def run_mlp(size, hidden_units, live, recv, x, dy, inv_t, inv, vectors, fc_in, fc_in_bias, fc_out):
    channels = size.channels
    width = HIDDEN_BLOCK
    fixed = pl.BlockSpec(memory_space=pltpu.VMEM)
    tokens = (size.tokens, channels)
    return pl.pallas_call(
        functools.partial(mlp_kernel, size),
        grid=(hidden_units // width,),
        in_specs=[pl.BlockSpec(memory_space=pltpu.SMEM)]
        + [fixed] * 6
        + [
            pl.BlockSpec((channels, width), lambda i: (0, i)),
            pl.BlockSpec((1, width), lambda i: (0, i)),
            pl.BlockSpec((width, channels), lambda i: (i, 0)),
        ],
        out_specs=(
            fixed,
            fixed,
            fixed,
            pl.BlockSpec((width, 2 * channels), lambda i: (i, 0)),
            pl.BlockSpec((1, width), lambda i: (0, i)),
            fixed,
        ),
        out_shape=(
            struct(x.shape, bf16),
            struct(tokens, f32),
            struct((size.per_image, size.piece, size.half), bf16),
            struct((hidden_units, 2 * channels), bf16),
            struct((1, hidden_units), f32),
            struct((8, channels), f32),
        ),
        scratch_shapes=[
            pltpu.VMEM(tokens, f32),
            pltpu.VMEM(tokens, bf16),
            pltpu.VMEM(tokens, bf16),
            pltpu.VMEM(tokens, f32),
            pltpu.VMEM(tokens, f32),
        ],
        compiler_params=pltpu.CompilerParams(vmem_limit_bytes=VMEM_BYTES),
        name="mlp",
    )(live, recv, x, dy, inv_t, inv, vectors, fc_in, fc_in_bias, fc_out)


def last_kernel(size, recv_ref, x_ref, dh_ref, table_t_ref, vectors_ref, out_ref, small_ref):
    gain = vectors_ref[0:1, :]
    filtered = mm(table_t_ref[...], read_spectrum(size, recv_ref))
    gain_sum = jnp.zeros((1, size.channels), f32)
    shift_sum = jnp.zeros((1, size.channels), f32)
    for source, slot, start in planes(size):
        part = slice(start, start + size.lons_pad)
        unit, spread = norm_parts(pad_plane(size, x_ref[source, slot].astype(f32)))
        base = dh_ref[part, :]
        grad = base + filtered[part]
        gain_sum = gain_sum + jnp.sum(grad * unit, axis=0, keepdims=True)
        shift_sum = shift_sum + jnp.sum(grad, axis=0, keepdims=True)
        grad = base + norm_back(grad * gain, unit, spread)
        out_ref[source, slot] = grad[: size.lons_here].astype(bf16)
    small_ref[0:1, :] = gain_sum
    small_ref[1:2, :] = shift_sum


def partners(lon_count):
    row = lax.axis_index("rows")
    lon = lax.axis_index("lon")
    core = {"rows": row, "lon": lon + 1 - 2 * (lon % 2)}
    along_y = {"rows": row, "lon": (lon + 2) % 4}
    along_x = {"rows": row + 1 - 2 * (row % 2), "lon": lon}
    far_z = {"rows": (row + 4) % 8, "lon": lon}
    return core, along_y, along_x, far_z


def greet(lon_count, count):
    row = lax.axis_index("rows")
    lon = lax.axis_index("lon")
    me = row * lon_count + lon
    barrier = pltpu.get_barrier_semaphore()
    for offset in range(1, count):
        other = (me + offset) % count
        pl.semaphore_signal(
            barrier,
            inc=1,
            device_id={"rows": other // lon_count, "lon": other % lon_count},
            device_id_type=MESH,
        )
    pl.semaphore_wait(barrier, count - 1)


class Sender:
    def __init__(self, send_sem, recv_sem):
        self.send_sem = send_sem
        self.recv_sem = recv_sem
        self.used = 0

    def start(self, source, target, device):
        copy = pltpu.make_async_remote_copy(
            src_ref=source,
            dst_ref=target,
            send_sem=self.send_sem.at[self.used],
            recv_sem=self.recv_sem.at[self.used],
            device_id=device,
            device_id_type=MESH,
        )
        self.used += 1
        copy.start()
        return copy


class Mover:
    def __init__(self, sem):
        self.sem = sem
        self.used = 0

    def start(self, source, target):
        copy = pltpu.make_async_copy(source, target, self.sem.at[self.used])
        self.used += 1
        copy.start()
        return copy


def start_all(lon_count, source_ref, out_ref, sender, mover):
    me = lax.axis_index("rows") * lon_count + lax.axis_index("lon")
    count = source_ref.shape[0]
    copies = []
    for offset in range(1, count):
        other = (me + offset) % count
        copies.append(
            sender.start(
                source_ref.at[other],
                out_ref.at[me],
                {"rows": other // lon_count, "lon": other % lon_count},
            )
        )
    copies.append(mover.start(source_ref.at[me], out_ref.at[me]))
    return copies


def start_lon(source_ref, out_ref, sender, mover):
    row = lax.axis_index("rows")
    me = lax.axis_index("lon")
    count = source_ref.shape[0]
    copies = []
    for offset in range(1, count):
        other = (me + offset) % count
        copies.append(
            sender.start(source_ref.at[other], out_ref.at[me], {"rows": row, "lon": other})
        )
    copies.append(mover.start(source_ref.at[me], out_ref.at[me]))
    return copies


def finish(copies):
    for copy in copies:
        copy.wait()


def call_remote(kernel, name, number, outs, spaces, out_spaces, sends, moves, scratch, operands):
    return pl.pallas_call(
        kernel,
        out_shape=outs,
        in_specs=[pl.BlockSpec(memory_space=space) for space in spaces],
        out_specs=tuple(pl.BlockSpec(memory_space=space) for space in out_spaces),
        scratch_shapes=[
            pltpu.SemaphoreType.DMA((sends,)),
            pltpu.SemaphoreType.DMA((sends,)),
            pltpu.SemaphoreType.DMA((moves,)),
        ]
        + list(scratch),
        compiler_params=pltpu.CompilerParams(
            collective_id=number, has_side_effects=True, vmem_limit_bytes=VMEM_BYTES
        ),
        name=name,
    )(*operands)


def lon_kernel(lon_count, count, source_ref, out_ref, send_sem, recv_sem, move_sem):
    greet(lon_count, count)
    finish(start_lon(source_ref, out_ref, Sender(send_sem, recv_sem), Mover(move_sem)))


def all_kernel(lon_count, count, source_ref, out_ref, send_sem, recv_sem, move_sem):
    greet(lon_count, count)
    finish(start_all(lon_count, source_ref, out_ref, Sender(send_sem, recv_sem), Mover(move_sem)))


def all_lon_kernel(lon_count, count, source_ref, other_ref, out_ref, other_out_ref, send_sem, recv_sem, move_sem):
    greet(lon_count, count)
    sender, mover = Sender(send_sem, recv_sem), Mover(move_sem)
    copies = start_all(lon_count, source_ref, out_ref, sender, mover)
    copies += start_lon(other_ref, other_out_ref, sender, mover)
    finish(copies)


def exchange_lon(size, values, number):
    if size.images > 1:
        return lax.all_to_all(values, "lon", split_axis=0, concat_axis=0, tiled=True)
    return call_remote(
        functools.partial(lon_kernel, size.lon, size.devices),
        "exchange_lon" + str(number),
        number,
        (struct(values.shape, values.dtype),),
        [pl.ANY],
        [pl.ANY],
        size.lon,
        1,
        (),
        (values,),
    )[0]


def exchange_all(size, values, number):
    if size.images > 1:
        return lax.all_to_all(values, ("rows", "lon"), split_axis=0, concat_axis=0, tiled=True)
    return call_remote(
        functools.partial(all_kernel, size.lon, size.devices),
        "exchange_all" + str(number),
        number,
        (struct(values.shape, values.dtype),),
        [pl.ANY],
        [pl.ANY],
        size.devices,
        1,
        (),
        (values,),
    )[0]


def exchange_both(size, pieces, planes_sent, number):
    return call_remote(
        functools.partial(all_lon_kernel, size.lon, size.devices),
        "exchange_both" + str(number),
        number,
        (struct(pieces.shape, pieces.dtype), struct(planes_sent.shape, planes_sent.dtype)),
        [pl.ANY, pl.ANY],
        [pl.ANY, pl.ANY],
        size.devices + size.lon,
        2,
        (),
        (pieces, planes_sent),
    )


def add_planes(left_ref, right_ref, out_ref):
    @pl.loop(0, left_ref.shape[0])
    def _(first):
        for second in range(left_ref.shape[1]):
            total = left_ref[first, second].astype(f32) + right_ref[first, second].astype(f32)
            out_ref[first, second] = total.astype(out_ref.dtype)


def reduce_one_kernel(
    lon_count,
    count,
    pieces_ref,
    wide_ref,
    out_ref,
    a_ref,
    b_ref,
    send_sem,
    recv_sem,
    move_sem,
    a_go,
    a_go_in,
    b_go,
    b_go_in,
    a_keep,
    a_keep_in,
    b_keep,
    b_keep_in,
    a_land,
    b_land,
):
    x = lax.axis_index("rows") % 2
    y = lax.axis_index("lon") // 2
    core = lax.axis_index("lon") % 2
    to_core, to_y, to_x, _ = partners(lon_count)
    width = wide_ref.shape[-1] // 2
    first, second = pl.ds(0, width), pl.ds(width, width)
    sender, mover = Sender(send_sem, recv_sem), Mover(move_sem)
    greet(lon_count, count)
    views = (
        (lambda c: wide_ref.at[:, 1 - x, :, c, :, first], a_go, a_go_in),
        (lambda c: wide_ref.at[:, :, 1 - y, c, :, second], b_go, b_go_in),
        (lambda c: wide_ref.at[:, x, :, c, :, first], a_keep, a_keep_in),
        (lambda c: wide_ref.at[:, :, y, c, :, second], b_keep, b_keep_in),
    )
    pairs = []
    for view, own, landed in views[:2]:
        pairs.append((sender.start(view(1 - core), landed, to_core), mover.start(view(core), own)))
    pieces = start_all(lon_count, pieces_ref, out_ref, sender, mover)
    for view, own, landed in views[2:]:
        pairs.append((sender.start(view(1 - core), landed, to_core), mover.start(view(core), own)))
    hops = []
    for pair, own, landed, target, device in (
        (pairs[0], a_go, a_go_in, a_land, to_x),
        (pairs[1], b_go, b_go_in, b_land, to_y),
    ):
        finish(pair)
        add_planes(own, landed, own)
        hops.append(sender.start(own, target, device))
    for pair, own, landed in ((pairs[2], a_keep, a_keep_in), (pairs[3], b_keep, b_keep_in)):
        finish(pair)
        add_planes(own, landed, own)
    hops[0].wait()
    add_planes(a_keep, a_land, a_ref)
    hops[1].wait()
    add_planes(b_keep, b_land, b_ref)
    finish(pieces)


def reduce_one(size, pieces, wide, number):
    share, columns = wide.shape[0] // size.devices, wide.shape[1]
    part = (4, 2, share, columns // 2)
    return call_remote(
        functools.partial(reduce_one_kernel, size.lon, size.devices),
        "exchange_reduce" + str(number),
        number,
        (struct(pieces.shape, pieces.dtype), struct(part, bf16), struct(part, bf16)),
        [pl.ANY, pl.ANY],
        [pl.ANY, pltpu.VMEM, pltpu.VMEM],
        size.devices + 6,
        6,
        [pltpu.VMEM(part, bf16)] * 10,
        (pieces, wide.reshape(4, 2, 2, 2, share, columns)),
    )


def reduce_two_kernel(
    lon_count,
    count,
    groups,
    pieces_ref,
    a_in,
    b_in,
    mix_ref,
    out_ref,
    a_ref,
    b_ref,
    pair_ref,
    send_sem,
    recv_sem,
    move_sem,
    a_land,
    b_land,
    mix_land,
    mine,
):
    row = lax.axis_index("rows")
    lon = lax.axis_index("lon")
    x = row % 2
    y = lon // 2
    me = row * lon_count + lon
    group = me % groups
    base = me - group
    _, to_y, to_x, far_z = partners(lon_count)
    sender, mover = Sender(send_sem, recv_sem), Mover(move_sem)
    greet(lon_count, count)
    hops = [
        sender.start(a_in.at[:, 1 - y], a_land, to_y),
        sender.start(b_in.at[:, 1 - x], b_land, to_x),
    ]
    pieces = start_all(lon_count, pieces_ref, out_ref, sender, mover)
    parts = []
    for offset in range(1, groups):
        other = (group + offset) % groups
        device = base + other
        parts.append(
            sender.start(
                mix_ref.at[other],
                mix_land.at[group],
                {"rows": device // lon_count, "lon": device % lon_count},
            )
        )
    own = mover.start(mix_ref.at[group], mix_land.at[group])
    finish(parts)
    own.wait()
    total = mix_land[0]
    for index in range(1, groups):
        total = total + mix_land[index]
    mine[...] = total
    half = me // groups
    crossing = sender.start(mine, pair_ref.at[half], far_z)
    own = mover.start(mine, pair_ref.at[half])
    hops[0].wait()

    @pl.loop(0, 4)
    def _(z):
        total = a_in[z, y].astype(f32) + a_land[z].astype(f32)
        a_ref[z] = total.astype(bf16)

    hops[1].wait()

    @pl.loop(0, 4)
    def _(z):
        total = b_in[z, x].astype(f32) + b_land[z].astype(f32)
        b_ref[z] = total.astype(bf16)

    finish(pieces)
    own.wait()
    crossing.wait()


def reduce_two(size, pieces, a, b, mix, number):
    part = (4,) + a.shape[2:]
    return call_remote(
        functools.partial(reduce_two_kernel, size.lon, size.devices, size.groups),
        "exchange_reduce" + str(number),
        number,
        (
            struct(pieces.shape, pieces.dtype),
            struct(part, bf16),
            struct(part, bf16),
            struct((HALVES,) + mix.shape[1:], f32),
        ),
        [pl.ANY, pltpu.VMEM, pltpu.VMEM, pltpu.VMEM],
        [pl.ANY, pltpu.VMEM, pltpu.VMEM, pltpu.VMEM],
        size.devices + size.groups + 4,
        4,
        [
            pltpu.VMEM(part, bf16),
            pltpu.VMEM(part, bf16),
            pltpu.VMEM(mix.shape, f32),
            pltpu.VMEM(mix.shape[1:], f32),
        ],
        (pieces, a, b, mix),
    )


def reduce_three_kernel(
    lon_count,
    count,
    groups,
    token_ref,
    block_ref,
    a_in,
    b_in,
    pair_ref,
    small_ref,
    token_out,
    block_out,
    dense_ref,
    mix_out,
    sum_ref,
    send_sem,
    recv_sem,
    move_sem,
    a_land,
    b_land,
    small_land,
):
    row = lax.axis_index("rows")
    lon = lax.axis_index("lon")
    z = row // 2
    me = row * lon_count + lon
    group = me % groups
    base = me - group
    sender, mover = Sender(send_sem, recv_sem), Mover(move_sem)
    greet(lon_count, count)
    small = start_all_one(lon_count, count, small_ref, small_land, sender, mover)
    tokens = start_lon(token_ref, token_out, sender, mover)
    hops = []
    for offset in range(1, 4):
        other = (z + offset) % 4
        device = {"rows": other * 2 + row % 2, "lon": lon}
        hops.append(sender.start(a_in.at[other], a_land.at[offset], device))
        hops.append(sender.start(b_in.at[other], b_land.at[offset], device))
    parts = []
    for offset in range(1, groups):
        device = base + (group + offset) % groups
        parts.append(
            sender.start(
                pair_ref,
                mix_out.at[:, group],
                {"rows": device // lon_count, "lon": device % lon_count},
            )
        )
    parts.append(mover.start(pair_ref, mix_out.at[:, group]))
    blocks = start_lon(block_ref, block_out, sender, mover)
    finish(small)
    total = small_land[0]
    for index in range(1, count):
        total = total + small_land[index]
    sum_ref[...] = total
    finish(hops)
    for place, own, landed in ((0, a_in, a_land), (1, b_in, b_land)):
        total = own[z].astype(f32)
        for offset in range(1, 4):
            total = total + landed[offset].astype(f32)
        dense_ref[place] = total
    finish(parts)
    finish(tokens)
    finish(blocks)


def start_all_one(lon_count, count, source_ref, out_ref, sender, mover):
    me = lax.axis_index("rows") * lon_count + lax.axis_index("lon")
    copies = []
    for offset in range(1, count):
        other = (me + offset) % count
        copies.append(
            sender.start(
                source_ref, out_ref.at[me], {"rows": other // lon_count, "lon": other % lon_count}
            )
        )
    copies.append(mover.start(source_ref, out_ref.at[me]))
    return copies


def reduce_three(size, token_grad, block, a, b, pair, small, number):
    return call_remote(
        functools.partial(reduce_three_kernel, size.lon, size.devices, size.groups),
        "exchange_reduce" + str(number),
        number,
        (
            struct(token_grad.shape, bf16),
            struct(block.shape, bf16),
            struct((2,) + a.shape[1:], f32),
            struct((HALVES, size.groups) + pair.shape[1:], f32),
            struct(small.shape, f32),
        ),
        [pl.ANY, pl.ANY] + [pltpu.VMEM] * 4,
        [pl.ANY, pl.ANY] + [pltpu.VMEM] * 3,
        size.devices + size.groups + 6 + 2 * size.lon,
        4,
        [
            pltpu.VMEM(a.shape, bf16),
            pltpu.VMEM(b.shape, bf16),
            pltpu.VMEM((size.devices,) + small.shape, f32),
        ],
        (token_grad, block, a, b, pair, small),
    )


def to_modes(size, pieces, row_map, number):
    if size.images == 1:
        return exchange_all(size, pieces, number)
    sent = jnp.tile(pieces, (size.images, 1, 1))
    received = exchange_all(size, sent, number)
    used = size.slots_here * 2 * size.waves
    by_slot = received[:, :used].reshape(-1, 2 * size.waves, size.half)
    image = (lax.axis_index("rows") * size.lon + lax.axis_index("lon")) // size.per_image
    slots = row_map.shape[0]
    target = jnp.where(row_map >= 0, row_map, size.images * H)
    slot_of_row = (
        jnp.zeros((size.images * H,), jnp.int32)
        .at[target]
        .set(jnp.arange(slots, dtype=jnp.int32), mode="drop")
    )
    own = lax.dynamic_slice_in_dim(slot_of_row, image * H, H)
    picked = jnp.take(by_slot, own, axis=0)
    picked = jnp.pad(picked, ((0, size.virtual_slots - H), (0, 0), (0, 0)))
    picked = picked.reshape(size.per_image, used, size.half)
    return jnp.pad(picked, ((0, 0), (0, size.piece - used), (0, 0)))


def from_modes(size, pieces, row_map, number):
    if size.images == 1:
        return exchange_all(size, pieces, number)
    used = size.slots_here * 2 * size.waves
    by_lat = pieces[:, :used].reshape(-1, 2 * size.waves, size.half)
    image = (lax.axis_index("rows") * size.lon + lax.axis_index("lon")) // size.per_image
    live = (row_map >= 0) & (row_map // H == image)
    picked = jnp.take(by_lat, jnp.where(live, row_map % H, 0), axis=0)
    picked = picked * live.astype(bf16)[:, None, None]
    picked = picked.reshape(size.devices, used, size.half)
    sent = jnp.pad(picked, ((0, 0), (0, size.piece - used), (0, 0)))
    received = exchange_all(size, sent, number)
    received = received.reshape(size.images, size.per_image, size.piece, size.half)
    return jnp.sum(received.astype(f32), axis=0).astype(bf16)


def block_matrix(weight, half_index, blocks_here):
    block_size = weight.shape[2]
    own = lax.dynamic_slice_in_dim(weight, half_index * blocks_here, blocks_here, axis=1)
    eye = jnp.eye(blocks_here, dtype=bf16)
    real, imag = [
        (own[part][:, :, None, :] * eye[:, None, :, None]).reshape(
            blocks_here * block_size, blocks_here * block_size
        )
        for part in range(2)
    ]
    return jnp.concatenate(
        [jnp.concatenate([real, imag], axis=1), jnp.concatenate([-imag, real], axis=1)], axis=0
    )


def half_bias(bias, half_index, size):
    flat = bias.reshape(2, size.channels)
    own = lax.dynamic_slice_in_dim(flat, half_index * size.half, size.half, axis=1)
    return own.reshape(1, 2 * size.half)


def spread_half(row, half_index, size):
    parts = row.reshape(2, 1, size.half)
    return jnp.concatenate(
        [parts * (half_index == other).astype(f32) for other in range(HALVES)], axis=1
    ).reshape(2, size.channels)


def body(
    tokens,
    row_map,
    cotangent,
    norm_gain,
    norm_shift,
    mix_in,
    mix_in_bias,
    mix_out,
    mix_out_bias,
    post_gain,
    post_shift,
    fc_in,
    fc_in_bias,
    fc_out,
    fc_out_bias,
):
    size = Sizes(
        lax.axis_size("rows"), lax.axis_size("lon"), row_map.shape[0], tokens.shape[2]
    )
    channels = size.channels
    blocks = mix_in.shape[1]
    blocks_here = blocks // HALVES
    block_size = mix_in.shape[2]
    hidden_units = fc_in.shape[1]
    device = lax.axis_index("rows") * size.lon + lax.axis_index("lon")
    half_index = (device % size.per_image) // size.groups

    table, table_t, inv, inv_t = [jnp.asarray(t) for t in lon_tables(size)]
    if size.images == 1:
        slot_lat = row_map
    else:
        slot_lat = jnp.where(jnp.arange(size.virtual_slots) < H, jnp.arange(size.virtual_slots), -1)
    lat, lat_t = make_lat_tables(size, slot_lat)
    w1 = block_matrix(mix_in, half_index, blocks_here)
    w2 = block_matrix(mix_out, half_index, blocks_here)
    b1 = half_bias(mix_in_bias, half_index, size)
    b2 = half_bias(mix_out_bias, half_index, size)
    own_map = lax.dynamic_slice_in_dim(row_map, device * size.slots_here, size.slots_here)
    live = (own_map >= 0).astype(f32).reshape(1, size.slots_here)

    vectors = jnp.stack([norm_gain, norm_shift, post_gain, post_shift, fc_out_bias])
    shape = (size.lon, size.slots_here, size.lons_here, channels)
    x = exchange_lon(size, tokens.reshape(shape), 0)
    dy = cotangent.reshape(shape)

    piece_shape = struct((size.per_image, size.piece, size.half), bf16)
    sent = call_local(
        functools.partial(first_kernel, size),
        "lon_forward",
        piece_shape,
        [pltpu.VMEM((size.tokens, channels), bf16)],
    )(x, vectors, table)
    if size.images == 1:
        received, dy = exchange_both(size, sent, dy, 1)
    else:
        received, dy = to_modes(size, sent, row_map, 1), exchange_lon(size, dy, 2)
    mode_shape = (size.modes, 2 * size.half)
    sent, band, inner, gated, outer = call_local(
        functools.partial(mix_kernel, size),
        "mix_forward",
        (
            piece_shape,
            struct(mode_shape, bf16),
            struct(mode_shape, f32),
            struct(mode_shape, bf16),
            struct(mode_shape, f32),
        ),
    )(received, lat, lat_t, w1, b1, w2, b2)
    received = from_modes(size, sent, row_map, 3)
    block, dh, sent, wide, hidden_bias, small = run_mlp(
        size, hidden_units, live, received, x, dy, inv_t, inv, vectors, fc_in, fc_in_bias.reshape(1, -1), fc_out
    )
    early = lax.psum(
        jnp.concatenate([small[0:3], hidden_bias.reshape(-1, channels)], axis=0), ("rows", "lon")
    )
    if size.images == 1:
        received, sum_a, sum_b = reduce_one(size, sent, wide, 4)
    else:
        received = to_modes(size, sent, row_map, 4)
        dense = lax.psum_scatter(wide, ("rows", "lon"), scatter_dimension=0, tiled=True)
    blocks_shape = (4 * blocks_here, block_size, block_size)
    sent, mix_grad, bias_grad = call_local(
        functools.partial(mix_back_kernel, size),
        "mix_backward",
        (piece_shape, struct(blocks_shape, f32), struct((8, 2 * size.half), f32)),
    )(received, lat, lat_t, w1, w2, band, inner, gated, outer)
    bias_sum = lax.psum(
        jnp.concatenate([spread_half(bias_grad[i], half_index, size) for i in range(2)], axis=0),
        ("rows", "lon"),
    )
    if size.images == 1:
        received, sum_a, sum_b, mix_pair = reduce_two(size, sent, sum_a, sum_b, mix_grad, 5)
    else:
        received = from_modes(size, sent, row_map, 5)
        mix_total = lax.psum(
            jnp.stack([mix_grad * (half_index == other).astype(f32) for other in range(HALVES)]),
            ("rows", "lon"),
        )
    token_grad, small_last = call_local(
        functools.partial(last_kernel, size),
        "lon_backward",
        (struct(x.shape, bf16), struct((2, channels), f32)),
    )(received, x, dh, table_t, vectors)
    if size.images == 1:
        token_grad, block, dense, mix_total, late = reduce_three(
            size, token_grad, block, sum_a, sum_b, mix_pair, small_last, 6
        )
    else:
        token_grad = exchange_lon(size, token_grad, 6)
        block = exchange_lon(size, block, 7)
        late = lax.psum(small_last, ("rows", "lon"))
        dense = jnp.stack([dense[:, :channels], dense[:, channels:]]).astype(f32)
    mix_total = mix_total.reshape(HALVES, 2, 2, blocks_here, block_size, block_size)
    mix_total = jnp.transpose(mix_total, (1, 2, 0, 3, 4, 5)).reshape((2,) + mix_in.shape)
    share = hidden_units // size.devices
    return (
        block.reshape(tokens.shape),
        token_grad.reshape(tokens.shape).astype(f32),
        late[0],
        late[1],
        mix_total[0],
        bias_sum[0:2].reshape(mix_in_bias.shape),
        mix_total[1],
        bias_sum[2:4].reshape(mix_out_bias.shape),
        early[1],
        early[2],
        dense[0].T,
        lax.dynamic_slice_in_dim(early[3:].reshape(-1), device * share, share),
        dense[1],
        early[0],
    )


def solution(mesh):
    return jax.shard_map(
        body,
        mesh=mesh,
        in_specs=(P("rows", "lon", None), P(), P("rows", "lon", None)) + (P(),) * 12,
        out_specs=(
            P("rows", "lon", None),
            P("rows", "lon", None),
            P(),
            P(),
            P(),
            P(),
            P(),
            P(),
            P(),
            P(),
            P(None, ("rows", "lon")),
            P(("rows", "lon")),
            P(("rows", "lon"), None),
            P(),
        ),
        check_vma=False,
    )
```

```python
import functools
import math

import jax
import jax.numpy as jnp
import ml_dtypes
import numpy as np
from jax import lax
from jax.experimental import pallas as pl
from jax.experimental.pallas import tpu as pltpu
from jax.sharding import PartitionSpec as P

H = 90
W = 180
KX = 91
HALVES = 2
HIDDEN_BLOCK = 256
VMEM_BYTES = 58 * 1024 * 1024

norm_eps = 1e-06
shrink_level = 0.01
half_root = 0.7071067811865476
normal_peak = 0.3989422804014327
MESH = pl.DeviceIdType.MESH
f32 = jnp.float32
bf16 = jnp.bfloat16


def round_up(value, step):
    return -(-value // step) * step


class Sizes:
    def __init__(self, rows_count, lon_count, slots, channels):
        self.rows = rows_count
        self.lon = lon_count
        self.devices = rows_count * lon_count
        self.images = slots * 15 // (16 * H)
        self.per_image = self.devices // self.images
        self.groups = self.per_image // HALVES
        self.waves = -(-KX // self.groups)
        self.slots_here = slots // self.devices
        self.lons_here = W // lon_count
        self.lons_pad = round_up(self.lons_here, 16)
        self.tokens = lon_count * self.slots_here * self.lons_pad
        self.piece = round_up(self.slots_here * 2 * self.waves, 8)
        self.spectrum = self.groups * self.piece
        self.band = self.per_image * self.piece
        self.modes = round_up(H * self.waves, 16)
        self.virtual_slots = self.per_image * self.slots_here
        self.channels = channels
        self.half = channels // HALVES


def lon_tables(size):
    wave = np.arange(size.groups * size.waves)
    lon_index = np.arange(W)
    product = (lon_index[:, None] * wave[None, :]) % W
    angle = product.astype(np.float32) * np.float32(2.0 * math.pi / W)
    scale = np.float32(1.0 / math.sqrt(W))
    cosine = (np.cos(angle) * scale).astype(ml_dtypes.bfloat16).astype(np.float32)
    sine = (-np.sin(angle) * scale).astype(ml_dtypes.bfloat16).astype(np.float32)
    live = (wave < KX).astype(np.float32)
    factor = np.where((wave == 0) | (wave == W // 2), 1.0, 2.0).astype(np.float32)
    both = np.stack([cosine, sine]) * live
    result = []
    for weight in (np.ones_like(factor), factor):
        table = np.zeros(
            (
                size.groups,
                size.piece,
                size.lon,
                size.slots_here,
                size.lons_pad,
            ),
            np.float32,
        )
        values = (both * weight).reshape(2, size.lon, size.lons_here, size.groups, size.waves)
        values = np.transpose(values, (3, 0, 4, 1, 2)).reshape(
            size.groups, 2 * size.waves, size.lon, size.lons_here
        )
        for slot in range(size.slots_here):
            start = slot * 2 * size.waves
            table[:, start : start + 2 * size.waves, :, slot, : size.lons_here] = values
        flat = table.reshape(size.spectrum, size.tokens).astype(ml_dtypes.bfloat16)
        result.append(flat)
        result.append(np.ascontiguousarray(flat.T))
    return result


def lat_parts(size):
    lat_index = np.arange(H)
    angle = ((lat_index[:, None] * lat_index[None, :]) % H).astype(np.float32) * np.float32(
        2.0 * math.pi / H
    )
    scale = np.float32(1.0 / math.sqrt(H))
    cosine = np.zeros((96, 96), np.float32)
    sine = np.zeros((96, 96), np.float32)
    cosine[:H, :H] = np.cos(angle) * scale
    sine[:H, :H] = np.sin(angle) * scale
    spread_rows = np.zeros((2, size.modes, 2, 96), np.float32)
    row_wave = np.full((2, size.modes), -1, np.int32)
    for part in range(2):
        for lat in range(H):
            for wave in range(size.waves):
                spread_rows[part, lat * size.waves + wave, part, lat] = 1.0
                row_wave[part, lat * size.waves + wave] = wave
    spread_cols = np.zeros((2, 128, size.per_image, size.piece), np.float32)
    col_wave = np.full((size.per_image, size.piece), -2, np.int32)
    for device in range(size.per_image):
        for slot in range(size.slots_here):
            for part in range(2):
                for wave in range(size.waves):
                    place = (slot * 2 + part) * size.waves + wave
                    spread_cols[part, device * size.slots_here + slot, device, place] = 1.0
                    col_wave[device, place] = wave
    low = ml_dtypes.bfloat16
    return (
        cosine.astype(low),
        sine.astype(low),
        spread_rows.reshape(2 * size.modes, 192).astype(low),
        spread_cols.reshape(256, size.band).astype(low),
        row_wave.reshape(-1),
        col_wave.reshape(-1),
    )


def smooth_gate(values):
    return 0.5 * values * (1.0 + lax.erf(values * half_root))


def gate_both(values):
    half_phi = 0.5 * (1.0 + lax.erf(values * half_root))
    density = values * normal_peak * jnp.exp(-0.5 * values * values)
    return values * half_phi, half_phi + density


def gate_slope(values):
    return gate_both(values)[1]


def soft_shrink(values):
    return values - shrink_level * values * lax.rsqrt(values * values + shrink_level * shrink_level)


def shrink_slope(values):
    inverse = lax.rsqrt(values * values + shrink_level * shrink_level)
    return 1.0 - shrink_level * shrink_level * shrink_level * inverse * inverse * inverse


def norm_parts(values):
    center = values - jnp.mean(values, axis=-1, keepdims=True)
    spread = lax.rsqrt(jnp.mean(center * center, axis=-1, keepdims=True) + norm_eps)
    return center * spread, spread


def norm_back(scaled, unit, spread):
    return spread * (
        scaled
        - jnp.mean(scaled, axis=-1, keepdims=True)
        - unit * jnp.mean(scaled * unit, axis=-1, keepdims=True)
    )


def mm(left, right):
    return jnp.dot(left, right, preferred_element_type=f32)


def mm_t(left, right):
    return lax.dot_general(left, right, (((1,), (1,)), ((), ())), preferred_element_type=f32)


def t_mm(left, right):
    return lax.dot_general(left, right, (((0,), (0,)), ((), ())), preferred_element_type=f32)


def whole(count):
    return [pl.BlockSpec(memory_space=pltpu.VMEM)] * count


def call_local(kernel, name, outs, scratch=()):
    def run(*operands):
        return pl.pallas_call(
            kernel,
            out_shape=outs,
            in_specs=whole(len(operands)),
            out_specs=jax.tree.map(lambda _: pl.BlockSpec(memory_space=pltpu.VMEM), outs),
            scratch_shapes=list(scratch),
            compiler_params=pltpu.CompilerParams(vmem_limit_bytes=VMEM_BYTES),
            name=name,
        )(*operands)

    return run


def struct(shape, dtype):
    return jax.ShapeDtypeStruct(shape, dtype)


def tables_kernel(rows_ref, cos_ref, sin_ref, er_ref, ec_ref, rw_ref, cw_ref, rwt_ref, cwt_ref, lat_ref, lat_t_ref):
    lat_of = lax.broadcasted_iota(jnp.int32, (96, 128), 0)
    hot = (lat_of == rows_ref[...]).astype(f32).astype(bf16)
    cosine = mm(cos_ref[...], hot)
    sine = mm(sin_ref[...], hot)
    top = jnp.concatenate([cosine, sine], axis=1)
    bottom = jnp.concatenate([-sine, cosine], axis=1)
    base = jnp.concatenate([top, bottom], axis=0).astype(bf16)
    columns = mm(base, ec_ref[...]).astype(bf16)
    table = mm(er_ref[...], columns)
    lat_ref[...] = jnp.where(rw_ref[...] == cw_ref[...], table, 0.0).astype(bf16)
    table_t = lax.dot_general(columns, er_ref[...], (((0,), (1,)), ((), ())), preferred_element_type=f32)
    lat_t_ref[...] = jnp.where(cwt_ref[...] == rwt_ref[...], table_t, 0.0).astype(bf16)


def make_lat_tables(size, slot_lat):
    cosine, sine, spread_rows, spread_cols, row_wave, col_wave = lat_parts(size)
    rows = jnp.full((1, 128), -1, jnp.int32).at[0, : size.virtual_slots].set(slot_lat)
    return call_local(
        tables_kernel,
        "lat_tables",
        (
            struct((2 * size.modes, size.band), bf16),
            struct((size.band, 2 * size.modes), bf16),
        ),
    )(
        rows,
        jnp.asarray(cosine),
        jnp.asarray(sine),
        jnp.asarray(spread_rows),
        jnp.asarray(spread_cols),
        jnp.asarray(row_wave[:, None]),
        jnp.asarray(col_wave[None, :]),
        jnp.asarray(row_wave[None, :]),
        jnp.asarray(col_wave[:, None]),
    )


def pad_plane(size, plane):
    extra = size.lons_pad - size.lons_here
    return jnp.concatenate([plane, jnp.zeros((extra, plane.shape[1]), plane.dtype)], axis=0)


def planes(size):
    for source in range(size.lon):
        for slot in range(size.slots_here):
            yield source, slot, (source * size.slots_here + slot) * size.lons_pad


def write_pieces(size, values, out_ref):
    for half in range(HALVES):
        for group in range(size.groups):
            out_ref[half * size.groups + group] = values[
                group * size.piece : (group + 1) * size.piece,
                half * size.half : (half + 1) * size.half,
            ].astype(bf16)


def read_pieces(ref, first, count):
    return jnp.concatenate([ref[first + i].astype(f32) for i in range(count)], axis=0).astype(bf16)


def read_spectrum(size, ref):
    return jnp.concatenate(
        [read_pieces(ref, half * size.groups, size.groups) for half in range(HALVES)], axis=1
    )


def first_kernel(size, x_ref, vectors_ref, table_ref, send_ref, low_ref):
    gain, shift = vectors_ref[0:1, :], vectors_ref[1:2, :]
    for source, slot, start in planes(size):
        x = pad_plane(size, x_ref[source, slot].astype(f32))
        unit, _ = norm_parts(x)
        low_ref[start : start + size.lons_pad, :] = (unit * gain + shift).astype(bf16)
    write_pieces(size, mm(table_ref[...], low_ref[...]), send_ref)


def mix_kernel(size, recv_ref, lat_ref, lat_t_ref, w1_ref, b1_ref, w2_ref, b2_ref, send_ref, band_ref, inner_ref, gated_ref, outer_ref):
    spectrum = read_pieces(recv_ref, 0, size.per_image)
    modes = mm(lat_ref[...], spectrum)
    band = jnp.concatenate([modes[: size.modes], modes[size.modes :]], axis=1).astype(bf16)
    band_ref[...] = band
    inner = mm(band, w1_ref[...]) + b1_ref[...]
    inner_ref[...] = inner
    gated = smooth_gate(inner).astype(bf16)
    gated_ref[...] = gated
    outer = mm(gated, w2_ref[...]) + b2_ref[...]
    outer_ref[...] = outer
    shrunk = soft_shrink(outer)
    stacked = jnp.concatenate([shrunk[:, : size.half], shrunk[:, size.half :]], axis=0).astype(bf16)
    back = mm(lat_t_ref[...], stacked)
    for source in range(size.per_image):
        send_ref[source] = back[source * size.piece : (source + 1) * size.piece].astype(bf16)


def write_blocks(total, half, first, out_ref):
    block_size = out_ref.shape[1]
    blocks = half // block_size
    for block in range(blocks):
        near = slice(block * block_size, (block + 1) * block_size)
        far = slice(half + block * block_size, half + (block + 1) * block_size)
        out_ref[first + block] = total[near, near] + total[far, far]
        out_ref[first + blocks + block] = total[near, far] - total[far, near]


def mix_back_data(size, recv_ref, lat_ref, lat_t_ref, w1_ref, w2_ref, inner_ref, outer_ref, send_ref, outer_grad_ref, inner_grad_ref):
    half = size.half
    spectrum = read_pieces(recv_ref, 0, size.per_image)
    modes = mm(lat_ref[...], spectrum)
    upstream = jnp.concatenate([modes[: size.modes], modes[size.modes :]], axis=1).astype(bf16)
    outer_grad = (upstream.astype(f32) * shrink_slope(outer_ref[...])).astype(bf16)
    outer_grad_ref[...] = outer_grad
    inner_grad = (mm_t(outer_grad, w2_ref[...]) * gate_slope(inner_ref[...])).astype(bf16)
    inner_grad_ref[...] = inner_grad
    band_grad = mm_t(inner_grad, w1_ref[...])
    stacked = jnp.concatenate([band_grad[:, :half], band_grad[:, half:]], axis=0).astype(bf16)
    back = mm(lat_t_ref[...], stacked)
    for source in range(size.per_image):
        send_ref[source] = back[source * size.piece : (source + 1) * size.piece].astype(bf16)


def mix_back_weights(size, band_ref, gated_ref, outer_grad_ref, inner_grad_ref, out_ref):
    half = size.half
    block_size = out_ref.shape[2]
    blocks = half // block_size
    rest = out_ref.shape[1] - block_size
    for layer, (value_ref, grad_ref) in enumerate(
        ((band_ref, inner_grad_ref), (gated_ref, outer_grad_ref))
    ):
        grad = grad_ref[...]
        total = t_mm(value_ref[...], grad)
        bias = jnp.sum(grad.astype(f32), axis=0, keepdims=True)
        for block in range(blocks):
            near = slice(block * block_size, (block + 1) * block_size)
            far = slice(half + block * block_size, half + (block + 1) * block_size)
            place = layer * 2 * blocks + block
            out_ref[place, :block_size] = (total[near, near] + total[far, far]).astype(bf16)
            out_ref[place + blocks, :block_size] = (total[near, far] - total[far, near]).astype(bf16)
            shape = (rest, block_size)
            out_ref[place, block_size:] = jnp.broadcast_to(bias[:, near], shape).astype(bf16)
            out_ref[place + blocks, block_size:] = jnp.broadcast_to(bias[:, far], shape).astype(bf16)


def mix_back_kernel(size, recv_ref, lat_ref, lat_t_ref, w1_ref, w2_ref, band_ref, inner_ref, gated_ref, outer_ref, send_ref, grad_ref, outer_grad_ref, inner_grad_ref):
    mix_back_data(
        size, recv_ref, lat_ref, lat_t_ref, w1_ref, w2_ref, inner_ref, outer_ref, send_ref, outer_grad_ref, inner_grad_ref
    )
    mix_back_weights(size, band_ref, gated_ref, outer_grad_ref, inner_grad_ref, grad_ref)


def mlp_kernel(
    size,
    live_ref,
    recv_ref,
    x_ref,
    dy_ref,
    inv_t_ref,
    inv_ref,
    vectors_ref,
    fc_in_ref,
    fc_in_bias_ref,
    fc_out_ref,
    block_ref,
    dh_ref,
    send_ref,
    wide_ref,
    hidden_bias_ref,
    small_ref,
    res_ref,
    low_ref,
    up_ref,
    acc_ref,
    back_ref,
):
    step = pl.program_id(0)
    gain1, shift1, gain2, shift2, out_bias = [vectors_ref[i : i + 1, :] for i in range(5)]

    @pl.when(step == 0)
    def _():
        res_ref[...] = mm(inv_t_ref[...], read_spectrum(size, recv_ref))
        up_sum = jnp.zeros((1, size.channels), f32)
        for source, slot, start in planes(size):
            part = slice(start, start + size.lons_pad)
            x = pad_plane(size, x_ref[source, slot].astype(f32))
            unit, _ = norm_parts(x)
            residual = res_ref[part, :] + (unit * gain1 + shift1) + x
            res_ref[part, :] = residual
            unit, _ = norm_parts(residual)
            low_ref[part, :] = (unit * gain2 + shift2).astype(bf16)
            up = pad_plane(size, dy_ref[source, slot].astype(f32) * live_ref[0, slot])
            up_ref[part, :] = up.astype(bf16)
            up_sum = up_sum + jnp.sum(up, axis=0, keepdims=True)
        small_ref[...] = jnp.zeros_like(small_ref)
        small_ref[0:1, :] = up_sum
        acc_ref[...] = jnp.zeros_like(acc_ref)
        back_ref[...] = jnp.zeros_like(back_ref)

    low = low_ref[...]
    up = up_ref[...]
    gate, slope = gate_both(mm(low, fc_in_ref[...]) + fc_in_bias_ref[...])
    hidden = gate.astype(bf16)
    acc_ref[...] += mm(hidden, fc_out_ref[...])
    hidden_grad = (mm_t(up, fc_out_ref[...]) * slope).astype(bf16)
    hidden_bias_ref[...] = jnp.sum(hidden_grad.astype(f32), axis=0, keepdims=True)
    back_ref[...] += mm_t(hidden_grad, fc_in_ref[...])
    wide_ref[:, : size.channels] = t_mm(hidden_grad, low).astype(bf16)
    wide_ref[:, size.channels :] = t_mm(hidden, up).astype(bf16)

    @pl.when(step == pl.num_programs(0) - 1)
    def _():
        gain_sum = jnp.zeros((1, size.channels), f32)
        shift_sum = jnp.zeros((1, size.channels), f32)
        for source, slot, start in planes(size):
            part = slice(start, start + size.lons_pad)
            residual = res_ref[part, :]
            block = (residual + (acc_ref[part, :] + out_bias)) * live_ref[0, slot]
            block_ref[source, slot] = block[: size.lons_here].astype(bf16)
            unit, spread = norm_parts(residual)
            grad = back_ref[part, :]
            gain_sum = gain_sum + jnp.sum(grad * unit, axis=0, keepdims=True)
            shift_sum = shift_sum + jnp.sum(grad, axis=0, keepdims=True)
            grad = up_ref[part, :].astype(f32) + norm_back(grad * gain2, unit, spread)
            dh_ref[part, :] = grad
            low_ref[part, :] = grad.astype(bf16)
        small_ref[1:2, :] = gain_sum
        small_ref[2:3, :] = shift_sum
        write_pieces(size, mm(inv_ref[...], low_ref[...]), send_ref)


def run_mlp(size, hidden_units, live, recv, x, dy, inv_t, inv, vectors, fc_in, fc_in_bias, fc_out):
    channels = size.channels
    width = HIDDEN_BLOCK
    fixed = pl.BlockSpec(memory_space=pltpu.VMEM)
    tokens = (size.tokens, channels)
    return pl.pallas_call(
        functools.partial(mlp_kernel, size),
        grid=(hidden_units // width,),
        in_specs=[pl.BlockSpec(memory_space=pltpu.SMEM)]
        + [fixed] * 6
        + [
            pl.BlockSpec((channels, width), lambda i: (0, i)),
            pl.BlockSpec((1, width), lambda i: (0, i)),
            pl.BlockSpec((width, channels), lambda i: (i, 0)),
        ],
        out_specs=(
            fixed,
            fixed,
            fixed,
            pl.BlockSpec((width, 2 * channels), lambda i: (i, 0)),
            pl.BlockSpec((1, width), lambda i: (0, i)),
            fixed,
        ),
        out_shape=(
            struct(x.shape, bf16),
            struct(tokens, f32),
            struct((size.per_image, size.piece, size.half), bf16),
            struct((hidden_units, 2 * channels), bf16),
            struct((1, hidden_units), f32),
            struct((8, channels), f32),
        ),
        scratch_shapes=[
            pltpu.VMEM(tokens, f32),
            pltpu.VMEM(tokens, bf16),
            pltpu.VMEM(tokens, bf16),
            pltpu.VMEM(tokens, f32),
            pltpu.VMEM(tokens, f32),
        ],
        compiler_params=pltpu.CompilerParams(vmem_limit_bytes=VMEM_BYTES),
        name="mlp",
    )(live, recv, x, dy, inv_t, inv, vectors, fc_in, fc_in_bias, fc_out)


def last_planes(size, recv_ref, x_ref, dh_ref, table_t_ref, vectors_ref, out_ref, landing_ref, small_ref, sender, mover):
    gain = vectors_ref[0:1, :]
    filtered = mm(table_t_ref[...], read_spectrum(size, recv_ref))
    gain_sum = jnp.zeros((1, size.channels), f32)
    shift_sum = jnp.zeros((1, size.channels), f32)
    for source, slot, start in planes(size):
        part = slice(start, start + size.lons_pad)
        unit, spread = norm_parts(pad_plane(size, x_ref[source, slot].astype(f32)))
        base = dh_ref[part, :]
        grad = base + filtered[part]
        gain_sum = gain_sum + jnp.sum(grad * unit, axis=0, keepdims=True)
        shift_sum = shift_sum + jnp.sum(grad, axis=0, keepdims=True)
        grad = base + norm_back(grad * gain, unit, spread)
        out_ref[source, slot] = grad[: size.lons_here].astype(bf16)
    small_ref[0:1, :] = gain_sum
    small_ref[1:2, :] = shift_sum
    if sender is None:
        return None
    return start_lon(out_ref, landing_ref, sender, mover)


def last_kernel(size, recv_ref, x_ref, dh_ref, table_t_ref, vectors_ref, out_ref, small_ref):
    last_planes(size, recv_ref, x_ref, dh_ref, table_t_ref, vectors_ref, out_ref, None, small_ref, None, None)


def partners(lon_count):
    row = lax.axis_index("rows")
    lon = lax.axis_index("lon")
    core = {"rows": row, "lon": lon + 1 - 2 * (lon % 2)}
    along_y = {"rows": row, "lon": (lon + 2) % 4}
    along_x = {"rows": row + 1 - 2 * (row % 2), "lon": lon}
    far_z = {"rows": (row + 4) % 8, "lon": lon}
    return core, along_y, along_x, far_z


def greet(lon_count, count):
    row = lax.axis_index("rows")
    lon = lax.axis_index("lon")
    me = row * lon_count + lon
    barrier = pltpu.get_barrier_semaphore()
    for offset in range(1, count):
        other = (me + offset) % count
        pl.semaphore_signal(
            barrier,
            inc=1,
            device_id={"rows": other // lon_count, "lon": other % lon_count},
            device_id_type=MESH,
        )
    pl.semaphore_wait(barrier, count - 1)


class Sender:
    def __init__(self, send_sem, recv_sem):
        self.send_sem = send_sem
        self.recv_sem = recv_sem
        self.used = 0

    def start(self, source, target, device):
        copy = pltpu.make_async_remote_copy(
            src_ref=source,
            dst_ref=target,
            send_sem=self.send_sem.at[self.used],
            recv_sem=self.recv_sem.at[self.used],
            device_id=device,
            device_id_type=MESH,
        )
        self.used += 1
        copy.start()
        return copy


class Mover:
    def __init__(self, sem):
        self.sem = sem
        self.used = 0

    def start(self, source, target):
        copy = pltpu.make_async_copy(source, target, self.sem.at[self.used])
        self.used += 1
        copy.start()
        return copy


def start_all(lon_count, source_ref, out_ref, sender, mover):
    me = lax.axis_index("rows") * lon_count + lax.axis_index("lon")
    count = source_ref.shape[0]
    copies = []
    for offset in range(1, count):
        other = (me + offset) % count
        copies.append(
            sender.start(
                source_ref.at[other],
                out_ref.at[me],
                {"rows": other // lon_count, "lon": other % lon_count},
            )
        )
    copies.append(mover.start(source_ref.at[me], out_ref.at[me]))
    return copies


def start_lon(source_ref, out_ref, sender, mover):
    row = lax.axis_index("rows")
    me = lax.axis_index("lon")
    count = source_ref.shape[0]
    copies = []
    for offset in range(1, count):
        other = (me + offset) % count
        copies.append(
            sender.start(source_ref.at[other], out_ref.at[me], {"rows": row, "lon": other})
        )
    copies.append(mover.start(source_ref.at[me], out_ref.at[me]))
    return copies


def finish(copies):
    for copy in copies:
        copy.wait()


def call_remote(kernel, name, number, outs, spaces, out_spaces, sends, moves, scratch, operands):
    return pl.pallas_call(
        kernel,
        out_shape=outs,
        in_specs=[pl.BlockSpec(memory_space=space) for space in spaces],
        out_specs=tuple(pl.BlockSpec(memory_space=space) for space in out_spaces),
        scratch_shapes=[
            pltpu.SemaphoreType.DMA((sends,)),
            pltpu.SemaphoreType.DMA((sends,)),
            pltpu.SemaphoreType.DMA((moves,)),
        ]
        + list(scratch),
        compiler_params=pltpu.CompilerParams(
            collective_id=number, has_side_effects=True, vmem_limit_bytes=VMEM_BYTES
        ),
        name=name,
    )(*operands)


def lon_kernel(lon_count, count, source_ref, out_ref, send_sem, recv_sem, move_sem):
    greet(lon_count, count)
    finish(start_lon(source_ref, out_ref, Sender(send_sem, recv_sem), Mover(move_sem)))


def all_kernel(lon_count, count, source_ref, out_ref, send_sem, recv_sem, move_sem):
    greet(lon_count, count)
    finish(start_all(lon_count, source_ref, out_ref, Sender(send_sem, recv_sem), Mover(move_sem)))


def all_lon_kernel(lon_count, count, source_ref, other_ref, out_ref, other_out_ref, send_sem, recv_sem, move_sem):
    greet(lon_count, count)
    sender, mover = Sender(send_sem, recv_sem), Mover(move_sem)
    copies = start_all(lon_count, source_ref, out_ref, sender, mover)
    copies += start_lon(other_ref, other_out_ref, sender, mover)
    finish(copies)


def exchange_lon(size, values, number):
    if size.images > 1:
        return lax.all_to_all(values, "lon", split_axis=0, concat_axis=0, tiled=True)
    return call_remote(
        functools.partial(lon_kernel, size.lon, size.devices),
        "exchange_lon" + str(number),
        number,
        (struct(values.shape, values.dtype),),
        [pl.ANY],
        [pl.ANY],
        size.lon,
        1,
        (),
        (values,),
    )[0]


def exchange_all(size, values, number):
    if size.images > 1:
        return lax.all_to_all(values, ("rows", "lon"), split_axis=0, concat_axis=0, tiled=True)
    return call_remote(
        functools.partial(all_kernel, size.lon, size.devices),
        "exchange_all" + str(number),
        number,
        (struct(values.shape, values.dtype),),
        [pl.ANY],
        [pl.ANY],
        size.devices,
        1,
        (),
        (values,),
    )[0]


def exchange_both(size, pieces, planes_sent, number):
    return call_remote(
        functools.partial(all_lon_kernel, size.lon, size.devices),
        "exchange_both" + str(number),
        number,
        (struct(pieces.shape, pieces.dtype), struct(planes_sent.shape, planes_sent.dtype)),
        [pl.ANY, pl.ANY],
        [pl.ANY, pl.ANY],
        size.devices + size.lon,
        2,
        (),
        (pieces, planes_sent),
    )


def add_planes(left_ref, right_ref, out_ref):
    @pl.loop(0, left_ref.shape[0])
    def _(first):
        for second in range(left_ref.shape[1]):
            total = left_ref[first, second].astype(f32) + right_ref[first, second].astype(f32)
            out_ref[first, second] = total.astype(out_ref.dtype)


def start_same(lon_count, count, source_ref, out_ref, sender, mover):
    me = lax.axis_index("rows") * lon_count + lax.axis_index("lon")
    copies = []
    for offset in range(1, count):
        other = (me + offset) % count
        copies.append(
            sender.start(
                source_ref, out_ref.at[me], {"rows": other // lon_count, "lon": other % lon_count}
            )
        )
    copies.append(mover.start(source_ref, out_ref.at[me]))
    return copies


def backward_kernel(
    size,
    pieces_ref,
    wide_ref,
    block_ref,
    lat_hbm,
    lat_t_hbm,
    w1_hbm,
    w2_hbm,
    band_hbm,
    inner_hbm,
    gated_hbm,
    outer_hbm,
    x_hbm,
    dh_hbm,
    table_t_hbm,
    vectors_ref,
    early_ref,
    token_out,
    block_out,
    dense_ref,
    mix_out,
    early_out,
    late_out,
    send_sem,
    recv_sem,
    move_sem,
    lat_ref,
    lat_t_ref,
    w1_ref,
    w2_ref,
    band_ref,
    inner_ref,
    gated_ref,
    outer_ref,
    x_ref,
    dh_ref,
    table_t_ref,
    recv1,
    send2,
    recv2,
    token_ref,
    a_go,
    a_go_in,
    b_go,
    b_go_in,
    a_keep,
    a_keep_in,
    b_keep,
    b_keep_in,
    a_land,
    b_land,
    a2_land,
    b2_land,
    a2,
    b2,
    a3_land,
    b3_land,
    a3,
    b3,
    a4_land,
    b4_land,
    outer_grad_ref,
    inner_grad_ref,
    mix_ref,
    mix_land,
    pair_ref,
    early,
    early_land,
    late,
    late_land,
):
    lon_count, count, groups = size.lon, size.devices, size.groups
    row = lax.axis_index("rows")
    lon = lax.axis_index("lon")
    me = row * lon_count + lon
    z = row // 2
    x = row % 2
    y = lon // 2
    core = lon % 2
    group = me % groups
    base = me - group
    half = me // groups
    to_core, to_y, to_x, far_z = partners(lon_count)
    near = z + 1 - 2 * (z % 2)
    mirror = 3 - z
    to_near = {"rows": near * 2 + x, "lon": lon}
    to_mirror = {"rows": mirror * 2 + x, "lon": lon}
    width = wide_ref.shape[-1] // 2
    first, second = pl.ds(0, width), pl.ds(width, width)
    sender, mover = Sender(send_sem, recv_sem), Mover(move_sem)

    greet(lon_count, count)
    early[...] = early_ref[...]
    stage = 0

    def early_start(device):
        return sender.start(early, early_land.at[stage], device)

    early_hop = early_start(to_core)
    views = (
        (lambda c: wide_ref.at[:, 1 - x, :, c, :, first], a_go, a_go_in),
        (lambda c: wide_ref.at[:, :, 1 - y, c, :, second], b_go, b_go_in),
        (lambda c: wide_ref.at[:, x, :, c, :, first], a_keep, a_keep_in),
        (lambda c: wide_ref.at[:, :, y, c, :, second], b_keep, b_keep_in),
    )
    pairs = []
    for view, own, landed in views[:2]:
        pairs.append((sender.start(view(1 - core), landed, to_core), mover.start(view(core), own)))
    pieces = start_all(lon_count, pieces_ref, recv1, sender, mover)
    for view, own, landed in views[2:]:
        pairs.append((sender.start(view(1 - core), landed, to_core), mover.start(view(core), own)))
    loads = [
        mover.start(source, target)
        for source, target in (
            (lat_hbm, lat_ref),
            (outer_hbm, outer_ref),
            (w2_hbm, w2_ref),
            (inner_hbm, inner_ref),
            (w1_hbm, w1_ref),
            (lat_t_hbm, lat_t_ref),
            (gated_hbm, gated_ref),
            (band_hbm, band_ref),
            (x_hbm, x_ref),
            (dh_hbm, dh_ref),
            (table_t_hbm, table_t_ref),
        )
    ]

    hops = []
    for pair, own, landed, target, device in (
        (pairs[0], a_go, a_go_in, a_land, to_x),
        (pairs[1], b_go, b_go_in, b_land, to_y),
    ):
        finish(pair)
        add_planes(own, landed, own)
        hops.append(sender.start(own, target, device))
    early_hop.wait()
    early[...] = early[...] + early_land[0]
    stage = 1
    early_hop = early_start(to_x)
    for pair, own, landed in ((pairs[2], a_keep, a_keep_in), (pairs[3], b_keep, b_keep_in)):
        finish(pair)
        add_planes(own, landed, own)

    finish(pieces)
    finish(loads)
    mix_back_data(
        size, recv1, lat_ref, lat_t_ref, w1_ref, w2_ref, inner_ref, outer_ref, send2, outer_grad_ref, inner_grad_ref
    )
    pieces = start_all(lon_count, send2, recv2, sender, mover)
    mix_back_weights(size, band_ref, gated_ref, outer_grad_ref, inner_grad_ref, mix_ref)
    parts = []
    for offset in range(1, groups):
        other = (group + offset) % groups
        device = base + other
        parts.append(
            sender.start(
                mix_ref.at[other],
                mix_land.at[group],
                {"rows": device // lon_count, "lon": device % lon_count},
            )
        )
    parts.append(mover.start(mix_ref.at[group], mix_land.at[group]))

    hops[0].wait()
    add_planes(a_keep, a_land, a_keep)
    hops[1].wait()
    add_planes(b_keep, b_land, b_keep)
    hops = [
        sender.start(a_keep.at[:, 1 - y], a2_land, to_y),
        sender.start(b_keep.at[:, 1 - x], b2_land, to_x),
    ]
    early_hop.wait()
    early[...] = early[...] + early_land[1]
    stage = 2
    early_hop = early_start(to_y)
    blocks = start_lon(block_ref, block_out, sender, mover)

    finish(parts)
    total = mix_land[0].astype(f32)
    for index in range(1, groups):
        total = total + mix_land[index].astype(f32)
    pair_ref[half] = total.astype(bf16)
    crossing = sender.start(pair_ref.at[half], pair_ref.at[half], far_z)

    hops[0].wait()
    for place in range(4):
        a2[place] = (a_keep[place, y].astype(f32) + a2_land[place].astype(f32)).astype(bf16)
    hops[1].wait()
    for place in range(4):
        b2[place] = (b_keep[place, x].astype(f32) + b2_land[place].astype(f32)).astype(bf16)
    hops = [
        sender.start(a2.at[near], a3_land.at[0], to_near),
        sender.start(a2.at[3 - near], a3_land.at[1], to_near),
        sender.start(b2.at[near], b3_land.at[0], to_near),
        sender.start(b2.at[3 - near], b3_land.at[1], to_near),
    ]
    early_hop.wait()
    early[...] = early[...] + early_land[2]
    stage = 3
    early_hop = early_start(to_near)
    crossing.wait()
    gather = []
    for offset in range(1, groups):
        device = base + (group + offset) % groups
        gather.append(
            sender.start(
                pair_ref,
                mix_out.at[:, group],
                {"rows": device // lon_count, "lon": device % lon_count},
            )
        )
    gather.append(mover.start(pair_ref, mix_out.at[:, group]))

    finish(pieces)
    tokens = last_planes(size, recv2, x_ref, dh_ref, table_t_ref, vectors_ref, token_ref, token_out, late, sender, mover)
    smalls = start_same(lon_count, count, late, late_land, sender, mover)

    finish(hops)
    for land, kept, summed in ((a3_land, a2, a3), (b3_land, b2, b3)):
        summed[0] = (kept[z].astype(f32) + land[0].astype(f32)).astype(bf16)
        summed[1] = (kept[mirror].astype(f32) + land[1].astype(f32)).astype(bf16)
    hops = [
        sender.start(a3.at[1], a4_land, to_mirror),
        sender.start(b3.at[1], b4_land, to_mirror),
    ]
    early_hop.wait()
    early[...] = early[...] + early_land[3]
    stage = 4
    early_hop = early_start(to_mirror)
    finish(smalls)
    total = late_land[0]
    for index in range(1, count):
        total = total + late_land[index]
    late_out[...] = total
    finish(hops)
    dense_ref[0] = a3[0].astype(f32) + a4_land[...].astype(f32)
    dense_ref[1] = b3[0].astype(f32) + b4_land[...].astype(f32)
    early_hop.wait()
    early_out[...] = early[...] + early_land[4]
    finish(gather)
    finish(blocks)
    finish(tokens)


def run_backward(size, blocks_shape, pieces, wide, block, lat, lat_t, w1, w2, band, inner, gated, outer, x, dh, table_t, vectors, early, number):
    share, columns = wide.shape[0] // size.devices, wide.shape[1]
    part = (4, 2, share, columns // 2)
    row_part = (share, columns // 2)
    operands = (lat, lat_t, w1, w2, band, inner, gated, outer, x, dh, table_t)
    late = (2, size.channels)

    def spaces(count, space):
        return [space] * count

    scratch = [pltpu.VMEM(v.shape, v.dtype) for v in operands]
    scratch += [pltpu.VMEM(pieces.shape, bf16)] * 3
    scratch += [pltpu.VMEM(x.shape, bf16)]
    scratch += [pltpu.VMEM(part, bf16)] * 10
    scratch += [pltpu.VMEM((4,) + row_part, bf16)] * 4
    scratch += [pltpu.VMEM((2,) + row_part, bf16)] * 4
    scratch += [pltpu.VMEM(row_part, bf16)] * 2
    scratch += [pltpu.VMEM(band.shape, bf16)] * 2
    scratch += [pltpu.VMEM(blocks_shape, bf16)] * 2
    scratch += [pltpu.VMEM((HALVES,) + blocks_shape[1:], bf16)]
    scratch += [pltpu.VMEM(early.shape, f32), pltpu.VMEM((5,) + early.shape, f32)]
    scratch += [pltpu.VMEM(late, f32), pltpu.VMEM((size.devices,) + late, f32)]
    return call_remote(
        functools.partial(backward_kernel, size),
        "backward",
        number,
        (
            struct(x.shape, bf16),
            struct(block.shape, bf16),
            struct((2,) + row_part, f32),
            struct((HALVES,) + blocks_shape, bf16),
            struct(early.shape, f32),
            struct(late, f32),
        ),
        spaces(14, pl.ANY) + spaces(2, pltpu.VMEM),
        spaces(2, pl.ANY) + spaces(4, pltpu.VMEM),
        3 * size.devices + 2 * size.groups + 2 * size.lon + 32,
        32,
        scratch,
        (pieces, wide.reshape(4, 2, 2, 2, share, columns), block) + operands + (vectors, early),
    )


def to_modes(size, pieces, row_map, number):
    if size.images == 1:
        return exchange_all(size, pieces, number)
    sent = jnp.tile(pieces, (size.images, 1, 1))
    received = exchange_all(size, sent, number)
    used = size.slots_here * 2 * size.waves
    by_slot = received[:, :used].reshape(-1, 2 * size.waves, size.half)
    image = (lax.axis_index("rows") * size.lon + lax.axis_index("lon")) // size.per_image
    slots = row_map.shape[0]
    target = jnp.where(row_map >= 0, row_map, size.images * H)
    slot_of_row = (
        jnp.zeros((size.images * H,), jnp.int32)
        .at[target]
        .set(jnp.arange(slots, dtype=jnp.int32), mode="drop")
    )
    own = lax.dynamic_slice_in_dim(slot_of_row, image * H, H)
    picked = jnp.take(by_slot, own, axis=0)
    picked = jnp.pad(picked, ((0, size.virtual_slots - H), (0, 0), (0, 0)))
    picked = picked.reshape(size.per_image, used, size.half)
    return jnp.pad(picked, ((0, 0), (0, size.piece - used), (0, 0)))


def from_modes(size, pieces, row_map, number):
    if size.images == 1:
        return exchange_all(size, pieces, number)
    used = size.slots_here * 2 * size.waves
    by_lat = pieces[:, :used].reshape(-1, 2 * size.waves, size.half)
    image = (lax.axis_index("rows") * size.lon + lax.axis_index("lon")) // size.per_image
    live = (row_map >= 0) & (row_map // H == image)
    picked = jnp.take(by_lat, jnp.where(live, row_map % H, 0), axis=0)
    picked = picked * live.astype(bf16)[:, None, None]
    picked = picked.reshape(size.devices, used, size.half)
    sent = jnp.pad(picked, ((0, 0), (0, size.piece - used), (0, 0)))
    received = exchange_all(size, sent, number)
    received = received.reshape(size.images, size.per_image, size.piece, size.half)
    return jnp.sum(received.astype(f32), axis=0).astype(bf16)


def block_matrix(weight, half_index, blocks_here):
    block_size = weight.shape[2]
    own = lax.dynamic_slice_in_dim(weight, half_index * blocks_here, blocks_here, axis=1)
    eye = jnp.eye(blocks_here, dtype=bf16)
    real, imag = [
        (own[part][:, :, None, :] * eye[:, None, :, None]).reshape(
            blocks_here * block_size, blocks_here * block_size
        )
        for part in range(2)
    ]
    return jnp.concatenate(
        [jnp.concatenate([real, imag], axis=1), jnp.concatenate([-imag, real], axis=1)], axis=0
    )


def half_bias(bias, half_index, size):
    flat = bias.reshape(2, size.channels)
    own = lax.dynamic_slice_in_dim(flat, half_index * size.half, size.half, axis=1)
    return own.reshape(1, 2 * size.half)


def body(
    tokens,
    row_map,
    cotangent,
    norm_gain,
    norm_shift,
    mix_in,
    mix_in_bias,
    mix_out,
    mix_out_bias,
    post_gain,
    post_shift,
    fc_in,
    fc_in_bias,
    fc_out,
    fc_out_bias,
):
    size = Sizes(
        lax.axis_size("rows"), lax.axis_size("lon"), row_map.shape[0], tokens.shape[2]
    )
    channels = size.channels
    blocks = mix_in.shape[1]
    blocks_here = blocks // HALVES
    block_size = mix_in.shape[2]
    hidden_units = fc_in.shape[1]
    device = lax.axis_index("rows") * size.lon + lax.axis_index("lon")
    half_index = (device % size.per_image) // size.groups

    table, table_t, inv, inv_t = [jnp.asarray(t) for t in lon_tables(size)]
    if size.images == 1:
        slot_lat = row_map
    else:
        slot_lat = jnp.where(jnp.arange(size.virtual_slots) < H, jnp.arange(size.virtual_slots), -1)
    lat, lat_t = make_lat_tables(size, slot_lat)
    w1 = block_matrix(mix_in, half_index, blocks_here)
    w2 = block_matrix(mix_out, half_index, blocks_here)
    b1 = half_bias(mix_in_bias, half_index, size)
    b2 = half_bias(mix_out_bias, half_index, size)
    own_map = lax.dynamic_slice_in_dim(row_map, device * size.slots_here, size.slots_here)
    live = (own_map >= 0).astype(f32).reshape(1, size.slots_here)

    vectors = jnp.stack([norm_gain, norm_shift, post_gain, post_shift, fc_out_bias])
    shape = (size.lon, size.slots_here, size.lons_here, channels)
    x = exchange_lon(size, tokens.reshape(shape), 0)
    dy = cotangent.reshape(shape)

    piece_shape = struct((size.per_image, size.piece, size.half), bf16)
    sent = call_local(
        functools.partial(first_kernel, size),
        "lon_forward",
        piece_shape,
        [pltpu.VMEM((size.tokens, channels), bf16)],
    )(x, vectors, table)
    if size.images == 1:
        received, dy = exchange_both(size, sent, dy, 1)
    else:
        received, dy = to_modes(size, sent, row_map, 1), exchange_lon(size, dy, 2)
    mode_shape = (size.modes, 2 * size.half)
    sent, band, inner, gated, outer = call_local(
        functools.partial(mix_kernel, size),
        "mix_forward",
        (
            piece_shape,
            struct(mode_shape, bf16),
            struct(mode_shape, f32),
            struct(mode_shape, bf16),
            struct(mode_shape, f32),
        ),
    )(received, lat, lat_t, w1, b1, w2, b2)
    received = from_modes(size, sent, row_map, 3)
    block, dh, sent, wide, hidden_bias, small = run_mlp(
        size, hidden_units, live, received, x, dy, inv_t, inv, vectors, fc_in, fc_in_bias.reshape(1, -1), fc_out
    )
    early = jnp.concatenate(
        [small[0:3], hidden_bias.reshape(-1, channels), small[3:4]], axis=0
    )
    blocks_shape = (4 * blocks_here, round_up(block_size + 1, 16), block_size)
    if size.images == 1:
        token_grad, block, dense, mix_total, early, late = run_backward(
            size, blocks_shape, sent, wide, block, lat, lat_t, w1, w2, band, inner, gated, outer, x, dh, table_t, vectors, early, 4
        )
    else:
        names = ("rows", "lon")
        early = lax.psum(early, names)
        dense = lax.psum_scatter(wide, names, scatter_dimension=0, tiled=True)
        dense = jnp.stack([dense[:, :channels], dense[:, channels:]]).astype(f32)
        block = exchange_lon(size, block, 4)
        received = to_modes(size, sent, row_map, 5)
        sent, mix_grad = call_local(
            functools.partial(mix_back_kernel, size),
            "mix_backward",
            (piece_shape, struct(blocks_shape, bf16)),
            [pltpu.VMEM(mode_shape, bf16)] * 2,
        )(received, lat, lat_t, w1, w2, band, inner, gated, outer)
        mix_total = lax.psum(
            jnp.stack(
                [mix_grad.astype(f32) * (half_index == other).astype(f32) for other in range(HALVES)]
            ),
            names,
        )
        received = from_modes(size, sent, row_map, 6)
        token_grad, late = call_local(
            functools.partial(last_kernel, size),
            "lon_backward",
            (struct(x.shape, bf16), struct((2, channels), f32)),
        )(received, x, dh, table_t, vectors)
        token_grad = exchange_lon(size, token_grad, 7)
        late = lax.psum(late, names)
    mix_total = mix_total.astype(f32).reshape((HALVES, 2, 2, blocks_here) + blocks_shape[1:])
    mix_total = jnp.transpose(mix_total, (1, 2, 0, 3, 4, 5)).reshape((2, 2, blocks) + blocks_shape[1:])
    mix_bias = mix_total[:, :, :, block_size]
    mix_total = mix_total[:, :, :, :block_size]
    share = hidden_units // size.devices
    return (
        block.reshape(tokens.shape),
        token_grad.reshape(tokens.shape).astype(f32),
        late[0],
        late[1],
        mix_total[0],
        mix_bias[0],
        mix_total[1],
        mix_bias[1],
        early[1],
        early[2],
        dense[0].T,
        lax.dynamic_slice_in_dim(early[3:7].reshape(-1), device * share, share),
        dense[1],
        early[0],
    )


def solution(mesh):
    return jax.shard_map(
        body,
        mesh=mesh,
        in_specs=(P("rows", "lon", None), P(), P("rows", "lon", None)) + (P(),) * 12,
        out_specs=(
            P("rows", "lon", None),
            P("rows", "lon", None),
            P(),
            P(),
            P(),
            P(),
            P(),
            P(),
            P(),
            P(),
            P(None, ("rows", "lon")),
            P(("rows", "lon")),
            P(("rows", "lon"), None),
            P(),
        ),
        check_vma=False,
    )
```

```python
import functools
import math

import jax
import jax.numpy as jnp
import ml_dtypes
import numpy as np
from jax import lax
from jax.experimental import pallas as pl
from jax.experimental.pallas import tpu as pltpu
from jax.sharding import PartitionSpec as P

H = 90
W = 180
KX = 91
HALVES = 2
QUARTERS = 4
HIDDEN_BLOCK = 256
VMEM_BYTES = 58 * 1024 * 1024

norm_eps = 1e-06
shrink_level = 0.01
half_root = 0.7071067811865476
normal_peak = 0.3989422804014327
MESH = pl.DeviceIdType.MESH
f32 = jnp.float32
bf16 = jnp.bfloat16


def round_up(value, step):
    return -(-value // step) * step


class Sizes:
    def __init__(self, rows_count, lon_count, slots, channels):
        self.rows = rows_count
        self.lon = lon_count
        self.devices = rows_count * lon_count
        self.images = slots * 15 // (16 * H)
        self.per_image = self.devices // self.images
        self.groups = self.per_image // HALVES
        self.waves = -(-KX // self.groups)
        self.slots_here = slots // self.devices
        self.lons_here = W // lon_count
        self.lons_pad = round_up(self.lons_here, 16)
        self.tokens = lon_count * self.slots_here * self.lons_pad
        self.piece = round_up(self.slots_here * 2 * self.waves, 8)
        self.spectrum = self.groups * self.piece
        self.band = self.per_image * self.piece
        self.modes = round_up(H * self.waves, 16)
        self.virtual_slots = self.per_image * self.slots_here
        self.chunk = self.per_image // QUARTERS
        self.chunk_rows = self.chunk * self.piece
        self.channels = channels
        self.half = channels // HALVES


def place_of(size, row, lon):
    return (row % QUARTERS) * size.chunk + (row // QUARTERS) * size.lon + lon


def place_order(size):
    place = np.array([place_of(size, d // size.lon, d % size.lon) for d in range(size.per_image)])
    return np.argsort(place), place


def lon_tables(size):
    wave = np.arange(size.groups * size.waves)
    lon_index = np.arange(W)
    product = (lon_index[:, None] * wave[None, :]) % W
    angle = product.astype(np.float32) * np.float32(2.0 * math.pi / W)
    scale = np.float32(1.0 / math.sqrt(W))
    cosine = (np.cos(angle) * scale).astype(ml_dtypes.bfloat16).astype(np.float32)
    sine = (-np.sin(angle) * scale).astype(ml_dtypes.bfloat16).astype(np.float32)
    live = (wave < KX).astype(np.float32)
    factor = np.where((wave == 0) | (wave == W // 2), 1.0, 2.0).astype(np.float32)
    both = np.stack([cosine, sine]) * live
    result = []
    for weight in (np.ones_like(factor), factor):
        table = np.zeros(
            (
                size.groups,
                size.piece,
                size.lon,
                size.slots_here,
                size.lons_pad,
            ),
            np.float32,
        )
        values = (both * weight).reshape(2, size.lon, size.lons_here, size.groups, size.waves)
        values = np.transpose(values, (3, 0, 4, 1, 2)).reshape(
            size.groups, 2 * size.waves, size.lon, size.lons_here
        )
        for slot in range(size.slots_here):
            start = slot * 2 * size.waves
            table[:, start : start + 2 * size.waves, :, slot, : size.lons_here] = values
        flat = table.reshape(size.spectrum, size.tokens).astype(ml_dtypes.bfloat16)
        result.append(flat)
        result.append(np.ascontiguousarray(flat.T))
    return result


def lat_parts(size):
    lat_index = np.arange(H)
    angle = ((lat_index[:, None] * lat_index[None, :]) % H).astype(np.float32) * np.float32(
        2.0 * math.pi / H
    )
    scale = np.float32(1.0 / math.sqrt(H))
    cosine = np.zeros((96, 96), np.float32)
    sine = np.zeros((96, 96), np.float32)
    cosine[:H, :H] = np.cos(angle) * scale
    sine[:H, :H] = np.sin(angle) * scale
    spread_rows = np.zeros((2, size.modes, 2, 96), np.float32)
    for part in range(2):
        for lat in range(H):
            for wave in range(size.waves):
                spread_rows[part, lat * size.waves + wave, part, lat] = 1.0
    spread_cols = np.zeros((QUARTERS, 2, 128, size.chunk, size.piece), np.float32)
    for place, device in enumerate(place_order(size)[0]):
        for slot in range(size.slots_here):
            for part in range(2):
                for wave in range(size.waves):
                    spread_cols[
                        place // size.chunk,
                        part,
                        device * size.slots_here + slot,
                        place % size.chunk,
                        (slot * 2 + part) * size.waves + wave,
                    ] = 1.0
    low = ml_dtypes.bfloat16
    return (
        cosine.astype(low),
        sine.astype(low),
        spread_rows.reshape(2 * size.modes, 192).astype(low),
        spread_cols.reshape(QUARTERS, 256, size.chunk_rows).astype(low),
    )


def smooth_gate(values):
    return 0.5 * values * (1.0 + lax.erf(values * half_root))


def gate_both(values):
    half_phi = 0.5 * (1.0 + lax.erf(values * half_root))
    density = values * normal_peak * jnp.exp(-0.5 * values * values)
    return values * half_phi, half_phi + density


def gate_slope(values):
    return gate_both(values)[1]


def soft_shrink(values):
    return values - shrink_level * values * lax.rsqrt(values * values + shrink_level * shrink_level)


def shrink_slope(values):
    inverse = lax.rsqrt(values * values + shrink_level * shrink_level)
    return 1.0 - shrink_level * shrink_level * shrink_level * inverse * inverse * inverse


def norm_parts(values):
    center = values - jnp.mean(values, axis=-1, keepdims=True)
    spread = lax.rsqrt(jnp.mean(center * center, axis=-1, keepdims=True) + norm_eps)
    return center * spread, spread


def norm_back(scaled, unit, spread):
    return spread * (
        scaled
        - jnp.mean(scaled, axis=-1, keepdims=True)
        - unit * jnp.mean(scaled * unit, axis=-1, keepdims=True)
    )


def mm(left, right):
    return jnp.dot(left, right, preferred_element_type=f32)


def mm_t(left, right):
    return lax.dot_general(left, right, (((1,), (1,)), ((), ())), preferred_element_type=f32)


def t_mm(left, right):
    return lax.dot_general(left, right, (((0,), (0,)), ((), ())), preferred_element_type=f32)


def whole(count):
    return [pl.BlockSpec(memory_space=pltpu.VMEM)] * count


def call_local(kernel, name, outs, scratch=()):
    def run(*operands):
        return pl.pallas_call(
            kernel,
            out_shape=outs,
            in_specs=whole(len(operands)),
            out_specs=jax.tree.map(lambda _: pl.BlockSpec(memory_space=pltpu.VMEM), outs),
            scratch_shapes=list(scratch),
            compiler_params=pltpu.CompilerParams(vmem_limit_bytes=VMEM_BYTES),
            name=name,
        )(*operands)

    return run


def struct(shape, dtype):
    return jax.ShapeDtypeStruct(shape, dtype)


def wave_of(index, period, used, waves, other):
    within = index - period * jnp.floor((index + 0.5) * (1.0 / period))
    wave = within - waves * jnp.floor((within + 0.5) * (1.0 / waves))
    return jnp.where(within < used, wave, other)


def build_lat_tables(size, rows_ref, cos_ref, sin_ref, er_ref, ec_ref, lat_ref, lat_t_ref):
    lat_of = lax.broadcasted_iota(jnp.int32, (96, 128), 0)
    hot = (lat_of == rows_ref[...]).astype(f32).astype(bf16)
    cosine = mm(cos_ref[...], hot)
    sine = mm(sin_ref[...], hot)
    top = jnp.concatenate([cosine, sine], axis=1)
    bottom = jnp.concatenate([-sine, cosine], axis=1)
    base = jnp.concatenate([top, bottom], axis=0).astype(bf16)

    def row_waves(shape, dim):
        index = lax.broadcasted_iota(jnp.int32, shape, dim).astype(f32)
        return wave_of(index, size.modes, H * size.waves, size.waves, -1.0)

    def col_waves(shape, dim):
        index = lax.broadcasted_iota(jnp.int32, shape, dim).astype(f32)
        return wave_of(index, size.piece, size.slots_here * 2 * size.waves, size.waves, -2.0)

    modes, columns_here = 2 * size.modes, size.chunk_rows
    keep = row_waves((modes, 1), 0) == col_waves((1, columns_here), 1)
    keep_t = col_waves((columns_here, 1), 0) == row_waves((1, modes), 1)
    for quarter in range(QUARTERS):
        columns = mm(base, ec_ref[quarter]).astype(bf16)
        table = mm(er_ref[...], columns)
        lat_ref[quarter] = jnp.where(keep, table, 0.0).astype(bf16)
        table_t = lax.dot_general(
            columns, er_ref[...], (((0,), (1,)), ((), ())), preferred_element_type=f32
        )
        lat_t_ref[quarter] = jnp.where(keep_t, table_t, 0.0).astype(bf16)


def build_block_matrix(size, weight_ref, bias_ref, half, matrix_ref, row_ref):
    block_size = weight_ref.shape[2]
    blocks = size.half // block_size
    matrix_ref[...] = jnp.zeros_like(matrix_ref)
    for block in range(blocks):
        real = weight_ref[0, half * blocks + block]
        imag = weight_ref[1, half * blocks + block]
        near = slice(block * block_size, (block + 1) * block_size)
        far = slice(size.half + block * block_size, size.half + (block + 1) * block_size)
        matrix_ref[near, near] = real
        matrix_ref[near, far] = imag
        matrix_ref[far, near] = -imag
        matrix_ref[far, far] = real
        row_ref[0:1, near] = bias_ref[0, pl.ds(half * blocks + block, 1), :]
        row_ref[0:1, far] = bias_ref[1, pl.ds(half * blocks + block, 1), :]


def prepare_kernel(size, rows_ref, cos_ref, sin_ref, er_ref, ec_ref, mix_in_ref, bias_in_ref, mix_out_ref, bias_out_ref, lat_ref, lat_t_ref, w1_ref, w2_ref, b1_ref, b2_ref):
    half = half_of(size)
    build_lat_tables(size, rows_ref, cos_ref, sin_ref, er_ref, ec_ref, lat_ref, lat_t_ref)
    build_block_matrix(size, mix_in_ref, bias_in_ref, half, w1_ref, b1_ref)
    build_block_matrix(size, mix_out_ref, bias_out_ref, half, w2_ref, b2_ref)


def half_of(size):
    device = lax.axis_index("rows") * size.lon + lax.axis_index("lon")
    return (device % size.per_image) // size.groups


def pad_plane(size, plane):
    extra = size.lons_pad - size.lons_here
    return jnp.concatenate([plane, jnp.zeros((extra, plane.shape[1]), plane.dtype)], axis=0)


def planes(size):
    for source in range(size.lon):
        for slot in range(size.slots_here):
            yield source, slot, (source * size.slots_here + slot) * size.lons_pad


def write_quarter(size, quarter, values, out_ref):
    for half in range(HALVES):
        for lon in range(size.lon):
            out_ref[quarter * size.chunk + half * size.lon + lon] = values[
                lon * size.piece : (lon + 1) * size.piece,
                half * size.half : (half + 1) * size.half,
            ].astype(bf16)


def write_pieces(size, values, out_ref):
    rows = size.lon * size.piece
    for quarter in range(QUARTERS):
        write_quarter(size, quarter, values[quarter * rows : (quarter + 1) * rows], out_ref)


def read_pieces(ref, places):
    return jnp.concatenate([ref[place].astype(f32) for place in places], axis=0).astype(bf16)


def read_spectrum(size, ref):
    return jnp.concatenate(
        [
            read_pieces(
                ref,
                [
                    quarter * size.chunk + half * size.lon + lon
                    for quarter in range(QUARTERS)
                    for lon in range(size.lon)
                ],
            )
            for half in range(HALVES)
        ],
        axis=1,
    )


def first_norm(size, x_ref, gain, shift, low_ref):
    for source, slot, start in planes(size):
        x = pad_plane(size, x_ref[source, slot].astype(f32))
        unit, _ = norm_parts(x)
        low_ref[start : start + size.lons_pad, :] = (unit * gain + shift).astype(bf16)


def as_row(ref):
    return ref[...].reshape(1, -1)


def first_kernel(size, x_ref, gain_ref, shift_ref, table_ref, send_ref, low_ref):
    first_norm(size, x_ref, as_row(gain_ref), as_row(shift_ref), low_ref)
    for quarter in range(QUARTERS):
        write_quarter(size, quarter, mm(table_ref[quarter], low_ref[...]), send_ref)


def add_modes(size, quarter, is_first, recv_ref, lat_ref, modes_ref):
    spectrum = read_pieces(recv_ref, [quarter * size.chunk + i for i in range(size.chunk)])
    product = mm(lat_ref[quarter], spectrum)
    if is_first:
        modes_ref[...] = product
    else:
        modes_ref[...] += product


def side_by_side(size, modes_ref):
    return jnp.concatenate(
        [modes_ref[: size.modes, :], modes_ref[size.modes :, :]], axis=1
    ).astype(bf16)


def stack_parts(size, values, stacked_ref):
    stacked_ref[: size.modes, :] = values[:, : size.half].astype(bf16)
    stacked_ref[size.modes :, :] = values[:, size.half :].astype(bf16)


def mix_quarter_back(size, quarter, lat_t_ref, stacked_ref, send_ref):
    back = mm(lat_t_ref[quarter], stacked_ref[...])
    for i in range(size.chunk):
        send_ref[quarter * size.chunk + i] = back[i * size.piece : (i + 1) * size.piece].astype(bf16)


def mix_layers(size, modes_ref, w1_ref, b1_ref, w2_ref, b2_ref, band_ref, inner_ref, gated_ref, outer_ref, stacked_ref):
    band = side_by_side(size, modes_ref)
    band_ref[...] = band
    inner = mm(band, w1_ref[...]) + b1_ref[...]
    inner_ref[...] = inner
    gated = smooth_gate(inner).astype(bf16)
    gated_ref[...] = gated
    outer = mm(gated, w2_ref[...]) + b2_ref[...]
    outer_ref[...] = outer
    stack_parts(size, soft_shrink(outer), stacked_ref)


def mix_kernel(size, recv_ref, lat_ref, lat_t_ref, w1_ref, b1_ref, w2_ref, b2_ref, send_ref, band_ref, inner_ref, gated_ref, outer_ref, modes_ref, stacked_ref):
    for quarter in range(QUARTERS):
        add_modes(size, quarter, quarter == 0, recv_ref, lat_ref, modes_ref)
    mix_layers(size, modes_ref, w1_ref, b1_ref, w2_ref, b2_ref, band_ref, inner_ref, gated_ref, outer_ref, stacked_ref)
    for quarter in range(QUARTERS):
        mix_quarter_back(size, quarter, lat_t_ref, stacked_ref, send_ref)


def mix_layers_back(size, modes_ref, w1_ref, w2_ref, inner_ref, outer_ref, outer_grad_ref, inner_grad_ref, stacked_ref):
    upstream = side_by_side(size, modes_ref)
    outer_grad = (upstream.astype(f32) * shrink_slope(outer_ref[...])).astype(bf16)
    outer_grad_ref[...] = outer_grad
    inner_grad = (mm_t(outer_grad, w2_ref[...]) * gate_slope(inner_ref[...])).astype(bf16)
    inner_grad_ref[...] = inner_grad
    stack_parts(size, mm_t(inner_grad, w1_ref[...]), stacked_ref)


def mix_back_weights(size, band_ref, gated_ref, outer_grad_ref, inner_grad_ref, out_ref):
    half = size.half
    block_size = out_ref.shape[2]
    blocks = half // block_size
    rest = out_ref.shape[1] - block_size
    for layer, (value_ref, grad_ref) in enumerate(
        ((band_ref, inner_grad_ref), (gated_ref, outer_grad_ref))
    ):
        grad = grad_ref[...]
        total = t_mm(value_ref[...], grad)
        bias = jnp.sum(grad.astype(f32), axis=0, keepdims=True)
        for block in range(blocks):
            near = slice(block * block_size, (block + 1) * block_size)
            far = slice(half + block * block_size, half + (block + 1) * block_size)
            place = layer * 2 * blocks + block
            out_ref[place, :block_size] = (total[near, near] + total[far, far]).astype(bf16)
            out_ref[place + blocks, :block_size] = (total[near, far] - total[far, near]).astype(bf16)
            shape = (rest, block_size)
            out_ref[place, block_size:] = jnp.broadcast_to(bias[:, near], shape).astype(bf16)
            out_ref[place + blocks, block_size:] = jnp.broadcast_to(bias[:, far], shape).astype(bf16)


def mix_back_kernel(size, recv_ref, lat_ref, lat_t_ref, w1_ref, w2_ref, band_ref, inner_ref, gated_ref, outer_ref, send_ref, grad_ref, outer_grad_ref, inner_grad_ref, modes_ref, stacked_ref):
    for quarter in range(QUARTERS):
        add_modes(size, quarter, quarter == 0, recv_ref, lat_ref, modes_ref)
    mix_layers_back(size, modes_ref, w1_ref, w2_ref, inner_ref, outer_ref, outer_grad_ref, inner_grad_ref, stacked_ref)
    for quarter in range(QUARTERS):
        mix_quarter_back(size, quarter, lat_t_ref, stacked_ref, send_ref)
    mix_back_weights(size, band_ref, gated_ref, outer_grad_ref, inner_grad_ref, grad_ref)


def mlp_kernel(
    size,
    map_ref,
    recv_ref,
    x_ref,
    dy_ref,
    inv_t_ref,
    inv_ref,
    gain1_ref,
    shift1_ref,
    gain2_ref,
    shift2_ref,
    out_bias_ref,
    fc_in_ref,
    fc_in_bias_ref,
    fc_out_ref,
    block_ref,
    dh_ref,
    send_ref,
    wide_ref,
    small_ref,
    res_ref,
    low_ref,
    up_ref,
    acc_ref,
    back_ref,
):
    step = pl.program_id(0)
    gain2, shift2 = as_row(gain2_ref), as_row(shift2_ref)
    first_slot = (lax.axis_index("rows") * size.lon + lax.axis_index("lon")) * size.slots_here

    def live(slot):
        return jnp.where(map_ref[first_slot + slot] >= 0, 1.0, 0.0)


    @pl.when(step == 0)
    def _():
        res_ref[...] = mm(inv_t_ref[...], read_spectrum(size, recv_ref))
        up_sum = jnp.zeros((1, size.channels), f32)
        gain1, shift1 = as_row(gain1_ref), as_row(shift1_ref)
        for source, slot, start in planes(size):
            part = slice(start, start + size.lons_pad)
            x = pad_plane(size, x_ref[source, slot].astype(f32))
            unit, _ = norm_parts(x)
            residual = res_ref[part, :] + (unit * gain1 + shift1) + x
            res_ref[part, :] = residual
            unit, _ = norm_parts(residual)
            low_ref[part, :] = (unit * gain2 + shift2).astype(bf16)
            up = pad_plane(size, dy_ref[source, slot].astype(f32) * live(slot))
            up_ref[part, :] = up.astype(bf16)
            up_sum = up_sum + jnp.sum(up, axis=0, keepdims=True)
        small_ref[...] = jnp.zeros_like(small_ref)
        small_ref[0:1, :] = up_sum
        acc_ref[...] = jnp.zeros_like(acc_ref)
        back_ref[...] = jnp.zeros_like(back_ref)

    low = low_ref[...]
    up = up_ref[...]
    gate, slope = gate_both(mm(low, fc_in_ref[...]) + fc_in_bias_ref[...])
    hidden = gate.astype(bf16)
    acc_ref[...] += mm(hidden, fc_out_ref[...])
    hidden_grad = (mm_t(up, fc_out_ref[...]) * slope).astype(bf16)
    width = fc_in_ref.shape[1]
    per_row = size.channels // width
    small_ref[
        pl.ds(3 + step // per_row, 1), pl.ds(pl.multiple_of(step % per_row * width, width), width)
    ] = jnp.sum(hidden_grad.astype(f32), axis=0, keepdims=True)
    back_ref[...] += mm_t(hidden_grad, fc_in_ref[...])
    wide_ref[:, : size.channels] = t_mm(hidden_grad, low).astype(bf16)
    wide_ref[:, size.channels :] = t_mm(hidden, up).astype(bf16)

    @pl.when(step == pl.num_programs(0) - 1)
    def _():
        gain_sum = jnp.zeros((1, size.channels), f32)
        shift_sum = jnp.zeros((1, size.channels), f32)
        for source, slot, start in planes(size):
            part = slice(start, start + size.lons_pad)
            residual = res_ref[part, :]
            block = (residual + (acc_ref[part, :] + as_row(out_bias_ref))) * live(slot)
            block_ref[source, slot] = block[: size.lons_here].astype(bf16)
            unit, spread = norm_parts(residual)
            grad = back_ref[part, :]
            gain_sum = gain_sum + jnp.sum(grad * unit, axis=0, keepdims=True)
            shift_sum = shift_sum + jnp.sum(grad, axis=0, keepdims=True)
            grad = up_ref[part, :].astype(f32) + norm_back(grad * gain2, unit, spread)
            dh_ref[part, :] = grad
            low_ref[part, :] = grad.astype(bf16)
        small_ref[1:2, :] = gain_sum
        small_ref[2:3, :] = shift_sum
        write_pieces(size, mm(inv_ref[...], low_ref[...]), send_ref)


def run_mlp(size, hidden_units, row_map, recv, x, dy, inv_t, inv, vectors, fc_in, fc_in_bias, fc_out):
    channels = size.channels
    width = HIDDEN_BLOCK
    fixed = pl.BlockSpec(memory_space=pltpu.VMEM)
    tokens = (size.tokens, channels)
    return pl.pallas_call(
        functools.partial(mlp_kernel, size),
        grid=(hidden_units // width,),
        in_specs=[pl.BlockSpec(memory_space=pltpu.SMEM)]
        + [fixed] * (5 + len(vectors))
        + [
            pl.BlockSpec((channels, width), lambda i: (0, i)),
            pl.BlockSpec((1, width), lambda i: (0, i)),
            pl.BlockSpec((width, channels), lambda i: (i, 0)),
        ],
        out_specs=(
            fixed,
            fixed,
            fixed,
            pl.BlockSpec((width, 2 * channels), lambda i: (i, 0)),
            fixed,
        ),
        out_shape=(
            struct(x.shape, bf16),
            struct(tokens, f32),
            struct((size.per_image, size.piece, size.half), bf16),
            struct((hidden_units, 2 * channels), bf16),
            struct((8, channels), f32),
        ),
        scratch_shapes=[
            pltpu.VMEM(tokens, f32),
            pltpu.VMEM(tokens, bf16),
            pltpu.VMEM(tokens, bf16),
            pltpu.VMEM(tokens, f32),
            pltpu.VMEM(tokens, f32),
        ],
        compiler_params=pltpu.CompilerParams(vmem_limit_bytes=VMEM_BYTES),
        name="mlp",
    )(row_map, recv, x, dy, inv_t, inv, *vectors, fc_in, fc_in_bias, fc_out)


def last_planes(size, recv_ref, x_ref, dh_ref, table_t_ref, gain_ref, out_ref, landing_ref, small_ref, sender, mover):
    gain = as_row(gain_ref)
    filtered = mm(table_t_ref[...], read_spectrum(size, recv_ref))
    gain_sum = jnp.zeros((1, size.channels), f32)
    shift_sum = jnp.zeros((1, size.channels), f32)
    for source, slot, start in planes(size):
        part = slice(start, start + size.lons_pad)
        unit, spread = norm_parts(pad_plane(size, x_ref[source, slot].astype(f32)))
        base = dh_ref[part, :]
        grad = base + filtered[part]
        gain_sum = gain_sum + jnp.sum(grad * unit, axis=0, keepdims=True)
        shift_sum = shift_sum + jnp.sum(grad, axis=0, keepdims=True)
        grad = base + norm_back(grad * gain, unit, spread)
        out_ref[source, slot] = grad[: size.lons_here].astype(bf16)
    small_ref[0:1, :] = gain_sum
    small_ref[1:2, :] = shift_sum
    if sender is None:
        return None
    return start_lon(out_ref, landing_ref, sender, mover)


def last_kernel(size, recv_ref, x_ref, dh_ref, table_t_ref, gain_ref, out_ref, small_ref):
    last_planes(size, recv_ref, x_ref, dh_ref, table_t_ref, gain_ref, out_ref, None, small_ref, None, None)


def partners(lon_count):
    row = lax.axis_index("rows")
    lon = lax.axis_index("lon")
    core = {"rows": row, "lon": lon + 1 - 2 * (lon % 2)}
    along_y = {"rows": row, "lon": (lon + 2) % 4}
    along_x = {"rows": row + 1 - 2 * (row % 2), "lon": lon}
    far_z = {"rows": (row + 4) % 8, "lon": lon}
    return core, along_y, along_x, far_z


def greet(lon_count, count):
    row = lax.axis_index("rows")
    lon = lax.axis_index("lon")
    me = row * lon_count + lon
    barrier = pltpu.get_barrier_semaphore()
    for offset in range(1, count):
        other = (me + offset) % count
        pl.semaphore_signal(
            barrier,
            inc=1,
            device_id={"rows": other // lon_count, "lon": other % lon_count},
            device_id_type=MESH,
        )
    pl.semaphore_wait(barrier, count - 1)


class Sender:
    def __init__(self, send_sem, recv_sem):
        self.send_sem = send_sem
        self.recv_sem = recv_sem
        self.used = 0

    def start(self, source, target, device):
        copy = pltpu.make_async_remote_copy(
            src_ref=source,
            dst_ref=target,
            send_sem=self.send_sem.at[self.used],
            recv_sem=self.recv_sem.at[self.used],
            device_id=device,
            device_id_type=MESH,
        )
        self.used += 1
        copy.start()
        return copy


class Mover:
    def __init__(self, sem):
        self.sem = sem
        self.used = 0

    def start(self, source, target):
        copy = pltpu.make_async_copy(source, target, self.sem.at[self.used])
        self.used += 1
        copy.start()
        return copy


def start_quarter(size, step, source_ref, out_ref, sender, mover):
    row = lax.axis_index("rows")
    lon = lax.axis_index("lon")
    me = place_of(size, row, lon)
    copies = []
    for half_step in range(HALVES):
        for lon_step in range(size.lon):
            to_row = (row + step) % QUARTERS + (row // QUARTERS + half_step) % HALVES * QUARTERS
            to_lon = (lon + lon_step) % size.lon
            piece = source_ref.at[place_of(size, to_row, to_lon)]
            if step == 0 and half_step == 0 and lon_step == 0:
                copies.append(mover.start(piece, out_ref.at[me]))
            else:
                copies.append(
                    sender.start(piece, out_ref.at[me], {"rows": to_row, "lon": to_lon})
                )
    return copies


def start_lon(source_ref, out_ref, sender, mover):
    row = lax.axis_index("rows")
    me = lax.axis_index("lon")
    count = source_ref.shape[0]
    copies = []
    for offset in range(1, count):
        other = (me + offset) % count
        copies.append(
            sender.start(source_ref.at[other], out_ref.at[me], {"rows": row, "lon": other})
        )
    copies.append(mover.start(source_ref.at[me], out_ref.at[me]))
    return copies


def finish(copies):
    for copy in copies:
        copy.wait()


def call_remote(kernel, name, number, outs, spaces, out_spaces, sends, moves, scratch, operands):
    return pl.pallas_call(
        kernel,
        out_shape=outs,
        in_specs=[pl.BlockSpec(memory_space=space) for space in spaces],
        out_specs=tuple(pl.BlockSpec(memory_space=space) for space in out_spaces),
        scratch_shapes=[
            pltpu.SemaphoreType.DMA((sends,)),
            pltpu.SemaphoreType.DMA((sends,)),
            pltpu.SemaphoreType.DMA((moves,)),
        ]
        + list(scratch),
        compiler_params=pltpu.CompilerParams(
            collective_id=number, has_side_effects=True, vmem_limit_bytes=VMEM_BYTES
        ),
        name=name,
    )(*operands)


def forward_kernel(
    size,
    tokens_hbm,
    cot_hbm,
    table_hbm,
    er_hbm,
    ec_hbm,
    rows_ref,
    gain_ref,
    shift_ref,
    cos_ref,
    sin_ref,
    mix_in_ref,
    bias_in_ref,
    mix_out_ref,
    bias_out_ref,
    x_out,
    dy_out,
    recv_out,
    lat_out,
    lat_t_out,
    w1_out,
    w2_out,
    band_out,
    inner_out,
    gated_out,
    outer_out,
    send_sem,
    recv_sem,
    move_sem,
    x_ref,
    table_ref,
    er_ref,
    ec_ref,
    lat_ref,
    lat_t_ref,
    w1_ref,
    w2_ref,
    band_ref,
    inner_ref,
    gated_ref,
    outer_ref,
    b1_ref,
    b2_ref,
    low_ref,
    send1,
    recv1,
    send2,
    modes_ref,
    stacked_ref,
):
    sender, mover = Sender(send_sem, recv_sem), Mover(move_sem)
    mine = lax.axis_index("rows") % QUARTERS
    half = half_of(size)
    load = mover.start(table_hbm, table_ref)
    loads = [mover.start(er_hbm, er_ref), mover.start(ec_hbm, ec_ref)]
    greet(size.lon, size.devices)
    tokens = start_lon(tokens_hbm, x_ref, sender, mover)
    build_block_matrix(size, mix_in_ref, bias_in_ref, half, w1_ref, b1_ref)
    build_block_matrix(size, mix_out_ref, bias_out_ref, half, w2_ref, b2_ref)
    stores = [mover.start(w1_ref, w1_out), mover.start(w2_ref, w2_out)]
    finish(tokens)
    stores.append(mover.start(x_ref, x_out))
    first_norm(size, x_ref, as_row(gain_ref), as_row(shift_ref), low_ref)
    load.wait()
    steps = []
    for step in range(QUARTERS):
        quarter = (mine + step) % QUARTERS
        write_quarter(size, quarter, mm(table_ref[quarter], low_ref[...]), send1)
        steps.append(start_quarter(size, step, send1, recv1, sender, mover))
    cotangents = start_lon(cot_hbm, dy_out, sender, mover)
    finish(loads)
    build_lat_tables(size, rows_ref, cos_ref, sin_ref, er_ref, ec_ref, lat_ref, lat_t_ref)
    stores += [mover.start(lat_ref, lat_out), mover.start(lat_t_ref, lat_t_out)]
    for step in range(QUARTERS):
        finish(steps[step])
        quarter = (mine + QUARTERS - step) % QUARTERS
        add_modes(size, quarter, step == 0, recv1, lat_ref, modes_ref)
    mix_layers(size, modes_ref, w1_ref, b1_ref, w2_ref, b2_ref, band_ref, inner_ref, gated_ref, outer_ref, stacked_ref)
    steps = []
    for step in range(QUARTERS):
        quarter = (mine + step) % QUARTERS
        mix_quarter_back(size, quarter, lat_t_ref, stacked_ref, send2)
        steps.append(start_quarter(size, step, send2, recv_out, sender, mover))
    stores += [
        mover.start(band_ref, band_out),
        mover.start(inner_ref, inner_out),
        mover.start(gated_ref, gated_out),
        mover.start(outer_ref, outer_out),
    ]
    finish(cotangents)
    finish(stores)
    for step in range(QUARTERS):
        finish(steps[step])


def run_forward(size, tokens, cotangent, table, er, ec, rows, gain, shift, cosine, sine, mix_in, mix_in_bias, mix_out, mix_out_bias, number):
    piece = struct((size.per_image, size.piece, size.half), bf16)
    modes = (size.modes, 2 * size.half)
    square = struct((2 * size.half, 2 * size.half), bf16)
    kept = (
        struct((QUARTERS, 2 * size.modes, size.chunk_rows), bf16),
        struct((QUARTERS, size.chunk_rows, 2 * size.modes), bf16),
        square,
        square,
        struct(modes, bf16),
        struct(modes, f32),
        struct(modes, bf16),
        struct(modes, f32),
    )
    row = struct((1, 2 * size.half), f32)
    scratch = (
        (struct(tokens.shape, bf16), table, er, ec)
        + kept
        + (row, row, struct((size.tokens, size.channels), bf16), piece, piece, piece)
        + (struct((2 * size.modes, size.half), f32), struct((2 * size.modes, size.half), bf16))
    )
    small = (rows, gain, shift, cosine, sine, mix_in, mix_in_bias, mix_out, mix_out_bias)
    return call_remote(
        functools.partial(forward_kernel, size),
        "forward",
        number,
        (struct(tokens.shape, bf16), struct(tokens.shape, bf16), piece) + kept,
        [pl.ANY] * 5 + [pltpu.VMEM] * len(small),
        [pl.ANY] * (3 + len(kept)),
        2 * size.per_image + 2 * size.lon,
        24,
        [pltpu.VMEM(v.shape, v.dtype) for v in scratch],
        (tokens, cotangent, table, er, ec) + small,
    )


def add_planes(left_ref, right_ref, out_ref):
    @pl.loop(0, left_ref.shape[0])
    def _(first):
        for second in range(left_ref.shape[1]):
            total = left_ref[first, second].astype(f32) + right_ref[first, second].astype(f32)
            out_ref[first, second] = total.astype(out_ref.dtype)


def start_same(lon_count, count, source_ref, out_ref, sender, mover):
    me = lax.axis_index("rows") * lon_count + lax.axis_index("lon")
    copies = []
    for offset in range(1, count):
        other = (me + offset) % count
        copies.append(
            sender.start(
                source_ref, out_ref.at[me], {"rows": other // lon_count, "lon": other % lon_count}
            )
        )
    copies.append(mover.start(source_ref, out_ref.at[me]))
    return copies


def backward_kernel(
    size,
    pieces_ref,
    wide_ref,
    block_ref,
    lat_hbm,
    lat_t_hbm,
    w1_hbm,
    w2_hbm,
    band_hbm,
    inner_hbm,
    gated_hbm,
    outer_hbm,
    x_hbm,
    dh_hbm,
    table_t_hbm,
    gain_ref,
    early_ref,
    token_out,
    block_out,
    dense_ref,
    mix_out,
    early_out,
    late_out,
    send_sem,
    recv_sem,
    move_sem,
    lat_ref,
    lat_t_ref,
    w1_ref,
    w2_ref,
    band_ref,
    inner_ref,
    gated_ref,
    outer_ref,
    x_ref,
    dh_ref,
    table_t_ref,
    recv1,
    send2,
    recv2,
    token_ref,
    a_go,
    a_go_in,
    b_go,
    b_go_in,
    a_keep,
    a_keep_in,
    b_keep,
    b_keep_in,
    a_land,
    b_land,
    a2_land,
    b2_land,
    a2,
    b2,
    a3_land,
    b3_land,
    a3,
    b3,
    a4_land,
    b4_land,
    outer_grad_ref,
    inner_grad_ref,
    mix_ref,
    mix_land,
    pair_ref,
    early,
    early_land,
    late,
    late_land,
    modes_ref,
    stacked_ref,
):
    lon_count, count, groups = size.lon, size.devices, size.groups
    row = lax.axis_index("rows")
    lon = lax.axis_index("lon")
    me = row * lon_count + lon
    z = row // 2
    x = row % 2
    y = lon // 2
    core = lon % 2
    mine = row % QUARTERS
    group = me % groups
    base = me - group
    half = me // groups
    to_core, to_y, to_x, far_z = partners(lon_count)
    near = z + 1 - 2 * (z % 2)
    mirror = 3 - z
    to_near = {"rows": near * 2 + x, "lon": lon}
    to_mirror = {"rows": mirror * 2 + x, "lon": lon}
    width = wide_ref.shape[-1] // 2
    first, second = pl.ds(0, width), pl.ds(width, width)
    sender, mover = Sender(send_sem, recv_sem), Mover(move_sem)

    greet(lon_count, count)
    early[...] = early_ref[...]
    stage = 0

    def early_start(device):
        return sender.start(early, early_land.at[stage], device)

    early_hop = early_start(to_core)
    views = (
        (lambda c: wide_ref.at[:, 1 - x, :, c, :, first], a_go, a_go_in),
        (lambda c: wide_ref.at[:, :, 1 - y, c, :, second], b_go, b_go_in),
        (lambda c: wide_ref.at[:, x, :, c, :, first], a_keep, a_keep_in),
        (lambda c: wide_ref.at[:, :, y, c, :, second], b_keep, b_keep_in),
    )
    pairs = []
    for view, own, landed in views[:2]:
        pairs.append((sender.start(view(1 - core), landed, to_core), mover.start(view(core), own)))
    steps = [start_quarter(size, i, pieces_ref, recv1, sender, mover) for i in range(QUARTERS)]
    for view, own, landed in views[2:]:
        pairs.append((sender.start(view(1 - core), landed, to_core), mover.start(view(core), own)))
    loads = [
        mover.start(source, target)
        for source, target in (
            (lat_hbm, lat_ref),
            (outer_hbm, outer_ref),
            (w2_hbm, w2_ref),
            (inner_hbm, inner_ref),
            (w1_hbm, w1_ref),
            (lat_t_hbm, lat_t_ref),
            (gated_hbm, gated_ref),
            (band_hbm, band_ref),
            (x_hbm, x_ref),
            (dh_hbm, dh_ref),
            (table_t_hbm, table_t_ref),
        )
    ]

    hops = []
    for pair, own, landed, target, device in (
        (pairs[0], a_go, a_go_in, a_land, to_x),
        (pairs[1], b_go, b_go_in, b_land, to_y),
    ):
        finish(pair)
        add_planes(own, landed, own)
        hops.append(sender.start(own, target, device))
    early_hop.wait()
    early[...] = early[...] + early_land[0]
    stage = 1
    early_hop = early_start(to_x)
    for pair, own, landed in ((pairs[2], a_keep, a_keep_in), (pairs[3], b_keep, b_keep_in)):
        finish(pair)
        add_planes(own, landed, own)

    finish(loads)
    for step in range(QUARTERS):
        finish(steps[step])
        add_modes(size, (mine + QUARTERS - step) % QUARTERS, step == 0, recv1, lat_ref, modes_ref)
    mix_layers_back(size, modes_ref, w1_ref, w2_ref, inner_ref, outer_ref, outer_grad_ref, inner_grad_ref, stacked_ref)
    steps = []
    for step in range(QUARTERS):
        mix_quarter_back(size, (mine + step) % QUARTERS, lat_t_ref, stacked_ref, send2)
        steps.append(start_quarter(size, step, send2, recv2, sender, mover))
    mix_back_weights(size, band_ref, gated_ref, outer_grad_ref, inner_grad_ref, mix_ref)
    parts = []
    for offset in range(1, groups):
        other = (group + offset) % groups
        device = base + other
        parts.append(
            sender.start(
                mix_ref.at[other],
                mix_land.at[group],
                {"rows": device // lon_count, "lon": device % lon_count},
            )
        )
    parts.append(mover.start(mix_ref.at[group], mix_land.at[group]))

    hops[0].wait()
    add_planes(a_keep, a_land, a_keep)
    hops[1].wait()
    add_planes(b_keep, b_land, b_keep)
    hops = [
        sender.start(a_keep.at[:, 1 - y], a2_land, to_y),
        sender.start(b_keep.at[:, 1 - x], b2_land, to_x),
    ]
    early_hop.wait()
    early[...] = early[...] + early_land[1]
    stage = 2
    early_hop = early_start(to_y)
    blocks = start_lon(block_ref, block_out, sender, mover)

    finish(parts)
    total = mix_land[0].astype(f32)
    for index in range(1, groups):
        total = total + mix_land[index].astype(f32)
    pair_ref[half] = total.astype(bf16)
    crossing = sender.start(pair_ref.at[half], pair_ref.at[half], far_z)

    hops[0].wait()
    for place in range(4):
        a2[place] = (a_keep[place, y].astype(f32) + a2_land[place].astype(f32)).astype(bf16)
    hops[1].wait()
    for place in range(4):
        b2[place] = (b_keep[place, x].astype(f32) + b2_land[place].astype(f32)).astype(bf16)
    hops = [
        sender.start(a2.at[near], a3_land.at[0], to_near),
        sender.start(a2.at[3 - near], a3_land.at[1], to_near),
        sender.start(b2.at[near], b3_land.at[0], to_near),
        sender.start(b2.at[3 - near], b3_land.at[1], to_near),
    ]
    early_hop.wait()
    early[...] = early[...] + early_land[2]
    stage = 3
    early_hop = early_start(to_near)
    crossing.wait()
    gather = []
    for offset in range(1, groups):
        device = base + (group + offset) % groups
        gather.append(
            sender.start(
                pair_ref,
                mix_out.at[:, group],
                {"rows": device // lon_count, "lon": device % lon_count},
            )
        )
    gather.append(mover.start(pair_ref, mix_out.at[:, group]))

    for step in range(QUARTERS):
        finish(steps[step])
    tokens = last_planes(size, recv2, x_ref, dh_ref, table_t_ref, gain_ref, token_ref, token_out, late, sender, mover)
    smalls = start_same(lon_count, count, late, late_land, sender, mover)

    finish(hops)
    for land, kept, summed in ((a3_land, a2, a3), (b3_land, b2, b3)):
        summed[0] = (kept[z].astype(f32) + land[0].astype(f32)).astype(bf16)
        summed[1] = (kept[mirror].astype(f32) + land[1].astype(f32)).astype(bf16)
    hops = [
        sender.start(a3.at[1], a4_land, to_mirror),
        sender.start(b3.at[1], b4_land, to_mirror),
    ]
    early_hop.wait()
    early[...] = early[...] + early_land[3]
    stage = 4
    early_hop = early_start(to_mirror)
    finish(smalls)
    total = late_land[0]
    for index in range(1, count):
        total = total + late_land[index]
    late_out[...] = total
    finish(hops)
    dense_ref[0] = a3[0].astype(f32) + a4_land[...].astype(f32)
    dense_ref[1] = b3[0].astype(f32) + b4_land[...].astype(f32)
    early_hop.wait()
    early_out[...] = early[...] + early_land[4]
    finish(gather)
    finish(blocks)
    finish(tokens)


def run_backward(size, blocks_shape, pieces, wide, block, lat, lat_t, w1, w2, band, inner, gated, outer, x, dh, table_t, gain, early, number):
    share, columns = wide.shape[0] // size.devices, wide.shape[1]
    part = (4, 2, share, columns // 2)
    row_part = (share, columns // 2)
    operands = (lat, lat_t, w1, w2, band, inner, gated, outer, x, dh, table_t)
    late = (2, size.channels)

    def spaces(count, space):
        return [space] * count

    scratch = [pltpu.VMEM(v.shape, v.dtype) for v in operands]
    scratch += [pltpu.VMEM(pieces.shape, bf16)] * 3
    scratch += [pltpu.VMEM(x.shape, bf16)]
    scratch += [pltpu.VMEM(part, bf16)] * 10
    scratch += [pltpu.VMEM((4,) + row_part, bf16)] * 4
    scratch += [pltpu.VMEM((2,) + row_part, bf16)] * 4
    scratch += [pltpu.VMEM(row_part, bf16)] * 2
    scratch += [pltpu.VMEM(band.shape, bf16)] * 2
    scratch += [pltpu.VMEM(blocks_shape, bf16)] * 2
    scratch += [pltpu.VMEM((HALVES,) + blocks_shape[1:], bf16)]
    scratch += [pltpu.VMEM(early.shape, f32), pltpu.VMEM((5,) + early.shape, f32)]
    scratch += [pltpu.VMEM(late, f32), pltpu.VMEM((size.devices,) + late, f32)]
    modes = (2 * size.modes, size.half)
    scratch += [pltpu.VMEM(modes, f32), pltpu.VMEM(modes, bf16)]
    return call_remote(
        functools.partial(backward_kernel, size),
        "backward",
        number,
        (
            struct(x.shape, bf16),
            struct(block.shape, bf16),
            struct((2,) + row_part, f32),
            struct((HALVES,) + blocks_shape, bf16),
            struct(early.shape, f32),
            struct(late, f32),
        ),
        spaces(14, pl.ANY) + spaces(2, pltpu.VMEM),
        spaces(2, pl.ANY) + spaces(4, pltpu.VMEM),
        3 * size.devices + 2 * size.groups + 2 * size.lon + 32,
        32,
        scratch,
        (pieces, wide.reshape(4, 2, 2, 2, share, columns), block) + operands + (gain, early),
    )


def exchange_lon(values):
    return lax.all_to_all(values, "lon", split_axis=0, concat_axis=0, tiled=True)


def exchange_all(values):
    return lax.all_to_all(values, ("rows", "lon"), split_axis=0, concat_axis=0, tiled=True)


def to_modes(size, pieces, row_map):
    order, place = place_order(size)
    sent = jnp.tile(jnp.take(pieces, place, axis=0), (size.images, 1, 1))
    received = exchange_all(sent)
    used = size.slots_here * 2 * size.waves
    by_slot = received[:, :used].reshape(-1, 2 * size.waves, size.half)
    image = (lax.axis_index("rows") * size.lon + lax.axis_index("lon")) // size.per_image
    slots = row_map.shape[0]
    target = jnp.where(row_map >= 0, row_map, size.images * H)
    slot_of_row = (
        jnp.zeros((size.images * H,), jnp.int32)
        .at[target]
        .set(jnp.arange(slots, dtype=jnp.int32), mode="drop")
    )
    own = lax.dynamic_slice_in_dim(slot_of_row, image * H, H)
    picked = jnp.take(by_slot, own, axis=0)
    picked = jnp.pad(picked, ((0, size.virtual_slots - H), (0, 0), (0, 0)))
    picked = picked.reshape(size.per_image, used, size.half)
    return jnp.take(jnp.pad(picked, ((0, 0), (0, size.piece - used), (0, 0))), order, axis=0)


def from_modes(size, pieces, row_map):
    order, place = place_order(size)
    used = size.slots_here * 2 * size.waves
    by_lat = jnp.take(pieces, place, axis=0)[:, :used].reshape(-1, 2 * size.waves, size.half)
    image = (lax.axis_index("rows") * size.lon + lax.axis_index("lon")) // size.per_image
    live = (row_map >= 0) & (row_map // H == image)
    picked = jnp.take(by_lat, jnp.where(live, row_map % H, 0), axis=0)
    picked = picked * live.astype(bf16)[:, None, None]
    picked = picked.reshape(size.devices, used, size.half)
    sent = jnp.pad(picked, ((0, 0), (0, size.piece - used), (0, 0)))
    received = exchange_all(sent)
    received = received.reshape(size.images, size.per_image, size.piece, size.half)
    return jnp.take(jnp.sum(received.astype(f32), axis=0).astype(bf16), order, axis=0)


def body(
    tokens,
    row_map,
    cotangent,
    norm_gain,
    norm_shift,
    mix_in,
    mix_in_bias,
    mix_out,
    mix_out_bias,
    post_gain,
    post_shift,
    fc_in,
    fc_in_bias,
    fc_out,
    fc_out_bias,
):
    size = Sizes(
        lax.axis_size("rows"), lax.axis_size("lon"), row_map.shape[0], tokens.shape[2]
    )
    channels = size.channels
    blocks = mix_in.shape[1]
    blocks_here = blocks // HALVES
    block_size = mix_in.shape[2]
    hidden_units = fc_in.shape[1]
    device = lax.axis_index("rows") * size.lon + lax.axis_index("lon")
    half_index = (device % size.per_image) // size.groups

    table, table_t, inv, inv_t = [jnp.asarray(t) for t in lon_tables(size)]
    table = table.reshape(QUARTERS, size.spectrum // QUARTERS, size.tokens)
    cosine, sine, er, ec = [jnp.asarray(t) for t in lat_parts(size)]
    if size.images == 1:
        slot_lat = row_map
    else:
        slot_lat = jnp.where(jnp.arange(size.virtual_slots) < H, jnp.arange(size.virtual_slots), -1)
    rows = jnp.pad(slot_lat, (0, 128 - size.virtual_slots), constant_values=-1).reshape(1, 128)
    shape = (size.lon, size.slots_here, size.lons_here, channels)
    x, dy = tokens.reshape(shape), cotangent.reshape(shape)
    piece_shape = struct((size.per_image, size.piece, size.half), bf16)
    mode_shape = (size.modes, 2 * size.half)
    wide_modes = (2 * size.modes, size.half)
    mode_scratch = [pltpu.VMEM(wide_modes, f32), pltpu.VMEM(wide_modes, bf16)]
    if size.images == 1:
        x, dy, received, lat, lat_t, w1, w2, band, inner, gated, outer = run_forward(
            size, x, dy, table, er, ec, rows, norm_gain, norm_shift, cosine, sine, mix_in, mix_in_bias, mix_out, mix_out_bias, 0
        )
    else:
        square = struct((2 * size.half, 2 * size.half), bf16)
        flat = struct((1, 2 * size.half), f32)
        lat, lat_t, w1, w2, b1, b2 = call_local(
            functools.partial(prepare_kernel, size),
            "prepare",
            (
                struct((QUARTERS, 2 * size.modes, size.chunk_rows), bf16),
                struct((QUARTERS, size.chunk_rows, 2 * size.modes), bf16),
                square,
                square,
                flat,
                flat,
            ),
        )(rows, cosine, sine, er, ec, mix_in, mix_in_bias, mix_out, mix_out_bias)
        x, dy = exchange_lon(x), exchange_lon(dy)
        sent = call_local(
            functools.partial(first_kernel, size),
            "lon_forward",
            piece_shape,
            [pltpu.VMEM((size.tokens, channels), bf16)],
        )(x, norm_gain, norm_shift, table)
        received = to_modes(size, sent, row_map)
        sent, band, inner, gated, outer = call_local(
            functools.partial(mix_kernel, size),
            "mix_forward",
            (
                piece_shape,
                struct(mode_shape, bf16),
                struct(mode_shape, f32),
                struct(mode_shape, bf16),
                struct(mode_shape, f32),
            ),
            mode_scratch,
        )(received, lat, lat_t, w1, b1, w2, b2)
        received = from_modes(size, sent, row_map)
    vectors = (norm_gain, norm_shift, post_gain, post_shift, fc_out_bias)
    block, dh, sent, wide, early = run_mlp(
        size, hidden_units, row_map, received, x, dy, inv_t, inv, vectors, fc_in, fc_in_bias.reshape(1, -1), fc_out
    )
    blocks_shape = (4 * blocks_here, round_up(block_size + 1, 16), block_size)
    if size.images == 1:
        token_grad, block, dense, mix_total, early, late = run_backward(
            size, blocks_shape, sent, wide, block, lat, lat_t, w1, w2, band, inner, gated, outer, x, dh, table_t, norm_gain, early, 1
        )
    else:
        names = ("rows", "lon")
        early = lax.psum(early, names)
        dense = lax.psum_scatter(wide, names, scatter_dimension=0, tiled=True)
        dense = jnp.stack([dense[:, :channels], dense[:, channels:]]).astype(f32)
        block = exchange_lon(block)
        received = to_modes(size, sent, row_map)
        sent, mix_grad = call_local(
            functools.partial(mix_back_kernel, size),
            "mix_backward",
            (piece_shape, struct(blocks_shape, bf16)),
            [pltpu.VMEM(mode_shape, bf16)] * 2 + mode_scratch,
        )(received, lat, lat_t, w1, w2, band, inner, gated, outer)
        mix_total = lax.psum(
            jnp.stack(
                [mix_grad.astype(f32) * (half_index == other).astype(f32) for other in range(HALVES)]
            ),
            names,
        )
        received = from_modes(size, sent, row_map)
        token_grad, late = call_local(
            functools.partial(last_kernel, size),
            "lon_backward",
            (struct(x.shape, bf16), struct((2, channels), f32)),
        )(received, x, dh, table_t, norm_gain)
        token_grad = exchange_lon(token_grad)
        late = lax.psum(late, names)
    mix_total = mix_total.astype(f32).reshape((HALVES, 2, 2, blocks_here) + blocks_shape[1:])
    mix_total = jnp.transpose(mix_total, (1, 2, 0, 3, 4, 5)).reshape((2, 2, blocks) + blocks_shape[1:])
    mix_bias = mix_total[:, :, :, block_size]
    mix_total = mix_total[:, :, :, :block_size]
    share = hidden_units // size.devices
    return (
        block.reshape(tokens.shape),
        token_grad.reshape(tokens.shape).astype(f32),
        late[0],
        late[1],
        mix_total[0],
        mix_bias[0],
        mix_total[1],
        mix_bias[1],
        early[1],
        early[2],
        dense[0].T,
        lax.dynamic_slice_in_dim(early[3:7].reshape(-1), device * share, share),
        dense[1],
        early[0],
    )


def solution(mesh):
    return jax.shard_map(
        body,
        mesh=mesh,
        in_specs=(P("rows", "lon", None), P(), P("rows", "lon", None)) + (P(),) * 12,
        out_specs=(
            P("rows", "lon", None),
            P("rows", "lon", None),
            P(),
            P(),
            P(),
            P(),
            P(),
            P(),
            P(),
            P(),
            P(None, ("rows", "lon")),
            P(("rows", "lon")),
            P(("rows", "lon"), None),
            P(),
        ),
        check_vma=False,
    )
```

```python
import functools
import math

import jax
import jax.numpy as jnp
import ml_dtypes
import numpy as np
from jax import lax
from jax.experimental import pallas as pl
from jax.experimental.pallas import tpu as pltpu
from jax.sharding import PartitionSpec as P

H = 90
W = 180
KX = 91
HALVES = 2
QUARTERS = 4
VMEM_BYTES = 58 * 1024 * 1024

norm_eps = 1e-06
shrink_level = 0.01
half_root = 0.7071067811865476
normal_peak = 0.3989422804014327
MESH = pl.DeviceIdType.MESH
f32 = jnp.float32
bf16 = jnp.bfloat16


def round_up(value, step):
    return -(-value // step) * step


class Sizes:
    def __init__(self, rows_count, lon_count, slots, channels):
        self.rows = rows_count
        self.lon = lon_count
        self.devices = rows_count * lon_count
        self.images = slots * 15 // (16 * H)
        self.per_image = self.devices // self.images
        self.groups = self.per_image // HALVES
        self.waves = -(-KX // self.groups)
        self.slots_here = slots // self.devices
        self.lons_here = W // lon_count
        self.lons_pad = round_up(self.lons_here, 16)
        self.tokens = lon_count * self.slots_here * self.lons_pad
        self.piece = round_up(self.slots_here * 2 * self.waves, 8)
        self.spectrum = self.groups * self.piece
        self.band = self.per_image * self.piece
        self.modes = round_up(H * self.waves, 16)
        self.virtual_slots = self.per_image * self.slots_here
        self.chunk = self.per_image // QUARTERS
        self.chunk_rows = self.chunk * self.piece
        self.channels = channels
        self.half = channels // HALVES


def place_of(size, row, lon):
    return (row % QUARTERS) * size.chunk + (row // QUARTERS) * size.lon + lon


def place_order(size):
    place = np.array([place_of(size, d // size.lon, d % size.lon) for d in range(size.per_image)])
    return np.argsort(place), place


def lon_tables(size):
    wave = np.arange(size.groups * size.waves)
    lon_index = np.arange(W)
    product = (lon_index[:, None] * wave[None, :]) % W
    angle = product.astype(np.float32) * np.float32(2.0 * math.pi / W)
    scale = np.float32(1.0 / math.sqrt(W))
    cosine = (np.cos(angle) * scale).astype(ml_dtypes.bfloat16).astype(np.float32)
    sine = (-np.sin(angle) * scale).astype(ml_dtypes.bfloat16).astype(np.float32)
    live = (wave < KX).astype(np.float32)
    factor = np.where((wave == 0) | (wave == W // 2), 1.0, 2.0).astype(np.float32)
    both = np.stack([cosine, sine]) * live
    result = []
    for weight in (np.ones_like(factor), factor):
        table = np.zeros(
            (
                size.groups,
                size.piece,
                size.lon,
                size.slots_here,
                size.lons_pad,
            ),
            np.float32,
        )
        values = (both * weight).reshape(2, size.lon, size.lons_here, size.groups, size.waves)
        values = np.transpose(values, (3, 0, 4, 1, 2)).reshape(
            size.groups, 2 * size.waves, size.lon, size.lons_here
        )
        for slot in range(size.slots_here):
            start = slot * 2 * size.waves
            table[:, start : start + 2 * size.waves, :, slot, : size.lons_here] = values
        flat = table.reshape(size.spectrum, size.tokens).astype(ml_dtypes.bfloat16)
        result.append(flat)
        result.append(np.ascontiguousarray(flat.T))
    return result


def lat_parts(size):
    lat_index = np.arange(H)
    angle = ((lat_index[:, None] * lat_index[None, :]) % H).astype(np.float32) * np.float32(
        2.0 * math.pi / H
    )
    scale = np.float32(1.0 / math.sqrt(H))
    cosine = np.zeros((96, 96), np.float32)
    sine = np.zeros((96, 96), np.float32)
    cosine[:H, :H] = np.cos(angle) * scale
    sine[:H, :H] = np.sin(angle) * scale
    spread_rows = np.zeros((2, size.modes, 2, 96), np.float32)
    for part in range(2):
        for lat in range(H):
            for wave in range(size.waves):
                spread_rows[part, lat * size.waves + wave, part, lat] = 1.0
    spread_cols = np.zeros((QUARTERS, 2, 128, size.chunk, size.piece), np.float32)
    for place, device in enumerate(place_order(size)[0]):
        for slot in range(size.slots_here):
            for part in range(2):
                for wave in range(size.waves):
                    spread_cols[
                        place // size.chunk,
                        part,
                        device * size.slots_here + slot,
                        place % size.chunk,
                        (slot * 2 + part) * size.waves + wave,
                    ] = 1.0
    low = ml_dtypes.bfloat16
    return (
        cosine.astype(low),
        sine.astype(low),
        spread_rows.reshape(2 * size.modes, 192).astype(low),
        spread_cols.reshape(QUARTERS, 256, size.chunk_rows).astype(low),
    )


def smooth_gate(values):
    return 0.5 * values * (1.0 + lax.erf(values * half_root))


def gate_both(values):
    half_phi = 0.5 * (1.0 + lax.erf(values * half_root))
    density = values * normal_peak * jnp.exp(-0.5 * values * values)
    return values * half_phi, half_phi + density


def gate_slope(values):
    return gate_both(values)[1]


def soft_shrink(values):
    return values - shrink_level * values * lax.rsqrt(values * values + shrink_level * shrink_level)


def shrink_slope(values):
    inverse = lax.rsqrt(values * values + shrink_level * shrink_level)
    return 1.0 - shrink_level * shrink_level * shrink_level * inverse * inverse * inverse


def norm_parts(values):
    center = values - jnp.mean(values, axis=-1, keepdims=True)
    spread = lax.rsqrt(jnp.mean(center * center, axis=-1, keepdims=True) + norm_eps)
    return center * spread, spread


def norm_back(scaled, unit, spread):
    return spread * (
        scaled
        - jnp.mean(scaled, axis=-1, keepdims=True)
        - unit * jnp.mean(scaled * unit, axis=-1, keepdims=True)
    )


def mm(left, right):
    return jnp.dot(left, right, preferred_element_type=f32)


def mm_t(left, right):
    return lax.dot_general(left, right, (((1,), (1,)), ((), ())), preferred_element_type=f32)


def t_mm(left, right):
    return lax.dot_general(left, right, (((0,), (0,)), ((), ())), preferred_element_type=f32)


def whole(count):
    return [pl.BlockSpec(memory_space=pltpu.VMEM)] * count


def call_local(kernel, name, outs, scratch=()):
    def run(*operands):
        return pl.pallas_call(
            kernel,
            out_shape=outs,
            in_specs=whole(len(operands)),
            out_specs=jax.tree.map(lambda _: pl.BlockSpec(memory_space=pltpu.VMEM), outs),
            scratch_shapes=list(scratch),
            compiler_params=pltpu.CompilerParams(vmem_limit_bytes=VMEM_BYTES),
            name=name,
        )(*operands)

    return run


def struct(shape, dtype):
    return jax.ShapeDtypeStruct(shape, dtype)


def wave_of(index, period, used, waves, other):
    within = index - period * jnp.floor((index + 0.5) * (1.0 / period))
    wave = within - waves * jnp.floor((within + 0.5) * (1.0 / waves))
    return jnp.where(within < used, wave, other)


def build_lat_tables(size, rows_ref, cos_ref, sin_ref, er_ref, ec_ref, lat_ref, lat_t_ref):
    lat_of = lax.broadcasted_iota(jnp.int32, (96, 128), 0)
    hot = (lat_of == rows_ref[...]).astype(f32).astype(bf16)
    cosine = mm(cos_ref[...], hot)
    sine = mm(sin_ref[...], hot)
    top = jnp.concatenate([cosine, sine], axis=1)
    bottom = jnp.concatenate([-sine, cosine], axis=1)
    base = jnp.concatenate([top, bottom], axis=0).astype(bf16)

    def row_waves(shape, dim):
        index = lax.broadcasted_iota(jnp.int32, shape, dim).astype(f32)
        return wave_of(index, size.modes, H * size.waves, size.waves, -1.0)

    def col_waves(shape, dim):
        index = lax.broadcasted_iota(jnp.int32, shape, dim).astype(f32)
        return wave_of(index, size.piece, size.slots_here * 2 * size.waves, size.waves, -2.0)

    modes, columns_here = 2 * size.modes, size.chunk_rows
    keep = row_waves((modes, 1), 0) == col_waves((1, columns_here), 1)
    keep_t = col_waves((columns_here, 1), 0) == row_waves((1, modes), 1)
    for quarter in range(QUARTERS):
        columns = mm(base, ec_ref[quarter]).astype(bf16)
        table = mm(er_ref[...], columns)
        lat_ref[quarter] = jnp.where(keep, table, 0.0).astype(bf16)
        table_t = lax.dot_general(
            columns, er_ref[...], (((0,), (1,)), ((), ())), preferred_element_type=f32
        )
        lat_t_ref[quarter] = jnp.where(keep_t, table_t, 0.0).astype(bf16)


def build_block_matrix(size, weight_ref, bias_ref, half, matrix_ref, row_ref):
    block_size = weight_ref.shape[2]
    blocks = size.half // block_size
    matrix_ref[...] = jnp.zeros_like(matrix_ref)
    for block in range(blocks):
        real = weight_ref[0, half * blocks + block]
        imag = weight_ref[1, half * blocks + block]
        near = slice(block * block_size, (block + 1) * block_size)
        far = slice(size.half + block * block_size, size.half + (block + 1) * block_size)
        matrix_ref[near, near] = real
        matrix_ref[near, far] = imag
        matrix_ref[far, near] = -imag
        matrix_ref[far, far] = real
        row_ref[0:1, near] = bias_ref[0, pl.ds(half * blocks + block, 1), :]
        row_ref[0:1, far] = bias_ref[1, pl.ds(half * blocks + block, 1), :]


def prepare_kernel(size, rows_ref, cos_ref, sin_ref, er_ref, ec_ref, mix_in_ref, bias_in_ref, mix_out_ref, bias_out_ref, lat_ref, lat_t_ref, w1_ref, w2_ref, b1_ref, b2_ref):
    half = half_of(size)
    build_lat_tables(size, rows_ref, cos_ref, sin_ref, er_ref, ec_ref, lat_ref, lat_t_ref)
    build_block_matrix(size, mix_in_ref, bias_in_ref, half, w1_ref, b1_ref)
    build_block_matrix(size, mix_out_ref, bias_out_ref, half, w2_ref, b2_ref)


def half_of(size):
    device = lax.axis_index("rows") * size.lon + lax.axis_index("lon")
    return (device % size.per_image) // size.groups


def pad_plane(size, plane):
    extra = size.lons_pad - size.lons_here
    return jnp.concatenate([plane, jnp.zeros((extra, plane.shape[1]), plane.dtype)], axis=0)


def planes(size):
    for source in range(size.lon):
        for slot in range(size.slots_here):
            yield source, slot, (source * size.slots_here + slot) * size.lons_pad


def write_quarter(size, quarter, values, out_ref):
    for half in range(HALVES):
        for lon in range(size.lon):
            out_ref[quarter * size.chunk + half * size.lon + lon] = values[
                lon * size.piece : (lon + 1) * size.piece,
                half * size.half : (half + 1) * size.half,
            ].astype(bf16)


def write_pieces(size, values, out_ref):
    rows = size.lon * size.piece
    for quarter in range(QUARTERS):
        write_quarter(size, quarter, values[quarter * rows : (quarter + 1) * rows], out_ref)


def read_pieces(ref, places):
    return jnp.concatenate([ref[place].astype(f32) for place in places], axis=0).astype(bf16)


def read_spectrum(size, ref):
    return jnp.concatenate(
        [
            read_pieces(
                ref,
                [
                    quarter * size.chunk + half * size.lon + lon
                    for quarter in range(QUARTERS)
                    for lon in range(size.lon)
                ],
            )
            for half in range(HALVES)
        ],
        axis=1,
    )


def first_norm(size, x_ref, gain, shift, low_ref):
    for source, slot, start in planes(size):
        x = pad_plane(size, x_ref[source, slot].astype(f32))
        unit, _ = norm_parts(x)
        low_ref[start : start + size.lons_pad, :] = (unit * gain + shift).astype(bf16)


def as_row(ref):
    return ref[...].reshape(1, -1)


def first_kernel(size, x_ref, gain_ref, shift_ref, table_ref, send_ref, low_ref):
    first_norm(size, x_ref, as_row(gain_ref), as_row(shift_ref), low_ref)
    for quarter in range(QUARTERS):
        write_quarter(size, quarter, mm(table_ref[quarter], low_ref[...]), send_ref)


def add_modes(size, quarter, is_first, recv_ref, lat_ref, modes_ref):
    spectrum = read_pieces(recv_ref, [quarter * size.chunk + i for i in range(size.chunk)])
    product = mm(lat_ref[quarter], spectrum)
    if is_first:
        modes_ref[...] = product
    else:
        modes_ref[...] += product


def side_by_side(size, modes_ref):
    return jnp.concatenate(
        [modes_ref[: size.modes, :], modes_ref[size.modes :, :]], axis=1
    ).astype(bf16)


def stack_parts(size, values, stacked_ref):
    stacked_ref[: size.modes, :] = values[:, : size.half].astype(bf16)
    stacked_ref[size.modes :, :] = values[:, size.half :].astype(bf16)


def mix_quarter_back(size, quarter, lat_t_ref, stacked_ref, send_ref):
    back = mm(lat_t_ref[quarter], stacked_ref[...])
    for i in range(size.chunk):
        send_ref[quarter * size.chunk + i] = back[i * size.piece : (i + 1) * size.piece].astype(bf16)


def mix_layers(size, modes_ref, w1_ref, b1_ref, w2_ref, b2_ref, band_ref, inner_ref, gated_ref, outer_ref, stacked_ref):
    band = side_by_side(size, modes_ref)
    band_ref[...] = band
    inner = mm(band, w1_ref[...]) + b1_ref[...]
    inner_ref[...] = inner
    gated = smooth_gate(inner).astype(bf16)
    gated_ref[...] = gated
    outer = mm(gated, w2_ref[...]) + b2_ref[...]
    outer_ref[...] = outer
    stack_parts(size, soft_shrink(outer), stacked_ref)


def mix_kernel(size, recv_ref, lat_ref, lat_t_ref, w1_ref, b1_ref, w2_ref, b2_ref, send_ref, band_ref, inner_ref, gated_ref, outer_ref, modes_ref, stacked_ref):
    for quarter in range(QUARTERS):
        add_modes(size, quarter, quarter == 0, recv_ref, lat_ref, modes_ref)
    mix_layers(size, modes_ref, w1_ref, b1_ref, w2_ref, b2_ref, band_ref, inner_ref, gated_ref, outer_ref, stacked_ref)
    for quarter in range(QUARTERS):
        mix_quarter_back(size, quarter, lat_t_ref, stacked_ref, send_ref)


def mix_layers_back(size, modes_ref, w1_ref, w2_ref, inner_ref, outer_ref, outer_grad_ref, inner_grad_ref, stacked_ref):
    upstream = side_by_side(size, modes_ref)
    outer_grad = (upstream.astype(f32) * shrink_slope(outer_ref[...])).astype(bf16)
    outer_grad_ref[...] = outer_grad
    inner_grad = (mm_t(outer_grad, w2_ref[...]) * gate_slope(inner_ref[...])).astype(bf16)
    inner_grad_ref[...] = inner_grad
    stack_parts(size, mm_t(inner_grad, w1_ref[...]), stacked_ref)


def mix_back_weights(size, band_ref, gated_ref, outer_grad_ref, inner_grad_ref, out_ref):
    half = size.half
    block_size = out_ref.shape[2]
    blocks = half // block_size
    rest = out_ref.shape[1] - block_size
    for layer, (value_ref, grad_ref) in enumerate(
        ((band_ref, inner_grad_ref), (gated_ref, outer_grad_ref))
    ):
        grad = grad_ref[...]
        total = t_mm(value_ref[...], grad)
        bias = jnp.sum(grad.astype(f32), axis=0, keepdims=True)
        for block in range(blocks):
            near = slice(block * block_size, (block + 1) * block_size)
            far = slice(half + block * block_size, half + (block + 1) * block_size)
            place = layer * 2 * blocks + block
            out_ref[place, :block_size] = (total[near, near] + total[far, far]).astype(bf16)
            out_ref[place + blocks, :block_size] = (total[near, far] - total[far, near]).astype(bf16)
            shape = (rest, block_size)
            out_ref[place, block_size:] = jnp.broadcast_to(bias[:, near], shape).astype(bf16)
            out_ref[place + blocks, block_size:] = jnp.broadcast_to(bias[:, far], shape).astype(bf16)


def mix_back_kernel(size, recv_ref, lat_ref, lat_t_ref, w1_ref, w2_ref, band_ref, inner_ref, gated_ref, outer_ref, send_ref, grad_ref, outer_grad_ref, inner_grad_ref, modes_ref, stacked_ref):
    for quarter in range(QUARTERS):
        add_modes(size, quarter, quarter == 0, recv_ref, lat_ref, modes_ref)
    mix_layers_back(size, modes_ref, w1_ref, w2_ref, inner_ref, outer_ref, outer_grad_ref, inner_grad_ref, stacked_ref)
    for quarter in range(QUARTERS):
        mix_quarter_back(size, quarter, lat_t_ref, stacked_ref, send_ref)
    mix_back_weights(size, band_ref, gated_ref, outer_grad_ref, inner_grad_ref, grad_ref)


def mlp_kernel(
    size,
    map_ref,
    recv_ref,
    x_ref,
    dy_ref,
    inv_t_ref,
    inv_ref,
    gain1_ref,
    shift1_ref,
    gain2_ref,
    shift2_ref,
    out_bias_ref,
    fc_in_ref,
    fc_in_bias_ref,
    fc_out_ref,
    block_ref,
    dh_ref,
    send_ref,
    hidden_ref,
    hidden_grad_ref,
    low_ref,
    up_ref,
    small_ref,
    res_ref,
    grad_ref,
    acc_ref,
    back_ref,
):
    step = pl.program_id(0)
    gain2, shift2 = as_row(gain2_ref), as_row(shift2_ref)
    first_slot = (lax.axis_index("rows") * size.lon + lax.axis_index("lon")) * size.slots_here

    def live(slot):
        return jnp.where(map_ref[first_slot + slot] >= 0, 1.0, 0.0)


    @pl.when(step == 0)
    def _():
        res_ref[...] = mm(inv_t_ref[...], read_spectrum(size, recv_ref))
        up_sum = jnp.zeros((1, size.channels), f32)
        gain1, shift1 = as_row(gain1_ref), as_row(shift1_ref)
        for source, slot, start in planes(size):
            part = slice(start, start + size.lons_pad)
            x = pad_plane(size, x_ref[source, slot].astype(f32))
            unit, _ = norm_parts(x)
            residual = res_ref[part, :] + (unit * gain1 + shift1) + x
            res_ref[part, :] = residual
            unit, _ = norm_parts(residual)
            low_ref[part, :] = (unit * gain2 + shift2).astype(bf16)
            up = pad_plane(size, dy_ref[source, slot].astype(f32) * live(slot))
            up_ref[part, :] = up.astype(bf16)
            up_sum = up_sum + jnp.sum(up, axis=0, keepdims=True)
        small_ref[...] = jnp.zeros_like(small_ref)
        small_ref[0:1, :] = up_sum
        acc_ref[...] = jnp.zeros_like(acc_ref)
        back_ref[...] = jnp.zeros_like(back_ref)

    low = low_ref[...]
    up = up_ref[...]
    gate, slope = gate_both(mm(low, fc_in_ref[...]) + fc_in_bias_ref[...])
    hidden = gate.astype(bf16)
    acc_ref[...] += mm(hidden, fc_out_ref[...])
    hidden_grad = (mm_t(up, fc_out_ref[...]) * slope).astype(bf16)
    small_ref[pl.ds(3 + step, 1), :] = jnp.sum(hidden_grad.astype(f32), axis=0, keepdims=True)
    back_ref[...] += mm_t(hidden_grad, fc_in_ref[...])
    hidden_ref[...] = hidden
    hidden_grad_ref[...] = hidden_grad

    @pl.when(step == pl.num_programs(0) - 1)
    def _():
        gain_sum = jnp.zeros((1, size.channels), f32)
        shift_sum = jnp.zeros((1, size.channels), f32)
        for source, slot, start in planes(size):
            part = slice(start, start + size.lons_pad)
            residual = res_ref[part, :]
            block = (residual + (acc_ref[part, :] + as_row(out_bias_ref))) * live(slot)
            block_ref[source, slot] = block[: size.lons_here].astype(bf16)
            unit, spread = norm_parts(residual)
            grad = back_ref[part, :]
            gain_sum = gain_sum + jnp.sum(grad * unit, axis=0, keepdims=True)
            shift_sum = shift_sum + jnp.sum(grad, axis=0, keepdims=True)
            grad = up_ref[part, :].astype(f32) + norm_back(grad * gain2, unit, spread)
            dh_ref[part, :] = grad
            grad_ref[part, :] = grad.astype(bf16)
        small_ref[1:2, :] = gain_sum
        small_ref[2:3, :] = shift_sum
        write_pieces(size, mm(inv_ref[...], grad_ref[...]), send_ref)


def wide_kernel(hidden_ref, hidden_grad_ref, low_ref, up_ref, wide_ref):
    channels = low_ref.shape[1]
    for part in range(hidden_ref.shape[0]):
        rows = slice(part * channels, (part + 1) * channels)
        wide_ref[rows, :channels] = t_mm(hidden_grad_ref[part], low_ref[...]).astype(bf16)
        wide_ref[rows, channels:] = t_mm(hidden_ref[part], up_ref[...]).astype(bf16)


def run_mlp(size, hidden_units, row_map, recv, x, dy, inv_t, inv, vectors, fc_in, fc_in_bias, fc_out):
    channels = size.channels
    width = channels
    parts = hidden_units // width
    fixed = pl.BlockSpec(memory_space=pltpu.VMEM)
    tokens = (size.tokens, channels)
    return pl.pallas_call(
        functools.partial(mlp_kernel, size),
        grid=(parts,),
        in_specs=[pl.BlockSpec(memory_space=pltpu.SMEM)]
        + [fixed] * (5 + len(vectors))
        + [
            pl.BlockSpec((channels, width), lambda i: (0, i)),
            pl.BlockSpec((1, width), lambda i: (0, i)),
            pl.BlockSpec((width, channels), lambda i: (i, 0)),
        ],
        out_specs=(
            fixed,
            fixed,
            fixed,
            pl.BlockSpec((None, size.tokens, width), lambda i: (i, 0, 0)),
            pl.BlockSpec((None, size.tokens, width), lambda i: (i, 0, 0)),
            fixed,
            fixed,
            fixed,
        ),
        out_shape=(
            struct(x.shape, bf16),
            struct(tokens, f32),
            struct((size.per_image, size.piece, size.half), bf16),
            struct((parts,) + tokens, bf16),
            struct((parts,) + tokens, bf16),
            struct(tokens, bf16),
            struct(tokens, bf16),
            struct((round_up(3 + parts, 8), channels), f32),
        ),
        scratch_shapes=[
            pltpu.VMEM(tokens, f32),
            pltpu.VMEM(tokens, bf16),
            pltpu.VMEM(tokens, f32),
            pltpu.VMEM(tokens, f32),
        ],
        compiler_params=pltpu.CompilerParams(vmem_limit_bytes=VMEM_BYTES),
        name="mlp",
    )(row_map, recv, x, dy, inv_t, inv, *vectors, fc_in, fc_in_bias, fc_out)


def last_planes(size, recv_ref, x_ref, dh_ref, table_t_ref, gain_ref, out_ref, landing_ref, small_ref, sender, mover):
    gain = as_row(gain_ref)
    filtered = mm(table_t_ref[...], read_spectrum(size, recv_ref))
    gain_sum = jnp.zeros((1, size.channels), f32)
    shift_sum = jnp.zeros((1, size.channels), f32)
    for source, slot, start in planes(size):
        part = slice(start, start + size.lons_pad)
        unit, spread = norm_parts(pad_plane(size, x_ref[source, slot].astype(f32)))
        base = dh_ref[part, :]
        grad = base + filtered[part]
        gain_sum = gain_sum + jnp.sum(grad * unit, axis=0, keepdims=True)
        shift_sum = shift_sum + jnp.sum(grad, axis=0, keepdims=True)
        grad = base + norm_back(grad * gain, unit, spread)
        out_ref[source, slot] = grad[: size.lons_here].astype(bf16)
    small_ref[0:1, :] = gain_sum
    small_ref[1:2, :] = shift_sum
    if sender is None:
        return None
    return start_lon(out_ref, landing_ref, sender, mover)


def last_kernel(size, recv_ref, x_ref, dh_ref, table_t_ref, gain_ref, out_ref, small_ref):
    last_planes(size, recv_ref, x_ref, dh_ref, table_t_ref, gain_ref, out_ref, None, small_ref, None, None)


def partners(lon_count):
    row = lax.axis_index("rows")
    lon = lax.axis_index("lon")
    core = {"rows": row, "lon": lon + 1 - 2 * (lon % 2)}
    along_y = {"rows": row, "lon": (lon + 2) % 4}
    along_x = {"rows": row + 1 - 2 * (row % 2), "lon": lon}
    far_z = {"rows": (row + 4) % 8, "lon": lon}
    return core, along_y, along_x, far_z


def greet(lon_count, count):
    row = lax.axis_index("rows")
    lon = lax.axis_index("lon")
    me = row * lon_count + lon
    barrier = pltpu.get_barrier_semaphore()
    for offset in range(1, count):
        other = (me + offset) % count
        pl.semaphore_signal(
            barrier,
            inc=1,
            device_id={"rows": other // lon_count, "lon": other % lon_count},
            device_id_type=MESH,
        )
    pl.semaphore_wait(barrier, count - 1)


class Sender:
    def __init__(self, send_sem, recv_sem):
        self.send_sem = send_sem
        self.recv_sem = recv_sem
        self.used = 0

    def start(self, source, target, device):
        copy = pltpu.make_async_remote_copy(
            src_ref=source,
            dst_ref=target,
            send_sem=self.send_sem.at[self.used],
            recv_sem=self.recv_sem.at[self.used],
            device_id=device,
            device_id_type=MESH,
        )
        self.used += 1
        copy.start()
        return copy


class Mover:
    def __init__(self, sem):
        self.sem = sem
        self.used = 0

    def start(self, source, target):
        copy = pltpu.make_async_copy(source, target, self.sem.at[self.used])
        self.used += 1
        copy.start()
        return copy


def start_quarter(size, step, source_ref, out_ref, sender, mover):
    row = lax.axis_index("rows")
    lon = lax.axis_index("lon")
    me = place_of(size, row, lon)
    copies = []
    for half_step in range(HALVES):
        for lon_step in range(size.lon):
            to_row = (row + step) % QUARTERS + (row // QUARTERS + half_step) % HALVES * QUARTERS
            to_lon = (lon + lon_step) % size.lon
            piece = source_ref.at[place_of(size, to_row, to_lon)]
            if step == 0 and half_step == 0 and lon_step == 0:
                copies.append(mover.start(piece, out_ref.at[me]))
            else:
                copies.append(
                    sender.start(piece, out_ref.at[me], {"rows": to_row, "lon": to_lon})
                )
    return copies


def start_lon(source_ref, out_ref, sender, mover):
    row = lax.axis_index("rows")
    me = lax.axis_index("lon")
    count = source_ref.shape[0]
    copies = []
    for offset in range(1, count):
        other = (me + offset) % count
        copies.append(
            sender.start(source_ref.at[other], out_ref.at[me], {"rows": row, "lon": other})
        )
    copies.append(mover.start(source_ref.at[me], out_ref.at[me]))
    return copies


def finish(copies):
    for copy in copies:
        copy.wait()


def call_remote(kernel, name, number, outs, spaces, out_spaces, sends, moves, scratch, operands):
    return pl.pallas_call(
        kernel,
        out_shape=outs,
        in_specs=[pl.BlockSpec(memory_space=space) for space in spaces],
        out_specs=tuple(pl.BlockSpec(memory_space=space) for space in out_spaces),
        scratch_shapes=[
            pltpu.SemaphoreType.DMA((sends,)),
            pltpu.SemaphoreType.DMA((sends,)),
            pltpu.SemaphoreType.DMA((moves,)),
        ]
        + list(scratch),
        compiler_params=pltpu.CompilerParams(
            collective_id=number, has_side_effects=True, vmem_limit_bytes=VMEM_BYTES
        ),
        name=name,
    )(*operands)


def forward_kernel(
    size,
    tokens_hbm,
    cot_hbm,
    table_hbm,
    er_hbm,
    ec_hbm,
    rows_ref,
    gain_ref,
    shift_ref,
    cos_ref,
    sin_ref,
    mix_in_ref,
    bias_in_ref,
    mix_out_ref,
    bias_out_ref,
    x_out,
    dy_out,
    recv_out,
    lat_out,
    lat_t_out,
    w1_out,
    w2_out,
    band_out,
    inner_out,
    gated_out,
    outer_out,
    send_sem,
    recv_sem,
    move_sem,
    x_ref,
    table_ref,
    er_ref,
    ec_ref,
    lat_ref,
    lat_t_ref,
    w1_ref,
    w2_ref,
    band_ref,
    inner_ref,
    gated_ref,
    outer_ref,
    b1_ref,
    b2_ref,
    low_ref,
    send1,
    recv1,
    send2,
    modes_ref,
    stacked_ref,
):
    sender, mover = Sender(send_sem, recv_sem), Mover(move_sem)
    mine = lax.axis_index("rows") % QUARTERS
    half = half_of(size)
    load = mover.start(table_hbm, table_ref)
    loads = [mover.start(er_hbm, er_ref), mover.start(ec_hbm, ec_ref)]
    greet(size.lon, size.devices)
    tokens = start_lon(tokens_hbm, x_ref, sender, mover)
    build_block_matrix(size, mix_in_ref, bias_in_ref, half, w1_ref, b1_ref)
    build_block_matrix(size, mix_out_ref, bias_out_ref, half, w2_ref, b2_ref)
    stores = [mover.start(w1_ref, w1_out), mover.start(w2_ref, w2_out)]
    finish(tokens)
    stores.append(mover.start(x_ref, x_out))
    first_norm(size, x_ref, as_row(gain_ref), as_row(shift_ref), low_ref)
    load.wait()
    steps = []
    for step in range(QUARTERS):
        quarter = (mine + step) % QUARTERS
        write_quarter(size, quarter, mm(table_ref[quarter], low_ref[...]), send1)
        steps.append(start_quarter(size, step, send1, recv1, sender, mover))
    cotangents = start_lon(cot_hbm, dy_out, sender, mover)
    finish(loads)
    build_lat_tables(size, rows_ref, cos_ref, sin_ref, er_ref, ec_ref, lat_ref, lat_t_ref)
    stores += [mover.start(lat_ref, lat_out), mover.start(lat_t_ref, lat_t_out)]
    for step in range(QUARTERS):
        finish(steps[step])
        quarter = (mine + QUARTERS - step) % QUARTERS
        add_modes(size, quarter, step == 0, recv1, lat_ref, modes_ref)
    mix_layers(size, modes_ref, w1_ref, b1_ref, w2_ref, b2_ref, band_ref, inner_ref, gated_ref, outer_ref, stacked_ref)
    steps = []
    for step in range(QUARTERS):
        quarter = (mine + step) % QUARTERS
        mix_quarter_back(size, quarter, lat_t_ref, stacked_ref, send2)
        steps.append(start_quarter(size, step, send2, recv_out, sender, mover))
    stores += [
        mover.start(band_ref, band_out),
        mover.start(inner_ref, inner_out),
        mover.start(gated_ref, gated_out),
        mover.start(outer_ref, outer_out),
    ]
    finish(cotangents)
    finish(stores)
    for step in range(QUARTERS):
        finish(steps[step])


def run_forward(size, tokens, cotangent, table, er, ec, rows, gain, shift, cosine, sine, mix_in, mix_in_bias, mix_out, mix_out_bias, number):
    piece = struct((size.per_image, size.piece, size.half), bf16)
    modes = (size.modes, 2 * size.half)
    square = struct((2 * size.half, 2 * size.half), bf16)
    kept = (
        struct((QUARTERS, 2 * size.modes, size.chunk_rows), bf16),
        struct((QUARTERS, size.chunk_rows, 2 * size.modes), bf16),
        square,
        square,
        struct(modes, bf16),
        struct(modes, f32),
        struct(modes, bf16),
        struct(modes, f32),
    )
    row = struct((1, 2 * size.half), f32)
    scratch = (
        (struct(tokens.shape, bf16), table, er, ec)
        + kept
        + (row, row, struct((size.tokens, size.channels), bf16), piece, piece, piece)
        + (struct((2 * size.modes, size.half), f32), struct((2 * size.modes, size.half), bf16))
    )
    small = (rows, gain, shift, cosine, sine, mix_in, mix_in_bias, mix_out, mix_out_bias)
    return call_remote(
        functools.partial(forward_kernel, size),
        "forward",
        number,
        (struct(tokens.shape, bf16), struct(tokens.shape, bf16), piece) + kept,
        [pl.ANY] * 5 + [pltpu.VMEM] * len(small),
        [pl.ANY] * (3 + len(kept)),
        2 * size.per_image + 2 * size.lon,
        24,
        [pltpu.VMEM(v.shape, v.dtype) for v in scratch],
        (tokens, cotangent, table, er, ec) + small,
    )


def add_to(total_ref, other_ref):
    @pl.loop(0, total_ref.shape[0])
    def _(first):
        if len(total_ref.shape) == 3:
            total = total_ref[first].astype(f32) + other_ref[first].astype(f32)
            total_ref[first] = total.astype(total_ref.dtype)
        else:
            for second in range(total_ref.shape[1]):
                total = total_ref[first, second].astype(f32) + other_ref[first, second].astype(f32)
                total_ref[first, second] = total.astype(total_ref.dtype)


def start_same(lon_count, count, source_ref, out_ref, sender, mover):
    me = lax.axis_index("rows") * lon_count + lax.axis_index("lon")
    copies = []
    for offset in range(1, count):
        other = (me + offset) % count
        copies.append(
            sender.start(
                source_ref, out_ref.at[me], {"rows": other // lon_count, "lon": other % lon_count}
            )
        )
    copies.append(mover.start(source_ref, out_ref.at[me]))
    return copies


def backward_kernel(
    size,
    pieces_ref,
    hidden_hbm,
    hidden_grad_hbm,
    block_ref,
    low_hbm,
    up_hbm,
    lat_hbm,
    lat_t_hbm,
    w1_hbm,
    w2_hbm,
    band_hbm,
    inner_hbm,
    gated_hbm,
    outer_hbm,
    x_hbm,
    dh_hbm,
    table_t_hbm,
    gain_ref,
    early_ref,
    token_out,
    block_out,
    dense_ref,
    mix_out,
    early_out,
    late_out,
    send_sem,
    recv_sem,
    move_sem,
    low_ref,
    up_ref,
    lat_ref,
    lat_t_ref,
    w1_ref,
    w2_ref,
    band_ref,
    inner_ref,
    gated_ref,
    outer_ref,
    x_ref,
    dh_ref,
    table_t_ref,
    hidden_ref,
    hidden_grad_ref,
    recv1,
    send2,
    recv2,
    token_ref,
    a_wide,
    b_wide,
    a_core,
    b_core,
    a_one,
    b_one,
    a_two,
    b_two,
    a_near,
    b_near,
    a_last,
    b_last,
    outer_grad_ref,
    inner_grad_ref,
    mix_ref,
    mix_land,
    pair_ref,
    early,
    early_land,
    late,
    late_land,
    modes_ref,
    stacked_ref,
):
    lon_count, count, groups = size.lon, size.devices, size.groups
    row = lax.axis_index("rows")
    lon = lax.axis_index("lon")
    me = row * lon_count + lon
    z = row // 2
    x = row % 2
    y = lon // 2
    core = lon % 2
    mine = row % QUARTERS
    group = me % groups
    base = me - group
    half = me // groups
    to_core, to_y, to_x, far_z = partners(lon_count)
    near = z + 1 - 2 * (z % 2)
    mirror = 3 - z
    to_near = {"rows": near * 2 + x, "lon": lon}
    to_mirror = {"rows": mirror * 2 + x, "lon": lon}
    order = (near, 3 - near, z, mirror)
    parts = len(order)
    share = a_wide.shape[-2]
    sender, mover = Sender(send_sem, recv_sem), Mover(move_sem)

    def load_part(step):
        slot = step % 2
        return [
            mover.start(hidden_grad_hbm.at[order[step]], hidden_grad_ref.at[slot]),
            mover.start(hidden_hbm.at[order[step]], hidden_ref.at[slot]),
        ]

    greet(lon_count, count)
    steps = [start_quarter(size, i, pieces_ref, recv1, sender, mover) for i in range(QUARTERS)]
    first_loads = [mover.start(low_hbm, low_ref), mover.start(up_hbm, up_ref)]
    part_loads = [load_part(0), load_part(1)]
    early[...] = early_ref[...]
    early_hop = sender.start(early, early_land.at[0], to_core)
    loads = [
        mover.start(source, target)
        for source, target in (
            (lat_hbm, lat_ref),
            (outer_hbm, outer_ref),
            (w2_hbm, w2_ref),
            (inner_hbm, inner_ref),
            (w1_hbm, w1_ref),
            (lat_t_hbm, lat_t_ref),
            (gated_hbm, gated_ref),
            (band_hbm, band_ref),
            (x_hbm, x_ref),
            (dh_hbm, dh_ref),
            (table_t_hbm, table_t_ref),
        )
    ]

    def put_rows(values, target):
        for i in range(8):
            target[i // 4, i // 2 % 2, i % 2] = values[i * share : (i + 1) * share].astype(bf16)

    def core_start(step):
        slot = step % 2
        return [
            sender.start(a_wide.at[slot, :, :, 1 - core], a_core.at[step], to_core),
            sender.start(b_wide.at[slot, :, :, 1 - core], b_core.at[step], to_core),
        ]

    def core_end(step, copies):
        slot = step % 2
        finish(copies)
        add_to(a_core.at[step], a_wide.at[slot, :, :, core])
        one = sender.start(a_core.at[step, 1 - x], a_one.at[step], to_x)
        add_to(b_core.at[step], b_wide.at[slot, :, :, core])
        return [one, sender.start(b_core.at[step, :, 1 - y], b_one.at[step], to_y)]

    def one_end(step, copies):
        copies[0].wait()
        add_to(a_one.at[step], a_core.at[step, x])
        one = sender.start(a_one.at[step, 1 - y], a_two.at[step], to_y)
        copies[1].wait()
        add_to(b_one.at[step], b_core.at[step, :, y])
        return [one, sender.start(b_one.at[step, 1 - x], b_two.at[step], to_x)]

    def two_end(step, copies):
        finish(copies)
        for total, kept in ((a_two, a_one.at[step, y]), (b_two, b_one.at[step, x])):
            total[step] = (total[step].astype(f32) + kept[...].astype(f32)).astype(bf16)

    finish(first_loads)
    by_core, by_one, by_two = [], [], []
    for step in range(parts):
        slot = step % 2
        finish(part_loads[step])
        put_rows(t_mm(hidden_grad_ref[slot], low_ref[...]), a_wide.at[slot])
        put_rows(t_mm(hidden_ref[slot], up_ref[...]), b_wide.at[slot])
        by_core.append(core_start(step))
        if step + 2 < parts:
            part_loads.append(load_part(step + 2))
        if step:
            by_one.append(core_end(step - 1, by_core[step - 1]))
    by_one.append(core_end(parts - 1, by_core[parts - 1]))
    early_hop.wait()
    early[...] = early[...] + early_land[0]
    early_hop = sender.start(early, early_land.at[1], to_x)
    for step in range(2):
        by_two.append(one_end(step, by_one[step]))

    finish(loads)
    for step in range(QUARTERS):
        finish(steps[step])
        add_modes(size, (mine + QUARTERS - step) % QUARTERS, step == 0, recv1, lat_ref, modes_ref)
    mix_layers_back(size, modes_ref, w1_ref, w2_ref, inner_ref, outer_ref, outer_grad_ref, inner_grad_ref, stacked_ref)
    steps = []
    for step in range(QUARTERS):
        mix_quarter_back(size, (mine + step) % QUARTERS, lat_t_ref, stacked_ref, send2)
        steps.append(start_quarter(size, step, send2, recv2, sender, mover))

    hops = []
    for step in range(2):
        two_end(step, by_two[step])
        hops.append(sender.start(a_two.at[step], a_near.at[step], to_near))
        hops.append(sender.start(b_two.at[step], b_near.at[step], to_near))
    for step in range(2, parts):
        by_two.append(one_end(step, by_one[step]))
    early_hop.wait()
    early[...] = early[...] + early_land[1]
    early_hop = sender.start(early, early_land.at[2], to_y)

    mix_back_weights(size, band_ref, gated_ref, outer_grad_ref, inner_grad_ref, mix_ref)
    mixes = []
    for offset in range(1, groups):
        other = (group + offset) % groups
        device = base + other
        mixes.append(
            sender.start(
                mix_ref.at[other],
                mix_land.at[group],
                {"rows": device // lon_count, "lon": device % lon_count},
            )
        )
    mixes.append(mover.start(mix_ref.at[group], mix_land.at[group]))
    blocks = start_lon(block_ref, block_out, sender, mover)

    for step in range(2, parts):
        two_end(step, by_two[step])
    finish(hops)
    for total, landed in ((a_two, a_near), (b_two, b_near)):
        for i in range(2):
            total[2 + i] = (total[2 + i].astype(f32) + landed[i].astype(f32)).astype(bf16)
    hops = [
        sender.start(a_two.at[3], a_last, to_mirror),
        sender.start(b_two.at[3], b_last, to_mirror),
    ]
    early_hop.wait()
    early[...] = early[...] + early_land[2]
    early_hop = sender.start(early, early_land.at[3], to_near)

    finish(mixes)
    total = mix_land[0].astype(f32)
    for index in range(1, groups):
        total = total + mix_land[index].astype(f32)
    pair_ref[half] = total.astype(bf16)
    sender.start(pair_ref.at[half], pair_ref.at[half], far_z).wait()
    gather = []
    for offset in range(1, groups):
        device = base + (group + offset) % groups
        gather.append(
            sender.start(
                pair_ref,
                mix_out.at[:, group],
                {"rows": device // lon_count, "lon": device % lon_count},
            )
        )
    gather.append(mover.start(pair_ref, mix_out.at[:, group]))

    for step in range(QUARTERS):
        finish(steps[step])
    tokens = last_planes(size, recv2, x_ref, dh_ref, table_t_ref, gain_ref, token_ref, token_out, late, sender, mover)
    smalls = start_same(lon_count, count, late, late_land, sender, mover)
    early_hop.wait()
    early[...] = early[...] + early_land[3]
    early_hop = sender.start(early, early_land.at[4], to_mirror)
    finish(hops)
    dense_ref[0] = a_two[2].astype(f32) + a_last[...].astype(f32)
    dense_ref[1] = b_two[2].astype(f32) + b_last[...].astype(f32)
    finish(smalls)
    total = late_land[0]
    for index in range(1, count):
        total = total + late_land[index]
    late_out[...] = total
    early_hop.wait()
    early_out[...] = early[...] + early_land[4]
    finish(gather)
    finish(blocks)
    finish(tokens)


def run_backward(size, blocks_shape, pieces, hidden, hidden_grad, block, low, up, lat, lat_t, w1, w2, band, inner, gated, outer, x, dh, table_t, gain, early, number):
    share = hidden.shape[0] * hidden.shape[2] // size.devices
    plane = (share, size.channels)
    loaded = (low, up, lat, lat_t, w1, w2, band, inner, gated, outer, x, dh, table_t)
    late = (2, size.channels)
    modes = (2 * size.modes, size.half)

    scratch = [pltpu.VMEM(v.shape, v.dtype) for v in loaded]
    scratch += [pltpu.VMEM((2,) + hidden.shape[1:], bf16)] * 2
    scratch += [pltpu.VMEM(pieces.shape, bf16)] * 3
    scratch += [pltpu.VMEM(x.shape, bf16)]
    for lead in ((2, 2, 2, 2), (4, 2, 2), (4, 2), (4,), (2,), ()):
        scratch += [pltpu.VMEM(lead + plane, bf16)] * 2
    scratch += [pltpu.VMEM(band.shape, bf16)] * 2
    scratch += [pltpu.VMEM(blocks_shape, bf16)] * 2
    scratch += [pltpu.VMEM((HALVES,) + blocks_shape[1:], bf16)]
    scratch += [pltpu.VMEM(early.shape, f32), pltpu.VMEM((5,) + early.shape, f32)]
    scratch += [pltpu.VMEM(late, f32), pltpu.VMEM((size.devices,) + late, f32)]
    scratch += [pltpu.VMEM(modes, f32), pltpu.VMEM(modes, bf16)]
    return call_remote(
        functools.partial(backward_kernel, size),
        "backward",
        number,
        (
            struct(x.shape, bf16),
            struct(block.shape, bf16),
            struct((2,) + plane, f32),
            struct((HALVES,) + blocks_shape, bf16),
            struct(early.shape, f32),
            struct(late, f32),
        ),
        [pl.ANY] * (4 + len(loaded)) + [pltpu.VMEM] * 2,
        [pl.ANY] * 2 + [pltpu.VMEM] * 4,
        3 * size.devices + 2 * size.groups + 2 * size.lon + 48,
        48,
        scratch,
        (pieces, hidden, hidden_grad, block) + loaded + (gain, early),
    )


def exchange_lon(values):
    return lax.all_to_all(values, "lon", split_axis=0, concat_axis=0, tiled=True)


def exchange_all(values):
    return lax.all_to_all(values, ("rows", "lon"), split_axis=0, concat_axis=0, tiled=True)


def to_modes(size, pieces, row_map):
    order, place = place_order(size)
    sent = jnp.tile(jnp.take(pieces, place, axis=0), (size.images, 1, 1))
    received = exchange_all(sent)
    used = size.slots_here * 2 * size.waves
    by_slot = received[:, :used].reshape(-1, 2 * size.waves, size.half)
    image = (lax.axis_index("rows") * size.lon + lax.axis_index("lon")) // size.per_image
    slots = row_map.shape[0]
    target = jnp.where(row_map >= 0, row_map, size.images * H)
    slot_of_row = (
        jnp.zeros((size.images * H,), jnp.int32)
        .at[target]
        .set(jnp.arange(slots, dtype=jnp.int32), mode="drop")
    )
    own = lax.dynamic_slice_in_dim(slot_of_row, image * H, H)
    picked = jnp.take(by_slot, own, axis=0)
    picked = jnp.pad(picked, ((0, size.virtual_slots - H), (0, 0), (0, 0)))
    picked = picked.reshape(size.per_image, used, size.half)
    return jnp.take(jnp.pad(picked, ((0, 0), (0, size.piece - used), (0, 0))), order, axis=0)


def from_modes(size, pieces, row_map):
    order, place = place_order(size)
    used = size.slots_here * 2 * size.waves
    by_lat = jnp.take(pieces, place, axis=0)[:, :used].reshape(-1, 2 * size.waves, size.half)
    image = (lax.axis_index("rows") * size.lon + lax.axis_index("lon")) // size.per_image
    live = (row_map >= 0) & (row_map // H == image)
    picked = jnp.take(by_lat, jnp.where(live, row_map % H, 0), axis=0)
    picked = picked * live.astype(bf16)[:, None, None]
    picked = picked.reshape(size.devices, used, size.half)
    sent = jnp.pad(picked, ((0, 0), (0, size.piece - used), (0, 0)))
    received = exchange_all(sent)
    received = received.reshape(size.images, size.per_image, size.piece, size.half)
    return jnp.take(jnp.sum(received.astype(f32), axis=0).astype(bf16), order, axis=0)


def body(
    tokens,
    row_map,
    cotangent,
    norm_gain,
    norm_shift,
    mix_in,
    mix_in_bias,
    mix_out,
    mix_out_bias,
    post_gain,
    post_shift,
    fc_in,
    fc_in_bias,
    fc_out,
    fc_out_bias,
):
    size = Sizes(
        lax.axis_size("rows"), lax.axis_size("lon"), row_map.shape[0], tokens.shape[2]
    )
    channels = size.channels
    blocks = mix_in.shape[1]
    blocks_here = blocks // HALVES
    block_size = mix_in.shape[2]
    hidden_units = fc_in.shape[1]
    device = lax.axis_index("rows") * size.lon + lax.axis_index("lon")
    half_index = (device % size.per_image) // size.groups

    table, table_t, inv, inv_t = [jnp.asarray(t) for t in lon_tables(size)]
    table = table.reshape(QUARTERS, size.spectrum // QUARTERS, size.tokens)
    cosine, sine, er, ec = [jnp.asarray(t) for t in lat_parts(size)]
    if size.images == 1:
        slot_lat = row_map
    else:
        slot_lat = jnp.where(jnp.arange(size.virtual_slots) < H, jnp.arange(size.virtual_slots), -1)
    rows = jnp.pad(slot_lat, (0, 128 - size.virtual_slots), constant_values=-1).reshape(1, 128)
    shape = (size.lon, size.slots_here, size.lons_here, channels)
    x, dy = tokens.reshape(shape), cotangent.reshape(shape)
    piece_shape = struct((size.per_image, size.piece, size.half), bf16)
    mode_shape = (size.modes, 2 * size.half)
    wide_modes = (2 * size.modes, size.half)
    mode_scratch = [pltpu.VMEM(wide_modes, f32), pltpu.VMEM(wide_modes, bf16)]
    if size.images == 1:
        x, dy, received, lat, lat_t, w1, w2, band, inner, gated, outer = run_forward(
            size, x, dy, table, er, ec, rows, norm_gain, norm_shift, cosine, sine, mix_in, mix_in_bias, mix_out, mix_out_bias, 0
        )
    else:
        square = struct((2 * size.half, 2 * size.half), bf16)
        flat = struct((1, 2 * size.half), f32)
        lat, lat_t, w1, w2, b1, b2 = call_local(
            functools.partial(prepare_kernel, size),
            "prepare",
            (
                struct((QUARTERS, 2 * size.modes, size.chunk_rows), bf16),
                struct((QUARTERS, size.chunk_rows, 2 * size.modes), bf16),
                square,
                square,
                flat,
                flat,
            ),
        )(rows, cosine, sine, er, ec, mix_in, mix_in_bias, mix_out, mix_out_bias)
        x, dy = exchange_lon(x), exchange_lon(dy)
        sent = call_local(
            functools.partial(first_kernel, size),
            "lon_forward",
            piece_shape,
            [pltpu.VMEM((size.tokens, channels), bf16)],
        )(x, norm_gain, norm_shift, table)
        received = to_modes(size, sent, row_map)
        sent, band, inner, gated, outer = call_local(
            functools.partial(mix_kernel, size),
            "mix_forward",
            (
                piece_shape,
                struct(mode_shape, bf16),
                struct(mode_shape, f32),
                struct(mode_shape, bf16),
                struct(mode_shape, f32),
            ),
            mode_scratch,
        )(received, lat, lat_t, w1, b1, w2, b2)
        received = from_modes(size, sent, row_map)
    vectors = (norm_gain, norm_shift, post_gain, post_shift, fc_out_bias)
    block, dh, sent, hidden, hidden_grad, low, up, early = run_mlp(
        size, hidden_units, row_map, received, x, dy, inv_t, inv, vectors, fc_in, fc_in_bias.reshape(1, -1), fc_out
    )
    blocks_shape = (4 * blocks_here, round_up(block_size + 1, 16), block_size)
    if size.images == 1:
        token_grad, block, dense, mix_total, early, late = run_backward(
            size, blocks_shape, sent, hidden, hidden_grad, block, low, up, lat, lat_t, w1, w2, band, inner, gated, outer, x, dh, table_t, norm_gain, early, 1
        )
    else:
        names = ("rows", "lon")
        early = lax.psum(early, names)
        wide = call_local(
            wide_kernel, "weights_backward", struct((hidden_units, 2 * channels), bf16)
        )(hidden, hidden_grad, low, up)
        dense = lax.psum_scatter(wide, names, scatter_dimension=0, tiled=True)
        dense = jnp.stack([dense[:, :channels], dense[:, channels:]]).astype(f32)
        block = exchange_lon(block)
        received = to_modes(size, sent, row_map)
        sent, mix_grad = call_local(
            functools.partial(mix_back_kernel, size),
            "mix_backward",
            (piece_shape, struct(blocks_shape, bf16)),
            [pltpu.VMEM(mode_shape, bf16)] * 2 + mode_scratch,
        )(received, lat, lat_t, w1, w2, band, inner, gated, outer)
        mix_total = lax.psum(
            jnp.stack(
                [mix_grad.astype(f32) * (half_index == other).astype(f32) for other in range(HALVES)]
            ),
            names,
        )
        received = from_modes(size, sent, row_map)
        token_grad, late = call_local(
            functools.partial(last_kernel, size),
            "lon_backward",
            (struct(x.shape, bf16), struct((2, channels), f32)),
        )(received, x, dh, table_t, norm_gain)
        token_grad = exchange_lon(token_grad)
        late = lax.psum(late, names)
    mix_total = mix_total.astype(f32).reshape((HALVES, 2, 2, blocks_here) + blocks_shape[1:])
    mix_total = jnp.transpose(mix_total, (1, 2, 0, 3, 4, 5)).reshape((2, 2, blocks) + blocks_shape[1:])
    mix_bias = mix_total[:, :, :, block_size]
    mix_total = mix_total[:, :, :, :block_size]
    share = hidden_units // size.devices
    return (
        block.reshape(tokens.shape),
        token_grad.reshape(tokens.shape).astype(f32),
        late[0],
        late[1],
        mix_total[0],
        mix_bias[0],
        mix_total[1],
        mix_bias[1],
        early[1],
        early[2],
        dense[0].T,
        lax.dynamic_slice_in_dim(early[3:7].reshape(-1), device * share, share),
        dense[1],
        early[0],
    )


def solution(mesh):
    return jax.shard_map(
        body,
        mesh=mesh,
        in_specs=(P("rows", "lon", None), P(), P("rows", "lon", None)) + (P(),) * 12,
        out_specs=(
            P("rows", "lon", None),
            P("rows", "lon", None),
            P(),
            P(),
            P(),
            P(),
            P(),
            P(),
            P(),
            P(),
            P(None, ("rows", "lon")),
            P(("rows", "lon")),
            P(("rows", "lon"), None),
            P(),
        ),
        check_vma=False,
    )
```

```python
import functools
import math

import jax
import jax.numpy as jnp
import ml_dtypes
import numpy as np
from jax import lax
from jax.experimental import pallas as pl
from jax.experimental.pallas import tpu as pltpu
from jax.sharding import PartitionSpec as P

H = 90
W = 180
KX = 91
HALVES = 2
QUARTERS = 4
VMEM_BYTES = 58 * 1024 * 1024

norm_eps = 1e-06
shrink_level = 0.01
half_root = 0.7071067811865476
normal_peak = 0.3989422804014327
MESH = pl.DeviceIdType.MESH
f32 = jnp.float32
bf16 = jnp.bfloat16


def round_up(value, step):
    return -(-value // step) * step


class Sizes:
    def __init__(self, rows_count, lon_count, slots, channels):
        self.rows = rows_count
        self.lon = lon_count
        self.devices = rows_count * lon_count
        self.images = slots * 15 // (16 * H)
        self.per_image = self.devices // self.images
        self.groups = self.per_image // HALVES
        self.waves = -(-KX // self.groups)
        self.slots_here = slots // self.devices
        self.lons_here = W // lon_count
        self.lons_pad = round_up(self.lons_here, 16)
        self.tokens = lon_count * self.slots_here * self.lons_pad
        self.piece = round_up(self.slots_here * 2 * self.waves, 8)
        self.spectrum = self.groups * self.piece
        self.band = self.per_image * self.piece
        self.modes = round_up(H * self.waves, 16)
        self.virtual_slots = self.per_image * self.slots_here
        self.chunk = self.per_image // QUARTERS
        self.chunk_rows = self.chunk * self.piece
        self.channels = channels
        self.half = channels // HALVES


def place_of(size, row, lon):
    return (row % QUARTERS) * size.chunk + (row // QUARTERS) * size.lon + lon


def place_order(size):
    place = np.array([place_of(size, d // size.lon, d % size.lon) for d in range(size.per_image)])
    return np.argsort(place), place


def lon_tables(size):
    wave = np.arange(size.groups * size.waves)
    lon_index = np.arange(W)
    product = (lon_index[:, None] * wave[None, :]) % W
    angle = product.astype(np.float32) * np.float32(2.0 * math.pi / W)
    scale = np.float32(1.0 / math.sqrt(W))
    cosine = (np.cos(angle) * scale).astype(ml_dtypes.bfloat16).astype(np.float32)
    sine = (-np.sin(angle) * scale).astype(ml_dtypes.bfloat16).astype(np.float32)
    live = (wave < KX).astype(np.float32)
    factor = np.where((wave == 0) | (wave == W // 2), 1.0, 2.0).astype(np.float32)
    both = np.stack([cosine, sine]) * live
    result = []
    for weight in (np.ones_like(factor), factor):
        table = np.zeros(
            (
                size.groups,
                size.piece,
                size.lon,
                size.slots_here,
                size.lons_pad,
            ),
            np.float32,
        )
        values = (both * weight).reshape(2, size.lon, size.lons_here, size.groups, size.waves)
        values = np.transpose(values, (3, 0, 4, 1, 2)).reshape(
            size.groups, 2 * size.waves, size.lon, size.lons_here
        )
        for slot in range(size.slots_here):
            start = slot * 2 * size.waves
            table[:, start : start + 2 * size.waves, :, slot, : size.lons_here] = values
        flat = table.reshape(size.spectrum, size.tokens).astype(ml_dtypes.bfloat16)
        result.append(flat)
        result.append(np.ascontiguousarray(flat.T))
    return result


def lat_parts(size):
    lat_index = np.arange(H)
    angle = ((lat_index[:, None] * lat_index[None, :]) % H).astype(np.float32) * np.float32(
        2.0 * math.pi / H
    )
    scale = np.float32(1.0 / math.sqrt(H))
    cosine = np.zeros((96, 96), np.float32)
    sine = np.zeros((96, 96), np.float32)
    cosine[:H, :H] = np.cos(angle) * scale
    sine[:H, :H] = np.sin(angle) * scale
    spread_rows = np.zeros((2, size.modes, 2, 96), np.float32)
    for part in range(2):
        for lat in range(H):
            for wave in range(size.waves):
                spread_rows[part, lat * size.waves + wave, part, lat] = 1.0
    spread_cols = np.zeros((QUARTERS, 2, 128, size.chunk, size.piece), np.float32)
    for place, device in enumerate(place_order(size)[0]):
        for slot in range(size.slots_here):
            for part in range(2):
                for wave in range(size.waves):
                    spread_cols[
                        place // size.chunk,
                        part,
                        device * size.slots_here + slot,
                        place % size.chunk,
                        (slot * 2 + part) * size.waves + wave,
                    ] = 1.0
    low = ml_dtypes.bfloat16
    return (
        cosine.astype(low),
        sine.astype(low),
        spread_rows.reshape(2 * size.modes, 192).astype(low),
        spread_cols.reshape(QUARTERS, 256, size.chunk_rows).astype(low),
    )


def smooth_gate(values):
    return 0.5 * values * (1.0 + lax.erf(values * half_root))


def gate_both(values):
    half_phi = 0.5 * (1.0 + lax.erf(values * half_root))
    density = values * normal_peak * jnp.exp(-0.5 * values * values)
    return values * half_phi, half_phi + density


def gate_slope(values):
    return gate_both(values)[1]


def soft_shrink(values):
    return values - shrink_level * values * lax.rsqrt(values * values + shrink_level * shrink_level)


def shrink_slope(values):
    inverse = lax.rsqrt(values * values + shrink_level * shrink_level)
    return 1.0 - shrink_level * shrink_level * shrink_level * inverse * inverse * inverse


def norm_parts(values):
    center = values - jnp.mean(values, axis=-1, keepdims=True)
    spread = lax.rsqrt(jnp.mean(center * center, axis=-1, keepdims=True) + norm_eps)
    return center * spread, spread


def norm_back(scaled, unit, spread):
    return spread * (
        scaled
        - jnp.mean(scaled, axis=-1, keepdims=True)
        - unit * jnp.mean(scaled * unit, axis=-1, keepdims=True)
    )


def mm(left, right):
    return jnp.dot(left, right, preferred_element_type=f32)


def mm_t(left, right):
    return lax.dot_general(left, right, (((1,), (1,)), ((), ())), preferred_element_type=f32)


def t_mm(left, right):
    return lax.dot_general(left, right, (((0,), (0,)), ((), ())), preferred_element_type=f32)


def whole(count):
    return [pl.BlockSpec(memory_space=pltpu.VMEM)] * count


def call_local(kernel, name, outs, scratch=()):
    def run(*operands):
        return pl.pallas_call(
            kernel,
            out_shape=outs,
            in_specs=whole(len(operands)),
            out_specs=jax.tree.map(lambda _: pl.BlockSpec(memory_space=pltpu.VMEM), outs),
            scratch_shapes=list(scratch),
            compiler_params=pltpu.CompilerParams(vmem_limit_bytes=VMEM_BYTES),
            name=name,
        )(*operands)

    return run


def struct(shape, dtype):
    return jax.ShapeDtypeStruct(shape, dtype)


def wave_of(index, period, used, waves, other):
    within = index - period * jnp.floor((index + 0.5) * (1.0 / period))
    wave = within - waves * jnp.floor((within + 0.5) * (1.0 / waves))
    return jnp.where(within < used, wave, other)


def build_lat_tables(size, rows_ref, cos_ref, sin_ref, er_ref, ec_ref, lat_ref, lat_t_ref):
    lat_of = lax.broadcasted_iota(jnp.int32, (96, 128), 0)
    hot = (lat_of == rows_ref[...]).astype(f32).astype(bf16)
    cosine = mm(cos_ref[...], hot)
    sine = mm(sin_ref[...], hot)
    top = jnp.concatenate([cosine, sine], axis=1)
    bottom = jnp.concatenate([-sine, cosine], axis=1)
    base = jnp.concatenate([top, bottom], axis=0).astype(bf16)

    def row_waves(shape, dim):
        index = lax.broadcasted_iota(jnp.int32, shape, dim).astype(f32)
        return wave_of(index, size.modes, H * size.waves, size.waves, -1.0)

    def col_waves(shape, dim):
        index = lax.broadcasted_iota(jnp.int32, shape, dim).astype(f32)
        return wave_of(index, size.piece, size.slots_here * 2 * size.waves, size.waves, -2.0)

    modes, columns_here = 2 * size.modes, size.chunk_rows
    keep = row_waves((modes, 1), 0) == col_waves((1, columns_here), 1)
    keep_t = col_waves((columns_here, 1), 0) == row_waves((1, modes), 1)
    for quarter in range(QUARTERS):
        columns = mm(base, ec_ref[quarter]).astype(bf16)
        table = mm(er_ref[...], columns)
        lat_ref[quarter] = jnp.where(keep, table, 0.0).astype(bf16)
        table_t = lax.dot_general(
            columns, er_ref[...], (((0,), (1,)), ((), ())), preferred_element_type=f32
        )
        lat_t_ref[quarter] = jnp.where(keep_t, table_t, 0.0).astype(bf16)


def build_block_matrix(size, weight_ref, bias_ref, half, matrix_ref, row_ref):
    block_size = weight_ref.shape[2]
    blocks = size.half // block_size
    matrix_ref[...] = jnp.zeros_like(matrix_ref)
    for block in range(blocks):
        real = weight_ref[0, half * blocks + block]
        imag = weight_ref[1, half * blocks + block]
        near = slice(block * block_size, (block + 1) * block_size)
        far = slice(size.half + block * block_size, size.half + (block + 1) * block_size)
        matrix_ref[near, near] = real
        matrix_ref[near, far] = imag
        matrix_ref[far, near] = -imag
        matrix_ref[far, far] = real
        row_ref[0:1, near] = bias_ref[0, pl.ds(half * blocks + block, 1), :]
        row_ref[0:1, far] = bias_ref[1, pl.ds(half * blocks + block, 1), :]


def prepare_kernel(size, rows_ref, cos_ref, sin_ref, er_ref, ec_ref, mix_in_ref, bias_in_ref, mix_out_ref, bias_out_ref, lat_ref, lat_t_ref, w1_ref, w2_ref, b1_ref, b2_ref):
    half = half_of(size)
    build_lat_tables(size, rows_ref, cos_ref, sin_ref, er_ref, ec_ref, lat_ref, lat_t_ref)
    build_block_matrix(size, mix_in_ref, bias_in_ref, half, w1_ref, b1_ref)
    build_block_matrix(size, mix_out_ref, bias_out_ref, half, w2_ref, b2_ref)


def half_of(size):
    device = lax.axis_index("rows") * size.lon + lax.axis_index("lon")
    return (device % size.per_image) // size.groups


def pad_plane(size, plane):
    extra = size.lons_pad - size.lons_here
    return jnp.concatenate([plane, jnp.zeros((extra, plane.shape[1]), plane.dtype)], axis=0)


def planes(size):
    for source in range(size.lon):
        for slot in range(size.slots_here):
            yield source, slot, (source * size.slots_here + slot) * size.lons_pad


def write_quarter(size, quarter, values, out_ref):
    for half in range(HALVES):
        for lon in range(size.lon):
            out_ref[quarter * size.chunk + half * size.lon + lon] = values[
                lon * size.piece : (lon + 1) * size.piece,
                half * size.half : (half + 1) * size.half,
            ].astype(bf16)


def write_pieces(size, values, out_ref):
    rows = size.lon * size.piece
    for quarter in range(QUARTERS):
        write_quarter(size, quarter, values[quarter * rows : (quarter + 1) * rows], out_ref)


def read_pieces(ref, places):
    return jnp.concatenate([ref[place].astype(f32) for place in places], axis=0).astype(bf16)


def read_spectrum(size, ref):
    return jnp.concatenate(
        [
            read_pieces(
                ref,
                [
                    quarter * size.chunk + half * size.lon + lon
                    for quarter in range(QUARTERS)
                    for lon in range(size.lon)
                ],
            )
            for half in range(HALVES)
        ],
        axis=1,
    )


def first_norm(size, x_ref, gain, shift, low_ref):
    for source, slot, start in planes(size):
        x = pad_plane(size, x_ref[source, slot].astype(f32))
        unit, _ = norm_parts(x)
        low_ref[start : start + size.lons_pad, :] = (unit * gain + shift).astype(bf16)


def as_row(ref):
    return ref[...].reshape(1, -1)


def first_kernel(size, x_ref, gain_ref, shift_ref, table_ref, send_ref, low_ref):
    first_norm(size, x_ref, as_row(gain_ref), as_row(shift_ref), low_ref)
    for quarter in range(QUARTERS):
        write_quarter(size, quarter, mm(table_ref[quarter], low_ref[...]), send_ref)


def add_modes(size, quarter, is_first, recv_ref, lat_ref, modes_ref):
    spectrum = read_pieces(recv_ref, [quarter * size.chunk + i for i in range(size.chunk)])
    product = mm(lat_ref[quarter], spectrum)
    if is_first:
        modes_ref[...] = product
    else:
        modes_ref[...] += product


def side_by_side(size, modes_ref):
    return jnp.concatenate(
        [modes_ref[: size.modes, :], modes_ref[size.modes :, :]], axis=1
    ).astype(bf16)


def stack_parts(size, values, stacked_ref):
    stacked_ref[: size.modes, :] = values[:, : size.half].astype(bf16)
    stacked_ref[size.modes :, :] = values[:, size.half :].astype(bf16)


def mix_quarter_back(size, quarter, lat_t_ref, stacked_ref, send_ref):
    back = mm(lat_t_ref[quarter], stacked_ref[...])
    for i in range(size.chunk):
        send_ref[quarter * size.chunk + i] = back[i * size.piece : (i + 1) * size.piece].astype(bf16)


def mix_layers(size, modes_ref, w1_ref, b1_ref, w2_ref, b2_ref, band_ref, inner_ref, gated_ref, outer_ref, stacked_ref):
    band = side_by_side(size, modes_ref)
    band_ref[...] = band
    inner = mm(band, w1_ref[...]) + b1_ref[...]
    inner_ref[...] = inner
    gated = smooth_gate(inner).astype(bf16)
    gated_ref[...] = gated
    outer = mm(gated, w2_ref[...]) + b2_ref[...]
    outer_ref[...] = outer
    stack_parts(size, soft_shrink(outer), stacked_ref)


def mix_kernel(size, recv_ref, lat_ref, lat_t_ref, w1_ref, b1_ref, w2_ref, b2_ref, send_ref, band_ref, inner_ref, gated_ref, outer_ref, modes_ref, stacked_ref):
    for quarter in range(QUARTERS):
        add_modes(size, quarter, quarter == 0, recv_ref, lat_ref, modes_ref)
    mix_layers(size, modes_ref, w1_ref, b1_ref, w2_ref, b2_ref, band_ref, inner_ref, gated_ref, outer_ref, stacked_ref)
    for quarter in range(QUARTERS):
        mix_quarter_back(size, quarter, lat_t_ref, stacked_ref, send_ref)


def mix_layers_back(size, modes_ref, w1_ref, w2_ref, inner_ref, outer_ref, outer_grad_ref, inner_grad_ref, stacked_ref):
    upstream = side_by_side(size, modes_ref)
    outer_grad = (upstream.astype(f32) * shrink_slope(outer_ref[...])).astype(bf16)
    outer_grad_ref[...] = outer_grad
    inner_grad = (mm_t(outer_grad, w2_ref[...]) * gate_slope(inner_ref[...])).astype(bf16)
    inner_grad_ref[...] = inner_grad
    stack_parts(size, mm_t(inner_grad, w1_ref[...]), stacked_ref)


def mix_back_weights(size, band_ref, gated_ref, outer_grad_ref, inner_grad_ref, out_ref):
    half = size.half
    block_size = out_ref.shape[-1]
    blocks = half // block_size
    rest = out_ref.shape[-2] - block_size
    for layer, (value_ref, grad_ref) in enumerate(
        ((band_ref, inner_grad_ref), (gated_ref, outer_grad_ref))
    ):
        grad = grad_ref[...]
        total = t_mm(value_ref[...], grad)
        bias = jnp.sum(grad.astype(f32), axis=0, keepdims=True)
        for block in range(blocks):
            near = slice(block * block_size, (block + 1) * block_size)
            far = slice(half + block * block_size, half + (block + 1) * block_size)
            for part, values, row in (
                (0, total[near, near] + total[far, far], bias[:, near]),
                (1, total[near, far] - total[far, near], bias[:, far]),
            ):
                place = (layer * 2 + part) * blocks + block
                at = (place // 2, place % 2) if len(out_ref.shape) == 4 else (place,)
                out_ref[at + (slice(0, block_size),)] = values.astype(bf16)
                out_ref[at + (slice(block_size, None),)] = jnp.broadcast_to(
                    row, (rest, block_size)
                ).astype(bf16)


def mix_back_kernel(size, recv_ref, lat_ref, lat_t_ref, w1_ref, w2_ref, band_ref, inner_ref, gated_ref, outer_ref, send_ref, grad_ref, outer_grad_ref, inner_grad_ref, modes_ref, stacked_ref):
    for quarter in range(QUARTERS):
        add_modes(size, quarter, quarter == 0, recv_ref, lat_ref, modes_ref)
    mix_layers_back(size, modes_ref, w1_ref, w2_ref, inner_ref, outer_ref, outer_grad_ref, inner_grad_ref, stacked_ref)
    for quarter in range(QUARTERS):
        mix_quarter_back(size, quarter, lat_t_ref, stacked_ref, send_ref)
    mix_back_weights(size, band_ref, gated_ref, outer_grad_ref, inner_grad_ref, grad_ref)


def residual_planes(size, map_ref, recv_ref, x_ref, dy_ref, inv_t_ref, gain1, shift1, gain2, shift2, res_ref, low_ref, up_ref):
    first_slot = (lax.axis_index("rows") * size.lon + lax.axis_index("lon")) * size.slots_here
    res_ref[...] = mm(inv_t_ref[...], read_spectrum(size, recv_ref))
    up_sum = jnp.zeros((1, size.channels), f32)
    for source, slot, start in planes(size):
        part = slice(start, start + size.lons_pad)
        x = pad_plane(size, x_ref[source, slot].astype(f32))
        unit, _ = norm_parts(x)
        residual = res_ref[part, :] + (unit * gain1 + shift1) + x
        res_ref[part, :] = residual
        unit, _ = norm_parts(residual)
        low_ref[part, :] = (unit * gain2 + shift2).astype(bf16)
        live = jnp.where(map_ref[first_slot + slot] >= 0, 1.0, 0.0)
        up = pad_plane(size, dy_ref[source, slot].astype(f32) * live)
        up_ref[part, :] = up.astype(bf16)
        up_sum = up_sum + jnp.sum(up, axis=0, keepdims=True)
    return up_sum


def hidden_part(low_ref, up_ref, fc_in, bias, fc_out, is_first, acc_ref, back_ref):
    gate, slope = gate_both(mm(low_ref[...], fc_in) + bias)
    hidden = gate.astype(bf16)
    forward = mm(hidden, fc_out)
    hidden_grad = (mm_t(up_ref[...], fc_out) * slope).astype(bf16)
    backward = mm_t(hidden_grad, fc_in)
    if is_first:
        acc_ref[...] = forward
        back_ref[...] = backward
    else:
        acc_ref[...] += forward
        back_ref[...] += backward
    return hidden, hidden_grad


def residual_back_planes(size, up_ref, res_ref, gain2, back_ref, grad_ref):
    gain_sum = jnp.zeros((1, size.channels), f32)
    shift_sum = jnp.zeros((1, size.channels), f32)
    for _, _, start in planes(size):
        part = slice(start, start + size.lons_pad)
        unit, spread = norm_parts(res_ref[part, :])
        grad = back_ref[part, :]
        gain_sum = gain_sum + jnp.sum(grad * unit, axis=0, keepdims=True)
        shift_sum = shift_sum + jnp.sum(grad, axis=0, keepdims=True)
        grad = up_ref[part, :].astype(f32) + norm_back(grad * gain2, unit, spread)
        back_ref[part, :] = grad
        grad_ref[part, :] = grad.astype(bf16)
    return gain_sum, shift_sum


def block_planes(size, map_ref, res_ref, acc_ref, out_bias, block_ref):
    first_slot = (lax.axis_index("rows") * size.lon + lax.axis_index("lon")) * size.slots_here
    for source, slot, start in planes(size):
        part = slice(start, start + size.lons_pad)
        live = jnp.where(map_ref[first_slot + slot] >= 0, 1.0, 0.0)
        block = (res_ref[part, :] + (acc_ref[part, :] + out_bias)) * live
        block_ref[source, slot] = block[: size.lons_here].astype(bf16)


def mlp_kernel(
    size,
    map_ref,
    recv_ref,
    x_ref,
    dy_ref,
    inv_t_ref,
    inv_ref,
    gain1_ref,
    shift1_ref,
    gain2_ref,
    shift2_ref,
    out_bias_ref,
    fc_in_ref,
    fc_in_bias_ref,
    fc_out_ref,
    block_ref,
    dh_ref,
    send_ref,
    hidden_ref,
    hidden_grad_ref,
    low_ref,
    up_ref,
    small_ref,
    res_ref,
    grad_ref,
    acc_ref,
):
    step = pl.program_id(0)

    @pl.when(step == 0)
    def _():
        small_ref[...] = jnp.zeros_like(small_ref)
        small_ref[0:1, :] = residual_planes(
            size, map_ref, recv_ref, x_ref, dy_ref, inv_t_ref, as_row(gain1_ref), as_row(shift1_ref), as_row(gain2_ref), as_row(shift2_ref), res_ref, low_ref, up_ref
        )
        acc_ref[...] = jnp.zeros_like(acc_ref)
        dh_ref[...] = jnp.zeros_like(dh_ref)

    hidden, hidden_grad = hidden_part(
        low_ref, up_ref, fc_in_ref[...], fc_in_bias_ref[...], fc_out_ref[...], False, acc_ref, dh_ref
    )
    small_ref[pl.ds(3 + step, 1), :] = jnp.sum(hidden_grad.astype(f32), axis=0, keepdims=True)
    hidden_ref[...] = hidden
    hidden_grad_ref[...] = hidden_grad

    @pl.when(step == pl.num_programs(0) - 1)
    def _():
        block_planes(size, map_ref, res_ref, acc_ref, as_row(out_bias_ref), block_ref)
        gain_sum, shift_sum = residual_back_planes(size, up_ref, res_ref, as_row(gain2_ref), dh_ref, grad_ref)
        small_ref[1:2, :] = gain_sum
        small_ref[2:3, :] = shift_sum
        write_pieces(size, mm(inv_ref[...], grad_ref[...]), send_ref)


def wide_kernel(hidden_ref, hidden_grad_ref, low_ref, up_ref, wide_ref):
    channels = low_ref.shape[1]
    for part in range(hidden_ref.shape[0]):
        rows = slice(part * channels, (part + 1) * channels)
        wide_ref[rows, :channels] = t_mm(hidden_grad_ref[part], low_ref[...]).astype(bf16)
        wide_ref[rows, channels:] = t_mm(hidden_ref[part], up_ref[...]).astype(bf16)


def run_mlp(size, hidden_units, row_map, recv, x, dy, inv_t, inv, vectors, fc_in, fc_in_bias, fc_out):
    channels = size.channels
    width = channels
    parts = hidden_units // width
    fixed = pl.BlockSpec(memory_space=pltpu.VMEM)
    tokens = (size.tokens, channels)
    return pl.pallas_call(
        functools.partial(mlp_kernel, size),
        grid=(parts,),
        in_specs=[pl.BlockSpec(memory_space=pltpu.SMEM)]
        + [fixed] * (5 + len(vectors))
        + [
            pl.BlockSpec((channels, width), lambda i: (0, i)),
            pl.BlockSpec((1, width), lambda i: (0, i)),
            pl.BlockSpec((width, channels), lambda i: (i, 0)),
        ],
        out_specs=(
            fixed,
            fixed,
            fixed,
            pl.BlockSpec((None, size.tokens, width), lambda i: (i, 0, 0)),
            pl.BlockSpec((None, size.tokens, width), lambda i: (i, 0, 0)),
            fixed,
            fixed,
            fixed,
        ),
        out_shape=(
            struct(x.shape, bf16),
            struct(tokens, f32),
            struct((size.per_image, size.piece, size.half), bf16),
            struct((parts,) + tokens, bf16),
            struct((parts,) + tokens, bf16),
            struct(tokens, bf16),
            struct(tokens, bf16),
            struct((round_up(3 + parts, 8), channels), f32),
        ),
        scratch_shapes=[
            pltpu.VMEM(tokens, f32),
            pltpu.VMEM(tokens, bf16),
            pltpu.VMEM(tokens, f32),
        ],
        compiler_params=pltpu.CompilerParams(vmem_limit_bytes=VMEM_BYTES),
        name="mlp",
    )(row_map, recv, x, dy, inv_t, inv, *vectors, fc_in, fc_in_bias, fc_out)


def last_planes(size, recv_ref, x_ref, dh_ref, table_t_ref, gain_ref, out_ref, landing_ref, small_ref, sender, mover):
    gain = as_row(gain_ref)
    filtered = mm(table_t_ref[...], read_spectrum(size, recv_ref))
    gain_sum = jnp.zeros((1, size.channels), f32)
    shift_sum = jnp.zeros((1, size.channels), f32)
    for source, slot, start in planes(size):
        part = slice(start, start + size.lons_pad)
        unit, spread = norm_parts(pad_plane(size, x_ref[source, slot].astype(f32)))
        base = dh_ref[part, :]
        grad = base + filtered[part]
        gain_sum = gain_sum + jnp.sum(grad * unit, axis=0, keepdims=True)
        shift_sum = shift_sum + jnp.sum(grad, axis=0, keepdims=True)
        grad = base + norm_back(grad * gain, unit, spread)
        out_ref[source, slot] = grad[: size.lons_here].astype(bf16)
    small_ref[0:1, :] = gain_sum
    small_ref[1:2, :] = shift_sum
    if sender is None:
        return None
    return start_lon(out_ref, landing_ref, sender, mover)


def last_kernel(size, recv_ref, x_ref, dh_ref, table_t_ref, gain_ref, out_ref, small_ref):
    last_planes(size, recv_ref, x_ref, dh_ref, table_t_ref, gain_ref, out_ref, None, small_ref, None, None)


def partners(lon_count):
    row = lax.axis_index("rows")
    lon = lax.axis_index("lon")
    core = {"rows": row, "lon": lon + 1 - 2 * (lon % 2)}
    along_y = {"rows": row, "lon": (lon + 2) % 4}
    along_x = {"rows": row + 1 - 2 * (row % 2), "lon": lon}
    far_z = {"rows": (row + 4) % 8, "lon": lon}
    return core, along_y, along_x, far_z


def greet(lon_count, count):
    row = lax.axis_index("rows")
    lon = lax.axis_index("lon")
    me = row * lon_count + lon
    barrier = pltpu.get_barrier_semaphore()
    for offset in range(1, count):
        other = (me + offset) % count
        pl.semaphore_signal(
            barrier,
            inc=1,
            device_id={"rows": other // lon_count, "lon": other % lon_count},
            device_id_type=MESH,
        )
    pl.semaphore_wait(barrier, count - 1)


class Sender:
    def __init__(self, send_sem, recv_sem):
        self.send_sem = send_sem
        self.recv_sem = recv_sem
        self.used = 0

    def make(self, source, target, device):
        copy = pltpu.make_async_remote_copy(
            src_ref=source,
            dst_ref=target,
            send_sem=self.send_sem.at[self.used],
            recv_sem=self.recv_sem.at[self.used],
            device_id=device,
            device_id_type=MESH,
        )
        self.used += 1
        return copy

    def start(self, source, target, device):
        copy = self.make(source, target, device)
        copy.start()
        return copy


class Mover:
    def __init__(self, sem):
        self.sem = sem
        self.used = 0

    def make(self, source, target):
        copy = pltpu.make_async_copy(source, target, self.sem.at[self.used])
        self.used += 1
        return copy

    def start(self, source, target):
        copy = self.make(source, target)
        copy.start()
        return copy


def make_quarter(size, step, source_ref, out_ref, sender, mover):
    row = lax.axis_index("rows")
    lon = lax.axis_index("lon")
    me = place_of(size, row, lon)
    copies = []
    for half_step in range(HALVES):
        for lon_step in range(size.lon):
            to_row = (row + step) % QUARTERS + (row // QUARTERS + half_step) % HALVES * QUARTERS
            to_lon = (lon + lon_step) % size.lon
            piece = source_ref.at[place_of(size, to_row, to_lon)]
            if step == 0 and half_step == 0 and lon_step == 0:
                copies.append(mover.make(piece, out_ref.at[me]))
            else:
                copies.append(
                    sender.make(piece, out_ref.at[me], {"rows": to_row, "lon": to_lon})
                )
    return copies


def start_quarter(size, step, source_ref, out_ref, sender, mover):
    return begin(make_quarter(size, step, source_ref, out_ref, sender, mover))


def make_lon(source_ref, out_ref, sender, mover):
    row = lax.axis_index("rows")
    me = lax.axis_index("lon")
    count = source_ref.shape[0]
    copies = []
    for offset in range(1, count):
        other = (me + offset) % count
        copies.append(
            sender.make(source_ref.at[other], out_ref.at[me], {"rows": row, "lon": other})
        )
    copies.append(mover.make(source_ref.at[me], out_ref.at[me]))
    return copies


def start_lon(source_ref, out_ref, sender, mover):
    return begin(make_lon(source_ref, out_ref, sender, mover))


def begin(copies):
    for copy in copies:
        copy.start()
    return copies


def finish(copies):
    for copy in copies:
        copy.wait()


def call_remote(kernel, name, number, outs, spaces, out_spaces, sends, moves, scratch, operands):
    return pl.pallas_call(
        kernel,
        out_shape=outs,
        in_specs=[pl.BlockSpec(memory_space=space) for space in spaces],
        out_specs=tuple(pl.BlockSpec(memory_space=space) for space in out_spaces),
        scratch_shapes=[
            pltpu.SemaphoreType.DMA((sends,)),
            pltpu.SemaphoreType.DMA((sends,)),
            pltpu.SemaphoreType.DMA((moves,)),
        ]
        + list(scratch),
        compiler_params=pltpu.CompilerParams(
            collective_id=number, has_side_effects=True, vmem_limit_bytes=VMEM_BYTES
        ),
        name=name,
    )(*operands)


def forward_kernel(
    size,
    tokens_hbm,
    cot_hbm,
    table_hbm,
    er_hbm,
    ec_hbm,
    rows_ref,
    gain_ref,
    shift_ref,
    cos_ref,
    sin_ref,
    mix_in_ref,
    bias_in_ref,
    mix_out_ref,
    bias_out_ref,
    x_out,
    dy_out,
    recv_out,
    lat_out,
    lat_t_out,
    w1_out,
    w2_out,
    band_out,
    inner_out,
    gated_out,
    outer_out,
    send_sem,
    recv_sem,
    move_sem,
    x_ref,
    table_ref,
    er_ref,
    ec_ref,
    lat_ref,
    lat_t_ref,
    w1_ref,
    w2_ref,
    band_ref,
    inner_ref,
    gated_ref,
    outer_ref,
    b1_ref,
    b2_ref,
    low_ref,
    send1,
    recv1,
    send2,
    modes_ref,
    stacked_ref,
):
    sender, mover = Sender(send_sem, recv_sem), Mover(move_sem)
    mine = lax.axis_index("rows") % QUARTERS
    half = half_of(size)
    load = mover.start(table_hbm, table_ref)
    loads = [mover.start(er_hbm, er_ref), mover.start(ec_hbm, ec_ref)]
    greet(size.lon, size.devices)
    tokens = start_lon(tokens_hbm, x_ref, sender, mover)
    build_block_matrix(size, mix_in_ref, bias_in_ref, half, w1_ref, b1_ref)
    build_block_matrix(size, mix_out_ref, bias_out_ref, half, w2_ref, b2_ref)
    stores = [mover.start(w1_ref, w1_out), mover.start(w2_ref, w2_out)]
    finish(tokens)
    stores.append(mover.start(x_ref, x_out))
    first_norm(size, x_ref, as_row(gain_ref), as_row(shift_ref), low_ref)
    load.wait()
    steps = []
    for step in range(QUARTERS):
        quarter = (mine + step) % QUARTERS
        write_quarter(size, quarter, mm(table_ref[quarter], low_ref[...]), send1)
        steps.append(start_quarter(size, step, send1, recv1, sender, mover))
    cotangents = start_lon(cot_hbm, dy_out, sender, mover)
    finish(loads)
    build_lat_tables(size, rows_ref, cos_ref, sin_ref, er_ref, ec_ref, lat_ref, lat_t_ref)
    stores += [mover.start(lat_ref, lat_out), mover.start(lat_t_ref, lat_t_out)]
    for step in range(QUARTERS):
        finish(steps[step])
        quarter = (mine + QUARTERS - step) % QUARTERS
        add_modes(size, quarter, step == 0, recv1, lat_ref, modes_ref)
    mix_layers(size, modes_ref, w1_ref, b1_ref, w2_ref, b2_ref, band_ref, inner_ref, gated_ref, outer_ref, stacked_ref)
    steps = []
    for step in range(QUARTERS):
        quarter = (mine + step) % QUARTERS
        mix_quarter_back(size, quarter, lat_t_ref, stacked_ref, send2)
        steps.append(start_quarter(size, step, send2, recv_out, sender, mover))
    stores += [
        mover.start(band_ref, band_out),
        mover.start(inner_ref, inner_out),
        mover.start(gated_ref, gated_out),
        mover.start(outer_ref, outer_out),
    ]
    finish(cotangents)
    finish(stores)
    for step in range(QUARTERS):
        finish(steps[step])


def run_forward(size, tokens, cotangent, table, er, ec, rows, gain, shift, cosine, sine, mix_in, mix_in_bias, mix_out, mix_out_bias, number):
    piece = struct((size.per_image, size.piece, size.half), bf16)
    modes = (size.modes, 2 * size.half)
    square = struct((2 * size.half, 2 * size.half), bf16)
    kept = (
        struct((QUARTERS, 2 * size.modes, size.chunk_rows), bf16),
        struct((QUARTERS, size.chunk_rows, 2 * size.modes), bf16),
        square,
        square,
        struct(modes, bf16),
        struct(modes, f32),
        struct(modes, bf16),
        struct(modes, f32),
    )
    row = struct((1, 2 * size.half), f32)
    scratch = (
        (struct(tokens.shape, bf16), table, er, ec)
        + kept
        + (row, row, struct((size.tokens, size.channels), bf16), piece, piece, piece)
        + (struct((2 * size.modes, size.half), f32), struct((2 * size.modes, size.half), bf16))
    )
    small = (rows, gain, shift, cosine, sine, mix_in, mix_in_bias, mix_out, mix_out_bias)
    return call_remote(
        functools.partial(forward_kernel, size),
        "forward",
        number,
        (struct(tokens.shape, bf16), struct(tokens.shape, bf16), piece) + kept,
        [pl.ANY] * 5 + [pltpu.VMEM] * len(small),
        [pl.ANY] * (3 + len(kept)),
        2 * size.per_image + 2 * size.lon,
        24,
        [pltpu.VMEM(v.shape, v.dtype) for v in scratch],
        (tokens, cotangent, table, er, ec) + small,
    )


def add_to(total_ref, other_ref):
    @pl.loop(0, total_ref.shape[0])
    def _(first):
        if len(total_ref.shape) == 3:
            total = total_ref[first].astype(f32) + other_ref[first].astype(f32)
            total_ref[first] = total.astype(total_ref.dtype)
        else:
            for second in range(total_ref.shape[1]):
                total = total_ref[first, second].astype(f32) + other_ref[first, second].astype(f32)
                total_ref[first, second] = total.astype(total_ref.dtype)


def start_same(lon_count, count, source_ref, out_ref, sender, mover):
    me = lax.axis_index("rows") * lon_count + lax.axis_index("lon")
    copies = []
    for offset in range(1, count):
        other = (me + offset) % count
        copies.append(
            sender.start(
                source_ref, out_ref.at[me], {"rows": other // lon_count, "lon": other % lon_count}
            )
        )
    copies.append(mover.start(source_ref, out_ref.at[me]))
    return copies


def backward_kernel(
    size,
    e_hbm,
    dy_hbm,
    inv_t_hbm,
    inv_hbm,
    fc_in_hbm,
    fc_out_hbm,
    lat_hbm,
    lat_t_hbm,
    w1_hbm,
    w2_hbm,
    band_hbm,
    inner_hbm,
    gated_hbm,
    outer_hbm,
    x_hbm,
    table_t_hbm,
    map_ref,
    gain1_ref,
    shift1_ref,
    gain2_ref,
    shift2_ref,
    out_bias_ref,
    fc_in_bias_ref,
    token_out,
    block_out,
    dense_ref,
    mix_out,
    early_out,
    late_out,
    send_sem,
    recv_sem,
    move_sem,
    x_ref,
    table_t_ref,
    dh_ref,
    send1,
    recv1,
    send2,
    recv2,
    token_ref,
    block_ref,
    a_wide,
    b_wide,
    a_core,
    b_core,
    a_one,
    b_one,
    a_two,
    b_two,
    a_near,
    b_near,
    a_last,
    b_last,
    mix_ref,
    mix_core,
    mix_land,
    pair_ref,
    early,
    early_land,
    late,
    late_land,
):
    channels = size.channels
    lon_count, count, groups = size.lon, size.devices, size.groups
    row = lax.axis_index("rows")
    lon = lax.axis_index("lon")
    me = row * lon_count + lon
    z = row // 2
    x = row % 2
    y = lon // 2
    core = lon % 2
    mine = row % QUARTERS
    group = me % groups
    base = me - group
    half = me // groups
    to_core, to_y, to_x, far_z = partners(lon_count)
    near = z + 1 - 2 * (z % 2)
    mirror = 3 - z
    to_near = {"rows": near * 2 + x, "lon": lon}
    to_mirror = {"rows": mirror * 2 + x, "lon": lon}
    order = (near, 3 - near, z, mirror)
    parts = len(order)
    share = a_wide.shape[-2]
    sender, mover = Sender(send_sem, recv_sem), Mover(move_sem)

    by_core = [
        [
            sender.make(a_wide.at[i % 2, :, :, 1 - core], a_core.at[i], to_core),
            sender.make(b_wide.at[i % 2, :, :, 1 - core], b_core.at[i], to_core),
        ]
        for i in range(parts)
    ]
    by_one = [
        [
            sender.make(a_core.at[i, 1 - x], a_one.at[i], to_x),
            sender.make(b_core.at[i, :, 1 - y], b_one.at[i], to_y),
        ]
        for i in range(parts)
    ]
    by_two = [
        [
            sender.make(a_one.at[i, 1 - y], a_two.at[i], to_y),
            sender.make(b_one.at[i, 1 - x], b_two.at[i], to_x),
        ]
        for i in range(parts)
    ]
    by_near = [
        [
            sender.make(a_two.at[i], a_near.at[i], to_near),
            sender.make(b_two.at[i], b_near.at[i], to_near),
        ]
        for i in range(2)
    ]
    by_early = [
        sender.make(early, early_land.at[i], device)
        for i, device in enumerate((to_core, to_x, to_y, to_near, to_mirror))
    ]
    by_quarter = [make_quarter(size, i, send1, recv1, sender, mover) for i in range(QUARTERS)]
    blocks = make_lon(block_ref, block_out, sender, mover)
    late_loads = [mover.make(x_hbm, x_ref), mover.make(table_t_hbm, table_t_ref)]

    def core_end(step):
        finish(by_core[step])
        add_to(a_core.at[step], a_wide.at[step % 2, :, :, core])
        by_one[step][0].start()
        add_to(b_core.at[step], b_wide.at[step % 2, :, :, core])
        by_one[step][1].start()

    def one_end(step):
        by_one[step][0].wait()
        add_to(a_one.at[step], a_core.at[step, x])
        by_two[step][0].start()
        by_one[step][1].wait()
        add_to(b_one.at[step], b_core.at[step, :, y])
        by_two[step][1].start()

    def two_end(step):
        finish(by_two[step])
        for total, kept in ((a_two, a_one.at[step, y]), (b_two, b_one.at[step, x])):
            total[step] = (total[step].astype(f32) + kept[...].astype(f32)).astype(bf16)

    def early_step(step):
        by_early[step].wait()
        early[...] = early[...] + early_land[step]
        if step + 1 < len(by_early):
            by_early[step + 1].start()

    def front(
        e_ref,
        dy_ref,
        inv_t_ref,
        inv_ref,
        fc_in_ref,
        fc_out_ref,
        hidden_ref,
        hidden_grad_ref,
        low_ref,
        up_ref,
        grad_ref,
        res_ref,
        acc_ref,
    ):
        def load_part(step):
            slot = step % 2
            place = pl.ds(pl.multiple_of(order[step] * channels, channels), channels)
            return [
                mover.start(fc_in_hbm.at[:, place], fc_in_ref.at[slot]),
                mover.start(fc_out_hbm.at[place, :], fc_out_ref.at[slot]),
            ]

        late_loads[0].start()
        loads = [
            mover.start(e_hbm, e_ref),
            mover.start(inv_t_hbm, inv_t_ref),
            mover.start(dy_hbm, dy_ref),
        ]
        part_loads = [load_part(0), load_part(1)]
        inv_load = mover.start(inv_hbm, inv_ref)
        late_loads[1].start()
        greet(lon_count, count)
        finish(loads)
        late_loads[0].wait()
        early[...] = jnp.zeros_like(early)
        early[0:1, :] = residual_planes(
            size, map_ref, e_ref, x_ref, dy_ref, inv_t_ref, as_row(gain1_ref), as_row(shift1_ref), as_row(gain2_ref), as_row(shift2_ref), res_ref, low_ref, up_ref
        )

        def weights(step):
            slot = step % 2
            for values, other, target in (
                (hidden_grad_ref, low_ref, a_wide),
                (hidden_ref, up_ref, b_wide),
            ):
                product = t_mm(values[slot], other[...])
                for i in range(8):
                    target[slot, i // 4, i // 2 % 2, i % 2] = product[
                        i * share : (i + 1) * share
                    ].astype(bf16)
            begin(by_core[step])

        for step in range(parts):
            slot = step % 2
            finish(part_loads[step])
            place = pl.ds(pl.multiple_of(order[step] * channels, channels), channels)
            hidden, hidden_grad = hidden_part(
                low_ref, up_ref, fc_in_ref[slot], fc_in_bias_ref[:, place], fc_out_ref[slot], step == 0, acc_ref, dh_ref
            )
            early[pl.ds(3 + order[step], 1), :] = jnp.sum(
                hidden_grad.astype(f32), axis=0, keepdims=True
            )
            hidden_ref[slot] = hidden
            hidden_grad_ref[slot] = hidden_grad
            if step + 2 < parts:
                part_loads.append(load_part(step + 2))
            if step < 2:
                weights(step)
            if step in (1, 2):
                core_end(step - 1)
            if step == 3:
                one_end(0)

        gain_sum, shift_sum = residual_back_planes(size, up_ref, res_ref, as_row(gain2_ref), dh_ref, grad_ref)
        early[1:2, :] = gain_sum
        early[2:3, :] = shift_sum
        inv_load.wait()
        rows = size.spectrum // QUARTERS
        for step in range(QUARTERS):
            quarter = (mine + step) % QUARTERS
            write_quarter(size, quarter, mm(inv_ref[quarter], grad_ref[...]), send1)
            begin(by_quarter[step])
        by_early[0].start()
        one_end(1)
        weights(2)
        weights(3)
        core_end(2)
        core_end(3)
        block_planes(size, map_ref, res_ref, acc_ref, as_row(out_bias_ref), block_ref)
        begin(blocks)
        early_step(0)

    def back(
        lat_ref,
        lat_t_ref,
        w1_ref,
        w2_ref,
        band_ref,
        inner_ref,
        gated_ref,
        outer_ref,
        outer_grad_ref,
        inner_grad_ref,
        modes_ref,
        stacked_ref,
    ):
        loads = [
            mover.start(source, target)
            for source, target in (
                (lat_hbm, lat_ref),
                (outer_hbm, outer_ref),
                (w2_hbm, w2_ref),
                (inner_hbm, inner_ref),
                (w1_hbm, w1_ref),
                (lat_t_hbm, lat_t_ref),
                (gated_hbm, gated_ref),
                (band_hbm, band_ref),
            )
        ]
        for step in range(2):
            two_end(step)
            begin(by_near[step])
        finish(loads)
        for step in range(QUARTERS):
            finish(by_quarter[step])
            add_modes(size, (mine + QUARTERS - step) % QUARTERS, step == 0, recv1, lat_ref, modes_ref)
        mix_layers_back(size, modes_ref, w1_ref, w2_ref, inner_ref, outer_ref, outer_grad_ref, inner_grad_ref, stacked_ref)
        steps = []
        for step in range(QUARTERS):
            mix_quarter_back(size, (mine + step) % QUARTERS, lat_t_ref, stacked_ref, send2)
            steps.append(start_quarter(size, step, send2, recv2, sender, mover))
        one_end(2)
        one_end(3)
        early_step(1)

        mix_back_weights(size, band_ref, gated_ref, outer_grad_ref, inner_grad_ref, mix_ref)
        crossing = sender.start(mix_ref.at[:, 1 - core], mix_core, to_core)
        two_end(2)
        two_end(3)
        crossing.wait()
        add_to(mix_core, mix_ref.at[:, core])
        pair = group // 2
        mixes = []
        for offset in range(1, groups // 2):
            other = (pair + offset) % (groups // 2)
            device = base + other * 2 + core
            mixes.append(
                sender.start(
                    mix_core.at[other],
                    mix_land.at[pair],
                    {"rows": device // lon_count, "lon": device % lon_count},
                )
            )
        mixes.append(mover.start(mix_core.at[pair], mix_land.at[pair]))

        finish(by_near[0])
        finish(by_near[1])
        for total, landed in ((a_two, a_near), (b_two, b_near)):
            for i in range(2):
                total[2 + i] = (total[2 + i].astype(f32) + landed[i].astype(f32)).astype(bf16)
        hops = [
            sender.start(a_two.at[3], a_last, to_mirror),
            sender.start(b_two.at[3], b_last, to_mirror),
        ]
        early_step(2)
        finish(mixes)
        total = mix_land[0].astype(f32)
        for index in range(1, groups // 2):
            total = total + mix_land[index].astype(f32)
        pair_ref[half] = total.astype(bf16)
        crossing = sender.start(pair_ref.at[half], pair_ref.at[half], far_z)

        for step in range(QUARTERS):
            finish(steps[step])
        crossing.wait()
        own_place = mix_out.at[pair // 4, pair // 2 % 2, :, pair % 2, core]
        gather = []
        for offset in range(1, groups // 2):
            device = base + (pair + offset) % (groups // 2) * 2 + core
            gather.append(
                sender.start(
                    pair_ref, own_place, {"rows": device // lon_count, "lon": device % lon_count}
                )
            )
        gather.append(mover.start(pair_ref, own_place))
        tokens = last_planes(size, recv2, x_ref, dh_ref, table_t_ref, gain1_ref, token_ref, token_out, late, sender, mover)
        smalls = start_same(lon_count, count, late, late_land, sender, mover)
        early_step(3)
        finish(hops)
        dense_ref[0] = a_two[2].astype(f32) + a_last[...].astype(f32)
        dense_ref[1] = b_two[2].astype(f32) + b_last[...].astype(f32)
        finish(gather)
        own_core = mix_out.at[:, :, :, :, core]
        gather = sender.start(own_core, own_core, to_core)
        finish(smalls)
        total = late_land[0]
        for index in range(1, count):
            total = total + late_land[index]
        late_out[...] = total
        early_step(4)
        early_out[...] = early[...]
        gather.wait()
        finish(blocks)
        finish(tokens)

    piece = send1.shape
    tokens = dh_ref.shape
    wide = (2, channels, channels)
    pl.run_scoped(
        front,
        pltpu.VMEM(piece, bf16),
        pltpu.VMEM(x_ref.shape, bf16),
        pltpu.VMEM(inv_t_hbm.shape, bf16),
        pltpu.VMEM(inv_hbm.shape, bf16),
        pltpu.VMEM(wide, bf16),
        pltpu.VMEM(wide, bf16),
        pltpu.VMEM((2,) + tokens, bf16),
        pltpu.VMEM((2,) + tokens, bf16),
        pltpu.VMEM(tokens, bf16),
        pltpu.VMEM(tokens, bf16),
        pltpu.VMEM(tokens, bf16),
        pltpu.VMEM(tokens, f32),
        pltpu.VMEM(tokens, f32),
    )
    modes = (2 * size.modes, size.half)
    late_loads[1].wait()
    pl.run_scoped(
        back,
        *[
            pltpu.VMEM(ref.shape, ref.dtype)
            for ref in (lat_hbm, lat_t_hbm, w1_hbm, w2_hbm, band_hbm, inner_hbm, gated_hbm, outer_hbm)
        ],
        pltpu.VMEM(band_hbm.shape, bf16),
        pltpu.VMEM(band_hbm.shape, bf16),
        pltpu.VMEM(modes, f32),
        pltpu.VMEM(modes, bf16),
    )


def run_backward(size, blocks_shape, e, dy, inv_t, inv, fc_in, fc_out, lat, lat_t, w1, w2, band, inner, gated, outer, x, table_t, row_map, vectors, fc_in_bias, number):
    parts = fc_out.shape[0] // size.channels
    plane = (fc_out.shape[0] // size.devices, size.channels)
    large = (e, dy, inv_t, inv, fc_in, fc_out, lat, lat_t, w1, w2, band, inner, gated, outer, x, table_t)
    early = (round_up(3 + parts, 8), size.channels)
    late = (2, size.channels)
    block = blocks_shape[1:]
    half_blocks = (blocks_shape[0] // 2,) + block

    scratch = [pltpu.VMEM(x.shape, bf16), pltpu.VMEM(table_t.shape, bf16)]
    scratch += [pltpu.VMEM((size.tokens, size.channels), f32)]
    scratch += [pltpu.VMEM(e.shape, bf16)] * 4
    scratch += [pltpu.VMEM(x.shape, bf16)] * 2
    for lead in ((2, 2, 2, 2), (4, 2, 2), (4, 2), (4,), (2,), ()):
        scratch += [pltpu.VMEM(lead + plane, bf16)] * 2
    scratch += [pltpu.VMEM((blocks_shape[0] // 2, 2) + block, bf16)]
    scratch += [pltpu.VMEM(half_blocks, bf16)] * 2
    scratch += [pltpu.VMEM((HALVES,) + block, bf16)]
    scratch += [pltpu.VMEM(early, f32), pltpu.VMEM((5,) + early, f32)]
    scratch += [pltpu.VMEM(late, f32), pltpu.VMEM((size.devices,) + late, f32)]
    return call_remote(
        functools.partial(backward_kernel, size),
        "mlp_backward",
        number,
        (
            struct(x.shape, bf16),
            struct(x.shape, bf16),
            struct((2,) + plane, f32),
            struct((2, 2, HALVES, blocks_shape[0] // 8, 2) + block, bf16),
            struct(early, f32),
            struct(late, f32),
        ),
        [pl.ANY] * len(large) + [pltpu.SMEM] + [pltpu.VMEM] * (len(vectors) + 1),
        [pl.ANY] * 2 + [pltpu.VMEM] * 4,
        3 * size.devices + 2 * size.groups + 2 * size.lon + 48,
        48,
        scratch,
        large + (row_map,) + vectors + (fc_in_bias,),
    )


def exchange_lon(values):
    return lax.all_to_all(values, "lon", split_axis=0, concat_axis=0, tiled=True)


def exchange_all(values):
    return lax.all_to_all(values, ("rows", "lon"), split_axis=0, concat_axis=0, tiled=True)


def to_modes(size, pieces, row_map):
    order, place = place_order(size)
    sent = jnp.tile(jnp.take(pieces, place, axis=0), (size.images, 1, 1))
    received = exchange_all(sent)
    used = size.slots_here * 2 * size.waves
    by_slot = received[:, :used].reshape(-1, 2 * size.waves, size.half)
    image = (lax.axis_index("rows") * size.lon + lax.axis_index("lon")) // size.per_image
    slots = row_map.shape[0]
    target = jnp.where(row_map >= 0, row_map, size.images * H)
    slot_of_row = (
        jnp.zeros((size.images * H,), jnp.int32)
        .at[target]
        .set(jnp.arange(slots, dtype=jnp.int32), mode="drop")
    )
    own = lax.dynamic_slice_in_dim(slot_of_row, image * H, H)
    picked = jnp.take(by_slot, own, axis=0)
    picked = jnp.pad(picked, ((0, size.virtual_slots - H), (0, 0), (0, 0)))
    picked = picked.reshape(size.per_image, used, size.half)
    return jnp.take(jnp.pad(picked, ((0, 0), (0, size.piece - used), (0, 0))), order, axis=0)


def from_modes(size, pieces, row_map):
    order, place = place_order(size)
    used = size.slots_here * 2 * size.waves
    by_lat = jnp.take(pieces, place, axis=0)[:, :used].reshape(-1, 2 * size.waves, size.half)
    image = (lax.axis_index("rows") * size.lon + lax.axis_index("lon")) // size.per_image
    live = (row_map >= 0) & (row_map // H == image)
    picked = jnp.take(by_lat, jnp.where(live, row_map % H, 0), axis=0)
    picked = picked * live.astype(bf16)[:, None, None]
    picked = picked.reshape(size.devices, used, size.half)
    sent = jnp.pad(picked, ((0, 0), (0, size.piece - used), (0, 0)))
    received = exchange_all(sent)
    received = received.reshape(size.images, size.per_image, size.piece, size.half)
    return jnp.take(jnp.sum(received.astype(f32), axis=0).astype(bf16), order, axis=0)


def body(
    tokens,
    row_map,
    cotangent,
    norm_gain,
    norm_shift,
    mix_in,
    mix_in_bias,
    mix_out,
    mix_out_bias,
    post_gain,
    post_shift,
    fc_in,
    fc_in_bias,
    fc_out,
    fc_out_bias,
):
    size = Sizes(
        lax.axis_size("rows"), lax.axis_size("lon"), row_map.shape[0], tokens.shape[2]
    )
    channels = size.channels
    blocks = mix_in.shape[1]
    blocks_here = blocks // HALVES
    block_size = mix_in.shape[2]
    hidden_units = fc_in.shape[1]
    device = lax.axis_index("rows") * size.lon + lax.axis_index("lon")
    half_index = (device % size.per_image) // size.groups

    table, table_t, inv, inv_t = [jnp.asarray(t) for t in lon_tables(size)]
    table = table.reshape(QUARTERS, size.spectrum // QUARTERS, size.tokens)
    cosine, sine, er, ec = [jnp.asarray(t) for t in lat_parts(size)]
    if size.images == 1:
        slot_lat = row_map
    else:
        slot_lat = jnp.where(jnp.arange(size.virtual_slots) < H, jnp.arange(size.virtual_slots), -1)
    rows = jnp.pad(slot_lat, (0, 128 - size.virtual_slots), constant_values=-1).reshape(1, 128)
    shape = (size.lon, size.slots_here, size.lons_here, channels)
    x, dy = tokens.reshape(shape), cotangent.reshape(shape)
    piece_shape = struct((size.per_image, size.piece, size.half), bf16)
    mode_shape = (size.modes, 2 * size.half)
    wide_modes = (2 * size.modes, size.half)
    mode_scratch = [pltpu.VMEM(wide_modes, f32), pltpu.VMEM(wide_modes, bf16)]
    if size.images == 1:
        x, dy, received, lat, lat_t, w1, w2, band, inner, gated, outer = run_forward(
            size, x, dy, table, er, ec, rows, norm_gain, norm_shift, cosine, sine, mix_in, mix_in_bias, mix_out, mix_out_bias, 0
        )
    else:
        square = struct((2 * size.half, 2 * size.half), bf16)
        flat = struct((1, 2 * size.half), f32)
        lat, lat_t, w1, w2, b1, b2 = call_local(
            functools.partial(prepare_kernel, size),
            "prepare",
            (
                struct((QUARTERS, 2 * size.modes, size.chunk_rows), bf16),
                struct((QUARTERS, size.chunk_rows, 2 * size.modes), bf16),
                square,
                square,
                flat,
                flat,
            ),
        )(rows, cosine, sine, er, ec, mix_in, mix_in_bias, mix_out, mix_out_bias)
        x, dy = exchange_lon(x), exchange_lon(dy)
        sent = call_local(
            functools.partial(first_kernel, size),
            "lon_forward",
            piece_shape,
            [pltpu.VMEM((size.tokens, channels), bf16)],
        )(x, norm_gain, norm_shift, table)
        received = to_modes(size, sent, row_map)
        sent, band, inner, gated, outer = call_local(
            functools.partial(mix_kernel, size),
            "mix_forward",
            (
                piece_shape,
                struct(mode_shape, bf16),
                struct(mode_shape, f32),
                struct(mode_shape, bf16),
                struct(mode_shape, f32),
            ),
            mode_scratch,
        )(received, lat, lat_t, w1, b1, w2, b2)
        received = from_modes(size, sent, row_map)
    vectors = (norm_gain, norm_shift, post_gain, post_shift, fc_out_bias)
    blocks_shape = (4 * blocks_here, round_up(block_size + 1, 16), block_size)
    bias_row = fc_in_bias.reshape(1, -1)
    if size.images == 1:
        token_grad, block, dense, mix_total, early, late = run_backward(
            size, blocks_shape, received, dy, inv_t, inv.reshape(table.shape), fc_in, fc_out, lat, lat_t, w1, w2, band, inner, gated, outer, x, table_t, row_map, vectors, bias_row, 1
        )
    else:
        names = ("rows", "lon")
        block, dh, sent, hidden, hidden_grad, low, up, early = run_mlp(
            size, hidden_units, row_map, received, x, dy, inv_t, inv, vectors, fc_in, bias_row, fc_out
        )
        early = lax.psum(early, names)
        wide = call_local(
            wide_kernel, "weights_backward", struct((hidden_units, 2 * channels), bf16)
        )(hidden, hidden_grad, low, up)
        dense = lax.psum_scatter(wide, names, scatter_dimension=0, tiled=True)
        dense = jnp.stack([dense[:, :channels], dense[:, channels:]]).astype(f32)
        block = exchange_lon(block)
        received = to_modes(size, sent, row_map)
        sent, mix_grad = call_local(
            functools.partial(mix_back_kernel, size),
            "mix_backward",
            (piece_shape, struct(blocks_shape, bf16)),
            [pltpu.VMEM(mode_shape, bf16)] * 2 + mode_scratch,
        )(received, lat, lat_t, w1, w2, band, inner, gated, outer)
        mix_grad = mix_grad.astype(f32).reshape((2, 2, 1, blocks_here) + blocks_shape[1:])
        mix_total = lax.psum(
            jnp.concatenate(
                [mix_grad * (half_index == other).astype(f32) for other in range(HALVES)], axis=2
            ),
            names,
        )
        received = from_modes(size, sent, row_map)
        token_grad, late = call_local(
            functools.partial(last_kernel, size),
            "lon_backward",
            (struct(x.shape, bf16), struct((2, channels), f32)),
        )(received, x, dh, table_t, norm_gain)
        token_grad = exchange_lon(token_grad)
        late = lax.psum(late, names)
    mix_total = mix_total.reshape((2, 2, blocks) + blocks_shape[1:]).astype(f32)
    mix_bias = mix_total[:, :, :, block_size]
    mix_total = mix_total[:, :, :, :block_size]
    share = hidden_units // size.devices
    return (
        block.reshape(tokens.shape),
        token_grad.reshape(tokens.shape).astype(f32),
        late[0],
        late[1],
        mix_total[0],
        mix_bias[0],
        mix_total[1],
        mix_bias[1],
        early[1],
        early[2],
        dense[0].T,
        lax.dynamic_slice_in_dim(early[3:7].reshape(-1), device * share, share),
        dense[1],
        early[0],
    )


def solution(mesh):
    return jax.shard_map(
        body,
        mesh=mesh,
        in_specs=(P("rows", "lon", None), P(), P("rows", "lon", None)) + (P(),) * 12,
        out_specs=(
            P("rows", "lon", None),
            P("rows", "lon", None),
            P(),
            P(),
            P(),
            P(),
            P(),
            P(),
            P(),
            P(),
            P(None, ("rows", "lon")),
            P(("rows", "lon")),
            P(("rows", "lon"), None),
            P(),
        ),
        check_vma=False,
    )
```

```python
import functools
import math

import jax
import jax.numpy as jnp
import ml_dtypes
import numpy as np
from jax import lax
from jax.experimental import pallas as pl
from jax.experimental.pallas import tpu as pltpu
from jax.sharding import PartitionSpec as P

H = 90
W = 180
KX = 91
HALVES = 2
QUARTERS = 4
VMEM_BYTES = 58 * 1024 * 1024

norm_eps = 1e-06
shrink_level = 0.01
half_root = 0.7071067811865476
normal_peak = 0.3989422804014327
MESH = pl.DeviceIdType.MESH
f32 = jnp.float32
bf16 = jnp.bfloat16


def round_up(value, step):
    return -(-value // step) * step


class Sizes:
    def __init__(self, rows_count, lon_count, slots, channels):
        self.rows = rows_count
        self.lon = lon_count
        self.devices = rows_count * lon_count
        self.images = slots * 15 // (16 * H)
        self.per_image = self.devices // self.images
        self.groups = self.per_image // HALVES
        self.waves = -(-KX // self.groups)
        self.slots_here = slots // self.devices
        self.lons_here = W // lon_count
        self.lons_pad = round_up(self.lons_here, 16)
        self.tokens = lon_count * self.slots_here * self.lons_pad
        self.piece = round_up(self.slots_here * 2 * self.waves, 8)
        self.spectrum = self.groups * self.piece
        self.band = self.per_image * self.piece
        self.modes = round_up(H * self.waves, 16)
        self.virtual_slots = self.per_image * self.slots_here
        self.chunk = self.per_image // QUARTERS
        self.chunk_rows = self.chunk * self.piece
        self.channels = channels
        self.half = channels // HALVES


def place_of(size, row, lon):
    return (row % QUARTERS) * size.chunk + (row // QUARTERS) * size.lon + lon


def place_order(size):
    place = np.array([place_of(size, d // size.lon, d % size.lon) for d in range(size.per_image)])
    return np.argsort(place), place


def lon_tables(size):
    wave = np.arange(size.groups * size.waves)
    lon_index = np.arange(W)
    product = (lon_index[:, None] * wave[None, :]) % W
    angle = product.astype(np.float32) * np.float32(2.0 * math.pi / W)
    scale = np.float32(1.0 / math.sqrt(W))
    cosine = (np.cos(angle) * scale).astype(ml_dtypes.bfloat16).astype(np.float32)
    sine = (-np.sin(angle) * scale).astype(ml_dtypes.bfloat16).astype(np.float32)
    live = (wave < KX).astype(np.float32)
    factor = np.where((wave == 0) | (wave == W // 2), 1.0, 2.0).astype(np.float32)
    both = np.stack([cosine, sine]) * live
    result = []
    for weight in (np.ones_like(factor), factor):
        table = np.zeros(
            (
                size.groups,
                size.piece,
                size.lon,
                size.slots_here,
                size.lons_pad,
            ),
            np.float32,
        )
        values = (both * weight).reshape(2, size.lon, size.lons_here, size.groups, size.waves)
        values = np.transpose(values, (3, 0, 4, 1, 2)).reshape(
            size.groups, 2 * size.waves, size.lon, size.lons_here
        )
        for slot in range(size.slots_here):
            start = slot * 2 * size.waves
            table[:, start : start + 2 * size.waves, :, slot, : size.lons_here] = values
        flat = table.reshape(size.spectrum, size.tokens).astype(ml_dtypes.bfloat16)
        result.append(flat)
        result.append(np.ascontiguousarray(flat.T))
    return result


def lat_parts(size):
    lat_index = np.arange(H)
    angle = ((lat_index[:, None] * lat_index[None, :]) % H).astype(np.float32) * np.float32(
        2.0 * math.pi / H
    )
    scale = np.float32(1.0 / math.sqrt(H))
    cosine = np.zeros((96, 96), np.float32)
    sine = np.zeros((96, 96), np.float32)
    cosine[:H, :H] = np.cos(angle) * scale
    sine[:H, :H] = np.sin(angle) * scale
    spread_rows = np.zeros((2, size.modes, 2, 96), np.float32)
    for part in range(2):
        for lat in range(H):
            for wave in range(size.waves):
                spread_rows[part, lat * size.waves + wave, part, lat] = 1.0
    spread_cols = np.zeros((QUARTERS, 2, 128, size.chunk, size.piece), np.float32)
    for place, device in enumerate(place_order(size)[0]):
        for slot in range(size.slots_here):
            for part in range(2):
                for wave in range(size.waves):
                    spread_cols[
                        place // size.chunk,
                        part,
                        device * size.slots_here + slot,
                        place % size.chunk,
                        (slot * 2 + part) * size.waves + wave,
                    ] = 1.0
    low = ml_dtypes.bfloat16
    return (
        cosine.astype(low),
        sine.astype(low),
        spread_rows.reshape(2 * size.modes, 192).astype(low),
        spread_cols.reshape(QUARTERS, 256, size.chunk_rows).astype(low),
    )


def smooth_gate(values):
    return 0.5 * values * (1.0 + lax.erf(values * half_root))


def gate_both(values):
    half_phi = 0.5 * (1.0 + lax.erf(values * half_root))
    density = values * normal_peak * jnp.exp(-0.5 * values * values)
    return values * half_phi, half_phi + density


def gate_slope(values):
    return gate_both(values)[1]


def soft_shrink(values):
    return values - shrink_level * values * lax.rsqrt(values * values + shrink_level * shrink_level)


def shrink_slope(values):
    inverse = lax.rsqrt(values * values + shrink_level * shrink_level)
    return 1.0 - shrink_level * shrink_level * shrink_level * inverse * inverse * inverse


def norm_parts(values):
    center = values - jnp.mean(values, axis=-1, keepdims=True)
    spread = lax.rsqrt(jnp.mean(center * center, axis=-1, keepdims=True) + norm_eps)
    return center * spread, spread


def norm_back(scaled, unit, spread):
    return spread * (
        scaled
        - jnp.mean(scaled, axis=-1, keepdims=True)
        - unit * jnp.mean(scaled * unit, axis=-1, keepdims=True)
    )


def mm(left, right):
    return jnp.dot(left, right, preferred_element_type=f32)


def mm_t(left, right):
    return lax.dot_general(left, right, (((1,), (1,)), ((), ())), preferred_element_type=f32)


def t_mm(left, right):
    return lax.dot_general(left, right, (((0,), (0,)), ((), ())), preferred_element_type=f32)


def whole(count):
    return [pl.BlockSpec(memory_space=pltpu.VMEM)] * count


def call_local(kernel, name, outs, scratch=()):
    def run(*operands):
        return pl.pallas_call(
            kernel,
            out_shape=outs,
            in_specs=whole(len(operands)),
            out_specs=jax.tree.map(lambda _: pl.BlockSpec(memory_space=pltpu.VMEM), outs),
            scratch_shapes=list(scratch),
            compiler_params=pltpu.CompilerParams(vmem_limit_bytes=VMEM_BYTES),
            name=name,
        )(*operands)

    return run


def struct(shape, dtype):
    return jax.ShapeDtypeStruct(shape, dtype)


def wave_of(index, period, used, waves, other):
    within = index - period * jnp.floor((index + 0.5) * (1.0 / period))
    wave = within - waves * jnp.floor((within + 0.5) * (1.0 / waves))
    return jnp.where(within < used, wave, other)


def build_lat_tables(size, rows_ref, cos_ref, sin_ref, er_ref, ec_ref, lat_ref, lat_t_ref):
    lat_of = lax.broadcasted_iota(jnp.int32, (96, 128), 0)
    hot = (lat_of == rows_ref[...]).astype(f32).astype(bf16)
    cosine = mm(cos_ref[...], hot)
    sine = mm(sin_ref[...], hot)
    top = jnp.concatenate([cosine, sine], axis=1)
    bottom = jnp.concatenate([-sine, cosine], axis=1)
    base = jnp.concatenate([top, bottom], axis=0).astype(bf16)

    def row_waves(shape, dim):
        index = lax.broadcasted_iota(jnp.int32, shape, dim).astype(f32)
        return wave_of(index, size.modes, H * size.waves, size.waves, -1.0)

    def col_waves(shape, dim):
        index = lax.broadcasted_iota(jnp.int32, shape, dim).astype(f32)
        return wave_of(index, size.piece, size.slots_here * 2 * size.waves, size.waves, -2.0)

    modes, columns_here = 2 * size.modes, size.chunk_rows
    keep = row_waves((modes, 1), 0) == col_waves((1, columns_here), 1)
    keep_t = col_waves((columns_here, 1), 0) == row_waves((1, modes), 1)

    def build(quarter):
        columns = mm(base, ec_ref[quarter]).astype(bf16)
        table = mm(er_ref[...], columns)
        lat_ref[quarter] = jnp.where(keep, table, 0.0).astype(bf16)
        table_t = lax.dot_general(
            columns, er_ref[...], (((0,), (1,)), ((), ())), preferred_element_type=f32
        )
        lat_t_ref[quarter] = jnp.where(keep_t, table_t, 0.0).astype(bf16)

    over_quarters(build)


def build_block_matrix(size, weight_ref, bias_ref, half, matrix_ref, row_ref):
    block_size = weight_ref.shape[2]
    blocks = size.half // block_size
    matrix_ref[...] = jnp.zeros_like(matrix_ref)
    for block in range(blocks):
        real = weight_ref[0, half * blocks + block]
        imag = weight_ref[1, half * blocks + block]
        near = slice(block * block_size, (block + 1) * block_size)
        far = slice(size.half + block * block_size, size.half + (block + 1) * block_size)
        matrix_ref[near, near] = real
        matrix_ref[near, far] = imag
        matrix_ref[far, near] = -imag
        matrix_ref[far, far] = real
        row_ref[0:1, near] = bias_ref[0, pl.ds(half * blocks + block, 1), :]
        row_ref[0:1, far] = bias_ref[1, pl.ds(half * blocks + block, 1), :]


def prepare_kernel(size, rows_ref, cos_ref, sin_ref, er_ref, ec_ref, mix_in_ref, bias_in_ref, mix_out_ref, bias_out_ref, lat_ref, lat_t_ref, w1_ref, w2_ref, b1_ref, b2_ref):
    half = half_of(size)
    build_lat_tables(size, rows_ref, cos_ref, sin_ref, er_ref, ec_ref, lat_ref, lat_t_ref)
    build_block_matrix(size, mix_in_ref, bias_in_ref, half, w1_ref, b1_ref)
    build_block_matrix(size, mix_out_ref, bias_out_ref, half, w2_ref, b2_ref)


def half_of(size):
    device = lax.axis_index("rows") * size.lon + lax.axis_index("lon")
    return (device % size.per_image) // size.groups


def pad_plane(size, plane):
    extra = size.lons_pad - size.lons_here
    return jnp.concatenate([plane, jnp.zeros((extra, plane.shape[1]), plane.dtype)], axis=0)


def over_planes(size, body, *sums):
    def step(source, sums):
        for slot in range(size.slots_here):
            start = pl.multiple_of(
                (source * size.slots_here + slot) * size.lons_pad, size.lons_pad
            )
            sums = body(source, slot, pl.ds(start, size.lons_pad), *sums)
        return sums

    return lax.fori_loop(0, size.lon, step, sums)


def over_quarters(body):
    @pl.loop(0, QUARTERS)
    def _(step):
        body(step)


def at(step, count, action):
    for i in range(count):

        @pl.when(step == i)
        def _():
            action(i)


def write_quarter(size, quarter, values, out_ref):
    for half in range(HALVES):
        for lon in range(size.lon):
            out_ref[quarter * size.chunk + half * size.lon + lon] = values[
                lon * size.piece : (lon + 1) * size.piece,
                half * size.half : (half + 1) * size.half,
            ].astype(bf16)


def write_pieces(size, values, out_ref):
    rows = size.lon * size.piece
    for quarter in range(QUARTERS):
        write_quarter(size, quarter, values[quarter * rows : (quarter + 1) * rows], out_ref)


def read_pieces(ref, places):
    return jnp.concatenate([ref[place].astype(f32) for place in places], axis=0).astype(bf16)


def read_spectrum(size, ref):
    return jnp.concatenate(
        [
            read_pieces(
                ref,
                [
                    quarter * size.chunk + half * size.lon + lon
                    for quarter in range(QUARTERS)
                    for lon in range(size.lon)
                ],
            )
            for half in range(HALVES)
        ],
        axis=1,
    )


def first_norm(size, x_ref, gain, shift, low_ref):
    def plane(source, slot, rows):
        x = pad_plane(size, x_ref[source, slot].astype(f32))
        unit, _ = norm_parts(x)
        low_ref[rows, :] = (unit * gain + shift).astype(bf16)
        return ()

    over_planes(size, plane)


def as_row(ref):
    return ref[...].reshape(1, -1)


def first_kernel(size, x_ref, gain_ref, shift_ref, table_ref, send_ref, low_ref):
    first_norm(size, x_ref, as_row(gain_ref), as_row(shift_ref), low_ref)
    over_quarters(lambda i: write_quarter(size, i, mm(table_ref[i], low_ref[...]), send_ref))


def add_modes(size, quarter, recv_ref, lat_ref, modes_ref):
    spectrum = read_pieces(recv_ref, [quarter * size.chunk + i for i in range(size.chunk)])
    modes_ref[...] += mm(lat_ref[quarter], spectrum)


def side_by_side(size, modes_ref):
    return jnp.concatenate(
        [modes_ref[: size.modes, :], modes_ref[size.modes :, :]], axis=1
    ).astype(bf16)


def stack_parts(size, values, stacked_ref):
    stacked_ref[: size.modes, :] = values[:, : size.half].astype(bf16)
    stacked_ref[size.modes :, :] = values[:, size.half :].astype(bf16)


def mix_quarter_back(size, quarter, lat_t_ref, stacked_ref, send_ref):
    back = mm(lat_t_ref[quarter], stacked_ref[...])
    for i in range(size.chunk):
        send_ref[quarter * size.chunk + i] = back[i * size.piece : (i + 1) * size.piece].astype(bf16)


def mix_layers(size, modes_ref, w1_ref, b1_ref, w2_ref, b2_ref, band_ref, inner_ref, gated_ref, outer_ref, stacked_ref):
    band = side_by_side(size, modes_ref)
    band_ref[...] = band
    inner = mm(band, w1_ref[...]) + b1_ref[...]
    inner_ref[...] = inner
    gated = smooth_gate(inner).astype(bf16)
    gated_ref[...] = gated
    outer = mm(gated, w2_ref[...]) + b2_ref[...]
    outer_ref[...] = outer
    stack_parts(size, soft_shrink(outer), stacked_ref)


def mix_kernel(size, recv_ref, lat_ref, lat_t_ref, w1_ref, b1_ref, w2_ref, b2_ref, send_ref, band_ref, inner_ref, gated_ref, outer_ref, modes_ref, stacked_ref):
    modes_ref[...] = jnp.zeros_like(modes_ref)
    over_quarters(lambda i: add_modes(size, i, recv_ref, lat_ref, modes_ref))
    mix_layers(size, modes_ref, w1_ref, b1_ref, w2_ref, b2_ref, band_ref, inner_ref, gated_ref, outer_ref, stacked_ref)
    over_quarters(lambda i: mix_quarter_back(size, i, lat_t_ref, stacked_ref, send_ref))


def mix_layers_back(size, modes_ref, w1_ref, w2_ref, inner_ref, outer_ref, outer_grad_ref, inner_grad_ref, stacked_ref):
    upstream = side_by_side(size, modes_ref)
    outer_grad = (upstream.astype(f32) * shrink_slope(outer_ref[...])).astype(bf16)
    outer_grad_ref[...] = outer_grad
    inner_grad = (mm_t(outer_grad, w2_ref[...]) * gate_slope(inner_ref[...])).astype(bf16)
    inner_grad_ref[...] = inner_grad
    stack_parts(size, mm_t(inner_grad, w1_ref[...]), stacked_ref)


def mix_back_weights(size, band_ref, gated_ref, outer_grad_ref, inner_grad_ref, out_ref):
    half = size.half
    block_size = out_ref.shape[-1]
    blocks = half // block_size
    rest = out_ref.shape[-2] - block_size
    for layer, (value_ref, grad_ref) in enumerate(
        ((band_ref, inner_grad_ref), (gated_ref, outer_grad_ref))
    ):
        grad = grad_ref[...]
        total = t_mm(value_ref[...], grad)
        bias = jnp.sum(grad.astype(f32), axis=0, keepdims=True)
        for block in range(blocks):
            near = slice(block * block_size, (block + 1) * block_size)
            far = slice(half + block * block_size, half + (block + 1) * block_size)
            for part, values, row in (
                (0, total[near, near] + total[far, far], bias[:, near]),
                (1, total[near, far] - total[far, near], bias[:, far]),
            ):
                place = (layer * 2 + part) * blocks + block
                at = (place // 2, place % 2) if len(out_ref.shape) == 4 else (place,)
                out_ref[at + (slice(0, block_size),)] = values.astype(bf16)
                out_ref[at + (slice(block_size, None),)] = jnp.broadcast_to(
                    row, (rest, block_size)
                ).astype(bf16)


def mix_back_kernel(size, recv_ref, lat_ref, lat_t_ref, w1_ref, w2_ref, band_ref, inner_ref, gated_ref, outer_ref, send_ref, grad_ref, outer_grad_ref, inner_grad_ref, modes_ref, stacked_ref):
    modes_ref[...] = jnp.zeros_like(modes_ref)
    over_quarters(lambda i: add_modes(size, i, recv_ref, lat_ref, modes_ref))
    mix_layers_back(size, modes_ref, w1_ref, w2_ref, inner_ref, outer_ref, outer_grad_ref, inner_grad_ref, stacked_ref)
    over_quarters(lambda i: mix_quarter_back(size, i, lat_t_ref, stacked_ref, send_ref))
    mix_back_weights(size, band_ref, gated_ref, outer_grad_ref, inner_grad_ref, grad_ref)


def residual_planes(size, map_ref, recv_ref, x_ref, dy_ref, inv_t_ref, gain1, shift1, gain2, shift2, res_ref, low_ref, up_ref):
    first_slot = (lax.axis_index("rows") * size.lon + lax.axis_index("lon")) * size.slots_here
    res_ref[...] = mm(inv_t_ref[...], read_spectrum(size, recv_ref))

    def plane(source, slot, rows, up_sum):
        x = pad_plane(size, x_ref[source, slot].astype(f32))
        unit, _ = norm_parts(x)
        residual = res_ref[rows, :] + (unit * gain1 + shift1) + x
        res_ref[rows, :] = residual
        unit, _ = norm_parts(residual)
        low_ref[rows, :] = (unit * gain2 + shift2).astype(bf16)
        live = jnp.where(map_ref[first_slot + slot] >= 0, 1.0, 0.0)
        up = pad_plane(size, dy_ref[source, slot].astype(f32) * live)
        up_ref[rows, :] = up.astype(bf16)
        return (up_sum + jnp.sum(up, axis=0, keepdims=True),)

    return over_planes(size, plane, jnp.zeros((1, size.channels), f32))[0]


def hidden_part(low_ref, up_ref, fc_in, bias, fc_out, acc_ref, back_ref):
    gate, slope = gate_both(mm(low_ref[...], fc_in) + bias)
    hidden = gate.astype(bf16)
    acc_ref[...] += mm(hidden, fc_out)
    hidden_grad = (mm_t(up_ref[...], fc_out) * slope).astype(bf16)
    back_ref[...] += mm_t(hidden_grad, fc_in)
    return hidden, hidden_grad


def residual_back_planes(size, up_ref, res_ref, gain2, back_ref, grad_ref):
    def plane(source, slot, rows, gain_sum, shift_sum):
        unit, spread = norm_parts(res_ref[rows, :])
        grad = back_ref[rows, :]
        gain_sum = gain_sum + jnp.sum(grad * unit, axis=0, keepdims=True)
        shift_sum = shift_sum + jnp.sum(grad, axis=0, keepdims=True)
        grad = up_ref[rows, :].astype(f32) + norm_back(grad * gain2, unit, spread)
        back_ref[rows, :] = grad
        grad_ref[rows, :] = grad.astype(bf16)
        return gain_sum, shift_sum

    zero = jnp.zeros((1, size.channels), f32)
    return over_planes(size, plane, zero, zero)


def block_planes(size, map_ref, res_ref, acc_ref, out_bias, block_ref):
    first_slot = (lax.axis_index("rows") * size.lon + lax.axis_index("lon")) * size.slots_here

    def plane(source, slot, rows):
        live = jnp.where(map_ref[first_slot + slot] >= 0, 1.0, 0.0)
        block = (res_ref[rows, :] + (acc_ref[rows, :] + out_bias)) * live
        block_ref[source, slot] = block[: size.lons_here].astype(bf16)
        return ()

    over_planes(size, plane)


def mlp_kernel(
    size,
    map_ref,
    recv_ref,
    x_ref,
    dy_ref,
    inv_t_ref,
    inv_ref,
    gain1_ref,
    shift1_ref,
    gain2_ref,
    shift2_ref,
    out_bias_ref,
    fc_in_ref,
    fc_in_bias_ref,
    fc_out_ref,
    block_ref,
    dh_ref,
    send_ref,
    hidden_ref,
    hidden_grad_ref,
    low_ref,
    up_ref,
    small_ref,
    res_ref,
    grad_ref,
    acc_ref,
):
    step = pl.program_id(0)

    @pl.when(step == 0)
    def _():
        small_ref[...] = jnp.zeros_like(small_ref)
        small_ref[0:1, :] = residual_planes(
            size, map_ref, recv_ref, x_ref, dy_ref, inv_t_ref, as_row(gain1_ref), as_row(shift1_ref), as_row(gain2_ref), as_row(shift2_ref), res_ref, low_ref, up_ref
        )
        acc_ref[...] = jnp.zeros_like(acc_ref)
        dh_ref[...] = jnp.zeros_like(dh_ref)

    hidden, hidden_grad = hidden_part(
        low_ref, up_ref, fc_in_ref[...], fc_in_bias_ref[...], fc_out_ref[...], acc_ref, dh_ref
    )
    small_ref[pl.ds(3 + step, 1), :] = jnp.sum(hidden_grad.astype(f32), axis=0, keepdims=True)
    hidden_ref[...] = hidden
    hidden_grad_ref[...] = hidden_grad

    @pl.when(step == pl.num_programs(0) - 1)
    def _():
        block_planes(size, map_ref, res_ref, acc_ref, as_row(out_bias_ref), block_ref)
        gain_sum, shift_sum = residual_back_planes(size, up_ref, res_ref, as_row(gain2_ref), dh_ref, grad_ref)
        small_ref[1:2, :] = gain_sum
        small_ref[2:3, :] = shift_sum
        write_pieces(size, mm(inv_ref[...], grad_ref[...]), send_ref)


def wide_kernel(hidden_ref, hidden_grad_ref, low_ref, up_ref, wide_ref):
    channels = low_ref.shape[1]
    for part in range(hidden_ref.shape[0]):
        rows = slice(part * channels, (part + 1) * channels)
        wide_ref[rows, :channels] = t_mm(hidden_grad_ref[part], low_ref[...]).astype(bf16)
        wide_ref[rows, channels:] = t_mm(hidden_ref[part], up_ref[...]).astype(bf16)


def run_mlp(size, hidden_units, row_map, recv, x, dy, inv_t, inv, vectors, fc_in, fc_in_bias, fc_out):
    channels = size.channels
    width = channels
    parts = hidden_units // width
    fixed = pl.BlockSpec(memory_space=pltpu.VMEM)
    tokens = (size.tokens, channels)
    return pl.pallas_call(
        functools.partial(mlp_kernel, size),
        grid=(parts,),
        in_specs=[pl.BlockSpec(memory_space=pltpu.SMEM)]
        + [fixed] * (5 + len(vectors))
        + [
            pl.BlockSpec((channels, width), lambda i: (0, i)),
            pl.BlockSpec((1, width), lambda i: (0, i)),
            pl.BlockSpec((width, channels), lambda i: (i, 0)),
        ],
        out_specs=(
            fixed,
            fixed,
            fixed,
            pl.BlockSpec((None, size.tokens, width), lambda i: (i, 0, 0)),
            pl.BlockSpec((None, size.tokens, width), lambda i: (i, 0, 0)),
            fixed,
            fixed,
            fixed,
        ),
        out_shape=(
            struct(x.shape, bf16),
            struct(tokens, f32),
            struct((size.per_image, size.piece, size.half), bf16),
            struct((parts,) + tokens, bf16),
            struct((parts,) + tokens, bf16),
            struct(tokens, bf16),
            struct(tokens, bf16),
            struct((round_up(3 + parts, 8), channels), f32),
        ),
        scratch_shapes=[
            pltpu.VMEM(tokens, f32),
            pltpu.VMEM(tokens, bf16),
            pltpu.VMEM(tokens, f32),
        ],
        compiler_params=pltpu.CompilerParams(vmem_limit_bytes=VMEM_BYTES),
        name="mlp",
    )(row_map, recv, x, dy, inv_t, inv, *vectors, fc_in, fc_in_bias, fc_out)


def last_planes(size, recv_ref, x_ref, dh_ref, table_t_ref, gain_ref, filtered_ref, out_ref, small_ref):
    gain = as_row(gain_ref)
    filtered_ref[...] = mm(table_t_ref[...], read_spectrum(size, recv_ref))

    def plane(source, slot, rows, gain_sum, shift_sum):
        unit, spread = norm_parts(pad_plane(size, x_ref[source, slot].astype(f32)))
        base = dh_ref[rows, :]
        grad = base + filtered_ref[rows, :]
        gain_sum = gain_sum + jnp.sum(grad * unit, axis=0, keepdims=True)
        shift_sum = shift_sum + jnp.sum(grad, axis=0, keepdims=True)
        grad = base + norm_back(grad * gain, unit, spread)
        out_ref[source, slot] = grad[: size.lons_here].astype(bf16)
        return gain_sum, shift_sum

    zero = jnp.zeros((1, size.channels), f32)
    small_ref[0:1, :], small_ref[1:2, :] = over_planes(size, plane, zero, zero)


def last_kernel(size, recv_ref, x_ref, dh_ref, table_t_ref, gain_ref, out_ref, small_ref, filtered_ref):
    last_planes(size, recv_ref, x_ref, dh_ref, table_t_ref, gain_ref, filtered_ref, out_ref, small_ref)


def partners(lon_count):
    row = lax.axis_index("rows")
    lon = lax.axis_index("lon")
    core = {"rows": row, "lon": lon + 1 - 2 * (lon % 2)}
    along_y = {"rows": row, "lon": (lon + 2) % 4}
    along_x = {"rows": row + 1 - 2 * (row % 2), "lon": lon}
    far_z = {"rows": (row + 4) % 8, "lon": lon}
    return core, along_y, along_x, far_z


def greet(lon_count, count):
    row = lax.axis_index("rows")
    lon = lax.axis_index("lon")
    me = row * lon_count + lon
    barrier = pltpu.get_barrier_semaphore()
    for offset in range(1, count):
        other = (me + offset) % count
        pl.semaphore_signal(
            barrier,
            inc=1,
            device_id={"rows": other // lon_count, "lon": other % lon_count},
            device_id_type=MESH,
        )
    pl.semaphore_wait(barrier, count - 1)


class Sender:
    def __init__(self, send_sem, recv_sem):
        self.send_sem = send_sem
        self.recv_sem = recv_sem
        self.used = 0

    def make(self, source, target, device):
        copy = pltpu.make_async_remote_copy(
            src_ref=source,
            dst_ref=target,
            send_sem=self.send_sem.at[self.used],
            recv_sem=self.recv_sem.at[self.used],
            device_id=device,
            device_id_type=MESH,
        )
        self.used += 1
        return copy

    def start(self, source, target, device):
        copy = self.make(source, target, device)
        copy.start()
        return copy


class Mover:
    def __init__(self, sem):
        self.sem = sem
        self.used = 0

    def make(self, source, target):
        copy = pltpu.make_async_copy(source, target, self.sem.at[self.used])
        self.used += 1
        return copy

    def start(self, source, target):
        copy = self.make(source, target)
        copy.start()
        return copy


def make_quarter(size, step, source_ref, out_ref, sender, mover):
    row = lax.axis_index("rows")
    lon = lax.axis_index("lon")
    me = place_of(size, row, lon)
    copies = []
    for half_step in range(HALVES):
        for lon_step in range(size.lon):
            to_row = (row + step) % QUARTERS + (row // QUARTERS + half_step) % HALVES * QUARTERS
            to_lon = (lon + lon_step) % size.lon
            piece = source_ref.at[place_of(size, to_row, to_lon)]
            if step == 0 and half_step == 0 and lon_step == 0:
                copies.append(mover.make(piece, out_ref.at[me]))
            else:
                copies.append(
                    sender.make(piece, out_ref.at[me], {"rows": to_row, "lon": to_lon})
                )
    return copies


def start_quarter(size, step, source_ref, out_ref, sender, mover):
    return begin(make_quarter(size, step, source_ref, out_ref, sender, mover))


def make_lon(source_ref, out_ref, sender, mover):
    row = lax.axis_index("rows")
    me = lax.axis_index("lon")
    count = source_ref.shape[0]
    copies = []
    for offset in range(1, count):
        other = (me + offset) % count
        copies.append(
            sender.make(source_ref.at[other], out_ref.at[me], {"rows": row, "lon": other})
        )
    copies.append(mover.make(source_ref.at[me], out_ref.at[me]))
    return copies


def start_lon(source_ref, out_ref, sender, mover):
    return begin(make_lon(source_ref, out_ref, sender, mover))


def begin(copies):
    for copy in copies:
        copy.start()
    return copies


def finish(copies):
    for copy in copies:
        copy.wait()


def call_remote(kernel, name, number, outs, spaces, out_spaces, sends, moves, scratch, operands):
    return pl.pallas_call(
        kernel,
        out_shape=outs,
        in_specs=[pl.BlockSpec(memory_space=space) for space in spaces],
        out_specs=tuple(pl.BlockSpec(memory_space=space) for space in out_spaces),
        scratch_shapes=[
            pltpu.SemaphoreType.DMA((sends,)),
            pltpu.SemaphoreType.DMA((sends,)),
            pltpu.SemaphoreType.DMA((moves,)),
        ]
        + list(scratch),
        compiler_params=pltpu.CompilerParams(
            collective_id=number, has_side_effects=True, vmem_limit_bytes=VMEM_BYTES
        ),
        name=name,
    )(*operands)


def forward_kernel(
    size,
    tokens_hbm,
    cot_hbm,
    table_hbm,
    er_hbm,
    ec_hbm,
    rows_ref,
    gain_ref,
    shift_ref,
    cos_ref,
    sin_ref,
    mix_in_ref,
    bias_in_ref,
    mix_out_ref,
    bias_out_ref,
    x_out,
    dy_out,
    recv_out,
    lat_out,
    lat_t_out,
    w1_out,
    w2_out,
    band_out,
    inner_out,
    gated_out,
    outer_out,
    send_sem,
    recv_sem,
    move_sem,
    x_ref,
    table_ref,
    er_ref,
    ec_ref,
    lat_ref,
    lat_t_ref,
    w1_ref,
    w2_ref,
    band_ref,
    inner_ref,
    gated_ref,
    outer_ref,
    b1_ref,
    b2_ref,
    low_ref,
    send1,
    recv1,
    send2,
    modes_ref,
    stacked_ref,
):
    sender, mover = Sender(send_sem, recv_sem), Mover(move_sem)
    mine = lax.axis_index("rows") % QUARTERS
    half = half_of(size)
    load = mover.start(table_hbm, table_ref)
    loads = [mover.start(er_hbm, er_ref), mover.start(ec_hbm, ec_ref)]
    greet(size.lon, size.devices)
    tokens = start_lon(tokens_hbm, x_ref, sender, mover)
    build_block_matrix(size, mix_in_ref, bias_in_ref, half, w1_ref, b1_ref)
    build_block_matrix(size, mix_out_ref, bias_out_ref, half, w2_ref, b2_ref)
    stores = [mover.start(w1_ref, w1_out), mover.start(w2_ref, w2_out)]
    finish(tokens)
    stores.append(mover.start(x_ref, x_out))
    first_norm(size, x_ref, as_row(gain_ref), as_row(shift_ref), low_ref)
    load.wait()
    steps = [make_quarter(size, i, send1, recv1, sender, mover) for i in range(QUARTERS)]

    def send_first(step):
        quarter = (mine + step) % QUARTERS
        write_quarter(size, quarter, mm(table_ref[quarter], low_ref[...]), send1)
        at(step, QUARTERS, lambda i: begin(steps[i]))

    over_quarters(send_first)
    cotangents = start_lon(cot_hbm, dy_out, sender, mover)
    finish(loads)
    build_lat_tables(size, rows_ref, cos_ref, sin_ref, er_ref, ec_ref, lat_ref, lat_t_ref)
    stores += [mover.start(lat_ref, lat_out), mover.start(lat_t_ref, lat_t_out)]
    modes_ref[...] = jnp.zeros_like(modes_ref)

    def receive(step):
        at(step, QUARTERS, lambda i: finish(steps[i]))
        add_modes(size, (mine + QUARTERS - step) % QUARTERS, recv1, lat_ref, modes_ref)

    over_quarters(receive)
    mix_layers(size, modes_ref, w1_ref, b1_ref, w2_ref, b2_ref, band_ref, inner_ref, gated_ref, outer_ref, stacked_ref)
    back_steps = [make_quarter(size, i, send2, recv_out, sender, mover) for i in range(QUARTERS)]

    def send_back(step):
        mix_quarter_back(size, (mine + step) % QUARTERS, lat_t_ref, stacked_ref, send2)
        at(step, QUARTERS, lambda i: begin(back_steps[i]))

    over_quarters(send_back)
    stores += [
        mover.start(band_ref, band_out),
        mover.start(inner_ref, inner_out),
        mover.start(gated_ref, gated_out),
        mover.start(outer_ref, outer_out),
    ]
    finish(cotangents)
    finish(stores)
    for copies in back_steps:
        finish(copies)


def run_forward(size, tokens, cotangent, table, er, ec, rows, gain, shift, cosine, sine, mix_in, mix_in_bias, mix_out, mix_out_bias, number):
    piece = struct((size.per_image, size.piece, size.half), bf16)
    modes = (size.modes, 2 * size.half)
    square = struct((2 * size.half, 2 * size.half), bf16)
    kept = (
        struct((QUARTERS, 2 * size.modes, size.chunk_rows), bf16),
        struct((QUARTERS, size.chunk_rows, 2 * size.modes), bf16),
        square,
        square,
        struct(modes, bf16),
        struct(modes, f32),
        struct(modes, bf16),
        struct(modes, f32),
    )
    row = struct((1, 2 * size.half), f32)
    scratch = (
        (struct(tokens.shape, bf16), table, er, ec)
        + kept
        + (row, row, struct((size.tokens, size.channels), bf16), piece, piece, piece)
        + (struct((2 * size.modes, size.half), f32), struct((2 * size.modes, size.half), bf16))
    )
    small = (rows, gain, shift, cosine, sine, mix_in, mix_in_bias, mix_out, mix_out_bias)
    return call_remote(
        functools.partial(forward_kernel, size),
        "forward",
        number,
        (struct(tokens.shape, bf16), struct(tokens.shape, bf16), piece) + kept,
        [pl.ANY] * 5 + [pltpu.VMEM] * len(small),
        [pl.ANY] * (3 + len(kept)),
        2 * size.per_image + 2 * size.lon,
        24,
        [pltpu.VMEM(v.shape, v.dtype) for v in scratch],
        (tokens, cotangent, table, er, ec) + small,
    )


def add_to(total_ref, other_ref):
    @pl.loop(0, total_ref.shape[0])
    def _(first):
        if len(total_ref.shape) == 3:
            total = total_ref[first].astype(f32) + other_ref[first].astype(f32)
            total_ref[first] = total.astype(total_ref.dtype)
        else:
            for second in range(total_ref.shape[1]):
                total = total_ref[first, second].astype(f32) + other_ref[first, second].astype(f32)
                total_ref[first, second] = total.astype(total_ref.dtype)


def start_same(lon_count, count, source_ref, out_ref, sender, mover):
    me = lax.axis_index("rows") * lon_count + lax.axis_index("lon")
    copies = []
    for offset in range(1, count):
        other = (me + offset) % count
        copies.append(
            sender.start(
                source_ref, out_ref.at[me], {"rows": other // lon_count, "lon": other % lon_count}
            )
        )
    copies.append(mover.start(source_ref, out_ref.at[me]))
    return copies


def backward_kernel(
    size,
    e_hbm,
    dy_hbm,
    inv_t_hbm,
    inv_hbm,
    fc_in_hbm,
    fc_out_hbm,
    lat_hbm,
    lat_t_hbm,
    w1_hbm,
    w2_hbm,
    band_hbm,
    inner_hbm,
    gated_hbm,
    outer_hbm,
    x_hbm,
    table_t_hbm,
    map_ref,
    gain1_ref,
    shift1_ref,
    gain2_ref,
    shift2_ref,
    out_bias_ref,
    fc_in_bias_ref,
    token_out,
    block_out,
    dense_ref,
    mix_out,
    early_out,
    late_out,
    send_sem,
    recv_sem,
    move_sem,
    x_ref,
    table_t_ref,
    dh_ref,
    send1,
    recv1,
    send2,
    recv2,
    token_ref,
    block_ref,
    wide,
    a_core,
    b_core,
    a_one,
    b_one,
    a_two,
    b_two,
    a_near,
    b_near,
    a_last,
    b_last,
    mix_ref,
    mix_core,
    mix_land,
    pair_ref,
    early,
    early_land,
    late,
    late_land,
):
    channels = size.channels
    lon_count, count, groups = size.lon, size.devices, size.groups
    row = lax.axis_index("rows")
    lon = lax.axis_index("lon")
    me = row * lon_count + lon
    z = row // 2
    x = row % 2
    y = lon // 2
    core = lon % 2
    mine = row % QUARTERS
    group = me % groups
    base = me - group
    half = me // groups
    to_core, to_y, to_x, far_z = partners(lon_count)
    near = z + 1 - 2 * (z % 2)
    mirror = 3 - z
    to_near = {"rows": near * 2 + x, "lon": lon}
    to_mirror = {"rows": mirror * 2 + x, "lon": lon}
    parts = 4

    def order(step):
        first = jnp.where(step < 2, near, z)
        return jnp.where(step % 2 == 0, first, 3 - first)

    share = wide.shape[-2]
    sender, mover = Sender(send_sem, recv_sem), Mover(move_sem)

    by_core = [
        [
            sender.make(wide.at[i % 2, 0, :, :, 1 - core], a_core.at[i], to_core),
            sender.make(wide.at[i % 2, 1, :, :, 1 - core], b_core.at[i], to_core),
        ]
        for i in range(parts)
    ]
    by_one = [
        [
            sender.make(a_core.at[i, 1 - x], a_one.at[i], to_x),
            sender.make(b_core.at[i, :, 1 - y], b_one.at[i], to_y),
        ]
        for i in range(parts)
    ]
    by_two = [
        [
            sender.make(a_one.at[i, 1 - y], a_two.at[i], to_y),
            sender.make(b_one.at[i, 1 - x], b_two.at[i], to_x),
        ]
        for i in range(parts)
    ]
    by_near = [
        [
            sender.make(a_two.at[i], a_near.at[i], to_near),
            sender.make(b_two.at[i], b_near.at[i], to_near),
        ]
        for i in range(2)
    ]
    by_early = [
        sender.make(early, early_land.at[i], device)
        for i, device in enumerate((to_core, to_x, to_y, to_near, to_mirror))
    ]
    by_quarter = [make_quarter(size, i, send1, recv1, sender, mover) for i in range(QUARTERS)]
    blocks = make_lon(block_ref, block_out, sender, mover)
    late_loads = [mover.make(x_hbm, x_ref), mover.make(table_t_hbm, table_t_ref)]

    def core_end(step):
        finish(by_core[step])
        add_to(a_core.at[step], wide.at[step % 2, 0, :, :, core])
        by_one[step][0].start()
        add_to(b_core.at[step], wide.at[step % 2, 1, :, :, core])
        by_one[step][1].start()

    def one_end(step):
        by_one[step][0].wait()
        add_to(a_one.at[step], a_core.at[step, x])
        by_two[step][0].start()
        by_one[step][1].wait()
        add_to(b_one.at[step], b_core.at[step, :, y])
        by_two[step][1].start()

    def two_end(step):
        finish(by_two[step])
        for total, kept in ((a_two, a_one.at[step, y]), (b_two, b_one.at[step, x])):
            total[step] = (total[step].astype(f32) + kept[...].astype(f32)).astype(bf16)

    def early_step(step):
        by_early[step].wait()
        early[...] = early[...] + early_land[step]
        if step + 1 < len(by_early):
            by_early[step + 1].start()

    def front(
        e_ref,
        dy_ref,
        inv_t_ref,
        inv_ref,
        fc_in_ref,
        fc_out_ref,
        hidden_ref,
        values_ref,
        grad_ref,
        res_ref,
        acc_ref,
    ):
        part_loads = []
        for step in range(parts):
            place = pl.ds(pl.multiple_of(order(step) * channels, channels), channels)
            part_loads.append(
                [
                    mover.make(fc_in_hbm.at[:, place], fc_in_ref.at[step % 2]),
                    mover.make(fc_out_hbm.at[place, :], fc_out_ref.at[step % 2]),
                ]
            )
        late_loads[0].start()
        loads = [
            mover.start(e_hbm, e_ref),
            mover.start(inv_t_hbm, inv_t_ref),
            mover.start(dy_hbm, dy_ref),
        ]
        begin(part_loads[0])
        begin(part_loads[1])
        inv_load = mover.start(inv_hbm, inv_ref)
        late_loads[1].start()
        greet(lon_count, count)
        finish(loads)
        late_loads[0].wait()
        early[...] = jnp.zeros_like(early)
        early[0:1, :] = residual_planes(
            size, map_ref, e_ref, x_ref, dy_ref, inv_t_ref, as_row(gain1_ref), as_row(shift1_ref), as_row(gain2_ref), as_row(shift2_ref), res_ref, values_ref.at[0], values_ref.at[1]
        )
        acc_ref[...] = jnp.zeros_like(acc_ref)
        dh_ref[...] = jnp.zeros_like(dh_ref)
        up_ref = values_ref.at[1]

        def weights(slot):
            @pl.loop(0, 2)
            def _(which):
                product = t_mm(hidden_ref[slot, which], values_ref[which])
                for i in range(8):
                    wide[slot, which, i // 4, i // 2 % 2, i % 2] = product[
                        i * share : (i + 1) * share
                    ].astype(bf16)

        @pl.loop(0, parts)
        def _(step):
            slot = step % 2
            at(step, parts, lambda i: finish(part_loads[i]))
            place = pl.ds(pl.multiple_of(order(step) * channels, channels), channels)
            hidden, hidden_grad = hidden_part(
                values_ref.at[0], up_ref, fc_in_ref[slot], fc_in_bias_ref[:, place], fc_out_ref[slot], acc_ref, dh_ref
            )
            early[pl.ds(3 + order(step), 1), :] = jnp.sum(
                hidden_grad.astype(f32), axis=0, keepdims=True
            )
            hidden_ref[slot, 0] = hidden_grad
            hidden_ref[slot, 1] = hidden
            at(step, parts - 2, lambda i: begin(part_loads[i + 2]))

            @pl.when(step < 2)
            def _():
                weights(slot)
                at(step, 2, lambda i: begin(by_core[i]))

            pl.when(step == 1)(lambda: core_end(0))
            pl.when(step == 2)(lambda: core_end(1))
            pl.when(step == 3)(lambda: one_end(0))

        gain_sum, shift_sum = residual_back_planes(size, up_ref, res_ref, as_row(gain2_ref), dh_ref, grad_ref)
        early[1:2, :] = gain_sum
        early[2:3, :] = shift_sum
        inv_load.wait()

        def send_spectrum(step):
            quarter = (mine + step) % QUARTERS
            write_quarter(size, quarter, mm(inv_ref[quarter], grad_ref[...]), send1)
            at(step, QUARTERS, lambda i: begin(by_quarter[i]))

        over_quarters(send_spectrum)
        by_early[0].start()
        one_end(1)

        @pl.loop(0, 2)
        def _(slot):
            weights(slot)
            at(slot, 2, lambda i: begin(by_core[2 + i]))

        core_end(2)
        core_end(3)
        block_planes(size, map_ref, res_ref, acc_ref, as_row(out_bias_ref), block_ref)
        begin(blocks)
        early_step(0)

    def back(
        lat_ref,
        lat_t_ref,
        w1_ref,
        w2_ref,
        band_ref,
        inner_ref,
        gated_ref,
        outer_ref,
        outer_grad_ref,
        inner_grad_ref,
        modes_ref,
        stacked_ref,
        filtered_ref,
    ):
        loads = [
            mover.start(source, target)
            for source, target in (
                (lat_hbm, lat_ref),
                (outer_hbm, outer_ref),
                (w2_hbm, w2_ref),
                (inner_hbm, inner_ref),
                (w1_hbm, w1_ref),
                (lat_t_hbm, lat_t_ref),
                (gated_hbm, gated_ref),
                (band_hbm, band_ref),
            )
        ]
        for step in range(2):
            two_end(step)
            begin(by_near[step])
        finish(loads)
        modes_ref[...] = jnp.zeros_like(modes_ref)

        def receive(step):
            at(step, QUARTERS, lambda i: finish(by_quarter[i]))
            add_modes(size, (mine + QUARTERS - step) % QUARTERS, recv1, lat_ref, modes_ref)

        over_quarters(receive)
        mix_layers_back(size, modes_ref, w1_ref, w2_ref, inner_ref, outer_ref, outer_grad_ref, inner_grad_ref, stacked_ref)
        steps = [make_quarter(size, i, send2, recv2, sender, mover) for i in range(QUARTERS)]

        def send_back(step):
            mix_quarter_back(size, (mine + step) % QUARTERS, lat_t_ref, stacked_ref, send2)
            at(step, QUARTERS, lambda i: begin(steps[i]))

        over_quarters(send_back)
        one_end(2)
        one_end(3)
        early_step(1)

        mix_back_weights(size, band_ref, gated_ref, outer_grad_ref, inner_grad_ref, mix_ref)
        crossing = sender.start(mix_ref.at[:, 1 - core], mix_core, to_core)
        two_end(2)
        two_end(3)
        crossing.wait()
        add_to(mix_core, mix_ref.at[:, core])
        pair = group // 2
        mixes = []
        for offset in range(1, groups // 2):
            other = (pair + offset) % (groups // 2)
            device = base + other * 2 + core
            mixes.append(
                sender.start(
                    mix_core.at[other],
                    mix_land.at[pair],
                    {"rows": device // lon_count, "lon": device % lon_count},
                )
            )
        mixes.append(mover.start(mix_core.at[pair], mix_land.at[pair]))

        finish(by_near[0])
        finish(by_near[1])
        for total, landed in ((a_two, a_near), (b_two, b_near)):
            for i in range(2):
                total[2 + i] = (total[2 + i].astype(f32) + landed[i].astype(f32)).astype(bf16)
        hops = [
            sender.start(a_two.at[3], a_last, to_mirror),
            sender.start(b_two.at[3], b_last, to_mirror),
        ]
        early_step(2)
        finish(mixes)
        total = mix_land[0].astype(f32)
        for index in range(1, groups // 2):
            total = total + mix_land[index].astype(f32)
        pair_ref[half] = total.astype(bf16)
        crossing = sender.start(pair_ref.at[half], pair_ref.at[half], far_z)

        for copies in steps:
            finish(copies)
        crossing.wait()
        own_place = mix_out.at[pair // 4, pair // 2 % 2, :, pair % 2, core]
        gather = []
        for offset in range(1, groups // 2):
            device = base + (pair + offset) % (groups // 2) * 2 + core
            gather.append(
                sender.start(
                    pair_ref, own_place, {"rows": device // lon_count, "lon": device % lon_count}
                )
            )
        gather.append(mover.start(pair_ref, own_place))
        last_planes(size, recv2, x_ref, dh_ref, table_t_ref, gain1_ref, filtered_ref, token_ref, late)
        tokens = start_lon(token_ref, token_out, sender, mover)
        smalls = start_same(lon_count, count, late, late_land, sender, mover)
        early_step(3)
        finish(hops)
        dense_ref[0] = a_two[2].astype(f32) + a_last[...].astype(f32)
        dense_ref[1] = b_two[2].astype(f32) + b_last[...].astype(f32)
        finish(gather)
        own_core = mix_out.at[:, :, :, :, core]
        gather = sender.start(own_core, own_core, to_core)
        finish(smalls)
        total = late_land[0]
        for index in range(1, count):
            total = total + late_land[index]
        late_out[...] = total
        early_step(4)
        early_out[...] = early[...]
        gather.wait()
        finish(blocks)
        finish(tokens)

    piece = send1.shape
    tokens = dh_ref.shape
    square = (2, channels, channels)
    pl.run_scoped(
        front,
        pltpu.VMEM(piece, bf16),
        pltpu.VMEM(x_ref.shape, bf16),
        pltpu.VMEM(inv_t_hbm.shape, bf16),
        pltpu.VMEM(inv_hbm.shape, bf16),
        pltpu.VMEM(square, bf16),
        pltpu.VMEM(square, bf16),
        pltpu.VMEM((2, 2) + tokens, bf16),
        pltpu.VMEM((2,) + tokens, bf16),
        pltpu.VMEM(tokens, bf16),
        pltpu.VMEM(tokens, f32),
        pltpu.VMEM(tokens, f32),
    )
    modes = (2 * size.modes, size.half)
    late_loads[1].wait()
    pl.run_scoped(
        back,
        *[
            pltpu.VMEM(ref.shape, ref.dtype)
            for ref in (lat_hbm, lat_t_hbm, w1_hbm, w2_hbm, band_hbm, inner_hbm, gated_hbm, outer_hbm)
        ],
        pltpu.VMEM(band_hbm.shape, bf16),
        pltpu.VMEM(band_hbm.shape, bf16),
        pltpu.VMEM(modes, f32),
        pltpu.VMEM(modes, bf16),
        pltpu.VMEM(tokens, f32),
    )


def run_backward(size, blocks_shape, e, dy, inv_t, inv, fc_in, fc_out, lat, lat_t, w1, w2, band, inner, gated, outer, x, table_t, row_map, vectors, fc_in_bias, number):
    parts = fc_out.shape[0] // size.channels
    plane = (fc_out.shape[0] // size.devices, size.channels)
    large = (e, dy, inv_t, inv, fc_in, fc_out, lat, lat_t, w1, w2, band, inner, gated, outer, x, table_t)
    early = (round_up(3 + parts, 8), size.channels)
    late = (2, size.channels)
    block = blocks_shape[1:]
    half_blocks = (blocks_shape[0] // 2,) + block

    scratch = [pltpu.VMEM(x.shape, bf16), pltpu.VMEM(table_t.shape, bf16)]
    scratch += [pltpu.VMEM((size.tokens, size.channels), f32)]
    scratch += [pltpu.VMEM(e.shape, bf16)] * 4
    scratch += [pltpu.VMEM(x.shape, bf16)] * 2
    scratch += [pltpu.VMEM((2, 2, 2, 2, 2) + plane, bf16)]
    for lead in ((4, 2, 2), (4, 2), (4,), (2,), ()):
        scratch += [pltpu.VMEM(lead + plane, bf16)] * 2
    scratch += [pltpu.VMEM((blocks_shape[0] // 2, 2) + block, bf16)]
    scratch += [pltpu.VMEM(half_blocks, bf16)] * 2
    scratch += [pltpu.VMEM((HALVES,) + block, bf16)]
    scratch += [pltpu.VMEM(early, f32), pltpu.VMEM((5,) + early, f32)]
    scratch += [pltpu.VMEM(late, f32), pltpu.VMEM((size.devices,) + late, f32)]
    return call_remote(
        functools.partial(backward_kernel, size),
        "mlp_backward",
        number,
        (
            struct(x.shape, bf16),
            struct(x.shape, bf16),
            struct((2,) + plane, f32),
            struct((2, 2, HALVES, blocks_shape[0] // 8, 2) + block, bf16),
            struct(early, f32),
            struct(late, f32),
        ),
        [pl.ANY] * len(large) + [pltpu.SMEM] + [pltpu.VMEM] * (len(vectors) + 1),
        [pl.ANY] * 2 + [pltpu.VMEM] * 4,
        3 * size.devices + 2 * size.groups + 2 * size.lon + 48,
        48,
        scratch,
        large + (row_map,) + vectors + (fc_in_bias,),
    )


def exchange_lon(values):
    return lax.all_to_all(values, "lon", split_axis=0, concat_axis=0, tiled=True)


def exchange_all(values):
    return lax.all_to_all(values, ("rows", "lon"), split_axis=0, concat_axis=0, tiled=True)


def to_modes(size, pieces, row_map):
    order, place = place_order(size)
    sent = jnp.tile(jnp.take(pieces, place, axis=0), (size.images, 1, 1))
    received = exchange_all(sent)
    used = size.slots_here * 2 * size.waves
    by_slot = received[:, :used].reshape(-1, 2 * size.waves, size.half)
    image = (lax.axis_index("rows") * size.lon + lax.axis_index("lon")) // size.per_image
    slots = row_map.shape[0]
    target = jnp.where(row_map >= 0, row_map, size.images * H)
    slot_of_row = (
        jnp.zeros((size.images * H,), jnp.int32)
        .at[target]
        .set(jnp.arange(slots, dtype=jnp.int32), mode="drop")
    )
    own = lax.dynamic_slice_in_dim(slot_of_row, image * H, H)
    picked = jnp.take(by_slot, own, axis=0)
    picked = jnp.pad(picked, ((0, size.virtual_slots - H), (0, 0), (0, 0)))
    picked = picked.reshape(size.per_image, used, size.half)
    return jnp.take(jnp.pad(picked, ((0, 0), (0, size.piece - used), (0, 0))), order, axis=0)


def from_modes(size, pieces, row_map):
    order, place = place_order(size)
    used = size.slots_here * 2 * size.waves
    by_lat = jnp.take(pieces, place, axis=0)[:, :used].reshape(-1, 2 * size.waves, size.half)
    image = (lax.axis_index("rows") * size.lon + lax.axis_index("lon")) // size.per_image
    live = (row_map >= 0) & (row_map // H == image)
    picked = jnp.take(by_lat, jnp.where(live, row_map % H, 0), axis=0)
    picked = picked * live.astype(bf16)[:, None, None]
    picked = picked.reshape(size.devices, used, size.half)
    sent = jnp.pad(picked, ((0, 0), (0, size.piece - used), (0, 0)))
    received = exchange_all(sent)
    received = received.reshape(size.images, size.per_image, size.piece, size.half)
    return jnp.take(jnp.sum(received.astype(f32), axis=0).astype(bf16), order, axis=0)


def body(
    tokens,
    row_map,
    cotangent,
    norm_gain,
    norm_shift,
    mix_in,
    mix_in_bias,
    mix_out,
    mix_out_bias,
    post_gain,
    post_shift,
    fc_in,
    fc_in_bias,
    fc_out,
    fc_out_bias,
):
    size = Sizes(
        lax.axis_size("rows"), lax.axis_size("lon"), row_map.shape[0], tokens.shape[2]
    )
    channels = size.channels
    blocks = mix_in.shape[1]
    blocks_here = blocks // HALVES
    block_size = mix_in.shape[2]
    hidden_units = fc_in.shape[1]
    device = lax.axis_index("rows") * size.lon + lax.axis_index("lon")
    half_index = (device % size.per_image) // size.groups

    table, table_t, inv, inv_t = [jnp.asarray(t) for t in lon_tables(size)]
    table = table.reshape(QUARTERS, size.spectrum // QUARTERS, size.tokens)
    cosine, sine, er, ec = [jnp.asarray(t) for t in lat_parts(size)]
    if size.images == 1:
        slot_lat = row_map
    else:
        slot_lat = jnp.where(jnp.arange(size.virtual_slots) < H, jnp.arange(size.virtual_slots), -1)
    rows = jnp.pad(slot_lat, (0, 128 - size.virtual_slots), constant_values=-1).reshape(1, 128)
    shape = (size.lon, size.slots_here, size.lons_here, channels)
    x, dy = tokens.reshape(shape), cotangent.reshape(shape)
    piece_shape = struct((size.per_image, size.piece, size.half), bf16)
    mode_shape = (size.modes, 2 * size.half)
    wide_modes = (2 * size.modes, size.half)
    mode_scratch = [pltpu.VMEM(wide_modes, f32), pltpu.VMEM(wide_modes, bf16)]
    if size.images == 1:
        x, dy, received, lat, lat_t, w1, w2, band, inner, gated, outer = run_forward(
            size, x, dy, table, er, ec, rows, norm_gain, norm_shift, cosine, sine, mix_in, mix_in_bias, mix_out, mix_out_bias, 0
        )
    else:
        square = struct((2 * size.half, 2 * size.half), bf16)
        flat = struct((1, 2 * size.half), f32)
        lat, lat_t, w1, w2, b1, b2 = call_local(
            functools.partial(prepare_kernel, size),
            "prepare",
            (
                struct((QUARTERS, 2 * size.modes, size.chunk_rows), bf16),
                struct((QUARTERS, size.chunk_rows, 2 * size.modes), bf16),
                square,
                square,
                flat,
                flat,
            ),
        )(rows, cosine, sine, er, ec, mix_in, mix_in_bias, mix_out, mix_out_bias)
        x, dy = exchange_lon(x), exchange_lon(dy)
        sent = call_local(
            functools.partial(first_kernel, size),
            "lon_forward",
            piece_shape,
            [pltpu.VMEM((size.tokens, channels), bf16)],
        )(x, norm_gain, norm_shift, table)
        received = to_modes(size, sent, row_map)
        sent, band, inner, gated, outer = call_local(
            functools.partial(mix_kernel, size),
            "mix_forward",
            (
                piece_shape,
                struct(mode_shape, bf16),
                struct(mode_shape, f32),
                struct(mode_shape, bf16),
                struct(mode_shape, f32),
            ),
            mode_scratch,
        )(received, lat, lat_t, w1, b1, w2, b2)
        received = from_modes(size, sent, row_map)
    vectors = (norm_gain, norm_shift, post_gain, post_shift, fc_out_bias)
    blocks_shape = (4 * blocks_here, round_up(block_size + 1, 16), block_size)
    bias_row = fc_in_bias.reshape(1, -1)
    if size.images == 1:
        token_grad, block, dense, mix_total, early, late = run_backward(
            size, blocks_shape, received, dy, inv_t, inv.reshape(table.shape), fc_in, fc_out, lat, lat_t, w1, w2, band, inner, gated, outer, x, table_t, row_map, vectors, bias_row, 1
        )
    else:
        names = ("rows", "lon")
        block, dh, sent, hidden, hidden_grad, low, up, early = run_mlp(
            size, hidden_units, row_map, received, x, dy, inv_t, inv, vectors, fc_in, bias_row, fc_out
        )
        early = lax.psum(early, names)
        wide = call_local(
            wide_kernel, "weights_backward", struct((hidden_units, 2 * channels), bf16)
        )(hidden, hidden_grad, low, up)
        dense = lax.psum_scatter(wide, names, scatter_dimension=0, tiled=True)
        dense = jnp.stack([dense[:, :channels], dense[:, channels:]]).astype(f32)
        block = exchange_lon(block)
        received = to_modes(size, sent, row_map)
        sent, mix_grad = call_local(
            functools.partial(mix_back_kernel, size),
            "mix_backward",
            (piece_shape, struct(blocks_shape, bf16)),
            [pltpu.VMEM(mode_shape, bf16)] * 2 + mode_scratch,
        )(received, lat, lat_t, w1, w2, band, inner, gated, outer)
        mix_grad = mix_grad.astype(f32).reshape((2, 2, 1, blocks_here) + blocks_shape[1:])
        mix_total = lax.psum(
            jnp.concatenate(
                [mix_grad * (half_index == other).astype(f32) for other in range(HALVES)], axis=2
            ),
            names,
        )
        received = from_modes(size, sent, row_map)
        token_grad, late = call_local(
            functools.partial(last_kernel, size),
            "lon_backward",
            (struct(x.shape, bf16), struct((2, channels), f32)),
            [pltpu.VMEM((size.tokens, channels), f32)],
        )(received, x, dh, table_t, norm_gain)
        token_grad = exchange_lon(token_grad)
        late = lax.psum(late, names)
    mix_total = mix_total.reshape((2, 2, blocks) + blocks_shape[1:]).astype(f32)
    mix_bias = mix_total[:, :, :, block_size]
    mix_total = mix_total[:, :, :, :block_size]
    share = hidden_units // size.devices
    return (
        block.reshape(tokens.shape),
        token_grad.reshape(tokens.shape).astype(f32),
        late[0],
        late[1],
        mix_total[0],
        mix_bias[0],
        mix_total[1],
        mix_bias[1],
        early[1],
        early[2],
        dense[0].T,
        lax.dynamic_slice_in_dim(early[3:7].reshape(-1), device * share, share),
        dense[1],
        early[0],
    )


def solution(mesh):
    return jax.shard_map(
        body,
        mesh=mesh,
        in_specs=(P("rows", "lon", None), P(), P("rows", "lon", None)) + (P(),) * 12,
        out_specs=(
            P("rows", "lon", None),
            P("rows", "lon", None),
            P(),
            P(),
            P(),
            P(),
            P(),
            P(),
            P(),
            P(),
            P(None, ("rows", "lon")),
            P(("rows", "lon")),
            P(("rows", "lon"), None),
            P(),
        ),
        check_vma=False,
    )
```

```python
import functools
import math

import jax
import jax.numpy as jnp
import ml_dtypes
import numpy as np
from jax import lax
from jax.experimental import pallas as pl
from jax.experimental.pallas import tpu as pltpu
from jax.sharding import PartitionSpec as P

H = 90
W = 180
KX = 91
HALVES = 2
QUARTERS = 4
VMEM_BYTES = 58 * 1024 * 1024

norm_eps = 1e-06
shrink_level = 0.01
half_root = 0.7071067811865476
normal_peak = 0.3989422804014327
MESH = pl.DeviceIdType.MESH
f32 = jnp.float32
bf16 = jnp.bfloat16


def round_up(value, step):
    return -(-value // step) * step


class Sizes:
    def __init__(self, rows_count, lon_count, slots, channels):
        self.rows = rows_count
        self.lon = lon_count
        self.devices = rows_count * lon_count
        self.images = slots * 15 // (16 * H)
        self.per_image = self.devices // self.images
        self.groups = self.per_image // HALVES
        self.waves = -(-KX // self.groups)
        self.slots_here = slots // self.devices
        self.lons_here = W // lon_count
        self.lons_pad = round_up(self.lons_here, 16)
        self.tokens = lon_count * self.slots_here * self.lons_pad
        self.piece = round_up(self.slots_here * 2 * self.waves, 8)
        self.spectrum = self.groups * self.piece
        self.band = self.per_image * self.piece
        self.modes = round_up(H * self.waves, 16)
        self.virtual_slots = self.per_image * self.slots_here
        self.chunk = self.per_image // QUARTERS
        self.chunk_rows = self.chunk * self.piece
        self.channels = channels
        self.half = channels // HALVES


def place_of(size, row, lon):
    return (row % QUARTERS) * size.chunk + (row // QUARTERS) * size.lon + lon


def place_order(size):
    place = np.array([place_of(size, d // size.lon, d % size.lon) for d in range(size.per_image)])
    return np.argsort(place), place


def lon_tables(size):
    wave = np.arange(size.groups * size.waves)
    lon_index = np.arange(W)
    product = (lon_index[:, None] * wave[None, :]) % W
    angle = product.astype(np.float32) * np.float32(2.0 * math.pi / W)
    scale = np.float32(1.0 / math.sqrt(W))
    cosine = (np.cos(angle) * scale).astype(ml_dtypes.bfloat16).astype(np.float32)
    sine = (-np.sin(angle) * scale).astype(ml_dtypes.bfloat16).astype(np.float32)
    live = (wave < KX).astype(np.float32)
    factor = np.where((wave == 0) | (wave == W // 2), 1.0, 2.0).astype(np.float32)
    both = np.stack([cosine, sine]) * live
    result = []
    for weight in (np.ones_like(factor), factor):
        table = np.zeros(
            (
                size.groups,
                size.piece,
                size.lon,
                size.slots_here,
                size.lons_pad,
            ),
            np.float32,
        )
        values = (both * weight).reshape(2, size.lon, size.lons_here, size.groups, size.waves)
        values = np.transpose(values, (3, 0, 4, 1, 2)).reshape(
            size.groups, 2 * size.waves, size.lon, size.lons_here
        )
        for slot in range(size.slots_here):
            start = slot * 2 * size.waves
            table[:, start : start + 2 * size.waves, :, slot, : size.lons_here] = values
        flat = table.reshape(size.spectrum, size.tokens).astype(ml_dtypes.bfloat16)
        result.append(flat)
        result.append(np.ascontiguousarray(flat.T))
    return result


def lat_parts(size):
    lat_index = np.arange(H)
    angle = ((lat_index[:, None] * lat_index[None, :]) % H).astype(np.float32) * np.float32(
        2.0 * math.pi / H
    )
    scale = np.float32(1.0 / math.sqrt(H))
    cosine = np.zeros((96, 96), np.float32)
    sine = np.zeros((96, 96), np.float32)
    cosine[:H, :H] = np.cos(angle) * scale
    sine[:H, :H] = np.sin(angle) * scale
    spread_rows = np.zeros((2, size.modes, 2, 96), np.float32)
    for part in range(2):
        for lat in range(H):
            for wave in range(size.waves):
                spread_rows[part, lat * size.waves + wave, part, lat] = 1.0
    spread_cols = np.zeros((QUARTERS, 2, 128, size.chunk, size.piece), np.float32)
    for place, device in enumerate(place_order(size)[0]):
        for slot in range(size.slots_here):
            for part in range(2):
                for wave in range(size.waves):
                    spread_cols[
                        place // size.chunk,
                        part,
                        device * size.slots_here + slot,
                        place % size.chunk,
                        (slot * 2 + part) * size.waves + wave,
                    ] = 1.0
    low = ml_dtypes.bfloat16
    return (
        cosine.astype(low),
        sine.astype(low),
        spread_rows.reshape(2 * size.modes, 192).astype(low),
        spread_cols.reshape(QUARTERS, 256, size.chunk_rows).astype(low),
    )


def smooth_gate(values):
    return 0.5 * values * (1.0 + lax.erf(values * half_root))


def gate_both(values):
    half_phi = 0.5 * (1.0 + lax.erf(values * half_root))
    density = values * normal_peak * jnp.exp(-0.5 * values * values)
    return values * half_phi, half_phi + density


def gate_slope(values):
    return gate_both(values)[1]


def soft_shrink(values):
    return values - shrink_level * values * lax.rsqrt(values * values + shrink_level * shrink_level)


def shrink_slope(values):
    inverse = lax.rsqrt(values * values + shrink_level * shrink_level)
    return 1.0 - shrink_level * shrink_level * shrink_level * inverse * inverse * inverse


def norm_parts(values):
    center = values - jnp.mean(values, axis=-1, keepdims=True)
    spread = lax.rsqrt(jnp.mean(center * center, axis=-1, keepdims=True) + norm_eps)
    return center * spread, spread


def norm_back(scaled, unit, spread):
    return spread * (
        scaled
        - jnp.mean(scaled, axis=-1, keepdims=True)
        - unit * jnp.mean(scaled * unit, axis=-1, keepdims=True)
    )


def mm(left, right):
    return jnp.dot(left, right, preferred_element_type=f32)


def mm_t(left, right):
    return lax.dot_general(left, right, (((1,), (1,)), ((), ())), preferred_element_type=f32)


def t_mm(left, right):
    return lax.dot_general(left, right, (((0,), (0,)), ((), ())), preferred_element_type=f32)


def whole(count):
    return [pl.BlockSpec(memory_space=pltpu.VMEM)] * count


def call_local(kernel, name, outs, scratch=()):
    def run(*operands):
        return pl.pallas_call(
            kernel,
            out_shape=outs,
            in_specs=whole(len(operands)),
            out_specs=jax.tree.map(lambda _: pl.BlockSpec(memory_space=pltpu.VMEM), outs),
            scratch_shapes=list(scratch),
            compiler_params=pltpu.CompilerParams(vmem_limit_bytes=VMEM_BYTES),
            name=name,
        )(*operands)

    return run


def struct(shape, dtype):
    return jax.ShapeDtypeStruct(shape, dtype)


def wave_of(index, period, used, waves, other):
    within = index - period * jnp.floor((index + 0.5) * (1.0 / period))
    wave = within - waves * jnp.floor((within + 0.5) * (1.0 / waves))
    return jnp.where(within < used, wave, other)


def build_lat_tables(size, rows_ref, cos_ref, sin_ref, er_ref, ec_ref, lat_ref, lat_t_ref):
    slots = rows_ref.shape[0]
    lat_of = lax.broadcasted_iota(jnp.int32, (96, slots), 0)
    hot = (lat_of == rows_ref[...].reshape(1, slots)).astype(f32)
    hot = jnp.concatenate([hot, jnp.zeros((96, 128 - slots), f32)], axis=1).astype(bf16)
    cosine = mm(cos_ref[...], hot)
    sine = mm(sin_ref[...], hot)
    top = jnp.concatenate([cosine, sine], axis=1)
    bottom = jnp.concatenate([-sine, cosine], axis=1)
    base = jnp.concatenate([top, bottom], axis=0).astype(bf16)

    def row_waves(shape, dim):
        index = lax.broadcasted_iota(jnp.int32, shape, dim).astype(f32)
        return wave_of(index, size.modes, H * size.waves, size.waves, -1.0)

    def col_waves(shape, dim):
        index = lax.broadcasted_iota(jnp.int32, shape, dim).astype(f32)
        return wave_of(index, size.piece, size.slots_here * 2 * size.waves, size.waves, -2.0)

    modes, columns_here = 2 * size.modes, size.chunk_rows
    keep = row_waves((modes, 1), 0) == col_waves((1, columns_here), 1)
    keep_t = col_waves((columns_here, 1), 0) == row_waves((1, modes), 1)

    def build(quarter):
        columns = mm(base, ec_ref[quarter]).astype(bf16)
        table = mm(er_ref[...], columns)
        lat_ref[quarter] = jnp.where(keep, table, 0.0).astype(bf16)
        table_t = lax.dot_general(
            columns, er_ref[...], (((0,), (1,)), ((), ())), preferred_element_type=f32
        )
        lat_t_ref[quarter] = jnp.where(keep_t, table_t, 0.0).astype(bf16)

    over_quarters(build)


def build_block_matrix(size, weight_ref, bias_ref, half, matrix_ref, row_ref):
    block_size = weight_ref.shape[2]
    blocks = size.half // block_size
    matrix_ref[...] = jnp.zeros_like(matrix_ref)
    for block in range(blocks):
        real = weight_ref[0, half * blocks + block]
        imag = weight_ref[1, half * blocks + block]
        near = slice(block * block_size, (block + 1) * block_size)
        far = slice(size.half + block * block_size, size.half + (block + 1) * block_size)
        matrix_ref[near, near] = real
        matrix_ref[near, far] = imag
        matrix_ref[far, near] = -imag
        matrix_ref[far, far] = real
        row_ref[0:1, near] = bias_ref[0, pl.ds(half * blocks + block, 1), :]
        row_ref[0:1, far] = bias_ref[1, pl.ds(half * blocks + block, 1), :]


def prepare_kernel(size, rows_ref, cos_ref, sin_ref, er_ref, ec_ref, mix_in_ref, bias_in_ref, mix_out_ref, bias_out_ref, lat_ref, lat_t_ref, w1_ref, w2_ref, b1_ref, b2_ref):
    half = half_of(size)
    build_lat_tables(size, rows_ref, cos_ref, sin_ref, er_ref, ec_ref, lat_ref, lat_t_ref)
    build_block_matrix(size, mix_in_ref, bias_in_ref, half, w1_ref, b1_ref)
    build_block_matrix(size, mix_out_ref, bias_out_ref, half, w2_ref, b2_ref)


def half_of(size):
    device = lax.axis_index("rows") * size.lon + lax.axis_index("lon")
    return (device % size.per_image) // size.groups


def pad_plane(size, plane):
    extra = size.lons_pad - size.lons_here
    return jnp.concatenate([plane, jnp.zeros((extra, plane.shape[1]), plane.dtype)], axis=0)


def over_planes(size, body, *sums, first=0, then=None):
    def step(index, sums):
        source = (first + index) % size.lon
        for slot in range(size.slots_here):
            start = pl.multiple_of(
                (source * size.slots_here + slot) * size.lons_pad, size.lons_pad
            )
            sums = body(source, slot, pl.ds(start, size.lons_pad), *sums)
        if then is not None:
            at(index, size.lon, then)
        return sums

    return lax.fori_loop(0, size.lon, step, sums)


def over_quarters(body):
    @pl.loop(0, QUARTERS)
    def _(step):
        body(step)


def at(step, count, action):
    for i in range(count):

        @pl.when(step == i)
        def _():
            action(i)


def write_quarter(size, quarter, values, out_ref):
    for half in range(HALVES):
        for lon in range(size.lon):
            out_ref[quarter * size.chunk + half * size.lon + lon] = values[
                lon * size.piece : (lon + 1) * size.piece,
                half * size.half : (half + 1) * size.half,
            ].astype(bf16)


def write_pieces(size, values, out_ref):
    rows = size.lon * size.piece
    for quarter in range(QUARTERS):
        write_quarter(size, quarter, values[quarter * rows : (quarter + 1) * rows], out_ref)


def read_pieces(ref, places):
    return jnp.concatenate([ref[place].astype(f32) for place in places], axis=0).astype(bf16)


def read_spectrum(size, ref):
    return jnp.concatenate(
        [
            read_pieces(
                ref,
                [
                    quarter * size.chunk + half * size.lon + lon
                    for quarter in range(QUARTERS)
                    for lon in range(size.lon)
                ],
            )
            for half in range(HALVES)
        ],
        axis=1,
    )


def first_norm(size, x_ref, gain, shift, low_ref):
    def plane(source, slot, rows):
        x = pad_plane(size, x_ref[source, slot].astype(f32))
        unit, _ = norm_parts(x)
        low_ref[rows, :] = (unit * gain + shift).astype(bf16)
        return ()

    over_planes(size, plane)


def as_row(ref):
    return ref[...].reshape(1, -1)


def first_kernel(size, x_ref, gain_ref, shift_ref, table_ref, send_ref, low_ref):
    first_norm(size, x_ref, as_row(gain_ref), as_row(shift_ref), low_ref)
    over_quarters(lambda i: write_quarter(size, i, mm(table_ref[i], low_ref[...]), send_ref))


def add_modes(size, quarter, recv_ref, lat_ref, modes_ref):
    spectrum = read_pieces(recv_ref, [quarter * size.chunk + i for i in range(size.chunk)])
    modes_ref[...] += mm(lat_ref[quarter], spectrum)


def side_by_side(size, modes_ref):
    return jnp.concatenate(
        [modes_ref[: size.modes, :], modes_ref[size.modes :, :]], axis=1
    ).astype(bf16)


def stack_parts(size, values, stacked_ref):
    stacked_ref[: size.modes, :] = values[:, : size.half].astype(bf16)
    stacked_ref[size.modes :, :] = values[:, size.half :].astype(bf16)


def mix_quarter_back(size, quarter, lat_t_ref, stacked_ref, send_ref):
    back = mm(lat_t_ref[quarter], stacked_ref[...])
    for i in range(size.chunk):
        send_ref[quarter * size.chunk + i] = back[i * size.piece : (i + 1) * size.piece].astype(bf16)


def mix_layers(size, modes_ref, w1_ref, b1_ref, w2_ref, b2_ref, band_ref, inner_ref, gated_ref, outer_ref, stacked_ref):
    band = side_by_side(size, modes_ref)
    band_ref[...] = band
    inner = mm(band, w1_ref[...]) + b1_ref[...]
    inner_ref[...] = inner
    gated = smooth_gate(inner).astype(bf16)
    gated_ref[...] = gated
    outer = mm(gated, w2_ref[...]) + b2_ref[...]
    outer_ref[...] = outer
    stack_parts(size, soft_shrink(outer), stacked_ref)


def mix_kernel(size, recv_ref, lat_ref, lat_t_ref, w1_ref, b1_ref, w2_ref, b2_ref, send_ref, band_ref, inner_ref, gated_ref, outer_ref, modes_ref, stacked_ref):
    modes_ref[...] = jnp.zeros_like(modes_ref)
    over_quarters(lambda i: add_modes(size, i, recv_ref, lat_ref, modes_ref))
    mix_layers(size, modes_ref, w1_ref, b1_ref, w2_ref, b2_ref, band_ref, inner_ref, gated_ref, outer_ref, stacked_ref)
    over_quarters(lambda i: mix_quarter_back(size, i, lat_t_ref, stacked_ref, send_ref))


def mix_layers_back(size, modes_ref, w1_ref, w2_ref, inner_ref, outer_ref, outer_grad_ref, inner_grad_ref, stacked_ref):
    upstream = side_by_side(size, modes_ref)
    outer_grad = (upstream.astype(f32) * shrink_slope(outer_ref[...])).astype(bf16)
    outer_grad_ref[...] = outer_grad
    inner_grad = (mm_t(outer_grad, w2_ref[...]) * gate_slope(inner_ref[...])).astype(bf16)
    inner_grad_ref[...] = inner_grad
    stack_parts(size, mm_t(inner_grad, w1_ref[...]), stacked_ref)


def mix_back_weights(size, band_ref, gated_ref, outer_grad_ref, inner_grad_ref, out_ref):
    half = size.half
    block_size = out_ref.shape[-1]
    blocks = half // block_size
    rest = out_ref.shape[-2] - block_size
    for layer, (value_ref, grad_ref) in enumerate(
        ((band_ref, inner_grad_ref), (gated_ref, outer_grad_ref))
    ):
        grad = grad_ref[...]
        total = t_mm(value_ref[...], grad)
        bias = jnp.sum(grad.astype(f32), axis=0, keepdims=True)
        for block in range(blocks):
            near = slice(block * block_size, (block + 1) * block_size)
            far = slice(half + block * block_size, half + (block + 1) * block_size)
            for part, values, row in (
                (0, total[near, near] + total[far, far], bias[:, near]),
                (1, total[near, far] - total[far, near], bias[:, far]),
            ):
                place = (layer * 2 + part) * blocks + block
                at = (place // 2, place % 2) if len(out_ref.shape) == 4 else (place,)
                out_ref[at + (slice(0, block_size),)] = values.astype(bf16)
                out_ref[at + (slice(block_size, None),)] = jnp.broadcast_to(
                    row, (rest, block_size)
                ).astype(bf16)


def mix_back_kernel(size, recv_ref, lat_ref, lat_t_ref, w1_ref, w2_ref, band_ref, inner_ref, gated_ref, outer_ref, send_ref, grad_ref, outer_grad_ref, inner_grad_ref, modes_ref, stacked_ref):
    modes_ref[...] = jnp.zeros_like(modes_ref)
    over_quarters(lambda i: add_modes(size, i, recv_ref, lat_ref, modes_ref))
    mix_layers_back(size, modes_ref, w1_ref, w2_ref, inner_ref, outer_ref, outer_grad_ref, inner_grad_ref, stacked_ref)
    over_quarters(lambda i: mix_quarter_back(size, i, lat_t_ref, stacked_ref, send_ref))
    mix_back_weights(size, band_ref, gated_ref, outer_grad_ref, inner_grad_ref, grad_ref)


def residual_planes(size, map_ref, recv_ref, x_ref, dy_ref, inv_t_ref, gain1, shift1, gain2, shift2, res_ref, low_ref, up_ref):
    first_slot = (lax.axis_index("rows") * size.lon + lax.axis_index("lon")) * size.slots_here
    res_ref[...] = mm(inv_t_ref[...], read_spectrum(size, recv_ref))

    def plane(source, slot, rows, up_sum):
        x = pad_plane(size, x_ref[source, slot].astype(f32))
        unit, _ = norm_parts(x)
        residual = res_ref[rows, :] + (unit * gain1 + shift1) + x
        res_ref[rows, :] = residual
        unit, _ = norm_parts(residual)
        low_ref[rows, :] = (unit * gain2 + shift2).astype(bf16)
        live = jnp.where(map_ref[first_slot + slot] >= 0, 1.0, 0.0)
        up = pad_plane(size, dy_ref[source, slot].astype(f32) * live)
        up_ref[rows, :] = up.astype(bf16)
        return (up_sum + jnp.sum(up, axis=0, keepdims=True),)

    return over_planes(size, plane, jnp.zeros((1, size.channels), f32))[0]


def hidden_part(low_ref, up_ref, fc_in, bias, fc_out, acc_ref, back_ref):
    gate, slope = gate_both(mm(low_ref[...], fc_in) + bias)
    hidden = gate.astype(bf16)
    acc_ref[...] += mm(hidden, fc_out)
    hidden_grad = (mm_t(up_ref[...], fc_out) * slope).astype(bf16)
    back_ref[...] += mm_t(hidden_grad, fc_in)
    return hidden, hidden_grad


def residual_back_planes(size, up_ref, res_ref, gain2, back_ref, grad_ref):
    def plane(source, slot, rows, gain_sum, shift_sum):
        unit, spread = norm_parts(res_ref[rows, :])
        grad = back_ref[rows, :]
        gain_sum = gain_sum + jnp.sum(grad * unit, axis=0, keepdims=True)
        shift_sum = shift_sum + jnp.sum(grad, axis=0, keepdims=True)
        grad = up_ref[rows, :].astype(f32) + norm_back(grad * gain2, unit, spread)
        back_ref[rows, :] = grad
        grad_ref[rows, :] = grad.astype(bf16)
        return gain_sum, shift_sum

    zero = jnp.zeros((1, size.channels), f32)
    return over_planes(size, plane, zero, zero)


def block_planes(size, map_ref, res_ref, acc_ref, out_bias, block_ref):
    first_slot = (lax.axis_index("rows") * size.lon + lax.axis_index("lon")) * size.slots_here

    def plane(source, slot, rows):
        live = jnp.where(map_ref[first_slot + slot] >= 0, 1.0, 0.0)
        block = (res_ref[rows, :] + (acc_ref[rows, :] + out_bias)) * live
        block_ref[source, slot] = block[: size.lons_here].astype(bf16)
        return ()

    over_planes(size, plane)


def mlp_kernel(
    size,
    map_ref,
    recv_ref,
    x_ref,
    dy_ref,
    inv_t_ref,
    inv_ref,
    gain1_ref,
    shift1_ref,
    gain2_ref,
    shift2_ref,
    out_bias_ref,
    fc_in_ref,
    fc_in_bias_ref,
    fc_out_ref,
    block_ref,
    dh_ref,
    send_ref,
    hidden_ref,
    hidden_grad_ref,
    low_ref,
    up_ref,
    small_ref,
    res_ref,
    grad_ref,
    acc_ref,
):
    step = pl.program_id(0)

    @pl.when(step == 0)
    def _():
        small_ref[...] = jnp.zeros_like(small_ref)
        small_ref[0:1, :] = residual_planes(
            size, map_ref, recv_ref, x_ref, dy_ref, inv_t_ref, as_row(gain1_ref), as_row(shift1_ref), as_row(gain2_ref), as_row(shift2_ref), res_ref, low_ref, up_ref
        )
        acc_ref[...] = jnp.zeros_like(acc_ref)
        dh_ref[...] = jnp.zeros_like(dh_ref)

    hidden, hidden_grad = hidden_part(
        low_ref, up_ref, fc_in_ref[...], fc_in_bias_ref[...], fc_out_ref[...], acc_ref, dh_ref
    )
    small_ref[pl.ds(3 + step, 1), :] = jnp.sum(hidden_grad.astype(f32), axis=0, keepdims=True)
    hidden_ref[...] = hidden
    hidden_grad_ref[...] = hidden_grad

    @pl.when(step == pl.num_programs(0) - 1)
    def _():
        block_planes(size, map_ref, res_ref, acc_ref, as_row(out_bias_ref), block_ref)
        gain_sum, shift_sum = residual_back_planes(size, up_ref, res_ref, as_row(gain2_ref), dh_ref, grad_ref)
        small_ref[1:2, :] = gain_sum
        small_ref[2:3, :] = shift_sum
        write_pieces(size, mm(inv_ref[...], grad_ref[...]), send_ref)


def wide_kernel(hidden_ref, hidden_grad_ref, low_ref, up_ref, wide_ref):
    channels = low_ref.shape[1]
    for part in range(hidden_ref.shape[0]):
        rows = slice(part * channels, (part + 1) * channels)
        wide_ref[rows, :channels] = t_mm(hidden_grad_ref[part], low_ref[...]).astype(bf16)
        wide_ref[rows, channels:] = t_mm(hidden_ref[part], up_ref[...]).astype(bf16)


def run_mlp(size, hidden_units, row_map, recv, x, dy, inv_t, inv, vectors, fc_in, fc_in_bias, fc_out):
    channels = size.channels
    width = channels
    parts = hidden_units // width
    fixed = pl.BlockSpec(memory_space=pltpu.VMEM)
    tokens = (size.tokens, channels)
    return pl.pallas_call(
        functools.partial(mlp_kernel, size),
        grid=(parts,),
        in_specs=[pl.BlockSpec(memory_space=pltpu.SMEM)]
        + [fixed] * (5 + len(vectors))
        + [
            pl.BlockSpec((channels, width), lambda i: (0, i)),
            pl.BlockSpec((1, width), lambda i: (0, i)),
            pl.BlockSpec((width, channels), lambda i: (i, 0)),
        ],
        out_specs=(
            fixed,
            fixed,
            fixed,
            pl.BlockSpec((None, size.tokens, width), lambda i: (i, 0, 0)),
            pl.BlockSpec((None, size.tokens, width), lambda i: (i, 0, 0)),
            fixed,
            fixed,
            fixed,
        ),
        out_shape=(
            struct(x.shape, bf16),
            struct(tokens, f32),
            struct((size.per_image, size.piece, size.half), bf16),
            struct((parts,) + tokens, bf16),
            struct((parts,) + tokens, bf16),
            struct(tokens, bf16),
            struct(tokens, bf16),
            struct((round_up(3 + parts, 8), channels), f32),
        ),
        scratch_shapes=[
            pltpu.VMEM(tokens, f32),
            pltpu.VMEM(tokens, bf16),
            pltpu.VMEM(tokens, f32),
        ],
        compiler_params=pltpu.CompilerParams(vmem_limit_bytes=VMEM_BYTES),
        name="mlp",
    )(row_map, recv, x, dy, inv_t, inv, *vectors, fc_in, fc_in_bias, fc_out)


def last_planes(size, recv_ref, x_ref, dh_ref, table_t_ref, gain_ref, filtered_ref, out_ref, small_ref, first=0, then=None):
    gain = as_row(gain_ref)
    filtered_ref[...] = mm(table_t_ref[...], read_spectrum(size, recv_ref))

    def plane(source, slot, rows, gain_sum, shift_sum):
        unit, spread = norm_parts(pad_plane(size, x_ref[source, slot].astype(f32)))
        base = dh_ref[rows, :]
        grad = base + filtered_ref[rows, :]
        gain_sum = gain_sum + jnp.sum(grad * unit, axis=0, keepdims=True)
        shift_sum = shift_sum + jnp.sum(grad, axis=0, keepdims=True)
        grad = base + norm_back(grad * gain, unit, spread)
        out_ref[source, slot] = grad[: size.lons_here].astype(bf16)
        return gain_sum, shift_sum

    zero = jnp.zeros((1, size.channels), f32)
    small_ref[0:1, :], small_ref[1:2, :] = over_planes(
        size, plane, zero, zero, first=first, then=then
    )


def last_kernel(size, recv_ref, x_ref, dh_ref, table_t_ref, gain_ref, out_ref, small_ref, filtered_ref):
    last_planes(size, recv_ref, x_ref, dh_ref, table_t_ref, gain_ref, filtered_ref, out_ref, small_ref)


def partners(lon_count):
    row = lax.axis_index("rows")
    lon = lax.axis_index("lon")
    core = {"rows": row, "lon": lon + 1 - 2 * (lon % 2)}
    along_y = {"rows": row, "lon": (lon + 2) % 4}
    along_x = {"rows": row + 1 - 2 * (row % 2), "lon": lon}
    far_z = {"rows": (row + 4) % 8, "lon": lon}
    return core, along_y, along_x, far_z


def greet(lon_count, count):
    row = lax.axis_index("rows")
    lon = lax.axis_index("lon")
    me = row * lon_count + lon
    barrier = pltpu.get_barrier_semaphore()
    for offset in range(1, count):
        other = (me + offset) % count
        pl.semaphore_signal(
            barrier,
            inc=1,
            device_id={"rows": other // lon_count, "lon": other % lon_count},
            device_id_type=MESH,
        )
    pl.semaphore_wait(barrier, count - 1)


class Sender:
    def __init__(self, send_sem, recv_sem):
        self.send_sem = send_sem
        self.recv_sem = recv_sem
        self.used = 0

    def make(self, source, target, device):
        copy = pltpu.make_async_remote_copy(
            src_ref=source,
            dst_ref=target,
            send_sem=self.send_sem.at[self.used],
            recv_sem=self.recv_sem.at[self.used],
            device_id=device,
            device_id_type=MESH,
        )
        self.used += 1
        return copy

    def start(self, source, target, device):
        copy = self.make(source, target, device)
        copy.start()
        return copy


class Mover:
    def __init__(self, sem):
        self.sem = sem
        self.used = 0

    def make(self, source, target):
        copy = pltpu.make_async_copy(source, target, self.sem.at[self.used])
        self.used += 1
        return copy

    def start(self, source, target):
        copy = self.make(source, target)
        copy.start()
        return copy


def make_quarter(size, step, source_ref, out_ref, sender, mover):
    row = lax.axis_index("rows")
    lon = lax.axis_index("lon")
    me = place_of(size, row, lon)
    copies = []
    for half_step in range(HALVES):
        for lon_step in range(size.lon):
            to_row = (row + step) % QUARTERS + (row // QUARTERS + half_step) % HALVES * QUARTERS
            to_lon = (lon + lon_step) % size.lon
            piece = source_ref.at[place_of(size, to_row, to_lon)]
            if step == 0 and half_step == 0 and lon_step == 0:
                copies.append(mover.make(piece, out_ref.at[me]))
            else:
                copies.append(
                    sender.make(piece, out_ref.at[me], {"rows": to_row, "lon": to_lon})
                )
    return copies


def start_quarter(size, step, source_ref, out_ref, sender, mover):
    return begin(make_quarter(size, step, source_ref, out_ref, sender, mover))


def make_lon(source_ref, out_ref, sender, mover):
    row = lax.axis_index("rows")
    me = lax.axis_index("lon")
    count = source_ref.shape[0]
    copies = []
    for offset in range(1, count):
        other = (me + offset) % count
        copies.append(
            sender.make(source_ref.at[other], out_ref.at[me], {"rows": row, "lon": other})
        )
    copies.append(mover.make(source_ref.at[me], out_ref.at[me]))
    return copies


def start_lon(source_ref, out_ref, sender, mover):
    return begin(make_lon(source_ref, out_ref, sender, mover))


def begin(copies):
    for copy in copies:
        copy.start()
    return copies


def finish(copies):
    for copy in copies:
        copy.wait()


def call_remote(kernel, name, number, outs, spaces, out_spaces, sends, moves, scratch, operands):
    return pl.pallas_call(
        kernel,
        out_shape=outs,
        in_specs=[pl.BlockSpec(memory_space=space) for space in spaces],
        out_specs=tuple(pl.BlockSpec(memory_space=space) for space in out_spaces),
        scratch_shapes=[
            pltpu.SemaphoreType.DMA((sends,)),
            pltpu.SemaphoreType.DMA((sends,)),
            pltpu.SemaphoreType.DMA((moves,)),
        ]
        + list(scratch),
        compiler_params=pltpu.CompilerParams(
            collective_id=number, has_side_effects=True, vmem_limit_bytes=VMEM_BYTES
        ),
        name=name,
    )(*operands)


def forward_kernel(
    size,
    tokens_hbm,
    cot_hbm,
    table_hbm,
    er_hbm,
    ec_hbm,
    rows_ref,
    gain_ref,
    shift_ref,
    cos_ref,
    sin_ref,
    mix_in_ref,
    bias_in_ref,
    mix_out_ref,
    bias_out_ref,
    x_out,
    dy_out,
    recv_out,
    lat_out,
    lat_t_out,
    w1_out,
    w2_out,
    band_out,
    inner_out,
    gated_out,
    outer_out,
    send_sem,
    recv_sem,
    move_sem,
    x_ref,
    table_ref,
    er_ref,
    ec_ref,
    lat_ref,
    lat_t_ref,
    w1_ref,
    w2_ref,
    band_ref,
    inner_ref,
    gated_ref,
    outer_ref,
    b1_ref,
    b2_ref,
    low_ref,
    send1,
    recv1,
    send2,
    modes_ref,
    stacked_ref,
):
    sender, mover = Sender(send_sem, recv_sem), Mover(move_sem)
    mine = lax.axis_index("rows") % QUARTERS
    half = half_of(size)
    load = mover.start(table_hbm, table_ref)
    loads = [mover.start(er_hbm, er_ref), mover.start(ec_hbm, ec_ref)]
    greet(size.lon, size.devices)
    tokens = start_lon(tokens_hbm, x_ref, sender, mover)
    build_block_matrix(size, mix_in_ref, bias_in_ref, half, w1_ref, b1_ref)
    build_block_matrix(size, mix_out_ref, bias_out_ref, half, w2_ref, b2_ref)
    stores = [mover.start(w1_ref, w1_out), mover.start(w2_ref, w2_out)]
    finish(tokens)
    stores.append(mover.start(x_ref, x_out))
    first_norm(size, x_ref, as_row(gain_ref), as_row(shift_ref), low_ref)
    load.wait()
    steps = [make_quarter(size, i, send1, recv1, sender, mover) for i in range(QUARTERS)]

    def send_first(step):
        quarter = (mine + step) % QUARTERS
        write_quarter(size, quarter, mm(table_ref[quarter], low_ref[...]), send1)
        at(step, QUARTERS, lambda i: begin(steps[i]))

    over_quarters(send_first)
    cotangents = start_lon(cot_hbm, dy_out, sender, mover)
    finish(loads)
    build_lat_tables(size, rows_ref, cos_ref, sin_ref, er_ref, ec_ref, lat_ref, lat_t_ref)
    stores += [mover.start(lat_ref, lat_out), mover.start(lat_t_ref, lat_t_out)]
    modes_ref[...] = jnp.zeros_like(modes_ref)

    def receive(step):
        at(step, QUARTERS, lambda i: finish(steps[i]))
        add_modes(size, (mine + QUARTERS - step) % QUARTERS, recv1, lat_ref, modes_ref)

    over_quarters(receive)
    mix_layers(size, modes_ref, w1_ref, b1_ref, w2_ref, b2_ref, band_ref, inner_ref, gated_ref, outer_ref, stacked_ref)
    back_steps = [make_quarter(size, i, send2, recv_out, sender, mover) for i in range(QUARTERS)]

    def send_back(step):
        mix_quarter_back(size, (mine + step) % QUARTERS, lat_t_ref, stacked_ref, send2)
        at(step, QUARTERS, lambda i: begin(back_steps[i]))

    over_quarters(send_back)
    stores += [
        mover.start(band_ref, band_out),
        mover.start(inner_ref, inner_out),
        mover.start(gated_ref, gated_out),
        mover.start(outer_ref, outer_out),
    ]
    finish(cotangents)
    finish(stores)
    for copies in back_steps:
        finish(copies)


def run_forward(size, tokens, cotangent, table, er, ec, rows, gain, shift, cosine, sine, mix_in, mix_in_bias, mix_out, mix_out_bias, number):
    piece = struct((size.per_image, size.piece, size.half), bf16)
    modes = (size.modes, 2 * size.half)
    square = struct((2 * size.half, 2 * size.half), bf16)
    kept = (
        struct((QUARTERS, 2 * size.modes, size.chunk_rows), bf16),
        struct((QUARTERS, size.chunk_rows, 2 * size.modes), bf16),
        square,
        square,
        struct(modes, bf16),
        struct(modes, f32),
        struct(modes, bf16),
        struct(modes, f32),
    )
    row = struct((1, 2 * size.half), f32)
    scratch = (
        (struct(tokens.shape, bf16), table, er, ec)
        + kept
        + (row, row, struct((size.tokens, size.channels), bf16), piece, piece, piece)
        + (struct((2 * size.modes, size.half), f32), struct((2 * size.modes, size.half), bf16))
    )
    small = (rows, gain, shift, cosine, sine, mix_in, mix_in_bias, mix_out, mix_out_bias)
    return call_remote(
        functools.partial(forward_kernel, size),
        "forward",
        number,
        (struct(tokens.shape, bf16), struct(tokens.shape, bf16), piece) + kept,
        [pl.ANY] * 5 + [pltpu.VMEM] * len(small),
        [pl.ANY] * (3 + len(kept)),
        2 * size.per_image + 2 * size.lon,
        24,
        [pltpu.VMEM(v.shape, v.dtype) for v in scratch],
        (tokens, cotangent, table, er, ec) + small,
    )


def add_to(total_ref, other_ref):
    @pl.loop(0, total_ref.shape[0])
    def _(first):
        if len(total_ref.shape) == 3:
            total = total_ref[first].astype(f32) + other_ref[first].astype(f32)
            total_ref[first] = total.astype(total_ref.dtype)
        else:
            for second in range(total_ref.shape[1]):
                total = total_ref[first, second].astype(f32) + other_ref[first, second].astype(f32)
                total_ref[first, second] = total.astype(total_ref.dtype)


def start_same(lon_count, count, source_ref, out_ref, sender, mover):
    me = lax.axis_index("rows") * lon_count + lax.axis_index("lon")
    copies = []
    for offset in range(1, count):
        other = (me + offset) % count
        copies.append(
            sender.start(
                source_ref, out_ref.at[me], {"rows": other // lon_count, "lon": other % lon_count}
            )
        )
    copies.append(mover.start(source_ref, out_ref.at[me]))
    return copies


def backward_kernel(
    size,
    e_hbm,
    dy_hbm,
    inv_t_hbm,
    inv_hbm,
    fc_in_hbm,
    fc_out_hbm,
    lat_hbm,
    lat_t_hbm,
    w1_hbm,
    w2_hbm,
    band_hbm,
    inner_hbm,
    gated_hbm,
    outer_hbm,
    x_hbm,
    table_t_hbm,
    map_ref,
    gain1_ref,
    shift1_ref,
    gain2_ref,
    shift2_ref,
    out_bias_ref,
    fc_in_bias_ref,
    token_out,
    block_out,
    dense_ref,
    mix_out,
    bias_out,
    early_out,
    late_out,
    send_sem,
    recv_sem,
    move_sem,
    x_ref,
    table_t_ref,
    dh_ref,
    send1,
    recv1,
    send2,
    recv2,
    token_ref,
    block_ref,
    wide,
    a_core,
    b_core,
    a_one,
    b_one,
    a_two,
    b_two,
    a_near,
    b_near,
    a_last,
    b_last,
    mix_ref,
    mix_core,
    mix_land,
    pair_ref,
    early,
    early_land,
    late,
    late_land,
):
    channels = size.channels
    lon_count, count, groups = size.lon, size.devices, size.groups
    row = lax.axis_index("rows")
    lon = lax.axis_index("lon")
    me = row * lon_count + lon
    z = row // 2
    x = row % 2
    y = lon // 2
    core = lon % 2
    mine = row % QUARTERS
    group = me % groups
    base = me - group
    half = me // groups
    to_core, to_y, to_x, far_z = partners(lon_count)
    near = z + 1 - 2 * (z % 2)
    mirror = 3 - z
    to_near = {"rows": near * 2 + x, "lon": lon}
    to_mirror = {"rows": mirror * 2 + x, "lon": lon}
    parts = 4

    def order(step):
        first = jnp.where(step < 2, near, mirror)
        return jnp.where(step % 2 == 0, first, 3 - first)

    share = wide.shape[-2]
    sender, mover = Sender(send_sem, recv_sem), Mover(move_sem)

    by_core = [
        [
            sender.make(wide.at[i % 2, 0, :, :, 1 - core], a_core.at[i], to_core),
            sender.make(wide.at[i % 2, 1, :, :, 1 - core], b_core.at[i], to_core),
        ]
        for i in range(parts)
    ]
    by_one = [
        [
            sender.make(a_core.at[i, 1 - x], a_one.at[i], to_x),
            sender.make(b_core.at[i, :, 1 - y], b_one.at[i], to_y),
        ]
        for i in range(parts)
    ]
    by_two = [
        [
            sender.make(a_one.at[i, 1 - y], a_two.at[i], to_y),
            sender.make(b_one.at[i, 1 - x], b_two.at[i], to_x),
        ]
        for i in range(parts)
    ]
    by_near = [
        [
            sender.make(a_two.at[i], a_near.at[i], to_near),
            sender.make(b_two.at[i], b_near.at[i], to_near),
        ]
        for i in range(2)
    ]
    by_early = [
        sender.make(early, early_land.at[i], device)
        for i, device in enumerate((to_core, to_x, to_y, to_near, to_mirror))
    ]
    by_quarter = [make_quarter(size, i, send1, recv1, sender, mover) for i in range(QUARTERS)]
    blocks = make_lon(block_ref, block_out, sender, mover)
    late_loads = [mover.make(x_hbm, x_ref), mover.make(table_t_hbm, table_t_ref)]

    def core_end(step):
        finish(by_core[step])
        add_to(a_core.at[step], wide.at[step % 2, 0, :, :, core])
        by_one[step][0].start()
        add_to(b_core.at[step], wide.at[step % 2, 1, :, :, core])
        by_one[step][1].start()

    def one_end(step):
        by_one[step][0].wait()
        add_to(a_one.at[step], a_core.at[step, x])
        by_two[step][0].start()
        by_one[step][1].wait()
        add_to(b_one.at[step], b_core.at[step, :, y])
        by_two[step][1].start()

    def two_end(step):
        finish(by_two[step])
        for total, kept in ((a_two, a_one.at[step, y]), (b_two, b_one.at[step, x])):
            total[step] = (total[step].astype(f32) + kept[...].astype(f32)).astype(bf16)

    def early_step(step):
        by_early[step].wait()
        early[...] = early[...] + early_land[step]
        if step + 1 < len(by_early):
            by_early[step + 1].start()

    def front(
        e_ref,
        dy_ref,
        inv_t_ref,
        inv_ref,
        fc_in_ref,
        fc_out_ref,
        hidden_ref,
        values_ref,
        grad_ref,
        res_ref,
        acc_ref,
    ):
        part_loads = []
        for step in range(parts):
            place = pl.ds(pl.multiple_of(order(step) * channels, channels), channels)
            part_loads.append(
                [
                    mover.make(fc_in_hbm.at[:, place], fc_in_ref.at[step % 2]),
                    mover.make(fc_out_hbm.at[place, :], fc_out_ref.at[step % 2]),
                ]
            )
        late_loads[0].start()
        loads = [
            mover.start(e_hbm, e_ref),
            mover.start(inv_t_hbm, inv_t_ref),
            mover.start(dy_hbm, dy_ref),
        ]
        begin(part_loads[0])
        begin(part_loads[1])
        inv_load = mover.start(inv_hbm, inv_ref)
        late_loads[1].start()
        greet(lon_count, count)
        finish(loads)
        late_loads[0].wait()
        early[...] = jnp.zeros_like(early)
        early[0:1, :] = residual_planes(
            size, map_ref, e_ref, x_ref, dy_ref, inv_t_ref, as_row(gain1_ref), as_row(shift1_ref), as_row(gain2_ref), as_row(shift2_ref), res_ref, values_ref.at[0], values_ref.at[1]
        )
        acc_ref[...] = jnp.zeros_like(acc_ref)
        dh_ref[...] = jnp.zeros_like(dh_ref)
        up_ref = values_ref.at[1]

        def weights(slot):
            @pl.loop(0, 2)
            def _(which):
                product = t_mm(hidden_ref[slot, which], values_ref[which])
                for i in range(8):
                    wide[slot, which, i // 4, i // 2 % 2, i % 2] = product[
                        i * share : (i + 1) * share
                    ].astype(bf16)

        @pl.loop(0, parts)
        def _(step):
            slot = step % 2
            at(step, parts, lambda i: finish(part_loads[i]))
            place = pl.ds(pl.multiple_of(order(step) * channels, channels), channels)
            hidden, hidden_grad = hidden_part(
                values_ref.at[0], up_ref, fc_in_ref[slot], fc_in_bias_ref[:, place], fc_out_ref[slot], acc_ref, dh_ref
            )
            early[pl.ds(3 + order(step), 1), :] = jnp.sum(
                hidden_grad.astype(f32), axis=0, keepdims=True
            )
            hidden_ref[slot, 0] = hidden_grad
            hidden_ref[slot, 1] = hidden
            at(step, parts - 2, lambda i: begin(part_loads[i + 2]))

            @pl.when(step > 0)
            def _():
                at(step, parts, lambda i: core_end(i - 1) if i else None)

            @pl.when(step < parts - 1)
            def _():
                weights(slot)
                at(step, parts - 1, lambda i: begin(by_core[i]))

            @pl.when(step == 2)
            def _():
                one_end(0)

            @pl.when(step == 3)
            def _():
                one_end(1)
                two_end(0)
                begin(by_near[0])

        gain_sum, shift_sum = residual_back_planes(size, up_ref, res_ref, as_row(gain2_ref), dh_ref, grad_ref)
        early[1:2, :] = gain_sum
        early[2:3, :] = shift_sum
        inv_load.wait()

        def send_spectrum(step):
            quarter = (mine + step) % QUARTERS
            write_quarter(size, quarter, mm(inv_ref[quarter], grad_ref[...]), send1)
            at(step, QUARTERS, lambda i: begin(by_quarter[i]))

        over_quarters(send_spectrum)
        by_early[0].start()
        weights((parts - 1) % 2)
        begin(by_core[parts - 1])
        two_end(1)
        begin(by_near[1])
        one_end(2)
        block_planes(size, map_ref, res_ref, acc_ref, as_row(out_bias_ref), block_ref)
        core_end(parts - 1)
        early_step(0)

    def back(
        lat_ref,
        lat_t_ref,
        w1_ref,
        w2_ref,
        band_ref,
        inner_ref,
        gated_ref,
        outer_ref,
        outer_grad_ref,
        inner_grad_ref,
        modes_ref,
        stacked_ref,
        filtered_ref,
    ):
        loads = [
            mover.start(source, target)
            for source, target in (
                (lat_hbm, lat_ref),
                (outer_hbm, outer_ref),
                (w2_hbm, w2_ref),
                (inner_hbm, inner_ref),
                (w1_hbm, w1_ref),
                (lat_t_hbm, lat_t_ref),
                (gated_hbm, gated_ref),
                (band_hbm, band_ref),
            )
        ]
        two_end(2)
        finish(loads)
        modes_ref[...] = jnp.zeros_like(modes_ref)

        def receive(step):
            at(step, QUARTERS, lambda i: finish(by_quarter[i]))
            add_modes(size, (mine + QUARTERS - step) % QUARTERS, recv1, lat_ref, modes_ref)

        over_quarters(receive)

        finish(by_near[1])
        for total, landed in ((a_two, a_near), (b_two, b_near)):
            total[2] = (total[2].astype(f32) + landed[1].astype(f32)).astype(bf16)
        hops = [
            sender.start(a_two.at[2], a_last, to_mirror),
            sender.start(b_two.at[2], b_last, to_mirror),
        ]
        begin(blocks)
        mix_layers_back(size, modes_ref, w1_ref, w2_ref, inner_ref, outer_ref, outer_grad_ref, inner_grad_ref, stacked_ref)
        steps = [make_quarter(size, i, send2, recv2, sender, mover) for i in range(QUARTERS)]

        def send_back(step):
            mix_quarter_back(size, (mine + step) % QUARTERS, lat_t_ref, stacked_ref, send2)
            at(step, QUARTERS, lambda i: begin(steps[i]))

        over_quarters(send_back)
        one_end(parts - 1)
        early_step(1)

        mix_back_weights(size, band_ref, gated_ref, outer_grad_ref, inner_grad_ref, mix_ref)
        crossing = sender.start(mix_ref.at[:, 1 - core], mix_core, to_core)
        two_end(parts - 1)
        crossing.wait()
        add_to(mix_core, mix_ref.at[:, core])
        pair = group // 2
        mixes = []
        for offset in range(1, groups // 2):
            other = (pair + offset) % (groups // 2)
            device = base + other * 2 + core
            mixes.append(
                sender.start(
                    mix_core.at[other],
                    mix_land.at[pair],
                    {"rows": device // lon_count, "lon": device % lon_count},
                )
            )
        mixes.append(mover.start(mix_core.at[pair], mix_land.at[pair]))

        finish(by_near[0])
        early_step(2)
        finish(mixes)
        total = mix_land[0].astype(f32)
        for index in range(1, groups // 2):
            total = total + mix_land[index].astype(f32)
        pair_ref[half] = total.astype(bf16)
        crossing = sender.start(pair_ref.at[half], pair_ref.at[half], far_z)

        for copies in steps:
            finish(copies)
        crossing.wait()
        block_size = mix_out.shape[-1]
        rest = bias_out.shape[-2]
        own_place = (pair // 4, pair // 2 % 2, slice(None), pair % 2, core)
        gather = []
        for source, target in (
            (pair_ref.at[:, pl.ds(0, block_size)], mix_out.at[own_place]),
            (pair_ref.at[:, pl.ds(block_size, rest)], bias_out.at[own_place]),
        ):
            for offset in range(1, groups // 2):
                device = base + (pair + offset) % (groups // 2) * 2 + core
                gather.append(
                    sender.start(
                        source, target, {"rows": device // lon_count, "lon": device % lon_count}
                    )
                )
            gather.append(mover.start(source, target))
        tokens = make_lon(token_ref, token_out, sender, mover)
        last_planes(
            size, recv2, x_ref, dh_ref, table_t_ref, gain1_ref, filtered_ref, token_ref, late, lon + 1, lambda i: tokens[i].start()
        )
        smalls = start_same(lon_count, count, late, late_land, sender, mover)
        early_step(3)
        finish(hops)
        for place, total, landed, last in ((0, a_two, a_near, a_last), (1, b_two, b_near, b_last)):
            dense_ref[place] = (
                total[3].astype(f32) + landed[0].astype(f32) + last[...].astype(f32)
            )
        finish(gather)
        gather = []
        for ref in (mix_out, bias_out):
            own_core = ref.at[:, :, :, :, core]
            gather.append(sender.start(own_core, own_core, to_core))
        finish(smalls)
        total = late_land[0]
        for index in range(1, count):
            total = total + late_land[index]
        late_out[...] = total
        early_step(4)
        early_out[...] = early[...]
        finish(gather)
        finish(blocks)
        finish(tokens)

    piece = send1.shape
    tokens = dh_ref.shape
    square = (2, channels, channels)
    pl.run_scoped(
        front,
        pltpu.VMEM(piece, bf16),
        pltpu.VMEM(x_ref.shape, bf16),
        pltpu.VMEM(inv_t_hbm.shape, bf16),
        pltpu.VMEM(inv_hbm.shape, bf16),
        pltpu.VMEM(square, bf16),
        pltpu.VMEM(square, bf16),
        pltpu.VMEM((2, 2) + tokens, bf16),
        pltpu.VMEM((2,) + tokens, bf16),
        pltpu.VMEM(tokens, bf16),
        pltpu.VMEM(tokens, f32),
        pltpu.VMEM(tokens, f32),
    )
    modes = (2 * size.modes, size.half)
    late_loads[1].wait()
    pl.run_scoped(
        back,
        *[
            pltpu.VMEM(ref.shape, ref.dtype)
            for ref in (lat_hbm, lat_t_hbm, w1_hbm, w2_hbm, band_hbm, inner_hbm, gated_hbm, outer_hbm)
        ],
        pltpu.VMEM(band_hbm.shape, bf16),
        pltpu.VMEM(band_hbm.shape, bf16),
        pltpu.VMEM(modes, f32),
        pltpu.VMEM(modes, bf16),
        pltpu.VMEM(tokens, f32),
    )


def run_backward(size, blocks_shape, e, dy, inv_t, inv, fc_in, fc_out, lat, lat_t, w1, w2, band, inner, gated, outer, x, table_t, row_map, vectors, fc_in_bias, number):
    parts = fc_out.shape[0] // size.channels
    plane = (fc_out.shape[0] // size.devices, size.channels)
    large = (e, dy, inv_t, inv, fc_in, fc_out, lat, lat_t, w1, w2, band, inner, gated, outer, x, table_t)
    early = (round_up(3 + parts, 8), size.channels)
    late = (2, size.channels)
    block = blocks_shape[1:]
    half_blocks = (blocks_shape[0] // 2,) + block

    scratch = [pltpu.VMEM(x.shape, bf16), pltpu.VMEM(table_t.shape, bf16)]
    scratch += [pltpu.VMEM((size.tokens, size.channels), f32)]
    scratch += [pltpu.VMEM(e.shape, bf16)] * 4
    scratch += [pltpu.VMEM(x.shape, bf16)] * 2
    scratch += [pltpu.VMEM((2, 2, 2, 2, 2) + plane, bf16)]
    for lead in ((4, 2, 2), (4, 2), (4,), (2,), ()):
        scratch += [pltpu.VMEM(lead + plane, bf16)] * 2
    scratch += [pltpu.VMEM((blocks_shape[0] // 2, 2) + block, bf16)]
    scratch += [pltpu.VMEM(half_blocks, bf16)] * 2
    scratch += [pltpu.VMEM((HALVES,) + block, bf16)]
    scratch += [pltpu.VMEM(early, f32), pltpu.VMEM((5,) + early, f32)]
    scratch += [pltpu.VMEM(late, f32), pltpu.VMEM((size.devices,) + late, f32)]
    return call_remote(
        functools.partial(backward_kernel, size),
        "mlp_backward",
        number,
        (
            struct(x.shape, bf16),
            struct(x.shape, bf16),
            struct((2,) + plane, f32),
            struct((2, 2, HALVES, blocks_shape[0] // 8, 2) + block[1:] * 2, bf16),
            struct((2, 2, HALVES, blocks_shape[0] // 8, 2, block[0] - block[1], block[1]), bf16),
            struct(early, f32),
            struct(late, f32),
        ),
        [pl.ANY] * len(large) + [pltpu.SMEM] + [pltpu.VMEM] * (len(vectors) + 1),
        [pl.ANY] * 2 + [pltpu.VMEM] * 5,
        3 * size.devices + 2 * size.groups + 2 * size.lon + 48,
        48,
        scratch,
        large + (row_map,) + vectors + (fc_in_bias,),
    )


def exchange_lon(values):
    return lax.all_to_all(values, "lon", split_axis=0, concat_axis=0, tiled=True)


def exchange_all(values):
    return lax.all_to_all(values, ("rows", "lon"), split_axis=0, concat_axis=0, tiled=True)


def to_modes(size, pieces, row_map):
    order, place = place_order(size)
    sent = jnp.tile(jnp.take(pieces, place, axis=0), (size.images, 1, 1))
    received = exchange_all(sent)
    used = size.slots_here * 2 * size.waves
    by_slot = received[:, :used].reshape(-1, 2 * size.waves, size.half)
    image = (lax.axis_index("rows") * size.lon + lax.axis_index("lon")) // size.per_image
    slots = row_map.shape[0]
    target = jnp.where(row_map >= 0, row_map, size.images * H)
    slot_of_row = (
        jnp.zeros((size.images * H,), jnp.int32)
        .at[target]
        .set(jnp.arange(slots, dtype=jnp.int32), mode="drop")
    )
    own = lax.dynamic_slice_in_dim(slot_of_row, image * H, H)
    picked = jnp.take(by_slot, own, axis=0)
    picked = jnp.pad(picked, ((0, size.virtual_slots - H), (0, 0), (0, 0)))
    picked = picked.reshape(size.per_image, used, size.half)
    return jnp.take(jnp.pad(picked, ((0, 0), (0, size.piece - used), (0, 0))), order, axis=0)


def from_modes(size, pieces, row_map):
    order, place = place_order(size)
    used = size.slots_here * 2 * size.waves
    by_lat = jnp.take(pieces, place, axis=0)[:, :used].reshape(-1, 2 * size.waves, size.half)
    image = (lax.axis_index("rows") * size.lon + lax.axis_index("lon")) // size.per_image
    live = (row_map >= 0) & (row_map // H == image)
    picked = jnp.take(by_lat, jnp.where(live, row_map % H, 0), axis=0)
    picked = picked * live.astype(bf16)[:, None, None]
    picked = picked.reshape(size.devices, used, size.half)
    sent = jnp.pad(picked, ((0, 0), (0, size.piece - used), (0, 0)))
    received = exchange_all(sent)
    received = received.reshape(size.images, size.per_image, size.piece, size.half)
    return jnp.take(jnp.sum(received.astype(f32), axis=0).astype(bf16), order, axis=0)


def body(
    tokens,
    row_map,
    cotangent,
    norm_gain,
    norm_shift,
    mix_in,
    mix_in_bias,
    mix_out,
    mix_out_bias,
    post_gain,
    post_shift,
    fc_in,
    fc_in_bias,
    fc_out,
    fc_out_bias,
):
    size = Sizes(
        lax.axis_size("rows"), lax.axis_size("lon"), row_map.shape[0], tokens.shape[2]
    )
    channels = size.channels
    blocks = mix_in.shape[1]
    blocks_here = blocks // HALVES
    block_size = mix_in.shape[2]
    hidden_units = fc_in.shape[1]
    device = lax.axis_index("rows") * size.lon + lax.axis_index("lon")
    half_index = (device % size.per_image) // size.groups

    table, table_t, inv, inv_t = [jnp.asarray(t) for t in lon_tables(size)]
    table = table.reshape(QUARTERS, size.spectrum // QUARTERS, size.tokens)
    cosine, sine, er, ec = [jnp.asarray(t) for t in lat_parts(size)]
    if size.images == 1:
        slot_lat = row_map
    else:
        slot_lat = jnp.where(jnp.arange(size.virtual_slots) < H, jnp.arange(size.virtual_slots), -1)
    rows = slot_lat
    shape = (size.lon, size.slots_here, size.lons_here, channels)
    x, dy = tokens.reshape(shape), cotangent.reshape(shape)
    piece_shape = struct((size.per_image, size.piece, size.half), bf16)
    mode_shape = (size.modes, 2 * size.half)
    wide_modes = (2 * size.modes, size.half)
    mode_scratch = [pltpu.VMEM(wide_modes, f32), pltpu.VMEM(wide_modes, bf16)]
    if size.images == 1:
        x, dy, received, lat, lat_t, w1, w2, band, inner, gated, outer = run_forward(
            size, x, dy, table, er, ec, rows, norm_gain, norm_shift, cosine, sine, mix_in, mix_in_bias, mix_out, mix_out_bias, 0
        )
    else:
        square = struct((2 * size.half, 2 * size.half), bf16)
        flat = struct((1, 2 * size.half), f32)
        lat, lat_t, w1, w2, b1, b2 = call_local(
            functools.partial(prepare_kernel, size),
            "prepare",
            (
                struct((QUARTERS, 2 * size.modes, size.chunk_rows), bf16),
                struct((QUARTERS, size.chunk_rows, 2 * size.modes), bf16),
                square,
                square,
                flat,
                flat,
            ),
        )(rows, cosine, sine, er, ec, mix_in, mix_in_bias, mix_out, mix_out_bias)
        x, dy = exchange_lon(x), exchange_lon(dy)
        sent = call_local(
            functools.partial(first_kernel, size),
            "lon_forward",
            piece_shape,
            [pltpu.VMEM((size.tokens, channels), bf16)],
        )(x, norm_gain, norm_shift, table)
        received = to_modes(size, sent, row_map)
        sent, band, inner, gated, outer = call_local(
            functools.partial(mix_kernel, size),
            "mix_forward",
            (
                piece_shape,
                struct(mode_shape, bf16),
                struct(mode_shape, f32),
                struct(mode_shape, bf16),
                struct(mode_shape, f32),
            ),
            mode_scratch,
        )(received, lat, lat_t, w1, b1, w2, b2)
        received = from_modes(size, sent, row_map)
    vectors = (norm_gain, norm_shift, post_gain, post_shift, fc_out_bias)
    blocks_shape = (4 * blocks_here, round_up(block_size + 1, 16), block_size)
    bias_row = fc_in_bias.reshape(1, -1)
    if size.images == 1:
        token_grad, block, dense, mix_total, mix_bias, early, late = run_backward(
            size, blocks_shape, received, dy, inv_t, inv.reshape(table.shape), fc_in, fc_out, lat, lat_t, w1, w2, band, inner, gated, outer, x, table_t, row_map, vectors, bias_row, 1
        )
    else:
        names = ("rows", "lon")
        block, dh, sent, hidden, hidden_grad, low, up, early = run_mlp(
            size, hidden_units, row_map, received, x, dy, inv_t, inv, vectors, fc_in, bias_row, fc_out
        )
        early = lax.psum(early, names)
        wide = call_local(
            wide_kernel, "weights_backward", struct((hidden_units, 2 * channels), bf16)
        )(hidden, hidden_grad, low, up)
        dense = lax.psum_scatter(wide, names, scatter_dimension=0, tiled=True)
        dense = jnp.stack([dense[:, :channels], dense[:, channels:]]).astype(f32)
        block = exchange_lon(block)
        received = to_modes(size, sent, row_map)
        sent, mix_grad = call_local(
            functools.partial(mix_back_kernel, size),
            "mix_backward",
            (piece_shape, struct(blocks_shape, bf16)),
            [pltpu.VMEM(mode_shape, bf16)] * 2 + mode_scratch,
        )(received, lat, lat_t, w1, w2, band, inner, gated, outer)
        mix_grad = mix_grad.astype(f32).reshape((2, 2, 1, blocks_here) + blocks_shape[1:])
        mix_total = lax.psum(
            jnp.concatenate(
                [mix_grad * (half_index == other).astype(f32) for other in range(HALVES)], axis=2
            ),
            names,
        )
        mix_bias = mix_total[..., block_size:, :]
        mix_total = mix_total[..., :block_size, :]
        received = from_modes(size, sent, row_map)
        token_grad, late = call_local(
            functools.partial(last_kernel, size),
            "lon_backward",
            (struct(x.shape, bf16), struct((2, channels), f32)),
            [pltpu.VMEM((size.tokens, channels), f32)],
        )(received, x, dh, table_t, norm_gain)
        token_grad = exchange_lon(token_grad)
        late = lax.psum(late, names)
    share = hidden_units // size.devices
    return (
        block.reshape(tokens.shape),
        token_grad.reshape(tokens.shape).astype(f32),
        late[0],
        late[1],
        mix_total[0].reshape(mix_in.shape).astype(f32),
        mix_bias[0, ..., 0, :].reshape(mix_in_bias.shape).astype(f32),
        mix_total[1].reshape(mix_in.shape).astype(f32),
        mix_bias[1, ..., 0, :].reshape(mix_out_bias.shape).astype(f32),
        early[1],
        early[2],
        dense[0].T,
        lax.dynamic_slice_in_dim(early[3:7].reshape(-1), device * share, share),
        dense[1],
        early[0],
    )


def solution(mesh):
    return jax.shard_map(
        body,
        mesh=mesh,
        in_specs=(P("rows", "lon", None), P(), P("rows", "lon", None)) + (P(),) * 12,
        out_specs=(
            P("rows", "lon", None),
            P("rows", "lon", None),
            P(),
            P(),
            P(),
            P(),
            P(),
            P(),
            P(),
            P(),
            P(None, ("rows", "lon")),
            P(("rows", "lon")),
            P(("rows", "lon"), None),
            P(),
        ),
        check_vma=False,
    )
```

```python
import functools
import math
import types

import jax
import jax.numpy as jnp
import ml_dtypes
import numpy as np
from jax import lax
from jax.experimental import pallas as pl
from jax.experimental.pallas import tpu as pltpu
from jax.sharding import PartitionSpec as P

H = 90
W = 180
KX = 91
HALVES = 2
SPLIT = 1 / 2
VMEM_BYTES = 58 * 1024 * 1024

norm_eps = 1e-06
shrink_level = 0.01
half_root = 0.7071067811865476
normal_peak = 0.3989422804014327
MESH = pl.DeviceIdType.MESH
f32 = jnp.float32
bf16 = jnp.bfloat16


def round_up(value, step):
    return -(-value // step) * step


class Stage:
    def __init__(self, size, slots, first_row):
        self.slots = slots
        self.rows = size.lon * len(slots) * size.lons_pad
        self.first_row = first_row
        self.part = slice(first_row, first_row + self.rows)
        self.used = len(slots) * 2 * size.waves
        self.piece = round_up(self.used, 8)
        self.spectrum = size.groups * self.piece
        self.band = size.per_image * self.piece


class Sizes:
    def __init__(self, rows_count, lon_count, slots, channels):
        self.rows = rows_count
        self.lon = lon_count
        self.devices = rows_count * lon_count
        self.images = slots * 15 // (16 * H)
        self.per_image = self.devices // self.images
        self.groups = self.per_image // HALVES
        self.waves = -(-KX // self.groups)
        self.slots_here = slots // self.devices
        self.lons_here = W // lon_count
        self.lons_pad = round_up(self.lons_here, 16)
        self.tokens = lon_count * self.slots_here * self.lons_pad
        self.modes = round_up(H * self.waves, 16)
        self.virtual_slots = self.per_image * self.slots_here
        self.channels = channels
        self.half = channels // HALVES
        cut = -(-self.slots_here * 2 // 3)
        self.stages = []
        first_row = 0
        for low, high in ((0, cut), (cut, self.slots_here)):
            if low < high:
                self.stages.append(Stage(self, tuple(range(low, high)), first_row))
                first_row += self.stages[-1].rows


def lon_tables(size):
    wave = np.arange(size.groups * size.waves)
    lon_index = np.arange(W)
    product = (lon_index[:, None] * wave[None, :]) % W
    angle = product.astype(np.float32) * np.float32(2.0 * math.pi / W)
    scale = np.float32(1.0 / math.sqrt(W))
    cosine = (np.cos(angle) * scale).astype(ml_dtypes.bfloat16).astype(np.float32)
    sine = (-np.sin(angle) * scale).astype(ml_dtypes.bfloat16).astype(np.float32)
    live = (wave < KX).astype(np.float32)
    factor = np.where((wave == 0) | (wave == W // 2), 1.0, 2.0).astype(np.float32)
    both = np.stack([cosine, sine]) * live
    result = []
    for weight in (np.ones_like(factor), factor):
        values = (both * weight).reshape(2, size.lon, size.lons_here, size.groups, size.waves)
        values = np.transpose(values, (3, 0, 4, 1, 2)).reshape(
            size.groups, 2 * size.waves, size.lon, size.lons_here
        )
        tables = []
        for stage in size.stages:
            count = len(stage.slots)
            table = np.zeros(
                (size.groups, stage.piece, size.lon, count, size.lons_pad), np.float32
            )
            for slot in range(count):
                start = slot * 2 * size.waves
                table[:, start : start + 2 * size.waves, :, slot, : size.lons_here] = values
            tables.append(table.reshape(stage.spectrum, stage.rows).astype(ml_dtypes.bfloat16))
        result.append([jnp.asarray(t) for t in tables])
        result.append([jnp.asarray(np.ascontiguousarray(t.T)) for t in tables])
    return result


def lat_parts(size):
    lat_index = np.arange(H)
    angle = ((lat_index[:, None] * lat_index[None, :]) % H).astype(np.float32) * np.float32(
        2.0 * math.pi / H
    )
    scale = np.float32(1.0 / math.sqrt(H))
    cosine = np.zeros((96, 96), np.float32)
    sine = np.zeros((96, 96), np.float32)
    cosine[:H, :H] = np.cos(angle) * scale
    sine[:H, :H] = np.sin(angle) * scale
    spread_rows = np.zeros((2, size.modes, 2, 96), np.float32)
    for part in range(2):
        for lat in range(H):
            for wave in range(size.waves):
                spread_rows[part, lat * size.waves + wave, part, lat] = 1.0
    spread_cols = []
    for stage in size.stages:
        spread = np.zeros((2, 128, size.per_image, stage.piece), np.float32)
        for device in range(size.per_image):
            for place, slot in enumerate(stage.slots):
                for part in range(2):
                    start = (place * 2 + part) * size.waves
                    spread[
                        part, device * size.slots_here + slot, device, start : start + size.waves
                    ] = 1.0
        spread_cols.append(spread.reshape(256, stage.band))
    low = ml_dtypes.bfloat16
    return (
        jnp.asarray(cosine.astype(low)),
        jnp.asarray(sine.astype(low)),
        jnp.asarray(spread_rows.reshape(2 * size.modes, 192).astype(low)),
        [jnp.asarray(spread.astype(low)) for spread in spread_cols],
    )


def smooth_gate(values):
    return 0.5 * values * (1.0 + lax.erf(values * half_root))


def gate_both(values):
    half_phi = 0.5 * (1.0 + lax.erf(values * half_root))
    density = values * normal_peak * jnp.exp(-0.5 * values * values)
    return values * half_phi, half_phi + density


def gate_slope(values):
    return gate_both(values)[1]


def soft_shrink(values):
    return values - shrink_level * values * lax.rsqrt(values * values + shrink_level * shrink_level)


def shrink_slope(values):
    inverse = lax.rsqrt(values * values + shrink_level * shrink_level)
    return 1.0 - shrink_level * shrink_level * shrink_level * inverse * inverse * inverse


def norm_parts(values):
    center = values - jnp.mean(values, axis=-1, keepdims=True)
    spread = lax.rsqrt(jnp.mean(center * center, axis=-1, keepdims=True) + norm_eps)
    return center * spread, spread


def norm_back(scaled, unit, spread):
    return spread * (
        scaled
        - jnp.mean(scaled, axis=-1, keepdims=True)
        - unit * jnp.mean(scaled * unit, axis=-1, keepdims=True)
    )


def mm(left, right):
    return jnp.dot(left, right, preferred_element_type=f32)


def mm_t(left, right):
    return lax.dot_general(left, right, (((1,), (1,)), ((), ())), preferred_element_type=f32)


def t_mm(left, right):
    return lax.dot_general(left, right, (((0,), (0,)), ((), ())), preferred_element_type=f32)


def whole(count):
    return [pl.BlockSpec(memory_space=pltpu.VMEM)] * count


def call_local(kernel, name, outs, scratch=()):
    def run(*operands):
        return pl.pallas_call(
            kernel,
            out_shape=outs,
            in_specs=whole(len(operands)),
            out_specs=jax.tree.map(lambda _: pl.BlockSpec(memory_space=pltpu.VMEM), outs),
            scratch_shapes=list(scratch),
            compiler_params=pltpu.CompilerParams(vmem_limit_bytes=VMEM_BYTES),
            name=name,
        )(*operands)

    return run


def struct(shape, dtype):
    return jax.ShapeDtypeStruct(shape, dtype)


def wave_of(index, period, used, waves, other):
    within = index - period * jnp.floor((index + 0.5) * (1.0 / period))
    wave = within - waves * jnp.floor((within + 0.5) * (1.0 / waves))
    return jnp.where(within < used, wave, other)


def build_lat_tables(size, rows_ref, cos_ref, sin_ref, er_ref, ec_refs, lat_refs, lat_t_refs):
    slots = rows_ref.shape[0]
    lat_of = lax.broadcasted_iota(jnp.int32, (96, slots), 0)
    hot = (lat_of == rows_ref[...].reshape(1, slots)).astype(f32)
    hot = jnp.concatenate([hot, jnp.zeros((96, 128 - slots), f32)], axis=1).astype(bf16)
    cosine = mm(cos_ref[...], hot)
    sine = mm(sin_ref[...], hot)
    top = jnp.concatenate([cosine, sine], axis=1)
    bottom = jnp.concatenate([-sine, cosine], axis=1)
    base = jnp.concatenate([top, bottom], axis=0).astype(bf16)

    def row_waves(shape, dim):
        index = lax.broadcasted_iota(jnp.int32, shape, dim).astype(f32)
        return wave_of(index, size.modes, H * size.waves, size.waves, -1.0)

    def col_waves(stage, shape, dim):
        index = lax.broadcasted_iota(jnp.int32, shape, dim).astype(f32)
        return wave_of(index, stage.piece, stage.used, size.waves, -2.0)

    modes = 2 * size.modes
    for stage, ec_ref, lat_ref, lat_t_ref in zip(size.stages, ec_refs, lat_refs, lat_t_refs):
        keep = row_waves((modes, 1), 0) == col_waves(stage, (1, stage.band), 1)
        keep_t = col_waves(stage, (stage.band, 1), 0) == row_waves((1, modes), 1)
        columns = mm(base, ec_ref[...]).astype(bf16)
        lat_ref[...] = jnp.where(keep, mm(er_ref[...], columns), 0.0).astype(bf16)
        table_t = lax.dot_general(
            columns, er_ref[...], (((0,), (1,)), ((), ())), preferred_element_type=f32
        )
        lat_t_ref[...] = jnp.where(keep_t, table_t, 0.0).astype(bf16)


def build_block_matrix(size, weight_ref, bias_ref, half, matrix_ref, row_ref):
    block_size = weight_ref.shape[2]
    blocks = size.half // block_size
    matrix_ref[...] = jnp.zeros_like(matrix_ref)
    for block in range(blocks):
        real = weight_ref[0, half * blocks + block]
        imag = weight_ref[1, half * blocks + block]
        near = slice(block * block_size, (block + 1) * block_size)
        far = slice(size.half + block * block_size, size.half + (block + 1) * block_size)
        matrix_ref[near, near] = real
        matrix_ref[near, far] = imag
        matrix_ref[far, near] = -imag
        matrix_ref[far, far] = real
        row_ref[0:1, near] = bias_ref[0, pl.ds(half * blocks + block, 1), :]
        row_ref[0:1, far] = bias_ref[1, pl.ds(half * blocks + block, 1), :]


def half_of(size):
    device = lax.axis_index("rows") * size.lon + lax.axis_index("lon")
    return (device % size.per_image) // size.groups


def pad_plane(size, plane):
    extra = size.lons_pad - size.lons_here
    return jnp.concatenate([plane, jnp.zeros((extra, plane.shape[1]), plane.dtype)], axis=0)


def at(step, count, action):
    for i in range(count):

        @pl.when(step == i)
        def _():
            action(i)


def over_planes(size, stage, body, *sums, first=0, then=None):
    def step(index, sums):
        source = (first + index) % size.lon
        for place, slot in enumerate(stage.slots):
            start = stage.first_row + pl.multiple_of(
                (source * len(stage.slots) + place) * size.lons_pad, size.lons_pad
            )
            start = pl.multiple_of(start, size.lons_pad)
            sums = body(source, slot, pl.ds(start, size.lons_pad), *sums)
        if then is not None:
            at(index, size.lon, then)
        return sums

    return lax.fori_loop(0, size.lon, step, sums)


def as_row(ref):
    return ref[...].reshape(1, -1)


def write_pieces(size, stage, values, out_ref):
    for half in range(HALVES):
        for group in range(size.groups):
            out_ref[half * size.groups + group] = values[
                group * stage.piece : (group + 1) * stage.piece,
                half * size.half : (half + 1) * size.half,
            ].astype(bf16)


def read_pieces(ref, first, count):
    return jnp.concatenate([ref[first + i].astype(f32) for i in range(count)], axis=0).astype(bf16)


def read_spectrum(size, ref):
    return jnp.concatenate(
        [read_pieces(ref, half * size.groups, size.groups) for half in range(HALVES)], axis=1
    )


def first_norm(size, stage, x_ref, gain, shift, low_ref):
    def plane(source, slot, rows):
        x = pad_plane(size, x_ref[source, slot].astype(f32))
        unit, _ = norm_parts(x)
        low_ref[rows, :] = (unit * gain + shift).astype(bf16)
        return ()

    over_planes(size, stage, plane)


def first_kernel(size, x_ref, gain_ref, shift_ref, *refs):
    count = len(size.stages)
    tables, sends, low_ref = refs[:count], refs[count : 2 * count], refs[-1]
    for stage, table_ref, send_ref in zip(size.stages, tables, sends):
        first_norm(size, stage, x_ref, as_row(gain_ref), as_row(shift_ref), low_ref)
        write_pieces(size, stage, mm(table_ref[...], low_ref[stage.part, :]), send_ref)


def add_modes(size, recv_ref, lat_ref, modes_ref):
    modes_ref[...] += mm(lat_ref[...], read_pieces(recv_ref, 0, size.per_image))


def side_by_side(size, modes_ref):
    return jnp.concatenate(
        [modes_ref[: size.modes, :], modes_ref[size.modes :, :]], axis=1
    ).astype(bf16)


def stack_parts(size, values, stacked_ref):
    stacked_ref[: size.modes, :] = values[:, : size.half].astype(bf16)
    stacked_ref[size.modes :, :] = values[:, size.half :].astype(bf16)


def modes_back(size, stage, lat_t_ref, stacked_ref, send_ref):
    back = mm(lat_t_ref[...], stacked_ref[...])
    for device in range(size.per_image):
        send_ref[device] = back[device * stage.piece : (device + 1) * stage.piece].astype(bf16)


def mix_layers(size, modes_ref, w1_ref, b1_ref, w2_ref, b2_ref, band_ref, inner_ref, gated_ref, outer_ref, stacked_ref):
    band = side_by_side(size, modes_ref)
    band_ref[...] = band
    inner = mm(band, w1_ref[...]) + b1_ref[...]
    inner_ref[...] = inner
    gated = smooth_gate(inner).astype(bf16)
    gated_ref[...] = gated
    outer = mm(gated, w2_ref[...]) + b2_ref[...]
    outer_ref[...] = outer
    stack_parts(size, soft_shrink(outer), stacked_ref)


def mix_kernel(size, w1_ref, b1_ref, w2_ref, b2_ref, *refs):
    count = len(size.stages)
    recvs, lats, lats_t, sends = [refs[i * count : (i + 1) * count] for i in range(4)]
    band_ref, inner_ref, gated_ref, outer_ref, modes_ref, stacked_ref = refs[4 * count :]
    modes_ref[...] = jnp.zeros_like(modes_ref)
    for recv_ref, lat_ref in zip(recvs, lats):
        add_modes(size, recv_ref, lat_ref, modes_ref)
    mix_layers(size, modes_ref, w1_ref, b1_ref, w2_ref, b2_ref, band_ref, inner_ref, gated_ref, outer_ref, stacked_ref)
    for stage, lat_t_ref, send_ref in zip(size.stages, lats_t, sends):
        modes_back(size, stage, lat_t_ref, stacked_ref, send_ref)


def mix_layers_back(size, modes_ref, w1_ref, w2_ref, inner_ref, outer_ref, outer_grad_ref, inner_grad_ref, stacked_ref):
    upstream = side_by_side(size, modes_ref)
    outer_grad = (upstream.astype(f32) * shrink_slope(outer_ref[...])).astype(bf16)
    outer_grad_ref[...] = outer_grad
    inner_grad = (mm_t(outer_grad, w2_ref[...]) * gate_slope(inner_ref[...])).astype(bf16)
    inner_grad_ref[...] = inner_grad
    stack_parts(size, mm_t(inner_grad, w1_ref[...]), stacked_ref)


def mix_back_weights(size, band_ref, gated_ref, outer_grad_ref, inner_grad_ref, out_ref):
    half = size.half
    block_size = out_ref.shape[-1]
    blocks = half // block_size
    rest = out_ref.shape[-2] - block_size
    for layer, (value_ref, grad_ref) in enumerate(
        ((band_ref, inner_grad_ref), (gated_ref, outer_grad_ref))
    ):
        grad = grad_ref[...]
        total = t_mm(value_ref[...], grad)
        bias = jnp.sum(grad.astype(f32), axis=0, keepdims=True)
        for block in range(blocks):
            near = slice(block * block_size, (block + 1) * block_size)
            far = slice(half + block * block_size, half + (block + 1) * block_size)
            for part, values, row in (
                (0, total[near, near] + total[far, far], bias[:, near]),
                (1, total[near, far] - total[far, near], bias[:, far]),
            ):
                place = (layer * 2 + part) * blocks + block
                at = (place // 2, place % 2) if len(out_ref.shape) == 4 else (place,)
                out_ref[at + (slice(0, block_size),)] = values.astype(bf16)
                out_ref[at + (slice(block_size, None),)] = jnp.broadcast_to(
                    row, (rest, block_size)
                ).astype(bf16)


def mix_back_kernel(size, w1_ref, w2_ref, band_ref, inner_ref, gated_ref, outer_ref, *refs):
    count = len(size.stages)
    recvs, lats, lats_t, sends = [refs[i * count : (i + 1) * count] for i in range(4)]
    grad_ref, outer_grad_ref, inner_grad_ref, modes_ref, stacked_ref = refs[4 * count :]
    modes_ref[...] = jnp.zeros_like(modes_ref)
    for recv_ref, lat_ref in zip(recvs, lats):
        add_modes(size, recv_ref, lat_ref, modes_ref)
    mix_layers_back(size, modes_ref, w1_ref, w2_ref, inner_ref, outer_ref, outer_grad_ref, inner_grad_ref, stacked_ref)
    for stage, lat_t_ref, send_ref in zip(size.stages, lats_t, sends):
        modes_back(size, stage, lat_t_ref, stacked_ref, send_ref)
    mix_back_weights(size, band_ref, gated_ref, outer_grad_ref, inner_grad_ref, grad_ref)


def live_of(size, map_ref, slot):
    first_slot = (lax.axis_index("rows") * size.lon + lax.axis_index("lon")) * size.slots_here
    return jnp.where(map_ref[first_slot + slot] >= 0, 1.0, 0.0)


def residual_planes(size, stage, map_ref, recv_ref, x_ref, dy_ref, inv_t_ref, gain1, shift1, gain2, shift2, res_ref, values_ref):
    res_ref[stage.part, :] = mm(inv_t_ref[...], read_spectrum(size, recv_ref))

    def plane(source, slot, rows, up_sum):
        x = pad_plane(size, x_ref[source, slot].astype(f32))
        unit, _ = norm_parts(x)
        residual = res_ref[rows, :] + (unit * gain1 + shift1) + x
        res_ref[rows, :] = residual
        unit, _ = norm_parts(residual)
        values_ref[0, rows, :] = (unit * gain2 + shift2).astype(bf16)
        up = pad_plane(size, dy_ref[source, slot].astype(f32) * live_of(size, map_ref, slot))
        values_ref[1, rows, :] = up.astype(bf16)
        return (up_sum + jnp.sum(up, axis=0, keepdims=True),)

    return over_planes(size, stage, plane, jnp.zeros((1, size.channels), f32))[0]


def hidden_part(part, values_ref, fc_in, bias, fc_out, acc_ref, back_ref):
    gate, slope = gate_both(mm(values_ref[0, part, :], fc_in) + bias)
    hidden = gate.astype(bf16)
    acc_ref[part, :] += mm(hidden, fc_out)
    hidden_grad = (mm_t(values_ref[1, part, :], fc_out) * slope).astype(bf16)
    back_ref[part, :] += mm_t(hidden_grad, fc_in)
    return hidden, hidden_grad


def residual_back_planes(size, stage, values_ref, res_ref, gain2, back_ref, grad_ref):
    def plane(source, slot, rows, gain_sum, shift_sum):
        unit, spread = norm_parts(res_ref[rows, :])
        grad = back_ref[rows, :]
        gain_sum = gain_sum + jnp.sum(grad * unit, axis=0, keepdims=True)
        shift_sum = shift_sum + jnp.sum(grad, axis=0, keepdims=True)
        grad = values_ref[1, rows, :].astype(f32) + norm_back(grad * gain2, unit, spread)
        back_ref[rows, :] = grad
        grad_ref[rows, :] = grad.astype(bf16)
        return gain_sum, shift_sum

    zero = jnp.zeros((1, size.channels), f32)
    return over_planes(size, stage, plane, zero, zero)


def block_planes(size, stage, map_ref, res_ref, acc_ref, out_bias, block_ref):
    def plane(source, slot, rows):
        block = (res_ref[rows, :] + (acc_ref[rows, :] + out_bias)) * live_of(size, map_ref, slot)
        block_ref[source, slot] = block[: size.lons_here].astype(bf16)
        return ()

    over_planes(size, stage, plane)


def mlp_kernel(
    size,
    map_ref,
    x_ref,
    dy_ref,
    gain1_ref,
    shift1_ref,
    gain2_ref,
    shift2_ref,
    out_bias_ref,
    fc_in_ref,
    fc_in_bias_ref,
    fc_out_ref,
    *refs,
):
    count = len(size.stages)
    recvs, invs_t, invs, sends = [refs[i * count : (i + 1) * count] for i in range(4)]
    block_ref, dh_ref, hidden_ref, values_ref, small_ref, res_ref, grad_ref, acc_ref = refs[4 * count :]
    step = pl.program_id(0)

    @pl.when(step == 0)
    def _():
        small_ref[...] = jnp.zeros_like(small_ref)
        for stage, recv_ref, inv_t_ref in zip(size.stages, recvs, invs_t):
            small_ref[0:1, :] += residual_planes(
                size, stage, map_ref, recv_ref, x_ref, dy_ref, inv_t_ref, as_row(gain1_ref), as_row(shift1_ref), as_row(gain2_ref), as_row(shift2_ref), res_ref, values_ref
            )
        acc_ref[...] = jnp.zeros_like(acc_ref)
        dh_ref[...] = jnp.zeros_like(dh_ref)

    hidden, hidden_grad = hidden_part(
        slice(0, size.tokens), values_ref, fc_in_ref[...], fc_in_bias_ref[...], fc_out_ref[...], acc_ref, dh_ref
    )
    small_ref[pl.ds(3 + step, 1), :] = jnp.sum(hidden_grad.astype(f32), axis=0, keepdims=True)
    hidden_ref[0] = hidden_grad
    hidden_ref[1] = hidden

    @pl.when(step == pl.num_programs(0) - 1)
    def _():
        for stage, inv_ref, send_ref in zip(size.stages, invs, sends):
            block_planes(size, stage, map_ref, res_ref, acc_ref, as_row(out_bias_ref), block_ref)
            gain_sum, shift_sum = residual_back_planes(
                size, stage, values_ref, res_ref, as_row(gain2_ref), dh_ref, grad_ref
            )
            small_ref[1:2, :] += gain_sum
            small_ref[2:3, :] += shift_sum
            write_pieces(size, stage, mm(inv_ref[...], grad_ref[stage.part, :]), send_ref)


def run_mlp(size, hidden_units, row_map, x, dy, vectors, fc_in, fc_in_bias, fc_out, received, invs_t, invs):
    channels = size.channels
    parts = hidden_units // channels
    fixed = pl.BlockSpec(memory_space=pltpu.VMEM)
    tokens = (size.tokens, channels)
    count = len(size.stages)
    out = pl.pallas_call(
        functools.partial(mlp_kernel, size),
        grid=(parts,),
        in_specs=[pl.BlockSpec(memory_space=pltpu.SMEM)]
        + [fixed] * (2 + len(vectors))
        + [
            pl.BlockSpec((channels, channels), lambda i: (0, i)),
            pl.BlockSpec((1, channels), lambda i: (0, i)),
            pl.BlockSpec((channels, channels), lambda i: (i, 0)),
        ]
        + [fixed] * (3 * count),
        out_specs=tuple(
            [fixed] * (count + 2)
            + [pl.BlockSpec((None, 2) + tokens, lambda i: (i, 0, 0, 0))]
            + [fixed] * 2
        ),
        out_shape=tuple(
            [struct(piece.shape, bf16) for piece in received]
            + [
                struct(x.shape, bf16),
                struct(tokens, f32),
                struct((parts, 2) + tokens, bf16),
                struct((2,) + tokens, bf16),
                struct((round_up(3 + parts, 8), channels), f32),
            ]
        ),
        scratch_shapes=[
            pltpu.VMEM(tokens, f32),
            pltpu.VMEM(tokens, bf16),
            pltpu.VMEM(tokens, f32),
        ],
        compiler_params=pltpu.CompilerParams(vmem_limit_bytes=VMEM_BYTES),
        name="mlp",
    )(row_map, x, dy, *vectors, fc_in, fc_in_bias, fc_out, *received, *invs_t, *invs)
    return (out[:count],) + tuple(out[count:])


def wide_kernel(hidden_ref, values_ref, wide_ref):
    channels = values_ref.shape[2]
    for part in range(hidden_ref.shape[0]):
        rows = slice(part * channels, (part + 1) * channels)
        wide_ref[rows, :channels] = t_mm(hidden_ref[part, 0], values_ref[0]).astype(bf16)
        wide_ref[rows, channels:] = t_mm(hidden_ref[part, 1], values_ref[1]).astype(bf16)


def last_planes(size, stage, recv_ref, x_ref, dh_ref, table_t_ref, gain_ref, filtered_ref, out_ref, first=0, then=None):
    gain = as_row(gain_ref)
    filtered_ref[stage.part, :] = mm(table_t_ref[...], read_spectrum(size, recv_ref))

    def plane(source, slot, rows, gain_sum, shift_sum):
        unit, spread = norm_parts(pad_plane(size, x_ref[source, slot].astype(f32)))
        base = dh_ref[rows, :]
        grad = base + filtered_ref[rows, :]
        gain_sum = gain_sum + jnp.sum(grad * unit, axis=0, keepdims=True)
        shift_sum = shift_sum + jnp.sum(grad, axis=0, keepdims=True)
        grad = base + norm_back(grad * gain, unit, spread)
        out_ref[source, slot] = grad[: size.lons_here].astype(bf16)
        return gain_sum, shift_sum

    zero = jnp.zeros((1, size.channels), f32)
    return over_planes(size, stage, plane, zero, zero, first=first, then=then)


def last_kernel(size, x_ref, dh_ref, gain_ref, *refs):
    count = len(size.stages)
    recvs, tables_t = refs[:count], refs[count : 2 * count]
    out_ref, small_ref, filtered_ref = refs[2 * count :]
    small_ref[...] = jnp.zeros_like(small_ref)
    for stage, recv_ref, table_t_ref in zip(size.stages, recvs, tables_t):
        gain_sum, shift_sum = last_planes(size, stage, recv_ref, x_ref, dh_ref, table_t_ref, gain_ref, filtered_ref, out_ref)
        small_ref[0:1, :] += gain_sum
        small_ref[1:2, :] += shift_sum


def partners(lon_count):
    row = lax.axis_index("rows")
    lon = lax.axis_index("lon")
    core = {"rows": row, "lon": lon + 1 - 2 * (lon % 2)}
    along_y = {"rows": row, "lon": (lon + 2) % 4}
    along_x = {"rows": row + 1 - 2 * (row % 2), "lon": lon}
    far_z = {"rows": (row + 4) % 8, "lon": lon}
    return core, along_y, along_x, far_z


def greet(lon_count, count):
    row = lax.axis_index("rows")
    lon = lax.axis_index("lon")
    me = row * lon_count + lon
    barrier = pltpu.get_barrier_semaphore()
    for offset in range(1, count):
        other = (me + offset) % count
        pl.semaphore_signal(
            barrier,
            inc=1,
            device_id={"rows": other // lon_count, "lon": other % lon_count},
            device_id_type=MESH,
        )
    pl.semaphore_wait(barrier, count - 1)


class Sender:
    def __init__(self, send_sem, recv_sem):
        self.send_sem = send_sem
        self.recv_sem = recv_sem
        self.used = 0

    def make(self, source, target, device):
        copy = pltpu.make_async_remote_copy(
            src_ref=source,
            dst_ref=target,
            send_sem=self.send_sem.at[self.used],
            recv_sem=self.recv_sem.at[self.used],
            device_id=device,
            device_id_type=MESH,
        )
        self.used += 1
        return copy

    def start(self, source, target, device):
        copy = self.make(source, target, device)
        copy.start()
        return copy


class Mover:
    def __init__(self, sem):
        self.sem = sem
        self.used = 0

    def make(self, source, target):
        copy = pltpu.make_async_copy(source, target, self.sem.at[self.used])
        self.used += 1
        return copy

    def start(self, source, target):
        copy = self.make(source, target)
        copy.start()
        return copy


def make_all(size, source_ref, out_ref, sender, mover):
    row = lax.axis_index("rows")
    lon = lax.axis_index("lon")
    me = row * size.lon + lon
    copies = []
    for row_step in range(size.rows):
        for lon_step in range(size.lon):
            to_row = (row + row_step) % size.rows
            to_lon = (lon + lon_step) % size.lon
            piece = source_ref.at[to_row * size.lon + to_lon]
            if row_step == 0 and lon_step == 0:
                copies.append(mover.make(piece, out_ref.at[me]))
            else:
                copies.append(
                    sender.make(piece, out_ref.at[me], {"rows": to_row, "lon": to_lon})
                )
    return copies


def make_lon(stage, source_ref, out_ref, sender, mover):
    row = lax.axis_index("rows")
    me = lax.axis_index("lon")
    count = source_ref.shape[0]
    slots = pl.ds(stage.slots[0], len(stage.slots))
    copies = []
    for offset in range(1, count):
        other = (me + offset) % count
        copies.append(
            sender.make(
                source_ref.at[other, slots], out_ref.at[me, slots], {"rows": row, "lon": other}
            )
        )
    copies.append(mover.make(source_ref.at[me, slots], out_ref.at[me, slots]))
    return copies


def begin(copies):
    for copy in copies:
        copy.start()
    return copies


def finish(copies):
    for copy in copies:
        copy.wait()


def call_remote(kernel, name, number, outs, spaces, out_spaces, sends, moves, scratch, operands):
    return pl.pallas_call(
        kernel,
        out_shape=outs,
        in_specs=[pl.BlockSpec(memory_space=space) for space in spaces],
        out_specs=tuple(pl.BlockSpec(memory_space=space) for space in out_spaces),
        scratch_shapes=[
            pltpu.SemaphoreType.DMA((sends,)),
            pltpu.SemaphoreType.DMA((sends,)),
            pltpu.SemaphoreType.DMA((moves,)),
        ]
        + list(scratch),
        compiler_params=pltpu.CompilerParams(
            collective_id=number, has_side_effects=True, vmem_limit_bytes=VMEM_BYTES
        ),
        name=name,
    )(*operands)


def add_to(total_ref, other_ref):
    @pl.loop(0, total_ref.shape[0])
    def _(first):
        if len(total_ref.shape) == 3:
            total = total_ref[first].astype(f32) + other_ref[first].astype(f32)
            total_ref[first] = total.astype(total_ref.dtype)
        else:
            for second in range(total_ref.shape[1]):
                total = total_ref[first, second].astype(f32) + other_ref[first, second].astype(f32)
                total_ref[first, second] = total.astype(total_ref.dtype)


def start_same(lon_count, count, source_ref, out_ref, sender, mover):
    me = lax.axis_index("rows") * lon_count + lax.axis_index("lon")
    copies = []
    for offset in range(1, count):
        other = (me + offset) % count
        copies.append(
            sender.start(
                source_ref, out_ref.at[me], {"rows": other // lon_count, "lon": other % lon_count}
            )
        )
    copies.append(mover.start(source_ref, out_ref.at[me]))
    return copies


def named(group, refs):
    leaves, tree = jax.tree.flatten(group)
    return jax.tree.unflatten(tree, [next(refs) for _ in leaves])


def layer_kernel(size, groups_of, *refs):
    found = iter(refs)
    r = types.SimpleNamespace()
    for arrays in groups_of:
        r.__dict__.update(named(arrays, found))
    r.hbm = types.SimpleNamespace(**r.large, **r.kept)
    stages = size.stages
    channels = size.channels
    lon_count, count, groups = size.lon, size.devices, size.groups
    row = lax.axis_index("rows")
    lon = lax.axis_index("lon")
    me = row * lon_count + lon
    z = row // 2
    x = row % 2
    y = lon // 2
    core = lon % 2
    group = me % groups
    base = me - group
    half = me // groups
    to_core, to_y, to_x, far_z = partners(lon_count)
    near = z + 1 - 2 * (z % 2)
    mirror = 3 - z
    to_near = {"rows": near * 2 + x, "lon": lon}
    to_mirror = {"rows": mirror * 2 + x, "lon": lon}
    parts = 4
    share = r.wide.shape[-2]
    split = r.a_one.shape[-1]
    first, second = pl.ds(0, split), pl.ds(split, r.b_one.shape[-1])
    sender, mover = Sender(r.a_send_sem, r.b_recv_sem), Mover(r.c_move_sem)

    def order(step):
        chip = jnp.where(step % 2 == 0, near, z)
        return jnp.where(step < 2, 3 - chip, chip)

    def part_place(step):
        return pl.ds(pl.multiple_of(order(step) * channels, channels), channels)

    cotangents = [make_lon(stage, r.hbm.cot, r.dy, sender, mover) for stage in stages]
    by_e = [
        make_all(size, source, target, sender, mover)
        for source, target in zip(r.send_e, r.recv_e)
    ]
    by_g = [
        make_all(size, source, target, sender, mover)
        for source, target in zip(r.send_g, r.recv_g)
    ]
    blocks = [make_lon(stage, r.block, r.block_out, sender, mover) for stage in stages]
    by_core = [
        [
            sender.make(r.wide.at[i % 2, :, :, 1 - core, :, first], r.a_core.at[i], to_core),
            sender.make(r.wide.at[i % 2, :, :, 1 - core, :, second], r.b_core.at[i], to_core),
        ]
        for i in range(parts)
    ]
    by_one = [
        [
            sender.make(r.a_core.at[i, 1 - x], r.a_one.at[i], to_x),
            sender.make(r.b_core.at[i, :, 1 - y], r.b_one.at[i], to_y),
        ]
        for i in range(parts)
    ]
    by_two = [
        [
            sender.make(r.a_one.at[i, 1 - y], r.a_two.at[i], to_y),
            sender.make(r.b_one.at[i, 1 - x], r.b_two.at[i], to_x),
        ]
        for i in range(parts)
    ]
    by_near = [
        [
            sender.make(r.a_two.at[2 * i], r.a_near.at[i], to_near),
            sender.make(r.b_two.at[2 * i], r.b_near.at[i], to_near),
        ]
        for i in range(2)
    ]
    by_early = [
        sender.make(r.early, r.early_land.at[i], device)
        for i, device in enumerate((to_core, to_x, to_y, to_near, to_mirror))
    ]
    tables_back = [
        mover.make(source, target)
        for source, target in zip(r.hbm.table_t, r.table_t)
    ]

    def core_end(step):
        finish(by_core[step])
        add_to(r.a_core.at[step], r.wide.at[step % 2, :, :, core, :, first])
        by_one[step][0].start()
        add_to(r.b_core.at[step], r.wide.at[step % 2, :, :, core, :, second])
        by_one[step][1].start()

    def one_end(step):
        by_one[step][0].wait()
        add_to(r.a_one.at[step], r.a_core.at[step, x])
        by_two[step][0].start()
        by_one[step][1].wait()
        add_to(r.b_one.at[step], r.b_core.at[step, :, y])
        by_two[step][1].start()

    def two_end(step):
        finish(by_two[step])
        for total, kept in ((r.a_two, r.a_one.at[step, y]), (r.b_two, r.b_one.at[step, x])):
            total[step] = (total[step].astype(f32) + kept[...].astype(f32)).astype(bf16)

    def early_step(step):
        by_early[step].wait()
        r.early[...] = r.early[...] + r.early_land[step]
        if step + 1 < len(by_early):
            by_early[step + 1].start()

    def forward(*scoped):
        f = types.SimpleNamespace(**named(forward_scratch(size), iter(scoped)))
        tables = [
            mover.start(source, target)
            for source, target in zip(r.hbm.table, f.table)
        ]
        loads = [mover.start(r.hbm.er, f.er)]
        loads += [mover.start(a, b) for a, b in zip(r.hbm.ec, f.ec)]
        begin(tables_back)
        greet(lon_count, count)
        tokens = [begin(make_lon(stage, r.hbm.tokens, r.x, sender, mover)) for stage in stages]
        build_block_matrix(size, r.mix_in, r.mix_in_bias, half, f.w1, f.b1)
        build_block_matrix(size, r.mix_out, r.mix_out_bias, half, f.w2, f.b2)
        stores = [mover.start(f.w1, r.hbm.w1), mover.start(f.w2, r.hbm.w2)]
        by_a = [
            make_all(size, source, target, sender, mover)
            for source, target in zip(f.send_a, r.recv_a)
        ]
        for i, stage in enumerate(stages):
            finish(tokens[i])
            first_norm(size, stage, r.x, as_row(r.gain1), as_row(r.shift1), f.low)
            tables[i].wait()
            write_pieces(size, stage, mm(f.table[i][...], f.low[stage.part, :]), f.send_a[i])
            begin(by_a[i])
        for copies in cotangents:
            begin(copies)
        finish(loads)
        build_lat_tables(size, r.rows, r.cosine, r.sine, f.er, f.ec, f.lat, f.lat_t)
        stores += [mover.start(a, b) for a, b in zip(f.lat, r.hbm.lat)]
        stores += [mover.start(a, b) for a, b in zip(f.lat_t, r.hbm.lat_t)]
        f.modes[...] = jnp.zeros_like(f.modes)
        for i in range(len(stages)):
            finish(by_a[i])
            add_modes(size, r.recv_a[i], f.lat[i], f.modes)
        mix_layers(size, f.modes, f.w1, f.b1, f.w2, f.b2, f.band, f.inner, f.gated, f.outer, f.stacked)
        for i, stage in enumerate(stages):
            modes_back(size, stage, f.lat_t[i], f.stacked, r.send_e[i])
            begin(by_e[i])
        stores += [
            mover.start(f.band, r.hbm.band),
            mover.start(f.inner, r.hbm.inner),
            mover.start(f.gated, r.hbm.gated),
            mover.start(f.outer, r.hbm.outer),
        ]
        finish(stores)

    def front(*scoped):
        f = types.SimpleNamespace(**named(front_scratch(size), iter(scoped)))
        rounds = len(stages) * parts
        part_loads = [
            [
                mover.make(r.hbm.fc_in.at[:, part_place(i % parts)], f.fc_in.at[i % 2]),
                mover.make(r.hbm.fc_out.at[part_place(i % parts), :], f.fc_out.at[i % 2]),
            ]
            for i in range(rounds)
        ]
        inv_t_loads = [mover.start(a, b) for a, b in zip(r.hbm.inv_t, f.inv_t)]
        begin(part_loads[0])
        begin(part_loads[1])
        inv_loads = [mover.start(a, b) for a, b in zip(r.hbm.inv, f.inv)]
        r.early[...] = jnp.zeros_like(r.early)
        f.acc[...] = jnp.zeros_like(f.acc)
        r.dh[...] = jnp.zeros_like(r.dh)
        finish(inv_t_loads)
        finish(inv_loads)

        def weights(step):
            @pl.loop(0, 2)
            def _(which):
                product = t_mm(f.hidden[step, which], f.values[which])
                columns = pl.ds(pl.multiple_of(which * channels, channels), channels)
                for i in range(8):
                    r.wide[step % 2, i // 4, i // 2 % 2, i % 2, :, columns] = product[
                        i * share : (i + 1) * share
                    ].astype(bf16)

        for i, stage in enumerate(stages):
            is_last = i == len(stages) - 1
            finish(cotangents[i])
            finish(by_e[i])
            r.early[0:1, :] += residual_planes(
                size, stage, r.map, r.recv_e[i], r.x, r.dy, f.inv_t[i], as_row(r.gain1), as_row(r.shift1), as_row(r.gain2), as_row(r.shift2), f.res, f.values
            )

            @pl.loop(0, parts)
            def _(step):
                slot = step % 2
                at(step, parts, lambda k: finish(part_loads[i * parts + k]))
                hidden, hidden_grad = hidden_part(
                    stage.part, f.values, f.fc_in[slot], r.fc_in_bias[:, part_place(step)], f.fc_out[slot], f.acc, r.dh
                )
                r.early[pl.ds(3 + order(step), 1), :] += jnp.sum(
                    hidden_grad.astype(f32), axis=0, keepdims=True
                )
                f.hidden[step, 0, stage.part] = hidden_grad
                f.hidden[step, 1, stage.part] = hidden

                def load_next(k):
                    if i * parts + k + 2 < rounds:
                        begin(part_loads[i * parts + k + 2])

                at(step, parts, load_next)
                if is_last:
                    at(step, 3, lambda k: core_end(k - 1) if k else None)

                    @pl.when(step < 2)
                    def _():
                        weights(step)
                        at(step, 2, lambda k: begin(by_core[k]))

                    pl.when(step == 3)(lambda: one_end(0))

            gain_sum, shift_sum = residual_back_planes(size, stage, f.values, f.res, as_row(r.gain2), r.dh, f.grad)
            r.early[1:2, :] += gain_sum
            r.early[2:3, :] += shift_sum
            write_pieces(size, stage, mm(f.inv[i][...], f.grad[stage.part, :]), r.send_g[i])
            begin(by_g[i])
            if not is_last:
                block_planes(size, stage, r.map, f.res, f.acc, as_row(r.out_bias), r.block)
                begin(blocks[i])
        by_early[0].start()

        @pl.loop(2, parts)
        def _(step):
            weights(step)
            at(step - 2, 2, lambda k: begin(by_core[2 + k]))

        core_end(2)
        core_end(3)
        two_end(0)
        begin(by_near[0])
        block_planes(size, stages[-1], r.map, f.res, f.acc, as_row(r.out_bias), r.block)
        begin(blocks[-1])
        early_step(0)

    def back(*scoped):
        f = types.SimpleNamespace(**named(back_scratch(size), iter(scoped)))
        loads = [
            mover.start(source, target)
            for source, target in zip(
                r.hbm.lat
                + [r.hbm.outer, r.hbm.w2, r.hbm.inner, r.hbm.w1]
                + r.hbm.lat_t
                + [r.hbm.gated, r.hbm.band],
                f.lat
                + [f.outer, f.w2, f.inner, f.w1]
                + f.lat_t
                + [f.gated, f.band],
            )
        ]
        f.modes[...] = jnp.zeros_like(f.modes)
        finish(loads)
        for i in range(len(stages)):
            if i == 1:
                one_end(1)
            finish(by_g[i])
            add_modes(size, r.recv_g[i], f.lat[i], f.modes)
        mix_layers_back(size, f.modes, f.w1, f.w2, f.inner, f.outer, f.outer_grad, f.inner_grad, f.stacked)
        by_d = [
            make_all(size, source, target, sender, mover)
            for source, target in zip(f.send_d, r.recv_d)
        ]
        for i, stage in enumerate(stages):
            modes_back(size, stage, f.lat_t[i], f.stacked, f.send_d[i])
            begin(by_d[i])
        early_step(1)

        mix_back_weights(size, f.band, f.gated, f.outer_grad, f.inner_grad, r.mix)
        crossing = sender.start(r.mix.at[:, 1 - core], r.mix_core, to_core)
        finish(by_near[0])
        two_end(1)
        for total, landed in ((r.a_two, r.a_near), (r.b_two, r.b_near)):
            total[1] = (total[1].astype(f32) + landed[0].astype(f32)).astype(bf16)
        hops = [
            sender.start(r.a_two.at[1], r.a_last, to_mirror),
            sender.start(r.b_two.at[1], r.b_last, to_mirror),
        ]
        crossing.wait()
        add_to(r.mix_core, r.mix.at[:, core])
        pair = group // 2
        mixes = []
        for offset in range(1, groups // 2):
            other = (pair + offset) % (groups // 2)
            device = base + other * 2 + core
            mixes.append(
                sender.start(
                    r.mix_core.at[other],
                    r.mix_land.at[pair],
                    {"rows": device // lon_count, "lon": device % lon_count},
                )
            )
        mixes.append(mover.start(r.mix_core.at[pair], r.mix_land.at[pair]))
        one_end(2)
        early_step(2)

        finish(tables_back)
        tokens = [make_lon(stage, r.token, r.token_out, sender, mover) for stage in stages]
        gather = []
        r.late[...] = jnp.zeros_like(r.late)
        for i, stage in enumerate(stages):
            finish(by_d[i])
            gain_sum, shift_sum = last_planes(
                size, stage, r.recv_d[i], r.x, r.dh, r.table_t[i], r.gain1, f.filtered, r.token, lon + 1, lambda k: tokens[i][k].start()
            )
            r.late[0:1, :] += gain_sum
            r.late[1:2, :] += shift_sum
            if i == 0:
                finish(mixes)
                total = r.mix_land[0].astype(f32)
                for index in range(1, groups // 2):
                    total = total + r.mix_land[index].astype(f32)
                r.pair[half] = total.astype(bf16)
                crossing = sender.start(r.pair.at[half], r.pair.at[half], far_z)
                two_end(2)
                begin(by_near[1])
                one_end(3)
                crossing.wait()
                block_size = r.mix_out_grad.shape[-1]
                rest = r.mix_out_bias_grad.shape[-2]
                own_place = (pair // 4, pair // 2 % 2, slice(None), pair % 2, core)
                for source, target in (
                    (r.pair.at[:, pl.ds(0, block_size)], r.mix_out_grad.at[own_place]),
                    (r.pair.at[:, pl.ds(block_size, rest)], r.mix_out_bias_grad.at[own_place]),
                ):
                    for offset in range(1, groups // 2):
                        device = base + (pair + offset) % (groups // 2) * 2 + core
                        gather.append(
                            sender.start(
                                source,
                                target,
                                {"rows": device // lon_count, "lon": device % lon_count},
                            )
                        )
                    gather.append(mover.start(source, target))
        smalls = start_same(lon_count, count, r.late, r.late_land, sender, mover)
        early_step(3)
        finish(gather)
        gather = []
        for ref in (r.mix_out_grad, r.mix_out_bias_grad):
            own_core = ref.at[:, :, :, :, core]
            gather.append(sender.start(own_core, own_core, to_core))
        finish(smalls)
        total = r.late_land[0]
        for index in range(1, count):
            total = total + r.late_land[index]
        r.late_out[...] = total
        two_end(3)
        finish(by_near[1])
        finish(hops)
        for columns, total, landed, last in (
            (first, r.a_two, r.a_near, r.a_last),
            (second, r.b_two, r.b_near, r.b_last),
        ):
            r.dense[:, columns] = (
                total[3].astype(f32) + landed[1].astype(f32) + last[...].astype(f32)
            )
        early_step(4)
        r.early_out[...] = r.early[...]
        finish(gather)
        for copies in blocks + tokens:
            finish(copies)

    for scope, arrays in (
        (forward, forward_scratch(size)),
        (front, front_scratch(size)),
        (back, back_scratch(size)),
    ):
        pl.run_scoped(scope, *in_vmem(arrays))


def in_vmem(group):
    return [pltpu.VMEM(leaf.shape, leaf.dtype) for leaf in jax.tree.leaves(group)]


def pieces_of(size):
    return [struct((size.per_image, stage.piece, size.half), bf16) for stage in size.stages]


def kept_arrays(size):
    modes, both = 2 * size.modes, 2 * size.half
    square = struct((both, both), bf16)
    narrow = struct((size.modes, both), bf16)
    wide = struct((size.modes, both), f32)
    return dict(
        lat=[struct((modes, stage.band), bf16) for stage in size.stages],
        lat_t=[struct((stage.band, modes), bf16) for stage in size.stages],
        w1=square,
        w2=square,
        band=narrow,
        gated=narrow,
        inner=wide,
        outer=wide,
    )


def mode_arrays(size):
    modes = (2 * size.modes, size.half)
    return dict(modes=struct(modes, f32), stacked=struct(modes, bf16))


def forward_scratch(size):
    row = struct((1, 2 * size.half), f32)
    return dict(
        table=[struct((stage.spectrum, stage.rows), bf16) for stage in size.stages],
        ec=[struct((256, stage.band), bf16) for stage in size.stages],
        er=struct((2 * size.modes, 192), bf16),
        b1=row,
        b2=row,
        low=struct((size.tokens, size.channels), bf16),
        send_a=pieces_of(size),
        **kept_arrays(size),
        **mode_arrays(size),
    )


def front_scratch(size):
    tokens = (size.tokens, size.channels)
    square = struct((2, size.channels, size.channels), bf16)
    return dict(
        inv_t=[struct((stage.rows, stage.spectrum), bf16) for stage in size.stages],
        inv=[struct((stage.spectrum, stage.rows), bf16) for stage in size.stages],
        fc_in=square,
        fc_out=square,
        hidden=struct((4, 2) + tokens, bf16),
        values=struct((2,) + tokens, bf16),
        grad=struct(tokens, bf16),
        res=struct(tokens, f32),
        acc=struct(tokens, f32),
    )


def back_scratch(size):
    grads = struct((size.modes, 2 * size.half), bf16)
    return dict(
        outer_grad=grads,
        inner_grad=grads,
        filtered=struct((size.tokens, size.channels), f32),
        send_d=pieces_of(size),
        **kept_arrays(size),
        **mode_arrays(size),
    )


def run_layer(size, large, small, row_map, blocks_shape, number):
    shape = large["tokens"].shape
    hidden_units = large["fc_out"].shape[0]
    parts = hidden_units // size.channels
    share = hidden_units // size.devices
    split = round(SPLIT * 2 * size.channels / 128) * 128
    block = blocks_shape[1:]
    lead = (2, 2, HALVES, blocks_shape[0] // 8, 2)
    early = struct((round_up(3 + parts, 8), size.channels), f32)
    late = struct((2, size.channels), f32)
    plane = struct(shape, bf16)
    half_blocks = struct((blocks_shape[0] // 2,) + block, bf16)
    far = dict(token_out=plane, block_out=plane)
    near = dict(
        dense=struct((share, 2 * size.channels), f32),
        mix_out_grad=struct(lead + (block[1], block[1]), bf16),
        mix_out_bias_grad=struct(lead + (block[0] - block[1], block[1]), bf16),
        early_out=early,
        late_out=late,
    )
    kept = dict(kept=kept_arrays(size))

    def sums(width):
        return [
            struct(lead + (share, width), bf16)
            for lead in ((4, 2, 2), (4, 2), (4,), (2,), ())
        ]

    a, b = sums(split), sums(2 * size.channels - split)
    scratch = dict(
        x=plane,
        dy=plane,
        token=plane,
        block=plane,
        table_t=[struct((stage.rows, stage.spectrum), bf16) for stage in size.stages],
        dh=struct((size.tokens, size.channels), f32),
        recv_a=pieces_of(size),
        send_e=pieces_of(size),
        recv_e=pieces_of(size),
        send_g=pieces_of(size),
        recv_g=pieces_of(size),
        recv_d=pieces_of(size),
        wide=struct((2, 2, 2, 2, share, 2 * size.channels), bf16),
        a_core=a[0],
        b_core=b[0],
        a_one=a[1],
        b_one=b[1],
        a_two=a[2],
        b_two=b[2],
        a_near=a[3],
        b_near=b[3],
        a_last=a[4],
        b_last=b[4],
        mix=struct((blocks_shape[0] // 2, 2) + block, bf16),
        mix_core=half_blocks,
        mix_land=half_blocks,
        pair=struct((HALVES,) + block, bf16),
        early=early,
        early_land=struct((5,) + early.shape, f32),
        late=late,
        late_land=struct((size.devices,) + late.shape, f32),
    )
    sems = dict(a_send_sem=0, b_recv_sem=0, c_move_sem=0)
    large_group = dict(large=large)
    map_group = dict(map=row_map)
    groups = [
        jax.tree.map(lambda leaf: 0, group)
        for group in (large_group, small, map_group, far, near, kept, sems, scratch)
    ]
    operands = jax.tree.leaves(large_group) + jax.tree.leaves(small) + [row_map]
    outs = [jax.tree.leaves(group) for group in (far, near, kept)]
    results = call_remote(
        functools.partial(layer_kernel, size, groups),
        "layer",
        number,
        tuple(outs[0] + outs[1] + outs[2]),
        [pl.ANY] * len(jax.tree.leaves(large_group))
        + [pltpu.VMEM] * len(small)
        + [pltpu.SMEM],
        [pl.ANY] * len(outs[0]) + [pltpu.VMEM] * len(outs[1]) + [pl.ANY] * len(outs[2]),
        10 * size.devices + 2 * size.groups + 16 * size.lon + 32,
        80,
        in_vmem(scratch),
        operands,
    )
    found = iter(results)
    return types.SimpleNamespace(**named(far, found), **named(near, found))


def prepare_kernel(size, rows_ref, cos_ref, sin_ref, er_ref, mix_in_ref, bias_in_ref, mix_out_ref, bias_out_ref, *refs):
    count = len(size.stages)
    ecs, lats, lats_t = [refs[i * count : (i + 1) * count] for i in range(3)]
    w1_ref, w2_ref, b1_ref, b2_ref = refs[3 * count :]
    half = half_of(size)
    build_lat_tables(size, rows_ref, cos_ref, sin_ref, er_ref, ecs, lats, lats_t)
    build_block_matrix(size, mix_in_ref, bias_in_ref, half, w1_ref, b1_ref)
    build_block_matrix(size, mix_out_ref, bias_out_ref, half, w2_ref, b2_ref)


def exchange_lon(values):
    return lax.all_to_all(values, "lon", split_axis=0, concat_axis=0, tiled=True)


def exchange_all(values):
    return lax.all_to_all(values, ("rows", "lon"), split_axis=0, concat_axis=0, tiled=True)


def join_stages(size, pieces):
    return jnp.concatenate(
        [piece[:, : stage.used] for stage, piece in zip(size.stages, pieces)], axis=1
    )


def cut_stages(size, values):
    pieces, start = [], 0
    for stage in size.stages:
        piece = values[:, start : start + stage.used]
        pieces.append(jnp.pad(piece, ((0, 0), (0, stage.piece - stage.used), (0, 0))))
        start += stage.used
    return pieces


def to_modes(size, pieces, row_map):
    sent = jnp.tile(join_stages(size, pieces), (size.images, 1, 1))
    received = exchange_all(sent)
    used = size.slots_here * 2 * size.waves
    by_slot = received.reshape(-1, 2 * size.waves, size.half)
    image = (lax.axis_index("rows") * size.lon + lax.axis_index("lon")) // size.per_image
    slots = row_map.shape[0]
    target = jnp.where(row_map >= 0, row_map, size.images * H)
    slot_of_row = (
        jnp.zeros((size.images * H,), jnp.int32)
        .at[target]
        .set(jnp.arange(slots, dtype=jnp.int32), mode="drop")
    )
    own = lax.dynamic_slice_in_dim(slot_of_row, image * H, H)
    picked = jnp.take(by_slot, own, axis=0)
    picked = jnp.pad(picked, ((0, size.virtual_slots - H), (0, 0), (0, 0)))
    return cut_stages(size, picked.reshape(size.per_image, used, size.half))


def from_modes(size, pieces, row_map):
    used = size.slots_here * 2 * size.waves
    by_lat = join_stages(size, pieces).reshape(-1, 2 * size.waves, size.half)
    image = (lax.axis_index("rows") * size.lon + lax.axis_index("lon")) // size.per_image
    live = (row_map >= 0) & (row_map // H == image)
    picked = jnp.take(by_lat, jnp.where(live, row_map % H, 0), axis=0)
    picked = picked * live.astype(bf16)[:, None, None]
    received = exchange_all(picked.reshape(size.devices, used, size.half))
    received = received.reshape(size.images, size.per_image, used, size.half)
    return cut_stages(size, jnp.sum(received.astype(f32), axis=0).astype(bf16))


def run_fields(
    size, blocks_shape, row_map, x, dy, tables, tables_t, invs, invs_t, lat_inputs, mixers, vectors, fc_in, fc_in_bias, fc_out
):
    channels = size.channels
    names = ("rows", "lon")
    kept_structs = types.SimpleNamespace(**kept_arrays(size))
    pieces = tuple(pieces_of(size))
    modes = [pltpu.VMEM(v.shape, v.dtype) for v in mode_arrays(size).values()]
    flat = struct((1, 2 * size.half), f32)
    cosine, sine, er, ecs = lat_inputs
    lats = jnp.arange(size.virtual_slots)
    rows = jnp.where(lats < H, lats, -1).astype(jnp.int32)
    prepared = call_local(
        functools.partial(prepare_kernel, size),
        "prepare",
        tuple(kept_structs.lat + kept_structs.lat_t)
        + (kept_structs.w1, kept_structs.w2, flat, flat),
    )(rows, cosine, sine, er, *mixers, *ecs)
    count = len(size.stages)
    lat, lat_t, (w1, w2, b1, b2) = prepared[:count], prepared[count : 2 * count], prepared[2 * count :]
    x, dy = exchange_lon(x), exchange_lon(dy)
    sent = call_local(
        functools.partial(first_kernel, size),
        "lon_forward",
        pieces,
        [pltpu.VMEM((size.tokens, channels), bf16)],
    )(x, vectors[0], vectors[1], *tables)
    received = to_modes(size, sent, row_map)
    kept = (kept_structs.band, kept_structs.inner, kept_structs.gated, kept_structs.outer)
    results = call_local(
        functools.partial(mix_kernel, size), "mix_forward", pieces + kept, modes
    )(w1, b1, w2, b2, *received, *lat, *lat_t)
    sent, kept = results[:count], results[count:]
    received = from_modes(size, sent, row_map)
    sent, block, dh, hidden, values, early = run_mlp(
        size, fc_out.shape[0], row_map, x, dy, vectors, fc_in, fc_in_bias, fc_out, received, invs_t, invs
    )
    early = lax.psum(early, names)
    wide = call_local(
        wide_kernel, "weights_backward", struct((fc_out.shape[0], 2 * channels), bf16)
    )(hidden, values)
    dense = lax.psum_scatter(wide, names, scatter_dimension=0, tiled=True).astype(f32)
    block = exchange_lon(block)
    received = to_modes(size, sent, row_map)
    results = call_local(
        functools.partial(mix_back_kernel, size),
        "mix_backward",
        pieces + (struct(blocks_shape, bf16),),
        [pltpu.VMEM((size.modes, 2 * size.half), bf16)] * 2 + modes,
    )(w1, w2, *kept, *received, *lat, *lat_t)
    sent, mix_grad = results[:count], results[count]
    half_index = half_of(size)
    mix_grad = mix_grad.astype(f32).reshape((2, 2, 1, blocks_shape[0] // 4) + blocks_shape[1:])
    mix_total = lax.psum(
        jnp.concatenate(
            [mix_grad * (half_index == other).astype(f32) for other in range(HALVES)], axis=2
        ),
        names,
    )
    received = from_modes(size, sent, row_map)
    token_grad, late = call_local(
        functools.partial(last_kernel, size),
        "lon_backward",
        (struct(x.shape, bf16), struct((2, channels), f32)),
        [pltpu.VMEM((size.tokens, channels), f32)],
    )(x, dh, vectors[0], *received, *tables_t)
    block_size = blocks_shape[2]
    return (
        exchange_lon(token_grad),
        block,
        dense,
        mix_total[..., :block_size, :],
        mix_total[..., block_size:, :],
        early,
        lax.psum(late, names),
    )


def body(
    tokens,
    row_map,
    cotangent,
    norm_gain,
    norm_shift,
    mix_in,
    mix_in_bias,
    mix_out,
    mix_out_bias,
    post_gain,
    post_shift,
    fc_in,
    fc_in_bias,
    fc_out,
    fc_out_bias,
):
    size = Sizes(
        lax.axis_size("rows"), lax.axis_size("lon"), row_map.shape[0], tokens.shape[2]
    )
    channels = size.channels
    block_size = mix_in.shape[2]
    hidden_units = fc_in.shape[1]
    blocks_shape = (4 * mix_in.shape[1] // HALVES, round_up(block_size + 1, 16), block_size)
    device = lax.axis_index("rows") * size.lon + lax.axis_index("lon")
    tables, tables_t, invs, invs_t = lon_tables(size)
    cosine, sine, er, ecs = lat_parts(size)
    shape = (size.lon, size.slots_here, size.lons_here, channels)
    x, dy = tokens.reshape(shape), cotangent.reshape(shape)
    vectors = (norm_gain, norm_shift, post_gain, post_shift, fc_out_bias)
    bias_row = fc_in_bias.reshape(1, -1)
    if size.images == 1:
        large = dict(
            tokens=x,
            cot=dy,
            table=tables,
            table_t=tables_t,
            inv=invs,
            inv_t=invs_t,
            ec=ecs,
            er=er,
            fc_in=fc_in,
            fc_out=fc_out,
        )
        small = dict(
            rows=row_map,
            cosine=cosine,
            sine=sine,
            mix_in=mix_in,
            mix_in_bias=mix_in_bias,
            mix_out=mix_out,
            mix_out_bias=mix_out_bias,
            gain1=norm_gain,
            shift1=norm_shift,
            gain2=post_gain,
            shift2=post_shift,
            out_bias=fc_out_bias,
            fc_in_bias=bias_row,
        )
        r = run_layer(size, large, small, row_map, blocks_shape, 0)
        results = (
            r.token_out,
            r.block_out,
            r.dense,
            r.mix_out_grad,
            r.mix_out_bias_grad,
            r.early_out,
            r.late_out,
        )
    else:
        results = run_fields(
            size, blocks_shape, row_map, x, dy, tables, tables_t, invs, invs_t, (cosine, sine, er, ecs), (mix_in, mix_in_bias, mix_out, mix_out_bias), vectors, fc_in, bias_row, fc_out
        )
    token_grad, block, dense, mix_total, mix_bias, early, late = results
    share = hidden_units // size.devices
    return (
        block.reshape(tokens.shape),
        token_grad.reshape(tokens.shape).astype(f32),
        late[0],
        late[1],
        mix_total[0].reshape(mix_in.shape).astype(f32),
        mix_bias[0, ..., 0, :].reshape(mix_in_bias.shape).astype(f32),
        mix_total[1].reshape(mix_in.shape).astype(f32),
        mix_bias[1, ..., 0, :].reshape(mix_out_bias.shape).astype(f32),
        early[1],
        early[2],
        dense[:, :channels].T,
        lax.dynamic_slice_in_dim(early[3:7].reshape(-1), device * share, share),
        dense[:, channels:],
        early[0],
    )


def solution(mesh):
    return jax.shard_map(
        body,
        mesh=mesh,
        in_specs=(P("rows", "lon", None), P(), P("rows", "lon", None)) + (P(),) * 12,
        out_specs=(
            P("rows", "lon", None),
            P("rows", "lon", None),
            P(),
            P(),
            P(),
            P(),
            P(),
            P(),
            P(),
            P(),
            P(None, ("rows", "lon")),
            P(("rows", "lon")),
            P(("rows", "lon"), None),
            P(),
        ),
        check_vma=False,
    )
```

```python
import functools
import math
import types

import jax
import jax.numpy as jnp
import ml_dtypes
import numpy as np
from jax import lax
from jax.experimental import pallas as pl
from jax.experimental.pallas import tpu as pltpu
from jax.sharding import PartitionSpec as P

H = 90
W = 180
KX = 91
HALVES = 2
VMEM_BYTES = 58 * 1024 * 1024

norm_eps = 1e-06
shrink_level = 0.01
half_root = 0.7071067811865476
normal_peak = 0.3989422804014327
MESH = pl.DeviceIdType.MESH
f32 = jnp.float32
bf16 = jnp.bfloat16


def round_up(value, step):
    return -(-value // step) * step


class Stage:
    def __init__(self, size, slots, first_row):
        self.slots = slots
        self.rows = size.lon * len(slots) * size.lons_pad
        self.first_row = first_row
        self.part = slice(first_row, first_row + self.rows)
        self.used = len(slots) * 2 * size.waves
        self.piece = round_up(self.used, 8)
        self.spectrum = size.groups * self.piece
        self.band = size.per_image * self.piece


class Sizes:
    def __init__(self, rows_count, lon_count, slots, channels):
        self.rows = rows_count
        self.lon = lon_count
        self.devices = rows_count * lon_count
        self.images = slots * 15 // (16 * H)
        self.per_image = self.devices // self.images
        self.groups = self.per_image // HALVES
        self.waves = -(-KX // self.groups)
        self.slots_here = slots // self.devices
        self.lons_here = W // lon_count
        self.lons_pad = round_up(self.lons_here, 16)
        self.tokens = lon_count * self.slots_here * self.lons_pad
        self.modes = round_up(H * self.waves, 16)
        self.virtual_slots = self.per_image * self.slots_here
        self.channels = channels
        self.half = channels // HALVES
        cut = -(-self.slots_here * 2 // 3)
        self.stages = []
        first_row = 0
        for low, high in ((0, cut), (cut, self.slots_here)):
            if low < high:
                self.stages.append(Stage(self, tuple(range(low, high)), first_row))
                first_row += self.stages[-1].rows


def lon_tables(size):
    wave = np.arange(size.groups * size.waves)
    lon_index = np.arange(W)
    product = (lon_index[:, None] * wave[None, :]) % W
    angle = product.astype(np.float32) * np.float32(2.0 * math.pi / W)
    scale = np.float32(1.0 / math.sqrt(W))
    cosine = (np.cos(angle) * scale).astype(ml_dtypes.bfloat16).astype(np.float32)
    sine = (-np.sin(angle) * scale).astype(ml_dtypes.bfloat16).astype(np.float32)
    live = (wave < KX).astype(np.float32)
    factor = np.where((wave == 0) | (wave == W // 2), 1.0, 2.0).astype(np.float32)
    both = np.stack([cosine, sine]) * live
    result = []
    for weight in (np.ones_like(factor), factor):
        values = (both * weight).reshape(2, size.lon, size.lons_here, size.groups, size.waves)
        values = np.transpose(values, (3, 0, 4, 1, 2)).reshape(
            size.groups, 2 * size.waves, size.lon, size.lons_here
        )
        tables = []
        for stage in size.stages:
            count = len(stage.slots)
            table = np.zeros(
                (size.groups, stage.piece, size.lon, count, size.lons_pad), np.float32
            )
            for slot in range(count):
                start = slot * 2 * size.waves
                table[:, start : start + 2 * size.waves, :, slot, : size.lons_here] = values
            tables.append(table.reshape(stage.spectrum, stage.rows).astype(ml_dtypes.bfloat16))
        result.append([jnp.asarray(t) for t in tables])
        result.append([jnp.asarray(np.ascontiguousarray(t.T)) for t in tables])
    return result


def lat_parts(size):
    lat_index = np.arange(H)
    angle = ((lat_index[:, None] * lat_index[None, :]) % H).astype(np.float32) * np.float32(
        2.0 * math.pi / H
    )
    scale = np.float32(1.0 / math.sqrt(H))
    cosine = np.zeros((96, 96), np.float32)
    sine = np.zeros((96, 96), np.float32)
    cosine[:H, :H] = np.cos(angle) * scale
    sine[:H, :H] = np.sin(angle) * scale
    spread_rows = np.zeros((2, size.modes, 2, 96), np.float32)
    for part in range(2):
        for lat in range(H):
            for wave in range(size.waves):
                spread_rows[part, lat * size.waves + wave, part, lat] = 1.0
    spread_cols = []
    for stage in size.stages:
        spread = np.zeros((2, 128, size.per_image, stage.piece), np.float32)
        for device in range(size.per_image):
            for place, slot in enumerate(stage.slots):
                for part in range(2):
                    start = (place * 2 + part) * size.waves
                    spread[
                        part, device * size.slots_here + slot, device, start : start + size.waves
                    ] = 1.0
        spread_cols.append(spread.reshape(256, stage.band))
    low = ml_dtypes.bfloat16
    return (
        jnp.asarray(cosine.astype(low)),
        jnp.asarray(sine.astype(low)),
        jnp.asarray(spread_rows.reshape(2 * size.modes, 192).astype(low)),
        [jnp.asarray(spread.astype(low)) for spread in spread_cols],
    )


def smooth_gate(values):
    return 0.5 * values * (1.0 + lax.erf(values * half_root))


def gate_both(values):
    half_phi = 0.5 * (1.0 + lax.erf(values * half_root))
    density = values * normal_peak * jnp.exp(-0.5 * values * values)
    return values * half_phi, half_phi + density


def gate_slope(values):
    return gate_both(values)[1]


def soft_shrink(values):
    return values - shrink_level * values * lax.rsqrt(values * values + shrink_level * shrink_level)


def shrink_slope(values):
    inverse = lax.rsqrt(values * values + shrink_level * shrink_level)
    return 1.0 - shrink_level * shrink_level * shrink_level * inverse * inverse * inverse


def norm_parts(values):
    center = values - jnp.mean(values, axis=-1, keepdims=True)
    spread = lax.rsqrt(jnp.mean(center * center, axis=-1, keepdims=True) + norm_eps)
    return center * spread, spread


def norm_back(scaled, unit, spread):
    return spread * (
        scaled
        - jnp.mean(scaled, axis=-1, keepdims=True)
        - unit * jnp.mean(scaled * unit, axis=-1, keepdims=True)
    )


def mm(left, right):
    return jnp.dot(left, right, preferred_element_type=f32)


def mm_t(left, right):
    return lax.dot_general(left, right, (((1,), (1,)), ((), ())), preferred_element_type=f32)


def t_mm(left, right):
    return lax.dot_general(left, right, (((0,), (0,)), ((), ())), preferred_element_type=f32)


def whole(count):
    return [pl.BlockSpec(memory_space=pltpu.VMEM)] * count


def call_local(kernel, name, outs, scratch=()):
    def run(*operands):
        return pl.pallas_call(
            kernel,
            out_shape=outs,
            in_specs=whole(len(operands)),
            out_specs=jax.tree.map(lambda _: pl.BlockSpec(memory_space=pltpu.VMEM), outs),
            scratch_shapes=list(scratch),
            compiler_params=pltpu.CompilerParams(vmem_limit_bytes=VMEM_BYTES),
            name=name,
        )(*operands)

    return run


def struct(shape, dtype):
    return jax.ShapeDtypeStruct(shape, dtype)


def wave_of(index, period, used, waves, other):
    within = index - period * jnp.floor((index + 0.5) * (1.0 / period))
    wave = within - waves * jnp.floor((within + 0.5) * (1.0 / waves))
    return jnp.where(within < used, wave, other)


def build_lat_tables(size, rows_ref, cos_ref, sin_ref, er_ref, ec_refs, lat_refs, lat_t_refs):
    slots = rows_ref.shape[0]
    lat_of = lax.broadcasted_iota(jnp.int32, (96, slots), 0)
    hot = (lat_of == rows_ref[...].reshape(1, slots)).astype(f32)
    hot = jnp.concatenate([hot, jnp.zeros((96, 128 - slots), f32)], axis=1).astype(bf16)
    cosine = mm(cos_ref[...], hot)
    sine = mm(sin_ref[...], hot)
    top = jnp.concatenate([cosine, sine], axis=1)
    bottom = jnp.concatenate([-sine, cosine], axis=1)
    base = jnp.concatenate([top, bottom], axis=0).astype(bf16)

    def row_waves(shape, dim):
        index = lax.broadcasted_iota(jnp.int32, shape, dim).astype(f32)
        return wave_of(index, size.modes, H * size.waves, size.waves, -1.0)

    def col_waves(stage, shape, dim):
        index = lax.broadcasted_iota(jnp.int32, shape, dim).astype(f32)
        return wave_of(index, stage.piece, stage.used, size.waves, -2.0)

    modes = 2 * size.modes
    for stage, ec_ref, lat_ref, lat_t_ref in zip(size.stages, ec_refs, lat_refs, lat_t_refs):
        keep = row_waves((modes, 1), 0) == col_waves(stage, (1, stage.band), 1)
        keep_t = col_waves(stage, (stage.band, 1), 0) == row_waves((1, modes), 1)
        columns = mm(base, ec_ref[...]).astype(bf16)
        lat_ref[...] = jnp.where(keep, mm(er_ref[...], columns), 0.0).astype(bf16)
        table_t = lax.dot_general(
            columns, er_ref[...], (((0,), (1,)), ((), ())), preferred_element_type=f32
        )
        lat_t_ref[...] = jnp.where(keep_t, table_t, 0.0).astype(bf16)


def build_block_matrix(size, weight_ref, bias_ref, half, matrix_ref, row_ref):
    block_size = weight_ref.shape[2]
    blocks = size.half // block_size
    matrix_ref[...] = jnp.zeros_like(matrix_ref)
    for block in range(blocks):
        real = weight_ref[0, half * blocks + block]
        imag = weight_ref[1, half * blocks + block]
        near = slice(block * block_size, (block + 1) * block_size)
        far = slice(size.half + block * block_size, size.half + (block + 1) * block_size)
        matrix_ref[near, near] = real
        matrix_ref[near, far] = imag
        matrix_ref[far, near] = -imag
        matrix_ref[far, far] = real
        row_ref[0:1, near] = bias_ref[0, pl.ds(half * blocks + block, 1), :]
        row_ref[0:1, far] = bias_ref[1, pl.ds(half * blocks + block, 1), :]


def half_of(size):
    device = lax.axis_index("rows") * size.lon + lax.axis_index("lon")
    return (device % size.per_image) // size.groups


def pad_plane(size, plane):
    extra = size.lons_pad - size.lons_here
    return jnp.concatenate([plane, jnp.zeros((extra, plane.shape[1]), plane.dtype)], axis=0)


def at(step, count, action):
    for i in range(count):

        @pl.when(step == i)
        def _():
            action(i)


def over_planes(size, stage, body, *sums, first=0, then=None):
    def step(index, sums):
        source = (first + index) % size.lon
        for place, slot in enumerate(stage.slots):
            start = stage.first_row + pl.multiple_of(
                (source * len(stage.slots) + place) * size.lons_pad, size.lons_pad
            )
            start = pl.multiple_of(start, size.lons_pad)
            sums = body(source, slot, pl.ds(start, size.lons_pad), *sums)
        if then is not None:
            at(index, size.lon, then)
        return sums

    return lax.fori_loop(0, size.lon, step, sums)


def as_row(ref):
    return ref[...].reshape(1, -1)


def write_pieces(size, stage, values, out_ref):
    for half in range(HALVES):
        for group in range(size.groups):
            out_ref[half * size.groups + group] = values[
                group * stage.piece : (group + 1) * stage.piece,
                half * size.half : (half + 1) * size.half,
            ].astype(bf16)


def read_pieces(ref, first, count):
    return jnp.concatenate([ref[first + i].astype(f32) for i in range(count)], axis=0).astype(bf16)


def read_spectrum(size, ref):
    return jnp.concatenate(
        [read_pieces(ref, half * size.groups, size.groups) for half in range(HALVES)], axis=1
    )


def first_norm(size, stage, x_ref, gain, shift, low_ref):
    def plane(source, slot, rows):
        x = pad_plane(size, x_ref[source, slot].astype(f32))
        unit, _ = norm_parts(x)
        low_ref[rows, :] = (unit * gain + shift).astype(bf16)
        return ()

    over_planes(size, stage, plane)


def first_kernel(size, x_ref, gain_ref, shift_ref, *refs):
    count = len(size.stages)
    tables, sends, low_ref = refs[:count], refs[count : 2 * count], refs[-1]
    for stage, table_ref, send_ref in zip(size.stages, tables, sends):
        first_norm(size, stage, x_ref, as_row(gain_ref), as_row(shift_ref), low_ref)
        write_pieces(size, stage, mm(table_ref[...], low_ref[stage.part, :]), send_ref)


def add_modes(size, recv_ref, lat_ref, modes_ref):
    modes_ref[...] += mm(lat_ref[...], read_pieces(recv_ref, 0, size.per_image))


def side_by_side(size, modes_ref):
    return jnp.concatenate(
        [modes_ref[: size.modes, :], modes_ref[size.modes :, :]], axis=1
    ).astype(bf16)


def stack_parts(size, values, stacked_ref):
    stacked_ref[: size.modes, :] = values[:, : size.half].astype(bf16)
    stacked_ref[size.modes :, :] = values[:, size.half :].astype(bf16)


def modes_back(size, stage, lat_t_ref, stacked_ref, send_ref):
    back = mm(lat_t_ref[...], stacked_ref[...])
    for device in range(size.per_image):
        send_ref[device] = back[device * stage.piece : (device + 1) * stage.piece].astype(bf16)


def mix_layers(size, modes_ref, w1_ref, b1_ref, w2_ref, b2_ref, band_ref, inner_ref, gated_ref, outer_ref, stacked_ref):
    band = side_by_side(size, modes_ref)
    band_ref[...] = band
    inner = mm(band, w1_ref[...]) + b1_ref[...]
    inner_ref[...] = inner
    gated = smooth_gate(inner).astype(bf16)
    gated_ref[...] = gated
    outer = mm(gated, w2_ref[...]) + b2_ref[...]
    outer_ref[...] = outer
    stack_parts(size, soft_shrink(outer), stacked_ref)


def slopes_in_place(inner_ref, outer_ref):
    inner_ref[...] = gate_slope(inner_ref[...])
    outer_ref[...] = shrink_slope(outer_ref[...])


def mix_kernel(size, w1_ref, b1_ref, w2_ref, b2_ref, *refs):
    count = len(size.stages)
    recvs, lats, lats_t, sends = [refs[i * count : (i + 1) * count] for i in range(4)]
    band_ref, inner_ref, gated_ref, outer_ref, modes_ref, stacked_ref = refs[4 * count :]
    modes_ref[...] = jnp.zeros_like(modes_ref)
    for recv_ref, lat_ref in zip(recvs, lats):
        add_modes(size, recv_ref, lat_ref, modes_ref)
    mix_layers(size, modes_ref, w1_ref, b1_ref, w2_ref, b2_ref, band_ref, inner_ref, gated_ref, outer_ref, stacked_ref)
    for stage, lat_t_ref, send_ref in zip(size.stages, lats_t, sends):
        modes_back(size, stage, lat_t_ref, stacked_ref, send_ref)
    slopes_in_place(inner_ref, outer_ref)


def mix_layers_back(size, modes_ref, w1_ref, w2_ref, inner_ref, outer_ref, outer_grad_ref, inner_grad_ref, stacked_ref):
    upstream = side_by_side(size, modes_ref)
    outer_grad = (upstream.astype(f32) * outer_ref[...]).astype(bf16)
    outer_grad_ref[...] = outer_grad
    inner_grad = (mm_t(outer_grad, w2_ref[...]) * inner_ref[...]).astype(bf16)
    inner_grad_ref[...] = inner_grad
    stack_parts(size, mm_t(inner_grad, w1_ref[...]), stacked_ref)


def mix_back_weights(size, band_ref, gated_ref, outer_grad_ref, inner_grad_ref, out_ref):
    half = size.half
    block_size = out_ref.shape[-1]
    blocks = half // block_size
    rest = out_ref.shape[-2] - block_size
    for layer, (value_ref, grad_ref) in enumerate(
        ((band_ref, inner_grad_ref), (gated_ref, outer_grad_ref))
    ):
        grad = grad_ref[...]
        total = t_mm(value_ref[...], grad)
        bias = jnp.sum(grad.astype(f32), axis=0, keepdims=True)
        for block in range(blocks):
            near = slice(block * block_size, (block + 1) * block_size)
            far = slice(half + block * block_size, half + (block + 1) * block_size)
            for part, values, row in (
                (0, total[near, near] + total[far, far], bias[:, near]),
                (1, total[near, far] - total[far, near], bias[:, far]),
            ):
                place = (layer * 2 + part) * blocks + block
                at = (place // 2, place % 2) if len(out_ref.shape) == 4 else (place,)
                out_ref[at + (slice(0, block_size),)] = values.astype(bf16)
                out_ref[at + (slice(block_size, None),)] = jnp.broadcast_to(
                    row, (rest, block_size)
                ).astype(bf16)


def mix_back_kernel(size, w1_ref, w2_ref, band_ref, inner_ref, gated_ref, outer_ref, *refs):
    count = len(size.stages)
    recvs, lats, lats_t, sends = [refs[i * count : (i + 1) * count] for i in range(4)]
    grad_ref, outer_grad_ref, inner_grad_ref, modes_ref, stacked_ref = refs[4 * count :]
    modes_ref[...] = jnp.zeros_like(modes_ref)
    for recv_ref, lat_ref in zip(recvs, lats):
        add_modes(size, recv_ref, lat_ref, modes_ref)
    mix_layers_back(size, modes_ref, w1_ref, w2_ref, inner_ref, outer_ref, outer_grad_ref, inner_grad_ref, stacked_ref)
    for stage, lat_t_ref, send_ref in zip(size.stages, lats_t, sends):
        modes_back(size, stage, lat_t_ref, stacked_ref, send_ref)
    mix_back_weights(size, band_ref, gated_ref, outer_grad_ref, inner_grad_ref, grad_ref)


def live_of(size, map_ref, slot):
    first_slot = (lax.axis_index("rows") * size.lon + lax.axis_index("lon")) * size.slots_here
    return jnp.where(map_ref[first_slot + slot] >= 0, 1.0, 0.0)


def local_planes(size, stage, map_ref, x_ref, dy_ref, gain1, shift1, res_ref, values_ref):
    def plane(source, slot, rows, up_sum):
        x = pad_plane(size, x_ref[source, slot].astype(f32))
        unit, _ = norm_parts(x)
        res_ref[rows, :] = (unit * gain1 + shift1) + x
        up = pad_plane(size, dy_ref[source, slot].astype(f32) * live_of(size, map_ref, slot))
        values_ref[1, rows, :] = up.astype(bf16)
        return (up_sum + jnp.sum(up, axis=0, keepdims=True),)

    return over_planes(size, stage, plane, jnp.zeros((1, size.channels), f32))[0]


def residual_planes(size, stage, recv_ref, inv_t_ref, gain2, shift2, res_ref, values_ref):
    res_ref[stage.part, :] += mm(inv_t_ref[...], read_spectrum(size, recv_ref))

    def plane(source, slot, rows):
        unit, _ = norm_parts(res_ref[rows, :])
        values_ref[0, rows, :] = (unit * gain2 + shift2).astype(bf16)
        return ()

    over_planes(size, stage, plane)


def hidden_part(part, values_ref, fc_in, bias, fc_out, acc_ref, back_ref):
    gate, slope = gate_both(mm(values_ref[0, part, :], fc_in) + bias)
    hidden = gate.astype(bf16)
    acc_ref[part, :] += mm(hidden, fc_out)
    hidden_grad = (mm_t(values_ref[1, part, :], fc_out) * slope).astype(bf16)
    back_ref[part, :] += mm_t(hidden_grad, fc_in)
    return hidden, hidden_grad


def residual_back_planes(size, stage, values_ref, res_ref, gain2, back_ref, grad_ref):
    def plane(source, slot, rows, gain_sum, shift_sum):
        unit, spread = norm_parts(res_ref[rows, :])
        grad = back_ref[rows, :]
        gain_sum = gain_sum + jnp.sum(grad * unit, axis=0, keepdims=True)
        shift_sum = shift_sum + jnp.sum(grad, axis=0, keepdims=True)
        grad = values_ref[1, rows, :].astype(f32) + norm_back(grad * gain2, unit, spread)
        back_ref[rows, :] = grad
        grad_ref[rows, :] = grad.astype(bf16)
        return gain_sum, shift_sum

    zero = jnp.zeros((1, size.channels), f32)
    return over_planes(size, stage, plane, zero, zero)


def block_planes(size, stage, map_ref, res_ref, acc_ref, out_bias, block_ref):
    def plane(source, slot, rows):
        block = (res_ref[rows, :] + (acc_ref[rows, :] + out_bias)) * live_of(size, map_ref, slot)
        block_ref[source, slot] = block[: size.lons_here].astype(bf16)
        return ()

    over_planes(size, stage, plane)


def mlp_kernel(
    size,
    map_ref,
    x_ref,
    dy_ref,
    gain1_ref,
    shift1_ref,
    gain2_ref,
    shift2_ref,
    out_bias_ref,
    fc_in_ref,
    fc_in_bias_ref,
    fc_out_ref,
    *refs,
):
    count = len(size.stages)
    recvs, invs_t, invs, sends = [refs[i * count : (i + 1) * count] for i in range(4)]
    block_ref, dh_ref, hidden_ref, values_ref, small_ref, res_ref, grad_ref, acc_ref = refs[4 * count :]
    step = pl.program_id(0)

    @pl.when(step == 0)
    def _():
        small_ref[...] = jnp.zeros_like(small_ref)
        for stage, recv_ref, inv_t_ref in zip(size.stages, recvs, invs_t):
            small_ref[0:1, :] += local_planes(
                size, stage, map_ref, x_ref, dy_ref, as_row(gain1_ref), as_row(shift1_ref), res_ref, values_ref
            )
            residual_planes(
                size, stage, recv_ref, inv_t_ref, as_row(gain2_ref), as_row(shift2_ref), res_ref, values_ref
            )
        acc_ref[...] = jnp.zeros_like(acc_ref)
        dh_ref[...] = jnp.zeros_like(dh_ref)

    hidden, hidden_grad = hidden_part(
        slice(0, size.tokens), values_ref, fc_in_ref[...], fc_in_bias_ref[...], fc_out_ref[...], acc_ref, dh_ref
    )
    small_ref[pl.ds(3 + step, 1), :] = jnp.sum(hidden_grad.astype(f32), axis=0, keepdims=True)
    hidden_ref[0] = hidden_grad
    hidden_ref[1] = hidden

    @pl.when(step == pl.num_programs(0) - 1)
    def _():
        for stage, inv_ref, send_ref in zip(size.stages, invs, sends):
            block_planes(size, stage, map_ref, res_ref, acc_ref, as_row(out_bias_ref), block_ref)
            gain_sum, shift_sum = residual_back_planes(
                size, stage, values_ref, res_ref, as_row(gain2_ref), dh_ref, grad_ref
            )
            small_ref[1:2, :] += gain_sum
            small_ref[2:3, :] += shift_sum
            write_pieces(size, stage, mm(inv_ref[...], grad_ref[stage.part, :]), send_ref)


def run_mlp(size, hidden_units, row_map, x, dy, vectors, fc_in, fc_in_bias, fc_out, received, invs_t, invs):
    channels = size.channels
    parts = hidden_units // channels
    fixed = pl.BlockSpec(memory_space=pltpu.VMEM)
    tokens = (size.tokens, channels)
    count = len(size.stages)
    out = pl.pallas_call(
        functools.partial(mlp_kernel, size),
        grid=(parts,),
        in_specs=[pl.BlockSpec(memory_space=pltpu.SMEM)]
        + [fixed] * (2 + len(vectors))
        + [
            pl.BlockSpec((channels, channels), lambda i: (0, i)),
            pl.BlockSpec((1, channels), lambda i: (0, i)),
            pl.BlockSpec((channels, channels), lambda i: (i, 0)),
        ]
        + [fixed] * (3 * count),
        out_specs=tuple(
            [fixed] * (count + 2)
            + [pl.BlockSpec((None, 2) + tokens, lambda i: (i, 0, 0, 0))]
            + [fixed] * 2
        ),
        out_shape=tuple(
            [struct(piece.shape, bf16) for piece in received]
            + [
                struct(x.shape, bf16),
                struct(tokens, f32),
                struct((parts, 2) + tokens, bf16),
                struct((2,) + tokens, bf16),
                struct((round_up(3 + parts, 8), channels), f32),
            ]
        ),
        scratch_shapes=[
            pltpu.VMEM(tokens, f32),
            pltpu.VMEM(tokens, bf16),
            pltpu.VMEM(tokens, f32),
        ],
        compiler_params=pltpu.CompilerParams(vmem_limit_bytes=VMEM_BYTES),
        name="mlp",
    )(row_map, x, dy, *vectors, fc_in, fc_in_bias, fc_out, *received, *invs_t, *invs)
    return (out[:count],) + tuple(out[count:])


def wide_kernel(hidden_ref, values_ref, wide_ref):
    channels = values_ref.shape[2]
    for part in range(hidden_ref.shape[0]):
        rows = slice(part * channels, (part + 1) * channels)
        wide_ref[rows, :channels] = t_mm(hidden_ref[part, 0], values_ref[0]).astype(bf16)
        wide_ref[rows, channels:] = t_mm(hidden_ref[part, 1], values_ref[1]).astype(bf16)


def last_planes(size, stage, recv_ref, x_ref, dh_ref, table_t_ref, gain_ref, filtered_ref, out_ref, first=0, then=None):
    gain = as_row(gain_ref)
    filtered_ref[stage.part, :] = mm(table_t_ref[...], read_spectrum(size, recv_ref))

    def plane(source, slot, rows, gain_sum, shift_sum):
        unit, spread = norm_parts(pad_plane(size, x_ref[source, slot].astype(f32)))
        base = dh_ref[rows, :]
        grad = base + filtered_ref[rows, :]
        gain_sum = gain_sum + jnp.sum(grad * unit, axis=0, keepdims=True)
        shift_sum = shift_sum + jnp.sum(grad, axis=0, keepdims=True)
        grad = base + norm_back(grad * gain, unit, spread)
        out_ref[source, slot] = grad[: size.lons_here].astype(bf16)
        return gain_sum, shift_sum

    zero = jnp.zeros((1, size.channels), f32)
    return over_planes(size, stage, plane, zero, zero, first=first, then=then)


def last_kernel(size, x_ref, dh_ref, gain_ref, *refs):
    count = len(size.stages)
    recvs, tables_t = refs[:count], refs[count : 2 * count]
    out_ref, small_ref, filtered_ref = refs[2 * count :]
    small_ref[...] = jnp.zeros_like(small_ref)
    for stage, recv_ref, table_t_ref in zip(size.stages, recvs, tables_t):
        gain_sum, shift_sum = last_planes(size, stage, recv_ref, x_ref, dh_ref, table_t_ref, gain_ref, filtered_ref, out_ref)
        small_ref[0:1, :] += gain_sum
        small_ref[1:2, :] += shift_sum


def partners(lon_count):
    row = lax.axis_index("rows")
    lon = lax.axis_index("lon")
    core = {"rows": row, "lon": lon + 1 - 2 * (lon % 2)}
    along_y = {"rows": row, "lon": (lon + 2) % 4}
    along_x = {"rows": row + 1 - 2 * (row % 2), "lon": lon}
    far_z = {"rows": (row + 4) % 8, "lon": lon}
    return core, along_y, along_x, far_z


def greet(lon_count, count):
    row = lax.axis_index("rows")
    lon = lax.axis_index("lon")
    me = row * lon_count + lon
    barrier = pltpu.get_barrier_semaphore()
    for offset in range(1, count):
        other = (me + offset) % count
        pl.semaphore_signal(
            barrier,
            inc=1,
            device_id={"rows": other // lon_count, "lon": other % lon_count},
            device_id_type=MESH,
        )
    pl.semaphore_wait(barrier, count - 1)


class Sender:
    def __init__(self, send_sem, recv_sem):
        self.send_sem = send_sem
        self.recv_sem = recv_sem
        self.used = 0

    def make(self, source, target, device):
        copy = pltpu.make_async_remote_copy(
            src_ref=source,
            dst_ref=target,
            send_sem=self.send_sem.at[self.used],
            recv_sem=self.recv_sem.at[self.used],
            device_id=device,
            device_id_type=MESH,
        )
        self.used += 1
        return copy

    def start(self, source, target, device):
        copy = self.make(source, target, device)
        copy.start()
        return copy


class Mover:
    def __init__(self, sem):
        self.sem = sem
        self.used = 0

    def make(self, source, target):
        copy = pltpu.make_async_copy(source, target, self.sem.at[self.used])
        self.used += 1
        return copy

    def start(self, source, target):
        copy = self.make(source, target)
        copy.start()
        return copy


def make_all(size, source_ref, out_ref, sender, mover):
    row = lax.axis_index("rows")
    lon = lax.axis_index("lon")
    me = row * size.lon + lon
    copies = []
    for row_step in range(size.rows):
        for lon_step in range(size.lon):
            to_row = (row + row_step) % size.rows
            to_lon = (lon + lon_step) % size.lon
            piece = source_ref.at[to_row * size.lon + to_lon]
            if row_step == 0 and lon_step == 0:
                copies.append(mover.make(piece, out_ref.at[me]))
            else:
                copies.append(
                    sender.make(piece, out_ref.at[me], {"rows": to_row, "lon": to_lon})
                )
    return copies


def make_lon(stage, source_ref, out_ref, sender, mover):
    row = lax.axis_index("rows")
    me = lax.axis_index("lon")
    count = source_ref.shape[0]
    slots = pl.ds(stage.slots[0], len(stage.slots))
    copies = []
    for offset in range(1, count):
        other = (me + offset) % count
        copies.append(
            sender.make(
                source_ref.at[other, slots], out_ref.at[me, slots], {"rows": row, "lon": other}
            )
        )
    copies.append(mover.make(source_ref.at[me, slots], out_ref.at[me, slots]))
    return copies


def begin(copies):
    for copy in copies:
        copy.start()
    return copies


def finish(copies):
    for copy in copies:
        copy.wait()


def call_remote(kernel, name, number, outs, spaces, out_spaces, sends, moves, scratch, operands):
    return pl.pallas_call(
        kernel,
        out_shape=outs,
        in_specs=[pl.BlockSpec(memory_space=space) for space in spaces],
        out_specs=tuple(pl.BlockSpec(memory_space=space) for space in out_spaces),
        scratch_shapes=[
            pltpu.SemaphoreType.DMA((sends,)),
            pltpu.SemaphoreType.DMA((sends,)),
            pltpu.SemaphoreType.DMA((moves,)),
        ]
        + list(scratch),
        compiler_params=pltpu.CompilerParams(
            collective_id=number, has_side_effects=True, vmem_limit_bytes=VMEM_BYTES
        ),
        name=name,
    )(*operands)


def add_to(total_ref, other_ref):
    @pl.loop(0, total_ref.shape[0])
    def _(first):
        if len(total_ref.shape) == 3:
            total = total_ref[first].astype(f32) + other_ref[first].astype(f32)
            total_ref[first] = total.astype(total_ref.dtype)
        else:
            for second in range(total_ref.shape[1]):
                total = total_ref[first, second].astype(f32) + other_ref[first, second].astype(f32)
                total_ref[first, second] = total.astype(total_ref.dtype)


def start_same(lon_count, count, source_ref, out_ref, sender, mover):
    me = lax.axis_index("rows") * lon_count + lax.axis_index("lon")
    copies = []
    for offset in range(1, count):
        other = (me + offset) % count
        copies.append(
            sender.start(
                source_ref, out_ref.at[me], {"rows": other // lon_count, "lon": other % lon_count}
            )
        )
    copies.append(mover.start(source_ref, out_ref.at[me]))
    return copies


def named(group, refs):
    leaves, tree = jax.tree.flatten(group)
    return jax.tree.unflatten(tree, [next(refs) for _ in leaves])


def layer_kernel(size, groups_of, *refs):
    found = iter(refs)
    r = types.SimpleNamespace()
    for arrays in groups_of:
        r.__dict__.update(named(arrays, found))
    r.hbm = types.SimpleNamespace(**r.large, **r.kept)
    stages = size.stages
    channels = size.channels
    lon_count, count, groups = size.lon, size.devices, size.groups
    row = lax.axis_index("rows")
    lon = lax.axis_index("lon")
    me = row * lon_count + lon
    z = row // 2
    x = row % 2
    y = lon // 2
    core = lon % 2
    group = me % groups
    base = me - group
    half = me // groups
    to_core, to_y, to_x, far_z = partners(lon_count)
    near = z + 1 - 2 * (z % 2)
    mirror = 3 - z
    to_near = {"rows": near * 2 + x, "lon": lon}
    to_mirror = {"rows": mirror * 2 + x, "lon": lon}
    parts = 4
    share = r.wide.shape[-2]
    sender, mover = Sender(r.a_send_sem, r.b_recv_sem), Mover(r.c_move_sem)

    def order(step):
        chip = jnp.where(step % 2 == 0, near, z)
        return jnp.where(step < 2, 3 - chip, chip)

    def part_place(step):
        return pl.ds(pl.multiple_of(order(step) * channels, channels), channels)

    cotangents = [make_lon(stage, r.hbm.cot, r.dy, sender, mover) for stage in stages]
    by_e = [
        make_all(size, source, target, sender, mover)
        for source, target in zip(r.send_e, r.recv_e)
    ]
    by_g = [
        make_all(size, source, target, sender, mover)
        for source, target in zip(r.send_g, r.recv_g)
    ]
    blocks = [make_lon(stage, r.block, r.block_out, sender, mover) for stage in stages]
    by_core = [
        [
            sender.make(r.wide.at[i % 2, 0, :, :, 1 - core], r.a_core.at[i], to_core),
            sender.make(r.wide.at[i % 2, 1, :, :, 1 - core], r.b_core.at[i], to_core),
        ]
        for i in range(parts)
    ]
    by_one = [
        [
            sender.make(r.a_core.at[i, 1 - x], r.a_one.at[i], to_x),
            sender.make(r.b_core.at[i, :, 1 - y], r.b_one.at[i], to_y),
        ]
        for i in range(parts)
    ]
    by_two = [
        [
            sender.make(r.a_one.at[i, 1 - y], r.a_two.at[i], to_y),
            sender.make(r.b_one.at[i, 1 - x], r.b_two.at[i], to_x),
        ]
        for i in range(parts)
    ]
    by_near = [
        [
            sender.make(r.a_two.at[2 * i], r.a_near.at[i], to_near),
            sender.make(r.b_two.at[2 * i], r.b_near.at[i], to_near),
        ]
        for i in range(2)
    ]
    by_early = [
        sender.make(r.early, r.early_land.at[i], device)
        for i, device in enumerate((to_core, to_x, to_y, to_near, to_mirror))
    ]
    tables_back = [
        mover.make(source, target)
        for source, target in zip(r.hbm.table_t, r.table_t)
    ]

    def core_end(step):
        finish(by_core[step])
        add_to(r.a_core.at[step], r.wide.at[step % 2, 0, :, :, core])
        by_one[step][0].start()
        add_to(r.b_core.at[step], r.wide.at[step % 2, 1, :, :, core])
        by_one[step][1].start()

    def one_end(step):
        by_one[step][0].wait()
        add_to(r.a_one.at[step], r.a_core.at[step, x])
        by_two[step][0].start()
        by_one[step][1].wait()
        add_to(r.b_one.at[step], r.b_core.at[step, :, y])
        by_two[step][1].start()

    def two_end(step):
        finish(by_two[step])
        for total, kept in ((r.a_two, r.a_one.at[step, y]), (r.b_two, r.b_one.at[step, x])):
            total[step] = (total[step].astype(f32) + kept[...].astype(f32)).astype(bf16)

    def early_step(step):
        by_early[step].wait()
        r.early[...] = r.early[...] + r.early_land[step]
        if step + 1 < len(by_early):
            by_early[step + 1].start()

    def forward(*scoped):
        f = types.SimpleNamespace(**named(forward_scratch(size), iter(scoped)))
        tables = [
            mover.start(source, target)
            for source, target in zip(r.hbm.table, f.table)
        ]
        loads = [mover.start(r.hbm.er, f.er)]
        loads += [mover.start(a, b) for a, b in zip(r.hbm.ec, f.ec)]
        begin(tables_back)
        greet(lon_count, count)
        tokens = [begin(make_lon(stage, r.hbm.tokens, r.x, sender, mover)) for stage in stages]
        build_block_matrix(size, r.mix_in, r.mix_in_bias, half, f.w1, f.b1)
        build_block_matrix(size, r.mix_out, r.mix_out_bias, half, f.w2, f.b2)
        stores = [mover.start(f.w1, r.hbm.w1), mover.start(f.w2, r.hbm.w2)]
        by_a = [
            make_all(size, source, target, sender, mover)
            for source, target in zip(f.send_a, r.recv_a)
        ]
        for i, stage in enumerate(stages):
            finish(tokens[i])
            first_norm(size, stage, r.x, as_row(r.gain1), as_row(r.shift1), f.low)
            tables[i].wait()
            write_pieces(size, stage, mm(f.table[i][...], f.low[stage.part, :]), f.send_a[i])
            begin(by_a[i])
        for copies in cotangents:
            begin(copies)
        finish(loads)
        build_lat_tables(size, r.rows, r.cosine, r.sine, f.er, f.ec, r.lat, r.lat_t)
        f.modes[...] = jnp.zeros_like(f.modes)
        for i in range(len(stages)):
            finish(by_a[i])
            add_modes(size, r.recv_a[i], r.lat[i], f.modes)
        mix_layers(size, f.modes, f.w1, f.b1, f.w2, f.b2, f.band, f.inner, f.gated, f.outer, f.stacked)
        for i, stage in enumerate(stages):
            modes_back(size, stage, r.lat_t[i], f.stacked, r.send_e[i])
            begin(by_e[i])
        stores += [mover.start(f.band, r.hbm.band), mover.start(f.gated, r.hbm.gated)]
        slopes_in_place(f.inner, f.outer)
        stores += [mover.start(f.inner, r.hbm.inner), mover.start(f.outer, r.hbm.outer)]
        finish(stores)

    def front(*scoped):
        f = types.SimpleNamespace(**named(front_scratch(size), iter(scoped)))
        rounds = len(stages) * parts
        part_loads = [
            [
                mover.make(r.hbm.fc_in.at[:, part_place(i % parts)], f.fc_in.at[i % 2]),
                mover.make(r.hbm.fc_out.at[part_place(i % parts), :], f.fc_out.at[i % 2]),
            ]
            for i in range(rounds)
        ]
        inv_t_loads = [mover.start(a, b) for a, b in zip(r.hbm.inv_t, f.inv_t)]
        begin(part_loads[0])
        begin(part_loads[1])
        inv_loads = [mover.start(a, b) for a, b in zip(r.hbm.inv, f.inv)]
        r.early[...] = jnp.zeros_like(r.early)
        f.acc[...] = jnp.zeros_like(f.acc)
        r.dh[...] = jnp.zeros_like(r.dh)
        for i, stage in enumerate(stages):
            finish(cotangents[i])
            r.early[0:1, :] += local_planes(
                size, stage, r.map, r.x, r.dy, as_row(r.gain1), as_row(r.shift1), f.res, f.values
            )
        finish(inv_t_loads)
        finish(inv_loads)

        def weights(step):
            @pl.loop(0, 2)
            def _(which):
                product = t_mm(f.hidden[step, which], f.values[which])
                for i in range(8):
                    r.wide[step % 2, which, i // 4, i // 2 % 2, i % 2] = product[
                        i * share : (i + 1) * share
                    ].astype(bf16)

        for i, stage in enumerate(stages):
            is_last = i == len(stages) - 1
            finish(by_e[i])
            residual_planes(
                size, stage, r.recv_e[i], f.inv_t[i], as_row(r.gain2), as_row(r.shift2), f.res, f.values
            )

            @pl.loop(0, parts)
            def _(step):
                slot = step % 2
                at(step, parts, lambda k: finish(part_loads[i * parts + k]))
                hidden, hidden_grad = hidden_part(
                    stage.part, f.values, f.fc_in[slot], r.fc_in_bias[:, part_place(step)], f.fc_out[slot], f.acc, r.dh
                )
                r.early[pl.ds(3 + order(step), 1), :] += jnp.sum(
                    hidden_grad.astype(f32), axis=0, keepdims=True
                )
                f.hidden[step, 0, stage.part] = hidden_grad
                f.hidden[step, 1, stage.part] = hidden

                def load_next(k):
                    if i * parts + k + 2 < rounds:
                        begin(part_loads[i * parts + k + 2])

                at(step, parts, load_next)
                if is_last:
                    at(step, 3, lambda k: core_end(k - 1) if k else None)

                    @pl.when(step < 2)
                    def _():
                        weights(step)
                        at(step, 2, lambda k: begin(by_core[k]))

                    pl.when(step == 3)(lambda: one_end(0))

            gain_sum, shift_sum = residual_back_planes(size, stage, f.values, f.res, as_row(r.gain2), r.dh, f.grad)
            r.early[1:2, :] += gain_sum
            r.early[2:3, :] += shift_sum
            write_pieces(size, stage, mm(f.inv[i][...], f.grad[stage.part, :]), r.send_g[i])
            begin(by_g[i])
            if not is_last:
                block_planes(size, stage, r.map, f.res, f.acc, as_row(r.out_bias), r.block)
                begin(blocks[i])
        by_early[0].start()

        @pl.loop(2, parts)
        def _(step):
            weights(step)
            at(step - 2, 2, lambda k: begin(by_core[2 + k]))

        core_end(2)
        core_end(3)
        two_end(0)
        begin(by_near[0])
        block_planes(size, stages[-1], r.map, f.res, f.acc, as_row(r.out_bias), r.block)
        begin(blocks[-1])
        early_step(0)

    def back(*scoped):
        f = types.SimpleNamespace(**named(back_scratch(size), iter(scoped)))
        loads = [
            mover.start(source, target)
            for source, target in (
                (r.hbm.outer, f.outer),
                (r.hbm.w2, f.w2),
                (r.hbm.inner, f.inner),
                (r.hbm.w1, f.w1),
                (r.hbm.gated, f.gated),
                (r.hbm.band, f.band),
            )
        ]
        f.modes[...] = jnp.zeros_like(f.modes)
        for i in range(len(stages)):
            if i == 1:
                one_end(1)
            finish(by_g[i])
            add_modes(size, r.recv_g[i], r.lat[i], f.modes)
        finish(loads)
        mix_layers_back(size, f.modes, f.w1, f.w2, f.inner, f.outer, f.outer_grad, f.inner_grad, f.stacked)
        by_d = [
            make_all(size, source, target, sender, mover)
            for source, target in zip(f.send_d, r.recv_d)
        ]
        for i, stage in enumerate(stages):
            modes_back(size, stage, r.lat_t[i], f.stacked, f.send_d[i])
            begin(by_d[i])
        early_step(1)

        mix_back_weights(size, f.band, f.gated, f.outer_grad, f.inner_grad, r.mix)
        crossing = sender.start(r.mix.at[:, 1 - core], r.mix_core, to_core)
        finish(by_near[0])
        two_end(1)
        for total, landed in ((r.a_two, r.a_near), (r.b_two, r.b_near)):
            total[1] = (total[1].astype(f32) + landed[0].astype(f32)).astype(bf16)
        hops = [
            sender.start(r.a_two.at[1], r.a_last, to_mirror),
            sender.start(r.b_two.at[1], r.b_last, to_mirror),
        ]
        crossing.wait()
        add_to(r.mix_core, r.mix.at[:, core])
        pair = group // 2
        mixes = []
        for offset in range(1, groups // 2):
            other = (pair + offset) % (groups // 2)
            device = base + other * 2 + core
            mixes.append(
                sender.start(
                    r.mix_core.at[other],
                    r.mix_land.at[pair],
                    {"rows": device // lon_count, "lon": device % lon_count},
                )
            )
        mixes.append(mover.start(r.mix_core.at[pair], r.mix_land.at[pair]))
        one_end(2)
        early_step(2)

        finish(tables_back)
        tokens = [make_lon(stage, r.token, r.token_out, sender, mover) for stage in stages]
        gather = []
        r.late[...] = jnp.zeros_like(r.late)
        for i, stage in enumerate(stages):
            finish(by_d[i])
            gain_sum, shift_sum = last_planes(
                size, stage, r.recv_d[i], r.x, r.dh, r.table_t[i], r.gain1, f.filtered, r.token, lon + 1, lambda k: tokens[i][k].start()
            )
            r.late[0:1, :] += gain_sum
            r.late[1:2, :] += shift_sum
            if i == 0:
                finish(mixes)
                total = r.mix_land[0].astype(f32)
                for index in range(1, groups // 2):
                    total = total + r.mix_land[index].astype(f32)
                r.pair[half] = total.astype(bf16)
                crossing = sender.start(r.pair.at[half], r.pair.at[half], far_z)
                two_end(2)
                begin(by_near[1])
                one_end(3)
                crossing.wait()
                block_size = r.mix_out_grad.shape[-1]
                rest = r.mix_out_bias_grad.shape[-2]
                own_place = (pair // 4, pair // 2 % 2, slice(None), pair % 2, core)
                for source, target in (
                    (r.pair.at[:, pl.ds(0, block_size)], r.mix_out_grad.at[own_place]),
                    (r.pair.at[:, pl.ds(block_size, rest)], r.mix_out_bias_grad.at[own_place]),
                ):
                    for offset in range(1, groups // 2):
                        device = base + (pair + offset) % (groups // 2) * 2 + core
                        gather.append(
                            sender.start(
                                source,
                                target,
                                {"rows": device // lon_count, "lon": device % lon_count},
                            )
                        )
                    gather.append(mover.start(source, target))
        smalls = start_same(lon_count, count, r.late, r.late_land, sender, mover)
        early_step(3)
        finish(gather)
        gather = []
        for ref in (r.mix_out_grad, r.mix_out_bias_grad):
            own_core = ref.at[:, :, :, :, core]
            gather.append(sender.start(own_core, own_core, to_core))
        finish(smalls)
        total = r.late_land[0]
        for index in range(1, count):
            total = total + r.late_land[index]
        r.late_out[...] = total
        two_end(3)
        finish(by_near[1])
        finish(hops)
        for place, total, landed, last in (
            (0, r.a_two, r.a_near, r.a_last),
            (1, r.b_two, r.b_near, r.b_last),
        ):
            r.dense[place] = (
                total[3].astype(f32) + landed[1].astype(f32) + last[...].astype(f32)
            )
        early_step(4)
        r.early_out[...] = r.early[...]
        finish(gather)
        bias = r.mix_out_bias_grad
        for layer in range(2):
            for part in range(2):
                for block in range(r.mix_bias_out.shape[2]):
                    value = bias[layer, part, block // 4, block // 2 % 2, block % 2]
                    r.mix_bias_out[layer, part, block : block + 1] = value[0:1].astype(f32)
        for copies in blocks + tokens:
            finish(copies)

    for scope, arrays in (
        (forward, forward_scratch(size)),
        (front, front_scratch(size)),
        (back, back_scratch(size)),
    ):
        pl.run_scoped(scope, *in_vmem(arrays))


def in_vmem(group):
    return [pltpu.VMEM(leaf.shape, leaf.dtype) for leaf in jax.tree.leaves(group)]


def pieces_of(size):
    return [struct((size.per_image, stage.piece, size.half), bf16) for stage in size.stages]


def kept_arrays(size):
    both = 2 * size.half
    square = struct((both, both), bf16)
    narrow = struct((size.modes, both), bf16)
    wide = struct((size.modes, both), f32)
    return dict(
        w1=square,
        w2=square,
        band=narrow,
        gated=narrow,
        inner=wide,
        outer=wide,
    )


def lat_arrays(size):
    modes = 2 * size.modes
    return dict(
        lat=[struct((modes, stage.band), bf16) for stage in size.stages],
        lat_t=[struct((stage.band, modes), bf16) for stage in size.stages],
    )


def mode_arrays(size):
    modes = (2 * size.modes, size.half)
    return dict(modes=struct(modes, f32), stacked=struct(modes, bf16))


def forward_scratch(size):
    row = struct((1, 2 * size.half), f32)
    return dict(
        table=[struct((stage.spectrum, stage.rows), bf16) for stage in size.stages],
        ec=[struct((256, stage.band), bf16) for stage in size.stages],
        er=struct((2 * size.modes, 192), bf16),
        b1=row,
        b2=row,
        low=struct((size.tokens, size.channels), bf16),
        send_a=pieces_of(size),
        **kept_arrays(size),
        **mode_arrays(size),
    )


def front_scratch(size):
    tokens = (size.tokens, size.channels)
    square = struct((2, size.channels, size.channels), bf16)
    return dict(
        inv_t=[struct((stage.rows, stage.spectrum), bf16) for stage in size.stages],
        inv=[struct((stage.spectrum, stage.rows), bf16) for stage in size.stages],
        fc_in=square,
        fc_out=square,
        hidden=struct((4, 2) + tokens, bf16),
        values=struct((2,) + tokens, bf16),
        grad=struct(tokens, bf16),
        res=struct(tokens, f32),
        acc=struct(tokens, f32),
    )


def back_scratch(size):
    grads = struct((size.modes, 2 * size.half), bf16)
    return dict(
        outer_grad=grads,
        inner_grad=grads,
        filtered=struct((size.tokens, size.channels), f32),
        send_d=pieces_of(size),
        **kept_arrays(size),
        **mode_arrays(size),
    )


def run_layer(size, large, small, row_map, blocks_shape, number):
    shape = large["tokens"].shape
    hidden_units = large["fc_out"].shape[0]
    parts = hidden_units // size.channels
    share = hidden_units // size.devices
    block = blocks_shape[1:]
    lead = (2, 2, HALVES, blocks_shape[0] // 8, 2)
    early = struct((round_up(3 + parts, 8), size.channels), f32)
    late = struct((2, size.channels), f32)
    plane = struct(shape, bf16)
    half_blocks = struct((blocks_shape[0] // 2,) + block, bf16)
    far = dict(token_out=plane, block_out=plane)
    near = dict(
        dense=struct((2, share, size.channels), f32),
        mix_out_grad=struct(lead + (block[1], block[1]), bf16),
        mix_bias_out=struct((2, 2, blocks_shape[0] // 2, block[1]), f32),
        early_out=early,
        late_out=late,
    )
    kept = dict(kept=kept_arrays(size))

    sums = [
        struct(lead + (share, size.channels), bf16)
        for lead in ((4, 2, 2), (4, 2), (4,), (2,), ())
    ]
    scratch = dict(
        x=plane,
        dy=plane,
        token=plane,
        block=plane,
        table_t=[struct((stage.rows, stage.spectrum), bf16) for stage in size.stages],
        dh=struct((size.tokens, size.channels), f32),
        recv_a=pieces_of(size),
        send_e=pieces_of(size),
        recv_e=pieces_of(size),
        send_g=pieces_of(size),
        recv_g=pieces_of(size),
        recv_d=pieces_of(size),
        wide=struct((2, 2, 2, 2, 2, share, size.channels), bf16),
        a_core=sums[0],
        b_core=sums[0],
        a_one=sums[1],
        b_one=sums[1],
        a_two=sums[2],
        b_two=sums[2],
        a_near=sums[3],
        b_near=sums[3],
        a_last=sums[4],
        b_last=sums[4],
        mix=struct((blocks_shape[0] // 2, 2) + block, bf16),
        mix_core=half_blocks,
        mix_land=half_blocks,
        pair=struct((HALVES,) + block, bf16),
        mix_out_bias_grad=struct(lead + (block[0] - block[1], block[1]), bf16),
        early=early,
        early_land=struct((5,) + early.shape, f32),
        late=late,
        late_land=struct((size.devices,) + late.shape, f32),
        **lat_arrays(size),
    )
    sems = dict(a_send_sem=0, b_recv_sem=0, c_move_sem=0)
    large_group = dict(large=large)
    map_group = dict(map=row_map)
    groups = [
        jax.tree.map(lambda leaf: 0, group)
        for group in (large_group, small, map_group, far, near, kept, sems, scratch)
    ]
    operands = jax.tree.leaves(large_group) + jax.tree.leaves(small) + [row_map]
    outs = [jax.tree.leaves(group) for group in (far, near, kept)]
    results = call_remote(
        functools.partial(layer_kernel, size, groups),
        "layer",
        number,
        tuple(outs[0] + outs[1] + outs[2]),
        [pl.ANY] * len(jax.tree.leaves(large_group))
        + [pltpu.VMEM] * len(small)
        + [pltpu.SMEM],
        [pl.ANY] * len(outs[0]) + [pltpu.VMEM] * len(outs[1]) + [pl.ANY] * len(outs[2]),
        10 * size.devices + 2 * size.groups + 16 * size.lon + 32,
        80,
        in_vmem(scratch),
        operands,
    )
    found = iter(results)
    return types.SimpleNamespace(**named(far, found), **named(near, found))


def prepare_kernel(size, rows_ref, cos_ref, sin_ref, er_ref, mix_in_ref, bias_in_ref, mix_out_ref, bias_out_ref, *refs):
    count = len(size.stages)
    ecs, lats, lats_t = [refs[i * count : (i + 1) * count] for i in range(3)]
    w1_ref, w2_ref, b1_ref, b2_ref = refs[3 * count :]
    half = half_of(size)
    build_lat_tables(size, rows_ref, cos_ref, sin_ref, er_ref, ecs, lats, lats_t)
    build_block_matrix(size, mix_in_ref, bias_in_ref, half, w1_ref, b1_ref)
    build_block_matrix(size, mix_out_ref, bias_out_ref, half, w2_ref, b2_ref)


def exchange_lon(values):
    return lax.all_to_all(values, "lon", split_axis=0, concat_axis=0, tiled=True)


def exchange_all(values):
    return lax.all_to_all(values, ("rows", "lon"), split_axis=0, concat_axis=0, tiled=True)


def join_stages(size, pieces):
    return jnp.concatenate(
        [piece[:, : stage.used] for stage, piece in zip(size.stages, pieces)], axis=1
    )


def cut_stages(size, values):
    pieces, start = [], 0
    for stage in size.stages:
        piece = values[:, start : start + stage.used]
        pieces.append(jnp.pad(piece, ((0, 0), (0, stage.piece - stage.used), (0, 0))))
        start += stage.used
    return pieces


def to_modes(size, pieces, row_map):
    sent = jnp.tile(join_stages(size, pieces), (size.images, 1, 1))
    received = exchange_all(sent)
    used = size.slots_here * 2 * size.waves
    by_slot = received.reshape(-1, 2 * size.waves, size.half)
    image = (lax.axis_index("rows") * size.lon + lax.axis_index("lon")) // size.per_image
    slots = row_map.shape[0]
    target = jnp.where(row_map >= 0, row_map, size.images * H)
    slot_of_row = (
        jnp.zeros((size.images * H,), jnp.int32)
        .at[target]
        .set(jnp.arange(slots, dtype=jnp.int32), mode="drop")
    )
    own = lax.dynamic_slice_in_dim(slot_of_row, image * H, H)
    picked = jnp.take(by_slot, own, axis=0)
    picked = jnp.pad(picked, ((0, size.virtual_slots - H), (0, 0), (0, 0)))
    return cut_stages(size, picked.reshape(size.per_image, used, size.half))


def from_modes(size, pieces, row_map):
    used = size.slots_here * 2 * size.waves
    by_lat = join_stages(size, pieces).reshape(-1, 2 * size.waves, size.half)
    image = (lax.axis_index("rows") * size.lon + lax.axis_index("lon")) // size.per_image
    live = (row_map >= 0) & (row_map // H == image)
    picked = jnp.take(by_lat, jnp.where(live, row_map % H, 0), axis=0)
    picked = picked * live.astype(bf16)[:, None, None]
    received = exchange_all(picked.reshape(size.devices, used, size.half))
    received = received.reshape(size.images, size.per_image, used, size.half)
    return cut_stages(size, jnp.sum(received.astype(f32), axis=0).astype(bf16))


def run_fields(
    size, blocks_shape, row_map, x, dy, tables, tables_t, invs, invs_t, lat_inputs, mixers, vectors, fc_in, fc_in_bias, fc_out
):
    channels = size.channels
    names = ("rows", "lon")
    kept_structs = types.SimpleNamespace(**kept_arrays(size), **lat_arrays(size))
    pieces = tuple(pieces_of(size))
    modes = [pltpu.VMEM(v.shape, v.dtype) for v in mode_arrays(size).values()]
    flat = struct((1, 2 * size.half), f32)
    cosine, sine, er, ecs = lat_inputs
    lats = jnp.arange(size.virtual_slots)
    rows = jnp.where(lats < H, lats, -1).astype(jnp.int32)
    prepared = call_local(
        functools.partial(prepare_kernel, size),
        "prepare",
        tuple(kept_structs.lat + kept_structs.lat_t)
        + (kept_structs.w1, kept_structs.w2, flat, flat),
    )(rows, cosine, sine, er, *mixers, *ecs)
    count = len(size.stages)
    lat, lat_t, (w1, w2, b1, b2) = prepared[:count], prepared[count : 2 * count], prepared[2 * count :]
    x, dy = exchange_lon(x), exchange_lon(dy)
    sent = call_local(
        functools.partial(first_kernel, size),
        "lon_forward",
        pieces,
        [pltpu.VMEM((size.tokens, channels), bf16)],
    )(x, vectors[0], vectors[1], *tables)
    received = to_modes(size, sent, row_map)
    kept = (kept_structs.band, kept_structs.inner, kept_structs.gated, kept_structs.outer)
    results = call_local(
        functools.partial(mix_kernel, size), "mix_forward", pieces + kept, modes
    )(w1, b1, w2, b2, *received, *lat, *lat_t)
    sent, kept = results[:count], results[count:]
    received = from_modes(size, sent, row_map)
    sent, block, dh, hidden, values, early = run_mlp(
        size, fc_out.shape[0], row_map, x, dy, vectors, fc_in, fc_in_bias, fc_out, received, invs_t, invs
    )
    early = lax.psum(early, names)
    wide = call_local(
        wide_kernel, "weights_backward", struct((fc_out.shape[0], 2 * channels), bf16)
    )(hidden, values)
    dense = lax.psum_scatter(wide, names, scatter_dimension=0, tiled=True).astype(f32)
    dense = jnp.stack([dense[:, :channels], dense[:, channels:]])
    block = exchange_lon(block)
    received = to_modes(size, sent, row_map)
    results = call_local(
        functools.partial(mix_back_kernel, size),
        "mix_backward",
        pieces + (struct(blocks_shape, bf16),),
        [pltpu.VMEM((size.modes, 2 * size.half), bf16)] * 2 + modes,
    )(w1, w2, *kept, *received, *lat, *lat_t)
    sent, mix_grad = results[:count], results[count]
    half_index = half_of(size)
    mix_grad = mix_grad.astype(f32).reshape((2, 2, 1, blocks_shape[0] // 4) + blocks_shape[1:])
    mix_total = lax.psum(
        jnp.concatenate(
            [mix_grad * (half_index == other).astype(f32) for other in range(HALVES)], axis=2
        ),
        names,
    )
    received = from_modes(size, sent, row_map)
    token_grad, late = call_local(
        functools.partial(last_kernel, size),
        "lon_backward",
        (struct(x.shape, bf16), struct((2, channels), f32)),
        [pltpu.VMEM((size.tokens, channels), f32)],
    )(x, dh, vectors[0], *received, *tables_t)
    block_size = blocks_shape[2]
    return (
        exchange_lon(token_grad),
        block,
        dense,
        mix_total[..., :block_size, :],
        mix_total[..., block_size, :].reshape(2, 2, -1, block_size),
        early,
        lax.psum(late, names),
    )


def body(
    tokens,
    row_map,
    cotangent,
    norm_gain,
    norm_shift,
    mix_in,
    mix_in_bias,
    mix_out,
    mix_out_bias,
    post_gain,
    post_shift,
    fc_in,
    fc_in_bias,
    fc_out,
    fc_out_bias,
):
    size = Sizes(
        lax.axis_size("rows"), lax.axis_size("lon"), row_map.shape[0], tokens.shape[2]
    )
    channels = size.channels
    block_size = mix_in.shape[2]
    hidden_units = fc_in.shape[1]
    blocks_shape = (4 * mix_in.shape[1] // HALVES, round_up(block_size + 1, 16), block_size)
    device = lax.axis_index("rows") * size.lon + lax.axis_index("lon")
    tables, tables_t, invs, invs_t = lon_tables(size)
    cosine, sine, er, ecs = lat_parts(size)
    shape = (size.lon, size.slots_here, size.lons_here, channels)
    x, dy = tokens.reshape(shape), cotangent.reshape(shape)
    vectors = (norm_gain, norm_shift, post_gain, post_shift, fc_out_bias)
    bias_row = fc_in_bias.reshape(1, -1)
    if size.images == 1:
        large = dict(
            tokens=x,
            cot=dy,
            table=tables,
            table_t=tables_t,
            inv=invs,
            inv_t=invs_t,
            ec=ecs,
            er=er,
            fc_in=fc_in,
            fc_out=fc_out,
        )
        small = dict(
            rows=row_map,
            cosine=cosine,
            sine=sine,
            mix_in=mix_in,
            mix_in_bias=mix_in_bias,
            mix_out=mix_out,
            mix_out_bias=mix_out_bias,
            gain1=norm_gain,
            shift1=norm_shift,
            gain2=post_gain,
            shift2=post_shift,
            out_bias=fc_out_bias,
            fc_in_bias=bias_row,
        )
        r = run_layer(size, large, small, row_map, blocks_shape, 0)
        results = (
            r.token_out,
            r.block_out,
            r.dense,
            r.mix_out_grad,
            r.mix_bias_out,
            r.early_out,
            r.late_out,
        )
    else:
        results = run_fields(
            size, blocks_shape, row_map, x, dy, tables, tables_t, invs, invs_t, (cosine, sine, er, ecs), (mix_in, mix_in_bias, mix_out, mix_out_bias), vectors, fc_in, bias_row, fc_out
        )
    token_grad, block, dense, mix_total, mix_bias, early, late = results
    share = hidden_units // size.devices
    return (
        block.reshape(tokens.shape),
        token_grad.reshape(tokens.shape).astype(f32),
        late[0],
        late[1],
        mix_total[0].reshape(mix_in.shape).astype(f32),
        mix_bias[0],
        mix_total[1].reshape(mix_in.shape).astype(f32),
        mix_bias[1],
        early[1],
        early[2],
        dense[0].T,
        lax.dynamic_slice_in_dim(early[3:7].reshape(-1), device * share, share),
        dense[1],
        early[0],
    )


def solution(mesh):
    return jax.shard_map(
        body,
        mesh=mesh,
        in_specs=(P("rows", "lon", None), P(), P("rows", "lon", None)) + (P(),) * 12,
        out_specs=(
            P("rows", "lon", None),
            P("rows", "lon", None),
            P(),
            P(),
            P(),
            P(),
            P(),
            P(),
            P(),
            P(),
            P(None, ("rows", "lon")),
            P(("rows", "lon")),
            P(("rows", "lon"), None),
            P(),
        ),
        check_vma=False,
    )
```

```python
import functools
import math
import types

import jax
import jax.numpy as jnp
import ml_dtypes
import numpy as np
from jax import lax
from jax.experimental import pallas as pl
from jax.experimental.pallas import tpu as pltpu
from jax.sharding import PartitionSpec as P

H = 90
W = 180
KX = 91
HALVES = 2
VMEM_BYTES = 58 * 1024 * 1024

norm_eps = 1e-06
shrink_level = 0.01
half_root = 0.7071067811865476
normal_peak = 0.3989422804014327
MESH = pl.DeviceIdType.MESH
f32 = jnp.float32
bf16 = jnp.bfloat16


def round_up(value, step):
    return -(-value // step) * step


class Stage:
    def __init__(self, size, slots, first_row):
        self.slots = slots
        self.rows = size.lon * len(slots) * size.lons_pad
        self.first_row = first_row
        self.part = slice(first_row, first_row + self.rows)
        self.used = len(slots) * 2 * size.waves
        self.piece = round_up(self.used, 8)
        self.spectrum = size.groups * self.piece
        self.band = size.per_image * self.piece


class Sizes:
    def __init__(self, rows_count, lon_count, slots, channels):
        self.rows = rows_count
        self.lon = lon_count
        self.devices = rows_count * lon_count
        self.images = slots * 15 // (16 * H)
        self.per_image = self.devices // self.images
        self.groups = self.per_image // HALVES
        self.waves = -(-KX // self.groups)
        self.slots_here = slots // self.devices
        self.lons_here = W // lon_count
        self.lons_pad = round_up(self.lons_here, 16)
        self.tokens = lon_count * self.slots_here * self.lons_pad
        self.modes = round_up(H * self.waves, 16)
        self.virtual_slots = self.per_image * self.slots_here
        self.channels = channels
        self.half = channels // HALVES
        cut = -(-self.slots_here * 2 // 3)
        self.stages = []
        first_row = 0
        for low, high in ((0, cut), (cut, self.slots_here)):
            if low < high:
                self.stages.append(Stage(self, tuple(range(low, high)), first_row))
                first_row += self.stages[-1].rows


def lon_tables(size):
    wave = np.arange(size.groups * size.waves)
    lon_index = np.arange(W)
    product = (lon_index[:, None] * wave[None, :]) % W
    angle = product.astype(np.float32) * np.float32(2.0 * math.pi / W)
    scale = np.float32(1.0 / math.sqrt(W))
    cosine = (np.cos(angle) * scale).astype(ml_dtypes.bfloat16).astype(np.float32)
    sine = (-np.sin(angle) * scale).astype(ml_dtypes.bfloat16).astype(np.float32)
    live = (wave < KX).astype(np.float32)
    factor = np.where((wave == 0) | (wave == W // 2), 1.0, 2.0).astype(np.float32)
    both = np.stack([cosine, sine]) * live
    result = []
    for weight in (np.ones_like(factor), factor):
        values = (both * weight).reshape(2, size.lon, size.lons_here, size.groups, size.waves)
        values = np.transpose(values, (3, 0, 4, 1, 2)).reshape(
            size.groups, 2 * size.waves, size.lon, size.lons_here
        )
        tables = []
        for stage in size.stages:
            count = len(stage.slots)
            table = np.zeros(
                (size.groups, stage.piece, size.lon, count, size.lons_pad), np.float32
            )
            for slot in range(count):
                start = slot * 2 * size.waves
                table[:, start : start + 2 * size.waves, :, slot, : size.lons_here] = values
            tables.append(table.reshape(stage.spectrum, stage.rows).astype(ml_dtypes.bfloat16))
        result.append([jnp.asarray(t) for t in tables])
        result.append([jnp.asarray(np.ascontiguousarray(t.T)) for t in tables])
    return result


def lat_parts(size):
    lat_index = np.arange(H)
    angle = ((lat_index[:, None] * lat_index[None, :]) % H).astype(np.float32) * np.float32(
        2.0 * math.pi / H
    )
    scale = np.float32(1.0 / math.sqrt(H))
    cosine = np.zeros((96, 96), np.float32)
    sine = np.zeros((96, 96), np.float32)
    cosine[:H, :H] = np.cos(angle) * scale
    sine[:H, :H] = np.sin(angle) * scale
    spread_rows = np.zeros((2, size.modes, 2, 96), np.float32)
    for part in range(2):
        for lat in range(H):
            for wave in range(size.waves):
                spread_rows[part, lat * size.waves + wave, part, lat] = 1.0
    spread_cols = []
    for stage in size.stages:
        spread = np.zeros((2, 128, size.per_image, stage.piece), np.float32)
        for device in range(size.per_image):
            for place, slot in enumerate(stage.slots):
                for part in range(2):
                    start = (place * 2 + part) * size.waves
                    spread[
                        part, device * size.slots_here + slot, device, start : start + size.waves
                    ] = 1.0
        spread_cols.append(spread.reshape(256, stage.band))
    low = ml_dtypes.bfloat16
    return (
        jnp.asarray(cosine.astype(low)),
        jnp.asarray(sine.astype(low)),
        jnp.asarray(spread_rows.reshape(2 * size.modes, 192).astype(low)),
        [jnp.asarray(spread.astype(low)) for spread in spread_cols],
    )


def smooth_gate(values):
    return 0.5 * values * (1.0 + lax.erf(values * half_root))


def gate_both(values):
    half_phi = 0.5 * (1.0 + lax.erf(values * half_root))
    density = values * normal_peak * jnp.exp(-0.5 * values * values)
    return values * half_phi, half_phi + density


def gate_slope(values):
    return gate_both(values)[1]


def soft_shrink(values):
    return values - shrink_level * values * lax.rsqrt(values * values + shrink_level * shrink_level)


def shrink_slope(values):
    inverse = lax.rsqrt(values * values + shrink_level * shrink_level)
    return 1.0 - shrink_level * shrink_level * shrink_level * inverse * inverse * inverse


def norm_parts(values):
    center = values - jnp.mean(values, axis=-1, keepdims=True)
    spread = lax.rsqrt(jnp.mean(center * center, axis=-1, keepdims=True) + norm_eps)
    return center * spread, spread


def norm_back(scaled, unit, spread):
    return spread * (
        scaled
        - jnp.mean(scaled, axis=-1, keepdims=True)
        - unit * jnp.mean(scaled * unit, axis=-1, keepdims=True)
    )


def mm(left, right):
    return jnp.dot(left, right, preferred_element_type=f32)


def mm_t(left, right):
    return lax.dot_general(left, right, (((1,), (1,)), ((), ())), preferred_element_type=f32)


def t_mm(left, right):
    return lax.dot_general(left, right, (((0,), (0,)), ((), ())), preferred_element_type=f32)


def whole(count):
    return [pl.BlockSpec(memory_space=pltpu.VMEM)] * count


def call_local(kernel, name, outs, scratch=()):
    def run(*operands):
        return pl.pallas_call(
            kernel,
            out_shape=outs,
            in_specs=whole(len(operands)),
            out_specs=jax.tree.map(lambda _: pl.BlockSpec(memory_space=pltpu.VMEM), outs),
            scratch_shapes=list(scratch),
            compiler_params=pltpu.CompilerParams(vmem_limit_bytes=VMEM_BYTES),
            name=name,
        )(*operands)

    return run


def struct(shape, dtype):
    return jax.ShapeDtypeStruct(shape, dtype)


def wave_of(index, period, used, waves, other):
    within = index - period * jnp.floor((index + 0.5) * (1.0 / period))
    wave = within - waves * jnp.floor((within + 0.5) * (1.0 / waves))
    return jnp.where(within < used, wave, other)


def build_lat_tables(size, rows_ref, cos_ref, sin_ref, er_ref, ec_refs, lat_refs, lat_t_refs):
    slots = rows_ref.shape[0]
    lat_of = lax.broadcasted_iota(jnp.int32, (96, slots), 0)
    hot = (lat_of == rows_ref[...].reshape(1, slots)).astype(f32)
    hot = jnp.concatenate([hot, jnp.zeros((96, 128 - slots), f32)], axis=1).astype(bf16)
    cosine = mm(cos_ref[...], hot)
    sine = mm(sin_ref[...], hot)
    top = jnp.concatenate([cosine, sine], axis=1)
    bottom = jnp.concatenate([-sine, cosine], axis=1)
    base = jnp.concatenate([top, bottom], axis=0).astype(bf16)

    def row_waves(shape, dim):
        index = lax.broadcasted_iota(jnp.int32, shape, dim).astype(f32)
        return wave_of(index, size.modes, H * size.waves, size.waves, -1.0)

    def col_waves(stage, shape, dim):
        index = lax.broadcasted_iota(jnp.int32, shape, dim).astype(f32)
        return wave_of(index, stage.piece, stage.used, size.waves, -2.0)

    modes = 2 * size.modes
    for stage, ec_ref, lat_ref, lat_t_ref in zip(size.stages, ec_refs, lat_refs, lat_t_refs):
        keep = row_waves((modes, 1), 0) == col_waves(stage, (1, stage.band), 1)
        keep_t = col_waves(stage, (stage.band, 1), 0) == row_waves((1, modes), 1)
        columns = mm(base, ec_ref[...]).astype(bf16)
        lat_ref[...] = jnp.where(keep, mm(er_ref[...], columns), 0.0).astype(bf16)
        table_t = lax.dot_general(
            columns, er_ref[...], (((0,), (1,)), ((), ())), preferred_element_type=f32
        )
        lat_t_ref[...] = jnp.where(keep_t, table_t, 0.0).astype(bf16)


def build_block_matrix(size, weight_ref, bias_ref, half, matrix_ref, row_ref):
    block_size = weight_ref.shape[2]
    blocks = size.half // block_size
    matrix_ref[...] = jnp.zeros_like(matrix_ref)
    for block in range(blocks):
        real = weight_ref[0, half * blocks + block]
        imag = weight_ref[1, half * blocks + block]
        near = slice(block * block_size, (block + 1) * block_size)
        far = slice(size.half + block * block_size, size.half + (block + 1) * block_size)
        matrix_ref[near, near] = real
        matrix_ref[near, far] = imag
        matrix_ref[far, near] = -imag
        matrix_ref[far, far] = real
        row_ref[0:1, near] = bias_ref[0, pl.ds(half * blocks + block, 1), :]
        row_ref[0:1, far] = bias_ref[1, pl.ds(half * blocks + block, 1), :]


def half_of(size):
    device = lax.axis_index("rows") * size.lon + lax.axis_index("lon")
    return (device % size.per_image) // size.groups


def pad_plane(size, plane):
    extra = size.lons_pad - size.lons_here
    return jnp.concatenate([plane, jnp.zeros((extra, plane.shape[1]), plane.dtype)], axis=0)


def at(step, count, action):
    for i in range(count):

        @pl.when(step == i)
        def _():
            action(i)


def over_planes(size, stage, body, *sums, first=0, then=None):
    def step(index, sums):
        source = (first + index) % size.lon
        for place, slot in enumerate(stage.slots):
            start = stage.first_row + pl.multiple_of(
                (source * len(stage.slots) + place) * size.lons_pad, size.lons_pad
            )
            start = pl.multiple_of(start, size.lons_pad)
            sums = body(source, slot, pl.ds(start, size.lons_pad), *sums)
        if then is not None:
            at(index, size.lon, then)
        return sums

    return lax.fori_loop(0, size.lon, step, sums)


def as_row(ref):
    return ref[...].reshape(1, -1)


def write_pieces(size, stage, values, out_ref):
    for half in range(HALVES):
        for group in range(size.groups):
            out_ref[half * size.groups + group] = values[
                group * stage.piece : (group + 1) * stage.piece,
                half * size.half : (half + 1) * size.half,
            ].astype(bf16)


def read_pieces(ref, first, count):
    return jnp.concatenate([ref[first + i].astype(f32) for i in range(count)], axis=0).astype(bf16)


def read_spectrum(size, ref):
    return jnp.concatenate(
        [read_pieces(ref, half * size.groups, size.groups) for half in range(HALVES)], axis=1
    )


def first_norm(size, stage, x_ref, gain, shift, low_ref):
    def plane(source, slot, rows):
        x = pad_plane(size, x_ref[source, slot].astype(f32))
        unit, _ = norm_parts(x)
        low_ref[rows, :] = (unit * gain + shift).astype(bf16)
        return ()

    over_planes(size, stage, plane)


def first_kernel(size, x_ref, gain_ref, shift_ref, *refs):
    count = len(size.stages)
    tables, sends, low_ref = refs[:count], refs[count : 2 * count], refs[-1]
    for stage, table_ref, send_ref in zip(size.stages, tables, sends):
        first_norm(size, stage, x_ref, as_row(gain_ref), as_row(shift_ref), low_ref)
        write_pieces(size, stage, mm(table_ref[...], low_ref[stage.part, :]), send_ref)


def add_modes(size, recv_ref, lat_ref, modes_ref):
    modes_ref[...] += mm(lat_ref[...], read_pieces(recv_ref, 0, size.per_image))


def side_by_side(size, modes_ref):
    return jnp.concatenate(
        [modes_ref[: size.modes, :], modes_ref[size.modes :, :]], axis=1
    ).astype(bf16)


def stack_parts(size, values, stacked_ref):
    stacked_ref[: size.modes, :] = values[:, : size.half].astype(bf16)
    stacked_ref[size.modes :, :] = values[:, size.half :].astype(bf16)


def modes_back(size, stage, lat_t_ref, stacked_ref, send_ref):
    back = mm(lat_t_ref[...], stacked_ref[...])
    for device in range(size.per_image):
        send_ref[device] = back[device * stage.piece : (device + 1) * stage.piece].astype(bf16)


def mix_layers(size, modes_ref, w1_ref, b1_ref, w2_ref, b2_ref, band_ref, inner_ref, gated_ref, outer_ref, stacked_ref):
    band = side_by_side(size, modes_ref)
    band_ref[...] = band
    inner = mm(band, w1_ref[...]) + b1_ref[...]
    inner_ref[...] = inner
    gated = smooth_gate(inner).astype(bf16)
    gated_ref[...] = gated
    outer = mm(gated, w2_ref[...]) + b2_ref[...]
    outer_ref[...] = outer
    stack_parts(size, soft_shrink(outer), stacked_ref)


def slopes_in_place(inner_ref, outer_ref):
    inner_ref[...] = gate_slope(inner_ref[...])
    outer_ref[...] = shrink_slope(outer_ref[...])


def mix_kernel(size, w1_ref, b1_ref, w2_ref, b2_ref, *refs):
    count = len(size.stages)
    recvs, lats, lats_t, sends = [refs[i * count : (i + 1) * count] for i in range(4)]
    band_ref, inner_ref, gated_ref, outer_ref, modes_ref, stacked_ref = refs[4 * count :]
    modes_ref[...] = jnp.zeros_like(modes_ref)
    for recv_ref, lat_ref in zip(recvs, lats):
        add_modes(size, recv_ref, lat_ref, modes_ref)
    mix_layers(size, modes_ref, w1_ref, b1_ref, w2_ref, b2_ref, band_ref, inner_ref, gated_ref, outer_ref, stacked_ref)
    for stage, lat_t_ref, send_ref in zip(size.stages, lats_t, sends):
        modes_back(size, stage, lat_t_ref, stacked_ref, send_ref)
    slopes_in_place(inner_ref, outer_ref)


def mix_layers_back(size, modes_ref, w1_ref, w2_ref, inner_ref, outer_ref, outer_grad_ref, inner_grad_ref, stacked_ref):
    upstream = side_by_side(size, modes_ref)
    outer_grad = (upstream.astype(f32) * outer_ref[...]).astype(bf16)
    outer_grad_ref[...] = outer_grad
    inner_grad = (mm_t(outer_grad, w2_ref[...]) * inner_ref[...]).astype(bf16)
    inner_grad_ref[...] = inner_grad
    stack_parts(size, mm_t(inner_grad, w1_ref[...]), stacked_ref)


def mix_back_weights(size, band_ref, gated_ref, outer_grad_ref, inner_grad_ref, out_ref):
    half = size.half
    block_size = out_ref.shape[-1]
    blocks = half // block_size
    rest = out_ref.shape[-2] - block_size
    for layer, (value_ref, grad_ref) in enumerate(
        ((band_ref, inner_grad_ref), (gated_ref, outer_grad_ref))
    ):
        grad = grad_ref[...]
        total = t_mm(value_ref[...], grad)
        bias = jnp.sum(grad.astype(f32), axis=0, keepdims=True)
        for block in range(blocks):
            near = slice(block * block_size, (block + 1) * block_size)
            far = slice(half + block * block_size, half + (block + 1) * block_size)
            for part, values, row in (
                (0, total[near, near] + total[far, far], bias[:, near]),
                (1, total[near, far] - total[far, near], bias[:, far]),
            ):
                place = (layer * 2 + part) * blocks + block
                at = (place // 2, place % 2) if len(out_ref.shape) == 4 else (place,)
                out_ref[at + (slice(0, block_size),)] = values.astype(bf16)
                out_ref[at + (slice(block_size, None),)] = jnp.broadcast_to(
                    row, (rest, block_size)
                ).astype(bf16)


def mix_back_kernel(size, w1_ref, w2_ref, band_ref, inner_ref, gated_ref, outer_ref, *refs):
    count = len(size.stages)
    recvs, lats, lats_t, sends = [refs[i * count : (i + 1) * count] for i in range(4)]
    grad_ref, outer_grad_ref, inner_grad_ref, modes_ref, stacked_ref = refs[4 * count :]
    modes_ref[...] = jnp.zeros_like(modes_ref)
    for recv_ref, lat_ref in zip(recvs, lats):
        add_modes(size, recv_ref, lat_ref, modes_ref)
    mix_layers_back(size, modes_ref, w1_ref, w2_ref, inner_ref, outer_ref, outer_grad_ref, inner_grad_ref, stacked_ref)
    for stage, lat_t_ref, send_ref in zip(size.stages, lats_t, sends):
        modes_back(size, stage, lat_t_ref, stacked_ref, send_ref)
    mix_back_weights(size, band_ref, gated_ref, outer_grad_ref, inner_grad_ref, grad_ref)


def live_of(size, map_ref, slot):
    first_slot = (lax.axis_index("rows") * size.lon + lax.axis_index("lon")) * size.slots_here
    return jnp.where(map_ref[first_slot + slot] >= 0, 1.0, 0.0)


def local_planes(size, stage, map_ref, x_ref, dy_ref, gain1, shift1, res_ref, values_ref):
    def plane(source, slot, rows, up_sum):
        x = pad_plane(size, x_ref[source, slot].astype(f32))
        unit, _ = norm_parts(x)
        res_ref[rows, :] = (unit * gain1 + shift1) + x
        up = pad_plane(size, dy_ref[source, slot].astype(f32) * live_of(size, map_ref, slot))
        values_ref[1, rows, :] = up.astype(bf16)
        return (up_sum + jnp.sum(up, axis=0, keepdims=True),)

    return over_planes(size, stage, plane, jnp.zeros((1, size.channels), f32))[0]


def residual_planes(size, stage, recv_ref, inv_t_ref, gain2, shift2, res_ref, values_ref):
    res_ref[stage.part, :] += mm(inv_t_ref[...], read_spectrum(size, recv_ref))

    def plane(source, slot, rows):
        unit, _ = norm_parts(res_ref[rows, :])
        values_ref[0, rows, :] = (unit * gain2 + shift2).astype(bf16)
        return ()

    over_planes(size, stage, plane)


def hidden_part(part, values_ref, fc_in, bias, fc_out, acc_ref, back_ref):
    gate, slope = gate_both(mm(values_ref[0, part, :], fc_in) + bias)
    hidden = gate.astype(bf16)
    acc_ref[part, :] += mm(hidden, fc_out)
    hidden_grad = (mm_t(values_ref[1, part, :], fc_out) * slope).astype(bf16)
    back_ref[part, :] += mm_t(hidden_grad, fc_in)
    return hidden, hidden_grad


def residual_back_planes(size, stage, values_ref, res_ref, gain2, back_ref, grad_ref):
    def plane(source, slot, rows, gain_sum, shift_sum):
        unit, spread = norm_parts(res_ref[rows, :])
        grad = back_ref[rows, :]
        gain_sum = gain_sum + jnp.sum(grad * unit, axis=0, keepdims=True)
        shift_sum = shift_sum + jnp.sum(grad, axis=0, keepdims=True)
        grad = values_ref[1, rows, :].astype(f32) + norm_back(grad * gain2, unit, spread)
        back_ref[rows, :] = grad
        grad_ref[rows, :] = grad.astype(bf16)
        return gain_sum, shift_sum

    zero = jnp.zeros((1, size.channels), f32)
    return over_planes(size, stage, plane, zero, zero)


def block_planes(size, stage, map_ref, res_ref, acc_ref, out_bias, block_ref):
    def plane(source, slot, rows):
        block = (res_ref[rows, :] + (acc_ref[rows, :] + out_bias)) * live_of(size, map_ref, slot)
        block_ref[source, slot] = block[: size.lons_here].astype(bf16)
        return ()

    over_planes(size, stage, plane)


def mlp_kernel(
    size,
    map_ref,
    x_ref,
    dy_ref,
    gain1_ref,
    shift1_ref,
    gain2_ref,
    shift2_ref,
    out_bias_ref,
    fc_in_ref,
    fc_in_bias_ref,
    fc_out_ref,
    *refs,
):
    count = len(size.stages)
    recvs, invs_t, invs, sends = [refs[i * count : (i + 1) * count] for i in range(4)]
    block_ref, dh_ref, hidden_ref, values_ref, small_ref, res_ref, grad_ref, acc_ref = refs[4 * count :]
    step = pl.program_id(0)

    @pl.when(step == 0)
    def _():
        small_ref[...] = jnp.zeros_like(small_ref)
        for stage, recv_ref, inv_t_ref in zip(size.stages, recvs, invs_t):
            small_ref[0:1, :] += local_planes(
                size, stage, map_ref, x_ref, dy_ref, as_row(gain1_ref), as_row(shift1_ref), res_ref, values_ref
            )
            residual_planes(
                size, stage, recv_ref, inv_t_ref, as_row(gain2_ref), as_row(shift2_ref), res_ref, values_ref
            )
        acc_ref[...] = jnp.zeros_like(acc_ref)
        dh_ref[...] = jnp.zeros_like(dh_ref)

    hidden, hidden_grad = hidden_part(
        slice(0, size.tokens), values_ref, fc_in_ref[...], fc_in_bias_ref[...], fc_out_ref[...], acc_ref, dh_ref
    )
    small_ref[pl.ds(3 + step, 1), :] = jnp.sum(hidden_grad.astype(f32), axis=0, keepdims=True)
    hidden_ref[0] = hidden_grad
    hidden_ref[1] = hidden

    @pl.when(step == pl.num_programs(0) - 1)
    def _():
        for stage, inv_ref, send_ref in zip(size.stages, invs, sends):
            block_planes(size, stage, map_ref, res_ref, acc_ref, as_row(out_bias_ref), block_ref)
            gain_sum, shift_sum = residual_back_planes(
                size, stage, values_ref, res_ref, as_row(gain2_ref), dh_ref, grad_ref
            )
            small_ref[1:2, :] += gain_sum
            small_ref[2:3, :] += shift_sum
            write_pieces(size, stage, mm(inv_ref[...], grad_ref[stage.part, :]), send_ref)


def run_mlp(size, hidden_units, row_map, x, dy, vectors, fc_in, fc_in_bias, fc_out, received, invs_t, invs):
    channels = size.channels
    parts = hidden_units // channels
    fixed = pl.BlockSpec(memory_space=pltpu.VMEM)
    tokens = (size.tokens, channels)
    count = len(size.stages)
    out = pl.pallas_call(
        functools.partial(mlp_kernel, size),
        grid=(parts,),
        in_specs=[pl.BlockSpec(memory_space=pltpu.SMEM)]
        + [fixed] * (2 + len(vectors))
        + [
            pl.BlockSpec((channels, channels), lambda i: (0, i)),
            pl.BlockSpec((1, channels), lambda i: (0, i)),
            pl.BlockSpec((channels, channels), lambda i: (i, 0)),
        ]
        + [fixed] * (3 * count),
        out_specs=tuple(
            [fixed] * (count + 2)
            + [pl.BlockSpec((None, 2) + tokens, lambda i: (i, 0, 0, 0))]
            + [fixed] * 2
        ),
        out_shape=tuple(
            [struct(piece.shape, bf16) for piece in received]
            + [
                struct(x.shape, bf16),
                struct(tokens, f32),
                struct((parts, 2) + tokens, bf16),
                struct((2,) + tokens, bf16),
                struct((round_up(3 + parts, 8), channels), f32),
            ]
        ),
        scratch_shapes=[
            pltpu.VMEM(tokens, f32),
            pltpu.VMEM(tokens, bf16),
            pltpu.VMEM(tokens, f32),
        ],
        compiler_params=pltpu.CompilerParams(vmem_limit_bytes=VMEM_BYTES),
        name="mlp",
    )(row_map, x, dy, *vectors, fc_in, fc_in_bias, fc_out, *received, *invs_t, *invs)
    return (out[:count],) + tuple(out[count:])


def wide_kernel(hidden_ref, values_ref, wide_ref):
    channels = values_ref.shape[2]
    for part in range(hidden_ref.shape[0]):
        rows = slice(part * channels, (part + 1) * channels)
        wide_ref[rows, :channels] = t_mm(hidden_ref[part, 0], values_ref[0]).astype(bf16)
        wide_ref[rows, channels:] = t_mm(hidden_ref[part, 1], values_ref[1]).astype(bf16)


def last_planes(size, stage, recv_ref, x_ref, dh_ref, table_t_ref, gain_ref, filtered_ref, out_ref, first=0, then=None):
    gain = as_row(gain_ref)
    filtered_ref[stage.part, :] = mm(table_t_ref[...], read_spectrum(size, recv_ref))

    def plane(source, slot, rows, gain_sum, shift_sum):
        unit, spread = norm_parts(pad_plane(size, x_ref[source, slot].astype(f32)))
        base = dh_ref[rows, :]
        grad = base + filtered_ref[rows, :]
        gain_sum = gain_sum + jnp.sum(grad * unit, axis=0, keepdims=True)
        shift_sum = shift_sum + jnp.sum(grad, axis=0, keepdims=True)
        grad = base + norm_back(grad * gain, unit, spread)
        out_ref[source, slot] = grad[: size.lons_here].astype(bf16)
        return gain_sum, shift_sum

    zero = jnp.zeros((1, size.channels), f32)
    return over_planes(size, stage, plane, zero, zero, first=first, then=then)


def last_kernel(size, x_ref, dh_ref, gain_ref, *refs):
    count = len(size.stages)
    recvs, tables_t = refs[:count], refs[count : 2 * count]
    out_ref, small_ref, filtered_ref = refs[2 * count :]
    small_ref[...] = jnp.zeros_like(small_ref)
    for stage, recv_ref, table_t_ref in zip(size.stages, recvs, tables_t):
        gain_sum, shift_sum = last_planes(size, stage, recv_ref, x_ref, dh_ref, table_t_ref, gain_ref, filtered_ref, out_ref)
        small_ref[0:1, :] += gain_sum
        small_ref[1:2, :] += shift_sum


def partners(lon_count):
    row = lax.axis_index("rows")
    lon = lax.axis_index("lon")
    core = {"rows": row, "lon": lon + 1 - 2 * (lon % 2)}
    along_y = {"rows": row, "lon": (lon + 2) % 4}
    along_x = {"rows": row + 1 - 2 * (row % 2), "lon": lon}
    far_z = {"rows": (row + 4) % 8, "lon": lon}
    return core, along_y, along_x, far_z


def greet(lon_count, count):
    row = lax.axis_index("rows")
    lon = lax.axis_index("lon")
    me = row * lon_count + lon
    barrier = pltpu.get_barrier_semaphore()
    for offset in range(1, count):
        other = (me + offset) % count
        pl.semaphore_signal(
            barrier,
            inc=1,
            device_id={"rows": other // lon_count, "lon": other % lon_count},
            device_id_type=MESH,
        )
    pl.semaphore_wait(barrier, count - 1)


class Sender:
    def __init__(self, send_sem, recv_sem):
        self.send_sem = send_sem
        self.recv_sem = recv_sem
        self.used = 0

    def make(self, source, target, device):
        copy = pltpu.make_async_remote_copy(
            src_ref=source,
            dst_ref=target,
            send_sem=self.send_sem.at[self.used],
            recv_sem=self.recv_sem.at[self.used],
            device_id=device,
            device_id_type=MESH,
        )
        self.used += 1
        return copy

    def start(self, source, target, device):
        copy = self.make(source, target, device)
        copy.start()
        return copy


class Mover:
    def __init__(self, sem):
        self.sem = sem
        self.used = 0

    def make(self, source, target):
        copy = pltpu.make_async_copy(source, target, self.sem.at[self.used])
        self.used += 1
        return copy

    def start(self, source, target):
        copy = self.make(source, target)
        copy.start()
        return copy


def make_all(size, source_ref, out_ref, sender, mover):
    row = lax.axis_index("rows")
    lon = lax.axis_index("lon")
    me = row * size.lon + lon
    copies = []
    for row_step in range(size.rows):
        for lon_step in range(size.lon):
            to_row = (row + row_step) % size.rows
            to_lon = (lon + lon_step) % size.lon
            piece = source_ref.at[to_row * size.lon + to_lon]
            if row_step == 0 and lon_step == 0:
                copies.append(mover.make(piece, out_ref.at[me]))
            else:
                copies.append(
                    sender.make(piece, out_ref.at[me], {"rows": to_row, "lon": to_lon})
                )
    return copies


def make_lon(stage, source_ref, out_ref, sender, mover):
    row = lax.axis_index("rows")
    me = lax.axis_index("lon")
    count = source_ref.shape[0]
    slots = pl.ds(stage.slots[0], len(stage.slots))
    copies = []
    for offset in range(1, count):
        other = (me + offset) % count
        copies.append(
            sender.make(
                source_ref.at[other, slots], out_ref.at[me, slots], {"rows": row, "lon": other}
            )
        )
    copies.append(mover.make(source_ref.at[me, slots], out_ref.at[me, slots]))
    return copies


def begin(copies):
    for copy in copies:
        copy.start()
    return copies


def finish(copies):
    for copy in copies:
        copy.wait()


def call_remote(kernel, name, number, outs, spaces, out_spaces, sends, moves, scratch, operands):
    return pl.pallas_call(
        kernel,
        out_shape=outs,
        in_specs=[pl.BlockSpec(memory_space=space) for space in spaces],
        out_specs=tuple(pl.BlockSpec(memory_space=space) for space in out_spaces),
        scratch_shapes=[
            pltpu.SemaphoreType.DMA((sends,)),
            pltpu.SemaphoreType.DMA((sends,)),
            pltpu.SemaphoreType.DMA((moves,)),
        ]
        + list(scratch),
        compiler_params=pltpu.CompilerParams(
            collective_id=number, has_side_effects=True, vmem_limit_bytes=VMEM_BYTES
        ),
        name=name,
    )(*operands)


def add_to(total_ref, other_ref):
    @pl.loop(0, total_ref.shape[0])
    def _(first):
        if len(total_ref.shape) == 3:
            total = total_ref[first].astype(f32) + other_ref[first].astype(f32)
            total_ref[first] = total.astype(total_ref.dtype)
        else:
            for second in range(total_ref.shape[1]):
                total = total_ref[first, second].astype(f32) + other_ref[first, second].astype(f32)
                total_ref[first, second] = total.astype(total_ref.dtype)


def start_same(lon_count, count, source_ref, out_ref, sender, mover):
    me = lax.axis_index("rows") * lon_count + lax.axis_index("lon")
    copies = []
    for offset in range(1, count):
        other = (me + offset) % count
        copies.append(
            sender.start(
                source_ref, out_ref.at[me], {"rows": other // lon_count, "lon": other % lon_count}
            )
        )
    copies.append(mover.start(source_ref, out_ref.at[me]))
    return copies


def named(group, refs):
    leaves, tree = jax.tree.flatten(group)
    return jax.tree.unflatten(tree, [next(refs) for _ in leaves])


def layer_kernel(size, groups_of, *refs):
    found = iter(refs)
    r = types.SimpleNamespace()
    for arrays in groups_of:
        r.__dict__.update(named(arrays, found))
    r.hbm = types.SimpleNamespace(**r.large, **r.kept)
    stages = size.stages
    channels = size.channels
    lon_count, count, groups = size.lon, size.devices, size.groups
    row = lax.axis_index("rows")
    lon = lax.axis_index("lon")
    me = row * lon_count + lon
    z = row // 2
    x = row % 2
    y = lon // 2
    core = lon % 2
    group = me % groups
    base = me - group
    half = me // groups
    to_core, to_y, to_x, far_z = partners(lon_count)
    near = z + 1 - 2 * (z % 2)
    mirror = 3 - z
    to_near = {"rows": near * 2 + x, "lon": lon}
    to_mirror = {"rows": mirror * 2 + x, "lon": lon}
    parts = 4
    share = r.wide.shape[-2]
    sender, mover = Sender(r.a_send_sem, r.b_recv_sem), Mover(r.c_move_sem)

    def order(step):
        chip = jnp.where(step % 2 == 0, near, z)
        return jnp.where(step < 2, 3 - chip, chip)

    def part_place(step):
        return pl.ds(pl.multiple_of(order(step) * channels, channels), channels)

    cotangents = [make_lon(stage, r.hbm.cot, r.dy, sender, mover) for stage in stages]
    by_e = [
        make_all(size, source, target, sender, mover)
        for source, target in zip(r.send_e, r.recv_e)
    ]
    by_g = [
        make_all(size, source, target, sender, mover)
        for source, target in zip(r.send_g, r.recv_g)
    ]
    blocks = [make_lon(stage, r.block, r.block_out, sender, mover) for stage in stages]
    by_core = [
        [
            sender.make(r.wide.at[i % 2, 0, :, :, 1 - core], r.a_core.at[i], to_core),
            sender.make(r.wide.at[i % 2, 1, :, :, 1 - core], r.b_core.at[i], to_core),
        ]
        for i in range(parts)
    ]
    by_one = [
        [
            sender.make(r.a_core.at[i, 1 - x], r.a_one.at[i], to_x),
            sender.make(r.b_core.at[i, :, 1 - y], r.b_one.at[i], to_y),
        ]
        for i in range(parts)
    ]
    by_two = [
        [
            sender.make(r.a_one.at[i, 1 - y], r.a_two.at[i], to_y),
            sender.make(r.b_one.at[i, 1 - x], r.b_two.at[i], to_x),
        ]
        for i in range(parts)
    ]
    by_near = [
        [
            sender.make(r.a_two.at[2 * i], r.a_near.at[i], to_near),
            sender.make(r.b_two.at[2 * i], r.b_near.at[i], to_near),
        ]
        for i in range(2)
    ]
    by_early = [
        sender.make(r.early, r.early_land.at[i], device)
        for i, device in enumerate((to_core, to_x, to_y, to_near, to_mirror))
    ]
    tables_back = [
        mover.make(source, target)
        for source, target in zip(r.hbm.table_t, r.table_t)
    ]

    def core_end(step):
        finish(by_core[step])
        add_to(r.a_core.at[step], r.wide.at[step % 2, 0, :, :, core])
        by_one[step][0].start()
        add_to(r.b_core.at[step], r.wide.at[step % 2, 1, :, :, core])
        by_one[step][1].start()

    def one_end(step):
        by_one[step][0].wait()
        add_to(r.a_one.at[step], r.a_core.at[step, x])
        by_two[step][0].start()
        by_one[step][1].wait()
        add_to(r.b_one.at[step], r.b_core.at[step, :, y])
        by_two[step][1].start()

    def two_end(step):
        finish(by_two[step])
        for total, kept in ((r.a_two, r.a_one.at[step, y]), (r.b_two, r.b_one.at[step, x])):
            total[step] = (total[step].astype(f32) + kept[...].astype(f32)).astype(bf16)

    def early_step(step):
        by_early[step].wait()
        r.early[...] = r.early[...] + r.early_land[step]
        if step + 1 < len(by_early):
            by_early[step + 1].start()

    def forward(*scoped):
        f = types.SimpleNamespace(**named(forward_scratch(size), iter(scoped)))
        tables = [
            mover.start(source, target)
            for source, target in zip(r.hbm.table, f.table)
        ]
        loads = [mover.start(r.hbm.er, f.er)]
        loads += [mover.start(a, b) for a, b in zip(r.hbm.ec, f.ec)]
        begin(tables_back)
        greet(lon_count, count)
        tokens = [begin(make_lon(stage, r.hbm.tokens, r.x, sender, mover)) for stage in stages]
        build_block_matrix(size, r.mix_in, r.mix_in_bias, half, f.w1, f.b1)
        build_block_matrix(size, r.mix_out, r.mix_out_bias, half, f.w2, f.b2)
        stores = [mover.start(f.w1, r.hbm.w1), mover.start(f.w2, r.hbm.w2)]
        by_a = [
            make_all(size, source, target, sender, mover)
            for source, target in zip(f.send_a, r.recv_a)
        ]
        for i, stage in enumerate(stages):
            finish(tokens[i])
            first_norm(size, stage, r.x, as_row(r.gain1), as_row(r.shift1), f.low)
            tables[i].wait()
            write_pieces(size, stage, mm(f.table[i][...], f.low[stage.part, :]), f.send_a[i])
            begin(by_a[i])
        for copies in cotangents:
            begin(copies)
        finish(loads)
        build_lat_tables(size, r.rows, r.cosine, r.sine, f.er, f.ec, r.lat, r.lat_t)
        f.modes[...] = jnp.zeros_like(f.modes)
        for i in range(len(stages)):
            finish(by_a[i])
            add_modes(size, r.recv_a[i], r.lat[i], f.modes)
        mix_layers(size, f.modes, f.w1, f.b1, f.w2, f.b2, f.band, f.inner, f.gated, f.outer, f.stacked)
        for i, stage in enumerate(stages):
            modes_back(size, stage, r.lat_t[i], f.stacked, r.send_e[i])
            begin(by_e[i])
        stores += [mover.start(f.band, r.hbm.band), mover.start(f.gated, r.hbm.gated)]
        slopes_in_place(f.inner, f.outer)
        stores += [mover.start(f.inner, r.hbm.inner), mover.start(f.outer, r.hbm.outer)]
        finish(stores)

    def front(*scoped):
        f = types.SimpleNamespace(**named(front_scratch(size), iter(scoped)))
        rounds = len(stages) * parts
        part_loads = [
            [
                mover.make(r.hbm.fc_in.at[:, part_place(i % parts)], f.fc_in.at[i % 2]),
                mover.make(r.hbm.fc_out.at[part_place(i % parts), :], f.fc_out.at[i % 2]),
            ]
            for i in range(rounds)
        ]
        inv_t_loads = [mover.start(a, b) for a, b in zip(r.hbm.inv_t, f.inv_t)]
        begin(part_loads[0])
        begin(part_loads[1])
        inv_loads = [mover.start(a, b) for a, b in zip(r.hbm.inv, f.inv)]
        r.early[...] = jnp.zeros_like(r.early)
        f.acc[...] = jnp.zeros_like(f.acc)
        r.dh[...] = jnp.zeros_like(r.dh)
        for i, stage in enumerate(stages):
            finish(cotangents[i])
            r.early[0:1, :] += local_planes(
                size, stage, r.map, r.x, r.dy, as_row(r.gain1), as_row(r.shift1), f.res, f.values
            )
        finish(inv_t_loads)
        finish(inv_loads)

        def weights(step):
            @pl.loop(0, 2)
            def _(which):
                product = t_mm(f.hidden[step, which], f.values[which])
                for i in range(8):
                    r.wide[step % 2, which, i // 4, i // 2 % 2, i % 2] = product[
                        i * share : (i + 1) * share
                    ].astype(bf16)

        for i, stage in enumerate(stages):
            is_last = i == len(stages) - 1
            finish(by_e[i])
            residual_planes(
                size, stage, r.recv_e[i], f.inv_t[i], as_row(r.gain2), as_row(r.shift2), f.res, f.values
            )

            @pl.loop(0, parts)
            def _(step):
                slot = step % 2
                at(step, parts, lambda k: finish(part_loads[i * parts + k]))
                hidden, hidden_grad = hidden_part(
                    stage.part, f.values, f.fc_in[slot], r.fc_in_bias[:, part_place(step)], f.fc_out[slot], f.acc, r.dh
                )
                r.early[pl.ds(3 + order(step), 1), :] += jnp.sum(
                    hidden_grad.astype(f32), axis=0, keepdims=True
                )
                f.hidden[step, 0, stage.part] = hidden_grad
                f.hidden[step, 1, stage.part] = hidden

                def load_next(k):
                    if i * parts + k + 2 < rounds:
                        begin(part_loads[i * parts + k + 2])

                at(step, parts, load_next)
                if is_last:
                    at(step, 3, lambda k: core_end(k - 1) if k else None)

                    @pl.when(step < 2)
                    def _():
                        weights(step)
                        at(step, 2, lambda k: begin(by_core[k]))

                    pl.when(step == 3)(lambda: one_end(0))

            gain_sum, shift_sum = residual_back_planes(size, stage, f.values, f.res, as_row(r.gain2), r.dh, f.grad)
            r.early[1:2, :] += gain_sum
            r.early[2:3, :] += shift_sum
            write_pieces(size, stage, mm(f.inv[i][...], f.grad[stage.part, :]), r.send_g[i])
            begin(by_g[i])
            if not is_last:
                block_planes(size, stage, r.map, f.res, f.acc, as_row(r.out_bias), r.block)
                begin(blocks[i])
        by_early[0].start()

        @pl.loop(2, parts)
        def _(step):
            weights(step)
            at(step - 2, 2, lambda k: begin(by_core[2 + k]))

        core_end(2)
        core_end(3)
        two_end(0)
        begin(by_near[0])
        block_planes(size, stages[-1], r.map, f.res, f.acc, as_row(r.out_bias), r.block)
        early_step(0)

    def back(*scoped):
        f = types.SimpleNamespace(**named(back_scratch(size), iter(scoped)))
        loads = [
            mover.start(source, target)
            for source, target in (
                (r.hbm.outer, f.outer),
                (r.hbm.w2, f.w2),
                (r.hbm.inner, f.inner),
                (r.hbm.w1, f.w1),
                (r.hbm.gated, f.gated),
                (r.hbm.band, f.band),
            )
        ]
        f.modes[...] = jnp.zeros_like(f.modes)
        for i in range(len(stages)):
            if i == 1:
                one_end(1)
            finish(by_g[i])
            add_modes(size, r.recv_g[i], r.lat[i], f.modes)
        finish(loads)
        mix_layers_back(size, f.modes, f.w1, f.w2, f.inner, f.outer, f.outer_grad, f.inner_grad, f.stacked)
        by_d = [
            make_all(size, source, target, sender, mover)
            for source, target in zip(f.send_d, r.recv_d)
        ]
        for i, stage in enumerate(stages):
            modes_back(size, stage, r.lat_t[i], f.stacked, f.send_d[i])
            begin(by_d[i])
        early_step(1)
        begin(blocks[-1])

        mix_back_weights(size, f.band, f.gated, f.outer_grad, f.inner_grad, r.mix)
        crossing = sender.start(r.mix.at[:, 1 - core], r.mix_core, to_core)
        finish(by_near[0])
        two_end(1)
        for total, landed in ((r.a_two, r.a_near), (r.b_two, r.b_near)):
            total[1] = (total[1].astype(f32) + landed[0].astype(f32)).astype(bf16)
        hops = [
            sender.start(r.a_two.at[1], r.a_last, to_mirror),
            sender.start(r.b_two.at[1], r.b_last, to_mirror),
        ]
        crossing.wait()
        add_to(r.mix_core, r.mix.at[:, core])
        pair = group // 2
        mixes = []
        for offset in range(1, groups // 2):
            other = (pair + offset) % (groups // 2)
            device = base + other * 2 + core
            mixes.append(
                sender.start(
                    r.mix_core.at[other],
                    r.mix_land.at[pair],
                    {"rows": device // lon_count, "lon": device % lon_count},
                )
            )
        mixes.append(mover.start(r.mix_core.at[pair], r.mix_land.at[pair]))
        one_end(2)
        early_step(2)

        finish(tables_back)
        tokens = [make_lon(stage, r.token, r.token_out, sender, mover) for stage in stages]
        gather = []
        r.late[...] = jnp.zeros_like(r.late)
        for i, stage in enumerate(stages):
            finish(by_d[i])
            gain_sum, shift_sum = last_planes(
                size, stage, r.recv_d[i], r.x, r.dh, r.table_t[i], r.gain1, f.filtered, r.token, lon + 1, lambda k: tokens[i][k].start()
            )
            r.late[0:1, :] += gain_sum
            r.late[1:2, :] += shift_sum
            if i == 0:
                finish(mixes)
                total = r.mix_land[0].astype(f32)
                for index in range(1, groups // 2):
                    total = total + r.mix_land[index].astype(f32)
                r.pair[half] = total.astype(bf16)
                crossing = sender.start(r.pair.at[half], r.pair.at[half], far_z)
                two_end(2)
                begin(by_near[1])
                one_end(3)
                crossing.wait()
                block_size = r.mix_out_grad.shape[-1]
                rest = r.mix_out_bias_grad.shape[-2]
                own_place = (pair // 4, pair // 2 % 2, slice(None), pair % 2, core)
                for source, target in (
                    (r.pair.at[:, pl.ds(0, block_size)], r.mix_out_grad.at[own_place]),
                    (r.pair.at[:, pl.ds(block_size, rest)], r.mix_out_bias_grad.at[own_place]),
                ):
                    for offset in range(1, groups // 2):
                        device = base + (pair + offset) % (groups // 2) * 2 + core
                        gather.append(
                            sender.start(
                                source,
                                target,
                                {"rows": device // lon_count, "lon": device % lon_count},
                            )
                        )
                    gather.append(mover.start(source, target))
        smalls = start_same(lon_count, count, r.late, r.late_land, sender, mover)
        early_step(3)
        finish(gather)
        gather = []
        for ref in (r.mix_out_grad, r.mix_out_bias_grad):
            own_core = ref.at[:, :, :, :, core]
            gather.append(sender.start(own_core, own_core, to_core))
        finish(smalls)
        total = r.late_land[0]
        for index in range(1, count):
            total = total + r.late_land[index]
        r.late_out[...] = total
        two_end(3)
        finish(by_near[1])
        finish(hops)
        for place, total, landed, last in (
            (0, r.a_two, r.a_near, r.a_last),
            (1, r.b_two, r.b_near, r.b_last),
        ):
            r.dense[place] = (
                total[3].astype(f32) + landed[1].astype(f32) + last[...].astype(f32)
            )
        early_step(4)
        r.early_out[...] = r.early[...]
        finish(gather)
        bias = r.mix_out_bias_grad
        for layer in range(2):
            for part in range(2):
                for block in range(r.mix_bias_out.shape[2]):
                    value = bias[layer, part, block // 4, block // 2 % 2, block % 2]
                    r.mix_bias_out[layer, part, block : block + 1] = value[0:1].astype(f32)
        for copies in blocks + tokens:
            finish(copies)

    for scope, arrays in (
        (forward, forward_scratch(size)),
        (front, front_scratch(size)),
        (back, back_scratch(size)),
    ):
        pl.run_scoped(scope, *in_vmem(arrays))


def in_vmem(group):
    return [pltpu.VMEM(leaf.shape, leaf.dtype) for leaf in jax.tree.leaves(group)]


def pieces_of(size):
    return [struct((size.per_image, stage.piece, size.half), bf16) for stage in size.stages]


def kept_arrays(size):
    both = 2 * size.half
    square = struct((both, both), bf16)
    narrow = struct((size.modes, both), bf16)
    wide = struct((size.modes, both), f32)
    return dict(
        w1=square,
        w2=square,
        band=narrow,
        gated=narrow,
        inner=wide,
        outer=wide,
    )


def lat_arrays(size):
    modes = 2 * size.modes
    return dict(
        lat=[struct((modes, stage.band), bf16) for stage in size.stages],
        lat_t=[struct((stage.band, modes), bf16) for stage in size.stages],
    )


def mode_arrays(size):
    modes = (2 * size.modes, size.half)
    return dict(modes=struct(modes, f32), stacked=struct(modes, bf16))


def forward_scratch(size):
    row = struct((1, 2 * size.half), f32)
    return dict(
        table=[struct((stage.spectrum, stage.rows), bf16) for stage in size.stages],
        ec=[struct((256, stage.band), bf16) for stage in size.stages],
        er=struct((2 * size.modes, 192), bf16),
        b1=row,
        b2=row,
        low=struct((size.tokens, size.channels), bf16),
        send_a=pieces_of(size),
        **kept_arrays(size),
        **mode_arrays(size),
    )


def front_scratch(size):
    tokens = (size.tokens, size.channels)
    square = struct((2, size.channels, size.channels), bf16)
    return dict(
        inv_t=[struct((stage.rows, stage.spectrum), bf16) for stage in size.stages],
        inv=[struct((stage.spectrum, stage.rows), bf16) for stage in size.stages],
        fc_in=square,
        fc_out=square,
        hidden=struct((4, 2) + tokens, bf16),
        values=struct((2,) + tokens, bf16),
        grad=struct(tokens, bf16),
        res=struct(tokens, f32),
        acc=struct(tokens, f32),
    )


def back_scratch(size):
    grads = struct((size.modes, 2 * size.half), bf16)
    return dict(
        outer_grad=grads,
        inner_grad=grads,
        filtered=struct((size.tokens, size.channels), f32),
        send_d=pieces_of(size),
        **kept_arrays(size),
        **mode_arrays(size),
    )


def run_layer(size, large, small, row_map, blocks_shape, number):
    shape = large["tokens"].shape
    hidden_units = large["fc_out"].shape[0]
    parts = hidden_units // size.channels
    share = hidden_units // size.devices
    block = blocks_shape[1:]
    lead = (2, 2, HALVES, blocks_shape[0] // 8, 2)
    early = struct((round_up(3 + parts, 8), size.channels), f32)
    late = struct((2, size.channels), f32)
    plane = struct(shape, bf16)
    half_blocks = struct((blocks_shape[0] // 2,) + block, bf16)
    far = dict(token_out=plane, block_out=plane)
    near = dict(
        dense=struct((2, share, size.channels), f32),
        mix_out_grad=struct(lead + (block[1], block[1]), bf16),
        mix_bias_out=struct((2, 2, blocks_shape[0] // 2, block[1]), f32),
        early_out=early,
        late_out=late,
    )
    kept = dict(kept=kept_arrays(size))

    sums = [
        struct(lead + (share, size.channels), bf16)
        for lead in ((4, 2, 2), (4, 2), (4,), (2,), ())
    ]
    scratch = dict(
        x=plane,
        dy=plane,
        token=plane,
        block=plane,
        table_t=[struct((stage.rows, stage.spectrum), bf16) for stage in size.stages],
        dh=struct((size.tokens, size.channels), f32),
        recv_a=pieces_of(size),
        send_e=pieces_of(size),
        recv_e=pieces_of(size),
        send_g=pieces_of(size),
        recv_g=pieces_of(size),
        recv_d=pieces_of(size),
        wide=struct((2, 2, 2, 2, 2, share, size.channels), bf16),
        a_core=sums[0],
        b_core=sums[0],
        a_one=sums[1],
        b_one=sums[1],
        a_two=sums[2],
        b_two=sums[2],
        a_near=sums[3],
        b_near=sums[3],
        a_last=sums[4],
        b_last=sums[4],
        mix=struct((blocks_shape[0] // 2, 2) + block, bf16),
        mix_core=half_blocks,
        mix_land=half_blocks,
        pair=struct((HALVES,) + block, bf16),
        mix_out_bias_grad=struct(lead + (block[0] - block[1], block[1]), bf16),
        early=early,
        early_land=struct((5,) + early.shape, f32),
        late=late,
        late_land=struct((size.devices,) + late.shape, f32),
        **lat_arrays(size),
    )
    sems = dict(a_send_sem=0, b_recv_sem=0, c_move_sem=0)
    large_group = dict(large=large)
    map_group = dict(map=row_map)
    groups = [
        jax.tree.map(lambda leaf: 0, group)
        for group in (large_group, small, map_group, far, near, kept, sems, scratch)
    ]
    operands = jax.tree.leaves(large_group) + jax.tree.leaves(small) + [row_map]
    outs = [jax.tree.leaves(group) for group in (far, near, kept)]
    results = call_remote(
        functools.partial(layer_kernel, size, groups),
        "layer",
        number,
        tuple(outs[0] + outs[1] + outs[2]),
        [pl.ANY] * len(jax.tree.leaves(large_group))
        + [pltpu.VMEM] * len(small)
        + [pltpu.SMEM],
        [pl.ANY] * len(outs[0]) + [pltpu.VMEM] * len(outs[1]) + [pl.ANY] * len(outs[2]),
        10 * size.devices + 2 * size.groups + 16 * size.lon + 32,
        80,
        in_vmem(scratch),
        operands,
    )
    found = iter(results)
    return types.SimpleNamespace(**named(far, found), **named(near, found))


def prepare_kernel(size, rows_ref, cos_ref, sin_ref, er_ref, mix_in_ref, bias_in_ref, mix_out_ref, bias_out_ref, *refs):
    count = len(size.stages)
    ecs, lats, lats_t = [refs[i * count : (i + 1) * count] for i in range(3)]
    w1_ref, w2_ref, b1_ref, b2_ref = refs[3 * count :]
    half = half_of(size)
    build_lat_tables(size, rows_ref, cos_ref, sin_ref, er_ref, ecs, lats, lats_t)
    build_block_matrix(size, mix_in_ref, bias_in_ref, half, w1_ref, b1_ref)
    build_block_matrix(size, mix_out_ref, bias_out_ref, half, w2_ref, b2_ref)


def exchange_lon(values):
    return lax.all_to_all(values, "lon", split_axis=0, concat_axis=0, tiled=True)


def exchange_all(values):
    return lax.all_to_all(values, ("rows", "lon"), split_axis=0, concat_axis=0, tiled=True)


def join_stages(size, pieces):
    return jnp.concatenate(
        [piece[:, : stage.used] for stage, piece in zip(size.stages, pieces)], axis=1
    )


def cut_stages(size, values):
    pieces, start = [], 0
    for stage in size.stages:
        piece = values[:, start : start + stage.used]
        pieces.append(jnp.pad(piece, ((0, 0), (0, stage.piece - stage.used), (0, 0))))
        start += stage.used
    return pieces


def to_modes(size, pieces, row_map):
    sent = jnp.tile(join_stages(size, pieces), (size.images, 1, 1))
    received = exchange_all(sent)
    used = size.slots_here * 2 * size.waves
    by_slot = received.reshape(-1, 2 * size.waves, size.half)
    image = (lax.axis_index("rows") * size.lon + lax.axis_index("lon")) // size.per_image
    slots = row_map.shape[0]
    target = jnp.where(row_map >= 0, row_map, size.images * H)
    slot_of_row = (
        jnp.zeros((size.images * H,), jnp.int32)
        .at[target]
        .set(jnp.arange(slots, dtype=jnp.int32), mode="drop")
    )
    own = lax.dynamic_slice_in_dim(slot_of_row, image * H, H)
    picked = jnp.take(by_slot, own, axis=0)
    picked = jnp.pad(picked, ((0, size.virtual_slots - H), (0, 0), (0, 0)))
    return cut_stages(size, picked.reshape(size.per_image, used, size.half))


def from_modes(size, pieces, row_map):
    used = size.slots_here * 2 * size.waves
    by_lat = join_stages(size, pieces).reshape(-1, 2 * size.waves, size.half)
    image = (lax.axis_index("rows") * size.lon + lax.axis_index("lon")) // size.per_image
    live = (row_map >= 0) & (row_map // H == image)
    picked = jnp.take(by_lat, jnp.where(live, row_map % H, 0), axis=0)
    picked = picked * live.astype(bf16)[:, None, None]
    received = exchange_all(picked.reshape(size.devices, used, size.half))
    received = received.reshape(size.images, size.per_image, used, size.half)
    return cut_stages(size, jnp.sum(received.astype(f32), axis=0).astype(bf16))


def run_fields(
    size, blocks_shape, row_map, x, dy, tables, tables_t, invs, invs_t, lat_inputs, mixers, vectors, fc_in, fc_in_bias, fc_out
):
    channels = size.channels
    names = ("rows", "lon")
    kept_structs = types.SimpleNamespace(**kept_arrays(size), **lat_arrays(size))
    pieces = tuple(pieces_of(size))
    modes = [pltpu.VMEM(v.shape, v.dtype) for v in mode_arrays(size).values()]
    flat = struct((1, 2 * size.half), f32)
    cosine, sine, er, ecs = lat_inputs
    lats = jnp.arange(size.virtual_slots)
    rows = jnp.where(lats < H, lats, -1).astype(jnp.int32)
    prepared = call_local(
        functools.partial(prepare_kernel, size),
        "prepare",
        tuple(kept_structs.lat + kept_structs.lat_t)
        + (kept_structs.w1, kept_structs.w2, flat, flat),
    )(rows, cosine, sine, er, *mixers, *ecs)
    count = len(size.stages)
    lat, lat_t, (w1, w2, b1, b2) = prepared[:count], prepared[count : 2 * count], prepared[2 * count :]
    x, dy = exchange_lon(x), exchange_lon(dy)
    sent = call_local(
        functools.partial(first_kernel, size),
        "lon_forward",
        pieces,
        [pltpu.VMEM((size.tokens, channels), bf16)],
    )(x, vectors[0], vectors[1], *tables)
    received = to_modes(size, sent, row_map)
    kept = (kept_structs.band, kept_structs.inner, kept_structs.gated, kept_structs.outer)
    results = call_local(
        functools.partial(mix_kernel, size), "mix_forward", pieces + kept, modes
    )(w1, b1, w2, b2, *received, *lat, *lat_t)
    sent, kept = results[:count], results[count:]
    received = from_modes(size, sent, row_map)
    sent, block, dh, hidden, values, early = run_mlp(
        size, fc_out.shape[0], row_map, x, dy, vectors, fc_in, fc_in_bias, fc_out, received, invs_t, invs
    )
    early = lax.psum(early, names)
    wide = call_local(
        wide_kernel, "weights_backward", struct((fc_out.shape[0], 2 * channels), bf16)
    )(hidden, values)
    dense = lax.psum_scatter(wide, names, scatter_dimension=0, tiled=True).astype(f32)
    dense = jnp.stack([dense[:, :channels], dense[:, channels:]])
    block = exchange_lon(block)
    received = to_modes(size, sent, row_map)
    results = call_local(
        functools.partial(mix_back_kernel, size),
        "mix_backward",
        pieces + (struct(blocks_shape, bf16),),
        [pltpu.VMEM((size.modes, 2 * size.half), bf16)] * 2 + modes,
    )(w1, w2, *kept, *received, *lat, *lat_t)
    sent, mix_grad = results[:count], results[count]
    half_index = half_of(size)
    mix_grad = mix_grad.astype(f32).reshape((2, 2, 1, blocks_shape[0] // 4) + blocks_shape[1:])
    mix_total = lax.psum(
        jnp.concatenate(
            [mix_grad * (half_index == other).astype(f32) for other in range(HALVES)], axis=2
        ),
        names,
    )
    received = from_modes(size, sent, row_map)
    token_grad, late = call_local(
        functools.partial(last_kernel, size),
        "lon_backward",
        (struct(x.shape, bf16), struct((2, channels), f32)),
        [pltpu.VMEM((size.tokens, channels), f32)],
    )(x, dh, vectors[0], *received, *tables_t)
    block_size = blocks_shape[2]
    return (
        exchange_lon(token_grad),
        block,
        dense,
        mix_total[..., :block_size, :],
        mix_total[..., block_size, :].reshape(2, 2, -1, block_size),
        early,
        lax.psum(late, names),
    )


def body(
    tokens,
    row_map,
    cotangent,
    norm_gain,
    norm_shift,
    mix_in,
    mix_in_bias,
    mix_out,
    mix_out_bias,
    post_gain,
    post_shift,
    fc_in,
    fc_in_bias,
    fc_out,
    fc_out_bias,
):
    size = Sizes(
        lax.axis_size("rows"), lax.axis_size("lon"), row_map.shape[0], tokens.shape[2]
    )
    channels = size.channels
    block_size = mix_in.shape[2]
    hidden_units = fc_in.shape[1]
    blocks_shape = (4 * mix_in.shape[1] // HALVES, round_up(block_size + 1, 16), block_size)
    device = lax.axis_index("rows") * size.lon + lax.axis_index("lon")
    tables, tables_t, invs, invs_t = lon_tables(size)
    cosine, sine, er, ecs = lat_parts(size)
    shape = (size.lon, size.slots_here, size.lons_here, channels)
    x, dy = tokens.reshape(shape), cotangent.reshape(shape)
    vectors = (norm_gain, norm_shift, post_gain, post_shift, fc_out_bias)
    bias_row = fc_in_bias.reshape(1, -1)
    if size.images == 1:
        large = dict(
            tokens=x,
            cot=dy,
            table=tables,
            table_t=tables_t,
            inv=invs,
            inv_t=invs_t,
            ec=ecs,
            er=er,
            fc_in=fc_in,
            fc_out=fc_out,
        )
        small = dict(
            rows=row_map,
            cosine=cosine,
            sine=sine,
            mix_in=mix_in,
            mix_in_bias=mix_in_bias,
            mix_out=mix_out,
            mix_out_bias=mix_out_bias,
            gain1=norm_gain,
            shift1=norm_shift,
            gain2=post_gain,
            shift2=post_shift,
            out_bias=fc_out_bias,
            fc_in_bias=bias_row,
        )
        r = run_layer(size, large, small, row_map, blocks_shape, 0)
        results = (
            r.token_out,
            r.block_out,
            r.dense,
            r.mix_out_grad,
            r.mix_bias_out,
            r.early_out,
            r.late_out,
        )
    else:
        results = run_fields(
            size, blocks_shape, row_map, x, dy, tables, tables_t, invs, invs_t, (cosine, sine, er, ecs), (mix_in, mix_in_bias, mix_out, mix_out_bias), vectors, fc_in, bias_row, fc_out
        )
    token_grad, block, dense, mix_total, mix_bias, early, late = results
    share = hidden_units // size.devices
    return (
        block.reshape(tokens.shape),
        token_grad.reshape(tokens.shape).astype(f32),
        late[0],
        late[1],
        mix_total[0].reshape(mix_in.shape).astype(f32),
        mix_bias[0],
        mix_total[1].reshape(mix_in.shape).astype(f32),
        mix_bias[1],
        early[1],
        early[2],
        dense[0].T,
        lax.dynamic_slice_in_dim(early[3:7].reshape(-1), device * share, share),
        dense[1],
        early[0],
    )


def solution(mesh):
    return jax.shard_map(
        body,
        mesh=mesh,
        in_specs=(P("rows", "lon", None), P(), P("rows", "lon", None)) + (P(),) * 12,
        out_specs=(
            P("rows", "lon", None),
            P("rows", "lon", None),
            P(),
            P(),
            P(),
            P(),
            P(),
            P(),
            P(),
            P(),
            P(None, ("rows", "lon")),
            P(("rows", "lon")),
            P(("rows", "lon"), None),
            P(),
        ),
        check_vma=False,
    )
```

```python
import functools
import math
import types

import jax
import jax.numpy as jnp
import ml_dtypes
import numpy as np
from jax import lax
from jax.experimental import pallas as pl
from jax.experimental.pallas import tpu as pltpu
from jax.sharding import PartitionSpec as P

H = 90
W = 180
KX = 91
HALVES = 2
VMEM_BYTES = 58 * 1024 * 1024

norm_eps = 1e-06
shrink_level = 0.01
half_root = 0.7071067811865476
normal_peak = 0.3989422804014327
MESH = pl.DeviceIdType.MESH
f32 = jnp.float32
bf16 = jnp.bfloat16


def round_up(value, step):
    return -(-value // step) * step


class Stage:
    def __init__(self, size, slots, first_row):
        self.slots = slots
        self.rows = size.lon * len(slots) * size.lons_pad
        self.first_row = first_row
        self.part = slice(first_row, first_row + self.rows)
        self.used = len(slots) * 2 * size.waves
        self.piece = round_up(self.used, 8)
        self.spectrum = size.groups * self.piece
        self.band = size.per_image * self.piece


class Sizes:
    def __init__(self, rows_count, lon_count, slots, channels):
        self.rows = rows_count
        self.lon = lon_count
        self.devices = rows_count * lon_count
        self.images = slots * 15 // (16 * H)
        self.per_image = self.devices // self.images
        self.groups = self.per_image // HALVES
        self.waves = -(-KX // self.groups)
        self.slots_here = slots // self.devices
        self.lons_here = W // lon_count
        self.lons_pad = round_up(self.lons_here, 16)
        self.tokens = lon_count * self.slots_here * self.lons_pad
        self.modes = round_up(H * self.waves, 16)
        self.virtual_slots = self.per_image * self.slots_here
        self.channels = channels
        self.half = channels // HALVES
        cut = -(-self.slots_here * 2 // 3)
        self.stages = []
        first_row = 0
        for low, high in ((0, cut), (cut, self.slots_here)):
            if low < high:
                self.stages.append(Stage(self, tuple(range(low, high)), first_row))
                first_row += self.stages[-1].rows


def lon_tables(size):
    wave = np.arange(size.groups * size.waves)
    lon_index = np.arange(W)
    product = (lon_index[:, None] * wave[None, :]) % W
    angle = product.astype(np.float32) * np.float32(2.0 * math.pi / W)
    scale = np.float32(1.0 / math.sqrt(W))
    cosine = (np.cos(angle) * scale).astype(ml_dtypes.bfloat16).astype(np.float32)
    sine = (-np.sin(angle) * scale).astype(ml_dtypes.bfloat16).astype(np.float32)
    live = (wave < KX).astype(np.float32)
    factor = np.where((wave == 0) | (wave == W // 2), 1.0, 2.0).astype(np.float32)
    both = np.stack([cosine, sine]) * live
    result = []
    for weight in (np.ones_like(factor), factor):
        values = (both * weight).reshape(2, size.lon, size.lons_here, size.groups, size.waves)
        values = np.transpose(values, (3, 0, 4, 1, 2)).reshape(
            size.groups, 2 * size.waves, size.lon, size.lons_here
        )
        tables = []
        for stage in size.stages:
            count = len(stage.slots)
            table = np.zeros(
                (size.groups, stage.piece, size.lon, count, size.lons_pad), np.float32
            )
            for slot in range(count):
                start = slot * 2 * size.waves
                table[:, start : start + 2 * size.waves, :, slot, : size.lons_here] = values
            tables.append(table.reshape(stage.spectrum, stage.rows).astype(ml_dtypes.bfloat16))
        result.append([jnp.asarray(t) for t in tables])
        result.append([jnp.asarray(np.ascontiguousarray(t.T)) for t in tables])
    return result


def lat_parts(size):
    lat_index = np.arange(H)
    angle = ((lat_index[:, None] * lat_index[None, :]) % H).astype(np.float32) * np.float32(
        2.0 * math.pi / H
    )
    scale = np.float32(1.0 / math.sqrt(H))
    cosine = np.zeros((96, 96), np.float32)
    sine = np.zeros((96, 96), np.float32)
    cosine[:H, :H] = np.cos(angle) * scale
    sine[:H, :H] = np.sin(angle) * scale
    spread_rows = np.zeros((2, size.modes, 2, 96), np.float32)
    for part in range(2):
        for lat in range(H):
            for wave in range(size.waves):
                spread_rows[part, lat * size.waves + wave, part, lat] = 1.0
    spread_cols = []
    for stage in size.stages:
        spread = np.zeros((2, 128, size.per_image, stage.piece), np.float32)
        for device in range(size.per_image):
            for place, slot in enumerate(stage.slots):
                for part in range(2):
                    start = (place * 2 + part) * size.waves
                    spread[
                        part, device * size.slots_here + slot, device, start : start + size.waves
                    ] = 1.0
        spread_cols.append(spread.reshape(256, stage.band))
    low = ml_dtypes.bfloat16
    return (
        jnp.asarray(cosine.astype(low)),
        jnp.asarray(sine.astype(low)),
        jnp.asarray(spread_rows.reshape(2 * size.modes, 192).astype(low)),
        [jnp.asarray(spread.astype(low)) for spread in spread_cols],
    )


def smooth_gate(values):
    return 0.5 * values * (1.0 + lax.erf(values * half_root))


def gate_both(values):
    half_phi = 0.5 * (1.0 + lax.erf(values * half_root))
    density = values * normal_peak * jnp.exp(-0.5 * values * values)
    return values * half_phi, half_phi + density


def gate_slope(values):
    return gate_both(values)[1]


def soft_shrink(values):
    return values - shrink_level * values * lax.rsqrt(values * values + shrink_level * shrink_level)


def shrink_slope(values):
    inverse = lax.rsqrt(values * values + shrink_level * shrink_level)
    return 1.0 - shrink_level * shrink_level * shrink_level * inverse * inverse * inverse


def norm_parts(values):
    center = values - jnp.mean(values, axis=-1, keepdims=True)
    spread = lax.rsqrt(jnp.mean(center * center, axis=-1, keepdims=True) + norm_eps)
    return center * spread, spread


def norm_back(scaled, unit, spread):
    return spread * (
        scaled
        - jnp.mean(scaled, axis=-1, keepdims=True)
        - unit * jnp.mean(scaled * unit, axis=-1, keepdims=True)
    )


def mm(left, right):
    return jnp.dot(left, right, preferred_element_type=f32)


def mm_t(left, right):
    return lax.dot_general(left, right, (((1,), (1,)), ((), ())), preferred_element_type=f32)


def t_mm(left, right):
    return lax.dot_general(left, right, (((0,), (0,)), ((), ())), preferred_element_type=f32)


def whole(count):
    return [pl.BlockSpec(memory_space=pltpu.VMEM)] * count


def call_local(kernel, name, outs, scratch=()):
    def run(*operands):
        return pl.pallas_call(
            kernel,
            out_shape=outs,
            in_specs=whole(len(operands)),
            out_specs=jax.tree.map(lambda _: pl.BlockSpec(memory_space=pltpu.VMEM), outs),
            scratch_shapes=list(scratch),
            compiler_params=pltpu.CompilerParams(vmem_limit_bytes=VMEM_BYTES),
            name=name,
        )(*operands)

    return run


def struct(shape, dtype):
    return jax.ShapeDtypeStruct(shape, dtype)


def wave_of(index, period, used, waves, other):
    within = index - period * jnp.floor((index + 0.5) * (1.0 / period))
    wave = within - waves * jnp.floor((within + 0.5) * (1.0 / waves))
    return jnp.where(within < used, wave, other)


def build_lat_tables(size, rows_ref, cos_ref, sin_ref, er_ref, ec_refs, lat_refs, lat_t_refs):
    slots = rows_ref.shape[0]
    lat_of = lax.broadcasted_iota(jnp.int32, (96, slots), 0)
    hot = (lat_of == rows_ref[...].reshape(1, slots)).astype(f32)
    hot = jnp.concatenate([hot, jnp.zeros((96, 128 - slots), f32)], axis=1).astype(bf16)
    cosine = mm(cos_ref[...], hot)
    sine = mm(sin_ref[...], hot)
    top = jnp.concatenate([cosine, sine], axis=1)
    bottom = jnp.concatenate([-sine, cosine], axis=1)
    base = jnp.concatenate([top, bottom], axis=0).astype(bf16)

    def row_waves(shape, dim):
        index = lax.broadcasted_iota(jnp.int32, shape, dim).astype(f32)
        return wave_of(index, size.modes, H * size.waves, size.waves, -1.0)

    def col_waves(stage, shape, dim):
        index = lax.broadcasted_iota(jnp.int32, shape, dim).astype(f32)
        return wave_of(index, stage.piece, stage.used, size.waves, -2.0)

    modes = 2 * size.modes
    for stage, ec_ref, lat_ref, lat_t_ref in zip(size.stages, ec_refs, lat_refs, lat_t_refs):
        keep = row_waves((modes, 1), 0) == col_waves(stage, (1, stage.band), 1)
        keep_t = col_waves(stage, (stage.band, 1), 0) == row_waves((1, modes), 1)
        columns = mm(base, ec_ref[...]).astype(bf16)
        lat_ref[...] = jnp.where(keep, mm(er_ref[...], columns), 0.0).astype(bf16)
        table_t = lax.dot_general(
            columns, er_ref[...], (((0,), (1,)), ((), ())), preferred_element_type=f32
        )
        lat_t_ref[...] = jnp.where(keep_t, table_t, 0.0).astype(bf16)


def build_block_matrix(size, weight_ref, bias_ref, half, matrix_ref, row_ref):
    block_size = weight_ref.shape[2]
    blocks = size.half // block_size
    matrix_ref[...] = jnp.zeros_like(matrix_ref)
    for block in range(blocks):
        real = weight_ref[0, half * blocks + block]
        imag = weight_ref[1, half * blocks + block]
        near = slice(block * block_size, (block + 1) * block_size)
        far = slice(size.half + block * block_size, size.half + (block + 1) * block_size)
        matrix_ref[near, near] = real
        matrix_ref[near, far] = imag
        matrix_ref[far, near] = -imag
        matrix_ref[far, far] = real
        row_ref[0:1, near] = bias_ref[0, pl.ds(half * blocks + block, 1), :]
        row_ref[0:1, far] = bias_ref[1, pl.ds(half * blocks + block, 1), :]


def half_of(size):
    device = lax.axis_index("rows") * size.lon + lax.axis_index("lon")
    return (device % size.per_image) // size.groups


def pad_plane(size, plane):
    extra = size.lons_pad - size.lons_here
    return jnp.concatenate([plane, jnp.zeros((extra, plane.shape[1]), plane.dtype)], axis=0)


def at(step, count, action):
    for i in range(count):

        @pl.when(step == i)
        def _():
            action(i)


def over_planes(size, stage, body, *sums, first=0, then=None):
    def step(index, sums):
        source = (first + index) % size.lon
        for place, slot in enumerate(stage.slots):
            start = stage.first_row + pl.multiple_of(
                (source * len(stage.slots) + place) * size.lons_pad, size.lons_pad
            )
            start = pl.multiple_of(start, size.lons_pad)
            sums = body(source, slot, pl.ds(start, size.lons_pad), *sums)
        if then is not None:
            at(index, size.lon, then)
        return sums

    return lax.fori_loop(0, size.lon, step, sums)


def as_row(ref):
    return ref[...].reshape(1, -1)


def write_pieces(size, stage, values, out_ref):
    for half in range(HALVES):
        for group in range(size.groups):
            out_ref[half * size.groups + group] = values[
                group * stage.piece : (group + 1) * stage.piece,
                half * size.half : (half + 1) * size.half,
            ].astype(bf16)


def read_pieces(ref, first, count):
    return jnp.concatenate([ref[first + i].astype(f32) for i in range(count)], axis=0).astype(bf16)


def read_spectrum(size, ref):
    return jnp.concatenate(
        [read_pieces(ref, half * size.groups, size.groups) for half in range(HALVES)], axis=1
    )


def first_norm(size, stage, x_ref, gain, shift, low_ref):
    def plane(source, slot, rows):
        x = pad_plane(size, x_ref[source, slot].astype(f32))
        unit, _ = norm_parts(x)
        low_ref[rows, :] = (unit * gain + shift).astype(bf16)
        return ()

    over_planes(size, stage, plane)


def first_kernel(size, x_ref, gain_ref, shift_ref, *refs):
    count = len(size.stages)
    tables, sends, low_ref = refs[:count], refs[count : 2 * count], refs[-1]
    for stage, table_ref, send_ref in zip(size.stages, tables, sends):
        first_norm(size, stage, x_ref, as_row(gain_ref), as_row(shift_ref), low_ref)
        write_pieces(size, stage, mm(table_ref[...], low_ref[stage.part, :]), send_ref)


def add_modes(size, recv_ref, lat_ref, modes_ref):
    modes_ref[...] += mm(lat_ref[...], read_pieces(recv_ref, 0, size.per_image))


def side_by_side(size, modes_ref):
    return jnp.concatenate(
        [modes_ref[: size.modes, :], modes_ref[size.modes :, :]], axis=1
    ).astype(bf16)


def stack_parts(size, values, stacked_ref):
    stacked_ref[: size.modes, :] = values[:, : size.half].astype(bf16)
    stacked_ref[size.modes :, :] = values[:, size.half :].astype(bf16)


def modes_back(size, stage, lat_t_ref, stacked_ref, send_ref):
    back = mm(lat_t_ref[...], stacked_ref[...])
    for device in range(size.per_image):
        send_ref[device] = back[device * stage.piece : (device + 1) * stage.piece].astype(bf16)


def mix_layers(size, modes_ref, w1_ref, b1_ref, w2_ref, b2_ref, band_ref, inner_ref, gated_ref, outer_ref, stacked_ref):
    band = side_by_side(size, modes_ref)
    band_ref[...] = band
    inner = mm(band, w1_ref[...]) + b1_ref[...]
    inner_ref[...] = inner
    gated = smooth_gate(inner).astype(bf16)
    gated_ref[...] = gated
    outer = mm(gated, w2_ref[...]) + b2_ref[...]
    outer_ref[...] = outer
    stack_parts(size, soft_shrink(outer), stacked_ref)


def slopes_in_place(inner_ref, outer_ref):
    inner_ref[...] = gate_slope(inner_ref[...])
    outer_ref[...] = shrink_slope(outer_ref[...])


def mix_kernel(size, w1_ref, b1_ref, w2_ref, b2_ref, *refs):
    count = len(size.stages)
    recvs, lats, lats_t, sends = [refs[i * count : (i + 1) * count] for i in range(4)]
    band_ref, inner_ref, gated_ref, outer_ref, modes_ref, stacked_ref = refs[4 * count :]
    modes_ref[...] = jnp.zeros_like(modes_ref)
    for recv_ref, lat_ref in zip(recvs, lats):
        add_modes(size, recv_ref, lat_ref, modes_ref)
    mix_layers(size, modes_ref, w1_ref, b1_ref, w2_ref, b2_ref, band_ref, inner_ref, gated_ref, outer_ref, stacked_ref)
    for stage, lat_t_ref, send_ref in zip(size.stages, lats_t, sends):
        modes_back(size, stage, lat_t_ref, stacked_ref, send_ref)
    slopes_in_place(inner_ref, outer_ref)


def mix_layers_back(size, modes_ref, w1_ref, w2_ref, inner_ref, outer_ref, outer_grad_ref, inner_grad_ref, stacked_ref):
    upstream = side_by_side(size, modes_ref)
    outer_grad = (upstream.astype(f32) * outer_ref[...]).astype(bf16)
    outer_grad_ref[...] = outer_grad
    inner_grad = (mm_t(outer_grad, w2_ref[...]) * inner_ref[...]).astype(bf16)
    inner_grad_ref[...] = inner_grad
    stack_parts(size, mm_t(inner_grad, w1_ref[...]), stacked_ref)


def mix_back_weights(size, band_ref, gated_ref, outer_grad_ref, inner_grad_ref, out_ref):
    half = size.half
    block_size = out_ref.shape[-1]
    blocks = half // block_size
    rest = out_ref.shape[-2] - block_size
    for layer, (value_ref, grad_ref) in enumerate(
        ((band_ref, inner_grad_ref), (gated_ref, outer_grad_ref))
    ):
        grad = grad_ref[...]
        total = t_mm(value_ref[...], grad)
        bias = jnp.sum(grad.astype(f32), axis=0, keepdims=True)
        for block in range(blocks):
            near = slice(block * block_size, (block + 1) * block_size)
            far = slice(half + block * block_size, half + (block + 1) * block_size)
            for part, values, row in (
                (0, total[near, near] + total[far, far], bias[:, near]),
                (1, total[near, far] - total[far, near], bias[:, far]),
            ):
                place = (layer * 2 + part) * blocks + block
                at = (place // 2, place % 2) if len(out_ref.shape) == 4 else (place,)
                out_ref[at + (slice(0, block_size),)] = values.astype(bf16)
                out_ref[at + (slice(block_size, None),)] = jnp.broadcast_to(
                    row, (rest, block_size)
                ).astype(bf16)


def mix_back_kernel(size, w1_ref, w2_ref, band_ref, inner_ref, gated_ref, outer_ref, *refs):
    count = len(size.stages)
    recvs, lats, lats_t, sends = [refs[i * count : (i + 1) * count] for i in range(4)]
    grad_ref, outer_grad_ref, inner_grad_ref, modes_ref, stacked_ref = refs[4 * count :]
    modes_ref[...] = jnp.zeros_like(modes_ref)
    for recv_ref, lat_ref in zip(recvs, lats):
        add_modes(size, recv_ref, lat_ref, modes_ref)
    mix_layers_back(size, modes_ref, w1_ref, w2_ref, inner_ref, outer_ref, outer_grad_ref, inner_grad_ref, stacked_ref)
    for stage, lat_t_ref, send_ref in zip(size.stages, lats_t, sends):
        modes_back(size, stage, lat_t_ref, stacked_ref, send_ref)
    mix_back_weights(size, band_ref, gated_ref, outer_grad_ref, inner_grad_ref, grad_ref)


def live_of(size, map_ref, slot):
    first_slot = (lax.axis_index("rows") * size.lon + lax.axis_index("lon")) * size.slots_here
    return jnp.where(map_ref[first_slot + slot] >= 0, 1.0, 0.0)


def local_planes(size, stage, map_ref, x_ref, dy_ref, gain1, shift1, res_ref, values_ref):
    def plane(source, slot, rows, up_sum):
        x = pad_plane(size, x_ref[source, slot].astype(f32))
        unit, _ = norm_parts(x)
        res_ref[rows, :] = (unit * gain1 + shift1) + x
        up = pad_plane(size, dy_ref[source, slot].astype(f32) * live_of(size, map_ref, slot))
        values_ref[1, rows, :] = up.astype(bf16)
        return (up_sum + jnp.sum(up, axis=0, keepdims=True),)

    return over_planes(size, stage, plane, jnp.zeros((1, size.channels), f32))[0]


def residual_planes(size, stage, recv_ref, inv_t_ref, gain2, shift2, res_ref, values_ref):
    res_ref[stage.part, :] += mm(inv_t_ref[...], read_spectrum(size, recv_ref))

    def plane(source, slot, rows):
        unit, _ = norm_parts(res_ref[rows, :])
        values_ref[0, rows, :] = (unit * gain2 + shift2).astype(bf16)
        return ()

    over_planes(size, stage, plane)


def hidden_part(part, values_ref, fc_in, bias, fc_out, acc_ref, back_ref):
    gate, slope = gate_both(mm(values_ref[0, part, :], fc_in) + bias)
    hidden = gate.astype(bf16)
    acc_ref[part, :] += mm(hidden, fc_out)
    hidden_grad = (mm_t(values_ref[1, part, :], fc_out) * slope).astype(bf16)
    back_ref[part, :] += mm_t(hidden_grad, fc_in)
    return hidden, hidden_grad


def residual_back_planes(size, stage, values_ref, res_ref, gain2, back_ref, grad_ref):
    def plane(source, slot, rows, gain_sum, shift_sum):
        unit, spread = norm_parts(res_ref[rows, :])
        grad = back_ref[rows, :]
        gain_sum = gain_sum + jnp.sum(grad * unit, axis=0, keepdims=True)
        shift_sum = shift_sum + jnp.sum(grad, axis=0, keepdims=True)
        grad = values_ref[1, rows, :].astype(f32) + norm_back(grad * gain2, unit, spread)
        back_ref[rows, :] = grad
        grad_ref[rows, :] = grad.astype(bf16)
        return gain_sum, shift_sum

    zero = jnp.zeros((1, size.channels), f32)
    return over_planes(size, stage, plane, zero, zero)


def block_planes(size, stage, map_ref, res_ref, acc_ref, out_bias, block_ref):
    def plane(source, slot, rows):
        block = (res_ref[rows, :] + (acc_ref[rows, :] + out_bias)) * live_of(size, map_ref, slot)
        block_ref[source, slot] = block[: size.lons_here].astype(bf16)
        return ()

    over_planes(size, stage, plane)


def mlp_kernel(
    size,
    map_ref,
    x_ref,
    dy_ref,
    gain1_ref,
    shift1_ref,
    gain2_ref,
    shift2_ref,
    out_bias_ref,
    fc_in_ref,
    fc_in_bias_ref,
    fc_out_ref,
    *refs,
):
    count = len(size.stages)
    recvs, invs_t, invs, sends = [refs[i * count : (i + 1) * count] for i in range(4)]
    block_ref, dh_ref, hidden_ref, values_ref, small_ref, res_ref, grad_ref, acc_ref = refs[4 * count :]
    step = pl.program_id(0)

    @pl.when(step == 0)
    def _():
        small_ref[...] = jnp.zeros_like(small_ref)
        for stage, recv_ref, inv_t_ref in zip(size.stages, recvs, invs_t):
            small_ref[0:1, :] += local_planes(
                size, stage, map_ref, x_ref, dy_ref, as_row(gain1_ref), as_row(shift1_ref), res_ref, values_ref
            )
            residual_planes(
                size, stage, recv_ref, inv_t_ref, as_row(gain2_ref), as_row(shift2_ref), res_ref, values_ref
            )
        acc_ref[...] = jnp.zeros_like(acc_ref)
        dh_ref[...] = jnp.zeros_like(dh_ref)

    hidden, hidden_grad = hidden_part(
        slice(0, size.tokens), values_ref, fc_in_ref[...], fc_in_bias_ref[...], fc_out_ref[...], acc_ref, dh_ref
    )
    small_ref[pl.ds(3 + step, 1), :] = jnp.sum(hidden_grad.astype(f32), axis=0, keepdims=True)
    hidden_ref[0] = hidden_grad
    hidden_ref[1] = hidden

    @pl.when(step == pl.num_programs(0) - 1)
    def _():
        for stage, inv_ref, send_ref in zip(size.stages, invs, sends):
            block_planes(size, stage, map_ref, res_ref, acc_ref, as_row(out_bias_ref), block_ref)
            gain_sum, shift_sum = residual_back_planes(
                size, stage, values_ref, res_ref, as_row(gain2_ref), dh_ref, grad_ref
            )
            small_ref[1:2, :] += gain_sum
            small_ref[2:3, :] += shift_sum
            write_pieces(size, stage, mm(inv_ref[...], grad_ref[stage.part, :]), send_ref)


def run_mlp(size, hidden_units, row_map, x, dy, vectors, fc_in, fc_in_bias, fc_out, received, invs_t, invs):
    channels = size.channels
    parts = hidden_units // channels
    fixed = pl.BlockSpec(memory_space=pltpu.VMEM)
    tokens = (size.tokens, channels)
    count = len(size.stages)
    out = pl.pallas_call(
        functools.partial(mlp_kernel, size),
        grid=(parts,),
        in_specs=[pl.BlockSpec(memory_space=pltpu.SMEM)]
        + [fixed] * (2 + len(vectors))
        + [
            pl.BlockSpec((channels, channels), lambda i: (0, i)),
            pl.BlockSpec((1, channels), lambda i: (0, i)),
            pl.BlockSpec((channels, channels), lambda i: (i, 0)),
        ]
        + [fixed] * (3 * count),
        out_specs=tuple(
            [fixed] * (count + 2)
            + [pl.BlockSpec((None, 2) + tokens, lambda i: (i, 0, 0, 0))]
            + [fixed] * 2
        ),
        out_shape=tuple(
            [struct(piece.shape, bf16) for piece in received]
            + [
                struct(x.shape, bf16),
                struct(tokens, f32),
                struct((parts, 2) + tokens, bf16),
                struct((2,) + tokens, bf16),
                struct((round_up(3 + parts, 8), channels), f32),
            ]
        ),
        scratch_shapes=[
            pltpu.VMEM(tokens, f32),
            pltpu.VMEM(tokens, bf16),
            pltpu.VMEM(tokens, f32),
        ],
        compiler_params=pltpu.CompilerParams(vmem_limit_bytes=VMEM_BYTES),
        name="mlp",
    )(row_map, x, dy, *vectors, fc_in, fc_in_bias, fc_out, *received, *invs_t, *invs)
    return (out[:count],) + tuple(out[count:])


def wide_kernel(hidden_ref, values_ref, wide_ref):
    channels = values_ref.shape[2]
    for part in range(hidden_ref.shape[0]):
        rows = slice(part * channels, (part + 1) * channels)
        wide_ref[rows, :channels] = t_mm(hidden_ref[part, 0], values_ref[0]).astype(bf16)
        wide_ref[rows, channels:] = t_mm(hidden_ref[part, 1], values_ref[1]).astype(bf16)


def last_planes(size, stage, recv_ref, x_ref, dh_ref, table_t_ref, gain_ref, filtered_ref, out_ref, first=0, then=None):
    gain = as_row(gain_ref)
    filtered_ref[stage.part, :] = mm(table_t_ref[...], read_spectrum(size, recv_ref))

    def plane(source, slot, rows, gain_sum, shift_sum):
        unit, spread = norm_parts(pad_plane(size, x_ref[source, slot].astype(f32)))
        base = dh_ref[rows, :]
        grad = base + filtered_ref[rows, :]
        gain_sum = gain_sum + jnp.sum(grad * unit, axis=0, keepdims=True)
        shift_sum = shift_sum + jnp.sum(grad, axis=0, keepdims=True)
        grad = base + norm_back(grad * gain, unit, spread)
        out_ref[source, slot] = grad[: size.lons_here].astype(bf16)
        return gain_sum, shift_sum

    zero = jnp.zeros((1, size.channels), f32)
    return over_planes(size, stage, plane, zero, zero, first=first, then=then)


def last_kernel(size, x_ref, dh_ref, gain_ref, *refs):
    count = len(size.stages)
    recvs, tables_t = refs[:count], refs[count : 2 * count]
    out_ref, small_ref, filtered_ref = refs[2 * count :]
    small_ref[...] = jnp.zeros_like(small_ref)
    for stage, recv_ref, table_t_ref in zip(size.stages, recvs, tables_t):
        gain_sum, shift_sum = last_planes(size, stage, recv_ref, x_ref, dh_ref, table_t_ref, gain_ref, filtered_ref, out_ref)
        small_ref[0:1, :] += gain_sum
        small_ref[1:2, :] += shift_sum


def partners(lon_count):
    row = lax.axis_index("rows")
    lon = lax.axis_index("lon")
    core = {"rows": row, "lon": lon + 1 - 2 * (lon % 2)}
    along_y = {"rows": row, "lon": (lon + 2) % 4}
    along_x = {"rows": row + 1 - 2 * (row % 2), "lon": lon}
    far_z = {"rows": (row + 4) % 8, "lon": lon}
    return core, along_y, along_x, far_z


def greet(lon_count, count):
    row = lax.axis_index("rows")
    lon = lax.axis_index("lon")
    me = row * lon_count + lon
    barrier = pltpu.get_barrier_semaphore()
    for offset in range(1, count):
        other = (me + offset) % count
        pl.semaphore_signal(
            barrier,
            inc=1,
            device_id={"rows": other // lon_count, "lon": other % lon_count},
            device_id_type=MESH,
        )
    pl.semaphore_wait(barrier, count - 1)


class Sender:
    def __init__(self, send_sem, recv_sem):
        self.send_sem = send_sem
        self.recv_sem = recv_sem
        self.used = 0

    def make(self, source, target, device):
        copy = pltpu.make_async_remote_copy(
            src_ref=source,
            dst_ref=target,
            send_sem=self.send_sem.at[self.used],
            recv_sem=self.recv_sem.at[self.used],
            device_id=device,
            device_id_type=MESH,
        )
        self.used += 1
        return copy

    def start(self, source, target, device):
        copy = self.make(source, target, device)
        copy.start()
        return copy


class Mover:
    def __init__(self, sem):
        self.sem = sem
        self.used = 0

    def make(self, source, target):
        copy = pltpu.make_async_copy(source, target, self.sem.at[self.used])
        self.used += 1
        return copy

    def start(self, source, target):
        copy = self.make(source, target)
        copy.start()
        return copy


def make_all(size, source_ref, out_ref, sender, mover):
    row = lax.axis_index("rows")
    lon = lax.axis_index("lon")
    me = row * size.lon + lon
    copies = []
    for row_step in range(size.rows):
        for lon_step in range(size.lon):
            to_row = (row + row_step) % size.rows
            to_lon = (lon + lon_step) % size.lon
            piece = source_ref.at[to_row * size.lon + to_lon]
            if row_step == 0 and lon_step == 0:
                copies.append(mover.make(piece, out_ref.at[me]))
            else:
                copies.append(
                    sender.make(piece, out_ref.at[me], {"rows": to_row, "lon": to_lon})
                )
    return copies


def make_lon(stage, source_ref, out_ref, sender, mover):
    row = lax.axis_index("rows")
    me = lax.axis_index("lon")
    count = source_ref.shape[0]
    slots = pl.ds(stage.slots[0], len(stage.slots))
    copies = []
    for offset in range(1, count):
        other = (me + offset) % count
        copies.append(
            sender.make(
                source_ref.at[other, slots], out_ref.at[me, slots], {"rows": row, "lon": other}
            )
        )
    copies.append(mover.make(source_ref.at[me, slots], out_ref.at[me, slots]))
    return copies


def begin(copies):
    for copy in copies:
        copy.start()
    return copies


def finish(copies):
    for copy in copies:
        copy.wait()


def call_remote(kernel, name, number, outs, spaces, out_spaces, sends, moves, scratch, operands):
    return pl.pallas_call(
        kernel,
        out_shape=outs,
        in_specs=[pl.BlockSpec(memory_space=space) for space in spaces],
        out_specs=tuple(pl.BlockSpec(memory_space=space) for space in out_spaces),
        scratch_shapes=[
            pltpu.SemaphoreType.DMA((sends,)),
            pltpu.SemaphoreType.DMA((sends,)),
            pltpu.SemaphoreType.DMA((moves,)),
        ]
        + list(scratch),
        compiler_params=pltpu.CompilerParams(
            collective_id=number, has_side_effects=True, vmem_limit_bytes=VMEM_BYTES
        ),
        name=name,
    )(*operands)


def add_to(total_ref, other_ref):
    @pl.loop(0, total_ref.shape[0])
    def _(first):
        if len(total_ref.shape) == 3:
            total = total_ref[first].astype(f32) + other_ref[first].astype(f32)
            total_ref[first] = total.astype(total_ref.dtype)
        else:
            for second in range(total_ref.shape[1]):
                total = total_ref[first, second].astype(f32) + other_ref[first, second].astype(f32)
                total_ref[first, second] = total.astype(total_ref.dtype)


def start_same(lon_count, count, source_ref, out_ref, sender, mover):
    me = lax.axis_index("rows") * lon_count + lax.axis_index("lon")
    copies = []
    for offset in range(1, count):
        other = (me + offset) % count
        copies.append(
            sender.start(
                source_ref, out_ref.at[me], {"rows": other // lon_count, "lon": other % lon_count}
            )
        )
    copies.append(mover.start(source_ref, out_ref.at[me]))
    return copies


def named(group, refs):
    leaves, tree = jax.tree.flatten(group)
    return jax.tree.unflatten(tree, [next(refs) for _ in leaves])


def layer_kernel(size, groups_of, *refs):
    found = iter(refs)
    r = types.SimpleNamespace()
    for arrays in groups_of:
        r.__dict__.update(named(arrays, found))
    r.hbm = types.SimpleNamespace(**r.large, **r.kept)
    stages = size.stages
    channels = size.channels
    lon_count, count, groups = size.lon, size.devices, size.groups
    row = lax.axis_index("rows")
    lon = lax.axis_index("lon")
    me = row * lon_count + lon
    z = row // 2
    x = row % 2
    y = lon // 2
    core = lon % 2
    group = me % groups
    base = me - group
    half = me // groups
    to_core, to_y, to_x, far_z = partners(lon_count)
    near = z + 1 - 2 * (z % 2)
    mirror = 3 - z
    to_near = {"rows": near * 2 + x, "lon": lon}
    to_mirror = {"rows": mirror * 2 + x, "lon": lon}
    parts = 4
    share = r.wide.shape[-2]
    sender, mover = Sender(r.a_send_sem, r.b_recv_sem), Mover(r.c_move_sem)

    def order(step):
        chip = jnp.where(step % 2 == 0, near, z)
        return jnp.where(step < 2, 3 - chip, chip)

    def part_place(step):
        return pl.ds(pl.multiple_of(order(step) * channels, channels), channels)

    cotangents = [make_lon(stage, r.hbm.cot, r.dy, sender, mover) for stage in stages]
    by_e = [
        make_all(size, source, target, sender, mover)
        for source, target in zip(r.send_e, r.recv_e)
    ]
    by_g = [
        make_all(size, source, target, sender, mover)
        for source, target in zip(r.send_g, r.recv_g)
    ]
    blocks = [make_lon(stage, r.block, r.block_out, sender, mover) for stage in stages]
    by_core = [
        [
            sender.make(r.wide.at[i % 2, 0, :, :, 1 - core], r.a_core.at[i], to_core),
            sender.make(r.wide.at[i % 2, 1, :, :, 1 - core], r.b_core.at[i], to_core),
        ]
        for i in range(parts)
    ]
    by_one = [
        [
            sender.make(r.a_core.at[i, 1 - x], r.a_one.at[i], to_x),
            sender.make(r.b_core.at[i, :, 1 - y], r.b_one.at[i], to_y),
        ]
        for i in range(parts)
    ]
    by_two = [
        [
            sender.make(r.a_one.at[i, 1 - y], r.a_two.at[i], to_y),
            sender.make(r.b_one.at[i, 1 - x], r.b_two.at[i], to_x),
        ]
        for i in range(parts)
    ]
    by_near = [
        [
            sender.make(r.a_two.at[2 * i], r.a_near.at[i], to_near),
            sender.make(r.b_two.at[2 * i], r.b_near.at[i], to_near),
        ]
        for i in range(2)
    ]
    by_early = [
        sender.make(r.early, r.early_land.at[i], device)
        for i, device in enumerate((to_core, to_x, to_y, to_near, to_mirror))
    ]
    tables_back = [
        mover.make(source, target)
        for source, target in zip(r.hbm.table_t, r.table_t)
    ]

    def core_end(step):
        finish(by_core[step])
        add_to(r.a_core.at[step], r.wide.at[step % 2, 0, :, :, core])
        by_one[step][0].start()
        add_to(r.b_core.at[step], r.wide.at[step % 2, 1, :, :, core])
        by_one[step][1].start()

    def one_end(step):
        by_one[step][0].wait()
        add_to(r.a_one.at[step], r.a_core.at[step, x])
        by_two[step][0].start()
        by_one[step][1].wait()
        add_to(r.b_one.at[step], r.b_core.at[step, :, y])
        by_two[step][1].start()

    def two_end(step):
        finish(by_two[step])
        for total, kept in ((r.a_two, r.a_one.at[step, y]), (r.b_two, r.b_one.at[step, x])):
            total[step] = (total[step].astype(f32) + kept[...].astype(f32)).astype(bf16)

    def early_step(step):
        by_early[step].wait()
        r.early[...] = r.early[...] + r.early_land[step]
        if step + 1 < len(by_early):
            by_early[step + 1].start()

    def forward(*scoped):
        f = types.SimpleNamespace(**named(forward_scratch(size), iter(scoped)))
        tables = [
            mover.start(source, target)
            for source, target in zip(r.hbm.table, f.table)
        ]
        loads = [mover.start(r.hbm.er, f.er)]
        loads += [mover.start(a, b) for a, b in zip(r.hbm.ec, f.ec)]
        begin(tables_back)
        greet(lon_count, count)
        tokens = [begin(make_lon(stage, r.hbm.tokens, r.x, sender, mover)) for stage in stages]
        build_block_matrix(size, r.mix_in, r.mix_in_bias, half, f.w1, f.b1)
        build_block_matrix(size, r.mix_out, r.mix_out_bias, half, f.w2, f.b2)
        stores = [mover.start(f.w1, r.hbm.w1), mover.start(f.w2, r.hbm.w2)]
        by_a = [
            make_all(size, source, target, sender, mover)
            for source, target in zip(f.send_a, r.recv_a)
        ]
        for i, stage in enumerate(stages):
            finish(tokens[i])
            first_norm(size, stage, r.x, as_row(r.gain1), as_row(r.shift1), f.low)
            tables[i].wait()
            write_pieces(size, stage, mm(f.table[i][...], f.low[stage.part, :]), f.send_a[i])
            begin(by_a[i])
        for copies in cotangents:
            begin(copies)
        finish(loads)
        build_lat_tables(size, r.rows, r.cosine, r.sine, f.er, f.ec, r.lat, r.lat_t)
        f.modes[...] = jnp.zeros_like(f.modes)
        for i in range(len(stages)):
            finish(by_a[i])
            add_modes(size, r.recv_a[i], r.lat[i], f.modes)
        mix_layers(size, f.modes, f.w1, f.b1, f.w2, f.b2, f.band, f.inner, f.gated, f.outer, f.stacked)
        for i, stage in enumerate(stages):
            modes_back(size, stage, r.lat_t[i], f.stacked, r.send_e[i])
            begin(by_e[i])
        stores += [mover.start(f.band, r.hbm.band), mover.start(f.gated, r.hbm.gated)]
        slopes_in_place(f.inner, f.outer)
        stores += [mover.start(f.inner, r.hbm.inner), mover.start(f.outer, r.hbm.outer)]
        finish(stores)

    def front(*scoped):
        f = types.SimpleNamespace(**named(front_scratch(size), iter(scoped)))
        rounds = len(stages) * parts
        part_loads = [
            [
                mover.make(r.hbm.fc_in.at[:, part_place(i % parts)], f.fc_in.at[i % 2]),
                mover.make(r.hbm.fc_out.at[part_place(i % parts), :], f.fc_out.at[i % 2]),
            ]
            for i in range(rounds)
        ]
        inv_t_loads = [mover.start(a, b) for a, b in zip(r.hbm.inv_t, f.inv_t)]
        begin(part_loads[0])
        begin(part_loads[1])
        inv_loads = [mover.start(a, b) for a, b in zip(r.hbm.inv, f.inv)]
        r.early[...] = jnp.zeros_like(r.early)
        f.acc[...] = jnp.zeros_like(f.acc)
        r.dh[...] = jnp.zeros_like(r.dh)
        for i, stage in enumerate(stages):
            finish(cotangents[i])
            r.early[0:1, :] += local_planes(
                size, stage, r.map, r.x, r.dy, as_row(r.gain1), as_row(r.shift1), f.res, f.values
            )
        finish(inv_t_loads)
        finish(inv_loads)

        def weights(step):
            @pl.loop(0, 2)
            def _(which):
                product = t_mm(f.hidden[step, which], f.values[which])
                for i in range(8):
                    r.wide[step % 2, which, i // 4, i // 2 % 2, i % 2] = product[
                        i * share : (i + 1) * share
                    ].astype(bf16)

        for i, stage in enumerate(stages):
            is_last = i == len(stages) - 1
            finish(by_e[i])
            residual_planes(
                size, stage, r.recv_e[i], f.inv_t[i], as_row(r.gain2), as_row(r.shift2), f.res, f.values
            )

            @pl.loop(0, parts)
            def _(step):
                slot = step % 2
                at(step, parts, lambda k: finish(part_loads[i * parts + k]))
                hidden, hidden_grad = hidden_part(
                    stage.part, f.values, f.fc_in[slot], r.fc_in_bias[:, part_place(step)], f.fc_out[slot], f.acc, r.dh
                )
                r.early[pl.ds(3 + order(step), 1), :] += jnp.sum(
                    hidden_grad.astype(f32), axis=0, keepdims=True
                )
                f.hidden[step, 0, stage.part] = hidden_grad
                f.hidden[step, 1, stage.part] = hidden

                def load_next(k):
                    if i * parts + k + 2 < rounds:
                        begin(part_loads[i * parts + k + 2])

                at(step, parts, load_next)
                if is_last:
                    at(step, 3, lambda k: core_end(k - 1) if k else None)

                    @pl.when(step < 2)
                    def _():
                        weights(step)
                        at(step, 2, lambda k: begin(by_core[k]))

                    pl.when(step == 3)(lambda: one_end(0))

            gain_sum, shift_sum = residual_back_planes(size, stage, f.values, f.res, as_row(r.gain2), r.dh, f.grad)
            r.early[1:2, :] += gain_sum
            r.early[2:3, :] += shift_sum
            write_pieces(size, stage, mm(f.inv[i][...], f.grad[stage.part, :]), r.send_g[i])
            begin(by_g[i])
            if not is_last:
                block_planes(size, stage, r.map, f.res, f.acc, as_row(r.out_bias), r.block)
                begin(blocks[i])
        by_early[0].start()

        @pl.loop(2, parts)
        def _(step):
            weights(step)
            at(step - 2, 2, lambda k: begin(by_core[2 + k]))

        core_end(2)
        core_end(3)
        two_end(0)
        block_planes(size, stages[-1], r.map, f.res, f.acc, as_row(r.out_bias), r.block)
        early_step(0)

    def back(*scoped):
        f = types.SimpleNamespace(**named(back_scratch(size), iter(scoped)))
        loads = [
            mover.start(source, target)
            for source, target in (
                (r.hbm.outer, f.outer),
                (r.hbm.w2, f.w2),
                (r.hbm.inner, f.inner),
                (r.hbm.w1, f.w1),
                (r.hbm.gated, f.gated),
                (r.hbm.band, f.band),
            )
        ]
        f.modes[...] = jnp.zeros_like(f.modes)
        for i in range(len(stages)):
            if i == 1:
                one_end(1)
            finish(by_g[i])
            add_modes(size, r.recv_g[i], r.lat[i], f.modes)
        begin(by_near[0])
        finish(loads)
        mix_layers_back(size, f.modes, f.w1, f.w2, f.inner, f.outer, f.outer_grad, f.inner_grad, f.stacked)
        by_d = [
            make_all(size, source, target, sender, mover)
            for source, target in zip(f.send_d, r.recv_d)
        ]
        for i, stage in enumerate(stages):
            modes_back(size, stage, r.lat_t[i], f.stacked, f.send_d[i])
            begin(by_d[i])
        early_step(1)
        begin(blocks[-1])

        mix_back_weights(size, f.band, f.gated, f.outer_grad, f.inner_grad, r.mix)
        crossing = sender.start(r.mix.at[:, 1 - core], r.mix_core, to_core)
        finish(by_near[0])
        two_end(1)
        for total, landed in ((r.a_two, r.a_near), (r.b_two, r.b_near)):
            total[1] = (total[1].astype(f32) + landed[0].astype(f32)).astype(bf16)
        hops = [
            sender.start(r.a_two.at[1], r.a_last, to_mirror),
            sender.start(r.b_two.at[1], r.b_last, to_mirror),
        ]
        crossing.wait()
        add_to(r.mix_core, r.mix.at[:, core])
        pair = group // 2
        mixes = []
        for offset in range(1, groups // 2):
            other = (pair + offset) % (groups // 2)
            device = base + other * 2 + core
            mixes.append(
                sender.start(
                    r.mix_core.at[other],
                    r.mix_land.at[pair],
                    {"rows": device // lon_count, "lon": device % lon_count},
                )
            )
        mixes.append(mover.start(r.mix_core.at[pair], r.mix_land.at[pair]))
        one_end(2)
        early_step(2)

        finish(tables_back)
        tokens = [make_lon(stage, r.token, r.token_out, sender, mover) for stage in stages]
        gather = []
        r.late[...] = jnp.zeros_like(r.late)
        for i, stage in enumerate(stages):
            finish(by_d[i])
            gain_sum, shift_sum = last_planes(
                size, stage, r.recv_d[i], r.x, r.dh, r.table_t[i], r.gain1, f.filtered, r.token, lon + 1, lambda k: tokens[i][k].start()
            )
            r.late[0:1, :] += gain_sum
            r.late[1:2, :] += shift_sum
            if i == 0:
                finish(mixes)
                total = r.mix_land[0].astype(f32)
                for index in range(1, groups // 2):
                    total = total + r.mix_land[index].astype(f32)
                r.pair[half] = total.astype(bf16)
                crossing = sender.start(r.pair.at[half], r.pair.at[half], far_z)
                two_end(2)
                begin(by_near[1])
                one_end(3)
                crossing.wait()
                block_size = r.mix_out_grad.shape[-1]
                rest = r.mix_out_bias_grad.shape[-2]
                own_place = (pair // 4, pair // 2 % 2, slice(None), pair % 2, core)
                for source, target in (
                    (r.pair.at[:, pl.ds(0, block_size)], r.mix_out_grad.at[own_place]),
                    (r.pair.at[:, pl.ds(block_size, rest)], r.mix_out_bias_grad.at[own_place]),
                ):
                    for offset in range(1, groups // 2):
                        device = base + (pair + offset) % (groups // 2) * 2 + core
                        gather.append(
                            sender.start(
                                source,
                                target,
                                {"rows": device // lon_count, "lon": device % lon_count},
                            )
                        )
                    gather.append(mover.start(source, target))
        smalls = start_same(lon_count, count, r.late, r.late_land, sender, mover)
        early_step(3)
        finish(gather)
        gather = []
        for ref in (r.mix_out_grad, r.mix_out_bias_grad):
            own_core = ref.at[:, :, :, :, core]
            gather.append(sender.start(own_core, own_core, to_core))
        finish(smalls)
        total = r.late_land[0]
        for index in range(1, count):
            total = total + r.late_land[index]
        r.late_out[...] = total
        two_end(3)
        finish(by_near[1])
        finish(hops)
        for place, total, landed, last in (
            (0, r.a_two, r.a_near, r.a_last),
            (1, r.b_two, r.b_near, r.b_last),
        ):
            r.dense[place] = (
                total[3].astype(f32) + landed[1].astype(f32) + last[...].astype(f32)
            )
        early_step(4)
        r.early_out[...] = r.early[...]
        finish(gather)
        bias = r.mix_out_bias_grad
        for layer in range(2):
            for part in range(2):
                for block in range(r.mix_bias_out.shape[2]):
                    value = bias[layer, part, block // 4, block // 2 % 2, block % 2]
                    r.mix_bias_out[layer, part, block : block + 1] = value[0:1].astype(f32)
        for copies in blocks + tokens:
            finish(copies)

    for scope, arrays in (
        (forward, forward_scratch(size)),
        (front, front_scratch(size)),
        (back, back_scratch(size)),
    ):
        pl.run_scoped(scope, *in_vmem(arrays))


def in_vmem(group):
    return [pltpu.VMEM(leaf.shape, leaf.dtype) for leaf in jax.tree.leaves(group)]


def pieces_of(size):
    return [struct((size.per_image, stage.piece, size.half), bf16) for stage in size.stages]


def kept_arrays(size):
    both = 2 * size.half
    square = struct((both, both), bf16)
    narrow = struct((size.modes, both), bf16)
    wide = struct((size.modes, both), f32)
    return dict(
        w1=square,
        w2=square,
        band=narrow,
        gated=narrow,
        inner=wide,
        outer=wide,
    )


def lat_arrays(size):
    modes = 2 * size.modes
    return dict(
        lat=[struct((modes, stage.band), bf16) for stage in size.stages],
        lat_t=[struct((stage.band, modes), bf16) for stage in size.stages],
    )


def mode_arrays(size):
    modes = (2 * size.modes, size.half)
    return dict(modes=struct(modes, f32), stacked=struct(modes, bf16))


def forward_scratch(size):
    row = struct((1, 2 * size.half), f32)
    return dict(
        table=[struct((stage.spectrum, stage.rows), bf16) for stage in size.stages],
        ec=[struct((256, stage.band), bf16) for stage in size.stages],
        er=struct((2 * size.modes, 192), bf16),
        b1=row,
        b2=row,
        low=struct((size.tokens, size.channels), bf16),
        send_a=pieces_of(size),
        **kept_arrays(size),
        **mode_arrays(size),
    )


def front_scratch(size):
    tokens = (size.tokens, size.channels)
    square = struct((2, size.channels, size.channels), bf16)
    return dict(
        inv_t=[struct((stage.rows, stage.spectrum), bf16) for stage in size.stages],
        inv=[struct((stage.spectrum, stage.rows), bf16) for stage in size.stages],
        fc_in=square,
        fc_out=square,
        hidden=struct((4, 2) + tokens, bf16),
        values=struct((2,) + tokens, bf16),
        grad=struct(tokens, bf16),
        res=struct(tokens, f32),
        acc=struct(tokens, f32),
    )


def back_scratch(size):
    grads = struct((size.modes, 2 * size.half), bf16)
    return dict(
        outer_grad=grads,
        inner_grad=grads,
        filtered=struct((size.tokens, size.channels), f32),
        send_d=pieces_of(size),
        **kept_arrays(size),
        **mode_arrays(size),
    )


def run_layer(size, large, small, row_map, blocks_shape, number):
    shape = large["tokens"].shape
    hidden_units = large["fc_out"].shape[0]
    parts = hidden_units // size.channels
    share = hidden_units // size.devices
    block = blocks_shape[1:]
    lead = (2, 2, HALVES, blocks_shape[0] // 8, 2)
    early = struct((round_up(3 + parts, 8), size.channels), f32)
    late = struct((2, size.channels), f32)
    plane = struct(shape, bf16)
    half_blocks = struct((blocks_shape[0] // 2,) + block, bf16)
    far = dict(token_out=plane, block_out=plane)
    near = dict(
        dense=struct((2, share, size.channels), f32),
        mix_out_grad=struct(lead + (block[1], block[1]), bf16),
        mix_bias_out=struct((2, 2, blocks_shape[0] // 2, block[1]), f32),
        early_out=early,
        late_out=late,
    )
    kept = dict(kept=kept_arrays(size))

    sums = [
        struct(lead + (share, size.channels), bf16)
        for lead in ((4, 2, 2), (4, 2), (4,), (2,), ())
    ]
    scratch = dict(
        x=plane,
        dy=plane,
        token=plane,
        block=plane,
        table_t=[struct((stage.rows, stage.spectrum), bf16) for stage in size.stages],
        dh=struct((size.tokens, size.channels), f32),
        recv_a=pieces_of(size),
        send_e=pieces_of(size),
        recv_e=pieces_of(size),
        send_g=pieces_of(size),
        recv_g=pieces_of(size),
        recv_d=pieces_of(size),
        wide=struct((2, 2, 2, 2, 2, share, size.channels), bf16),
        a_core=sums[0],
        b_core=sums[0],
        a_one=sums[1],
        b_one=sums[1],
        a_two=sums[2],
        b_two=sums[2],
        a_near=sums[3],
        b_near=sums[3],
        a_last=sums[4],
        b_last=sums[4],
        mix=struct((blocks_shape[0] // 2, 2) + block, bf16),
        mix_core=half_blocks,
        mix_land=half_blocks,
        pair=struct((HALVES,) + block, bf16),
        mix_out_bias_grad=struct(lead + (block[0] - block[1], block[1]), bf16),
        early=early,
        early_land=struct((5,) + early.shape, f32),
        late=late,
        late_land=struct((size.devices,) + late.shape, f32),
        **lat_arrays(size),
    )
    sems = dict(a_send_sem=0, b_recv_sem=0, c_move_sem=0)
    large_group = dict(large=large)
    map_group = dict(map=row_map)
    groups = [
        jax.tree.map(lambda leaf: 0, group)
        for group in (large_group, small, map_group, far, near, kept, sems, scratch)
    ]
    operands = jax.tree.leaves(large_group) + jax.tree.leaves(small) + [row_map]
    outs = [jax.tree.leaves(group) for group in (far, near, kept)]
    results = call_remote(
        functools.partial(layer_kernel, size, groups),
        "layer",
        number,
        tuple(outs[0] + outs[1] + outs[2]),
        [pl.ANY] * len(jax.tree.leaves(large_group))
        + [pltpu.VMEM] * len(small)
        + [pltpu.SMEM],
        [pl.ANY] * len(outs[0]) + [pltpu.VMEM] * len(outs[1]) + [pl.ANY] * len(outs[2]),
        10 * size.devices + 2 * size.groups + 16 * size.lon + 32,
        80,
        in_vmem(scratch),
        operands,
    )
    found = iter(results)
    return types.SimpleNamespace(**named(far, found), **named(near, found))


def prepare_kernel(size, rows_ref, cos_ref, sin_ref, er_ref, mix_in_ref, bias_in_ref, mix_out_ref, bias_out_ref, *refs):
    count = len(size.stages)
    ecs, lats, lats_t = [refs[i * count : (i + 1) * count] for i in range(3)]
    w1_ref, w2_ref, b1_ref, b2_ref = refs[3 * count :]
    half = half_of(size)
    build_lat_tables(size, rows_ref, cos_ref, sin_ref, er_ref, ecs, lats, lats_t)
    build_block_matrix(size, mix_in_ref, bias_in_ref, half, w1_ref, b1_ref)
    build_block_matrix(size, mix_out_ref, bias_out_ref, half, w2_ref, b2_ref)


def exchange_lon(values):
    return lax.all_to_all(values, "lon", split_axis=0, concat_axis=0, tiled=True)


def exchange_all(values):
    return lax.all_to_all(values, ("rows", "lon"), split_axis=0, concat_axis=0, tiled=True)


def join_stages(size, pieces):
    return jnp.concatenate(
        [piece[:, : stage.used] for stage, piece in zip(size.stages, pieces)], axis=1
    )


def cut_stages(size, values):
    pieces, start = [], 0
    for stage in size.stages:
        piece = values[:, start : start + stage.used]
        pieces.append(jnp.pad(piece, ((0, 0), (0, stage.piece - stage.used), (0, 0))))
        start += stage.used
    return pieces


def to_modes(size, pieces, row_map):
    sent = jnp.tile(join_stages(size, pieces), (size.images, 1, 1))
    received = exchange_all(sent)
    used = size.slots_here * 2 * size.waves
    by_slot = received.reshape(-1, 2 * size.waves, size.half)
    image = (lax.axis_index("rows") * size.lon + lax.axis_index("lon")) // size.per_image
    slots = row_map.shape[0]
    target = jnp.where(row_map >= 0, row_map, size.images * H)
    slot_of_row = (
        jnp.zeros((size.images * H,), jnp.int32)
        .at[target]
        .set(jnp.arange(slots, dtype=jnp.int32), mode="drop")
    )
    own = lax.dynamic_slice_in_dim(slot_of_row, image * H, H)
    picked = jnp.take(by_slot, own, axis=0)
    picked = jnp.pad(picked, ((0, size.virtual_slots - H), (0, 0), (0, 0)))
    return cut_stages(size, picked.reshape(size.per_image, used, size.half))


def from_modes(size, pieces, row_map):
    used = size.slots_here * 2 * size.waves
    by_lat = join_stages(size, pieces).reshape(-1, 2 * size.waves, size.half)
    image = (lax.axis_index("rows") * size.lon + lax.axis_index("lon")) // size.per_image
    live = (row_map >= 0) & (row_map // H == image)
    picked = jnp.take(by_lat, jnp.where(live, row_map % H, 0), axis=0)
    picked = picked * live.astype(bf16)[:, None, None]
    received = exchange_all(picked.reshape(size.devices, used, size.half))
    received = received.reshape(size.images, size.per_image, used, size.half)
    return cut_stages(size, jnp.sum(received.astype(f32), axis=0).astype(bf16))


def run_fields(
    size, blocks_shape, row_map, x, dy, tables, tables_t, invs, invs_t, lat_inputs, mixers, vectors, fc_in, fc_in_bias, fc_out
):
    channels = size.channels
    names = ("rows", "lon")
    kept_structs = types.SimpleNamespace(**kept_arrays(size), **lat_arrays(size))
    pieces = tuple(pieces_of(size))
    modes = [pltpu.VMEM(v.shape, v.dtype) for v in mode_arrays(size).values()]
    flat = struct((1, 2 * size.half), f32)
    cosine, sine, er, ecs = lat_inputs
    lats = jnp.arange(size.virtual_slots)
    rows = jnp.where(lats < H, lats, -1).astype(jnp.int32)
    prepared = call_local(
        functools.partial(prepare_kernel, size),
        "prepare",
        tuple(kept_structs.lat + kept_structs.lat_t)
        + (kept_structs.w1, kept_structs.w2, flat, flat),
    )(rows, cosine, sine, er, *mixers, *ecs)
    count = len(size.stages)
    lat, lat_t, (w1, w2, b1, b2) = prepared[:count], prepared[count : 2 * count], prepared[2 * count :]
    x, dy = exchange_lon(x), exchange_lon(dy)
    sent = call_local(
        functools.partial(first_kernel, size),
        "lon_forward",
        pieces,
        [pltpu.VMEM((size.tokens, channels), bf16)],
    )(x, vectors[0], vectors[1], *tables)
    received = to_modes(size, sent, row_map)
    kept = (kept_structs.band, kept_structs.inner, kept_structs.gated, kept_structs.outer)
    results = call_local(
        functools.partial(mix_kernel, size), "mix_forward", pieces + kept, modes
    )(w1, b1, w2, b2, *received, *lat, *lat_t)
    sent, kept = results[:count], results[count:]
    received = from_modes(size, sent, row_map)
    sent, block, dh, hidden, values, early = run_mlp(
        size, fc_out.shape[0], row_map, x, dy, vectors, fc_in, fc_in_bias, fc_out, received, invs_t, invs
    )
    early = lax.psum(early, names)
    wide = call_local(
        wide_kernel, "weights_backward", struct((fc_out.shape[0], 2 * channels), bf16)
    )(hidden, values)
    dense = lax.psum_scatter(wide, names, scatter_dimension=0, tiled=True).astype(f32)
    dense = jnp.stack([dense[:, :channels], dense[:, channels:]])
    block = exchange_lon(block)
    received = to_modes(size, sent, row_map)
    results = call_local(
        functools.partial(mix_back_kernel, size),
        "mix_backward",
        pieces + (struct(blocks_shape, bf16),),
        [pltpu.VMEM((size.modes, 2 * size.half), bf16)] * 2 + modes,
    )(w1, w2, *kept, *received, *lat, *lat_t)
    sent, mix_grad = results[:count], results[count]
    half_index = half_of(size)
    mix_grad = mix_grad.astype(f32).reshape((2, 2, 1, blocks_shape[0] // 4) + blocks_shape[1:])
    mix_total = lax.psum(
        jnp.concatenate(
            [mix_grad * (half_index == other).astype(f32) for other in range(HALVES)], axis=2
        ),
        names,
    )
    received = from_modes(size, sent, row_map)
    token_grad, late = call_local(
        functools.partial(last_kernel, size),
        "lon_backward",
        (struct(x.shape, bf16), struct((2, channels), f32)),
        [pltpu.VMEM((size.tokens, channels), f32)],
    )(x, dh, vectors[0], *received, *tables_t)
    block_size = blocks_shape[2]
    return (
        exchange_lon(token_grad),
        block,
        dense,
        mix_total[..., :block_size, :],
        mix_total[..., block_size, :].reshape(2, 2, -1, block_size),
        early,
        lax.psum(late, names),
    )


def body(
    tokens,
    row_map,
    cotangent,
    norm_gain,
    norm_shift,
    mix_in,
    mix_in_bias,
    mix_out,
    mix_out_bias,
    post_gain,
    post_shift,
    fc_in,
    fc_in_bias,
    fc_out,
    fc_out_bias,
):
    size = Sizes(
        lax.axis_size("rows"), lax.axis_size("lon"), row_map.shape[0], tokens.shape[2]
    )
    channels = size.channels
    block_size = mix_in.shape[2]
    hidden_units = fc_in.shape[1]
    blocks_shape = (4 * mix_in.shape[1] // HALVES, round_up(block_size + 1, 16), block_size)
    device = lax.axis_index("rows") * size.lon + lax.axis_index("lon")
    tables, tables_t, invs, invs_t = lon_tables(size)
    cosine, sine, er, ecs = lat_parts(size)
    shape = (size.lon, size.slots_here, size.lons_here, channels)
    x, dy = tokens.reshape(shape), cotangent.reshape(shape)
    vectors = (norm_gain, norm_shift, post_gain, post_shift, fc_out_bias)
    bias_row = fc_in_bias.reshape(1, -1)
    if size.images == 1:
        large = dict(
            tokens=x,
            cot=dy,
            table=tables,
            table_t=tables_t,
            inv=invs,
            inv_t=invs_t,
            ec=ecs,
            er=er,
            fc_in=fc_in,
            fc_out=fc_out,
        )
        small = dict(
            rows=row_map,
            cosine=cosine,
            sine=sine,
            mix_in=mix_in,
            mix_in_bias=mix_in_bias,
            mix_out=mix_out,
            mix_out_bias=mix_out_bias,
            gain1=norm_gain,
            shift1=norm_shift,
            gain2=post_gain,
            shift2=post_shift,
            out_bias=fc_out_bias,
            fc_in_bias=bias_row,
        )
        r = run_layer(size, large, small, row_map, blocks_shape, 0)
        results = (
            r.token_out,
            r.block_out,
            r.dense,
            r.mix_out_grad,
            r.mix_bias_out,
            r.early_out,
            r.late_out,
        )
    else:
        results = run_fields(
            size, blocks_shape, row_map, x, dy, tables, tables_t, invs, invs_t, (cosine, sine, er, ecs), (mix_in, mix_in_bias, mix_out, mix_out_bias), vectors, fc_in, bias_row, fc_out
        )
    token_grad, block, dense, mix_total, mix_bias, early, late = results
    share = hidden_units // size.devices
    return (
        block.reshape(tokens.shape),
        token_grad.reshape(tokens.shape).astype(f32),
        late[0],
        late[1],
        mix_total[0].reshape(mix_in.shape).astype(f32),
        mix_bias[0],
        mix_total[1].reshape(mix_in.shape).astype(f32),
        mix_bias[1],
        early[1],
        early[2],
        dense[0].T,
        lax.dynamic_slice_in_dim(early[3:7].reshape(-1), device * share, share),
        dense[1],
        early[0],
    )


def solution(mesh):
    return jax.shard_map(
        body,
        mesh=mesh,
        in_specs=(P("rows", "lon", None), P(), P("rows", "lon", None)) + (P(),) * 12,
        out_specs=(
            P("rows", "lon", None),
            P("rows", "lon", None),
            P(),
            P(),
            P(),
            P(),
            P(),
            P(),
            P(),
            P(),
            P(None, ("rows", "lon")),
            P(("rows", "lon")),
            P(("rows", "lon"), None),
            P(),
        ),
        check_vma=False,
    )
```
